32 devices in a mesh: heads: 4 (over z), experts: 8 (over y, x, core).
Axes of the slice: x: 2, y: 2, z: 4, core: 2. Of those that a mesh axis runs over, the one named last changes fastest.
Arguments:
- layer_input: bfloat16 [1024, 16, 1024], P('heads', 'experts'), may hold values from -6 to 6
- seq_lengths: int32 [16], P('experts'), may hold values from 256 to 1024, as said below
- expert_ids: int32 [1024, 16, 8], P('heads', 'experts'), may hold values from 0 to 31, all different within a row
- route_weight: float32 [1024, 16, 8], P('heads', 'experts'), may hold values from 0.06 to 0.25
- priority: int32 [1024, 16], P('heads', 'experts'), may hold values from 0 to 511, as said below
- attn_gain: float32 [1024], replicated, may hold values from 0.25 to 1.75
- moe_gain: float32 [1024], replicated, may hold values from 0.25 to 1.75
- query_matrix: bfloat16 [1024, 1024], P(None, 'heads'), may hold values from -0.375 to 0.375
- key_matrix: bfloat16 [1024, 512], P(None, 'heads'), may hold values from -0.1875 to 0.1875
- value_matrix: bfloat16 [1024, 512], P(None, 'heads'), may hold values from -0.1875 to 0.1875
- output_matrix: bfloat16 [1024, 1024], P('heads'), may hold values from -0.75 to 0.75
- expert_in: bfloat16 [32, 1024, 1024], P('experts'), may hold values from -0.1875 to 0.1875
- expert_down: bfloat16 [32, 512, 1024], P('experts'), may hold values from -1 to 1
- out_grad: bfloat16 [1024, 16, 1024], P('heads', 'experts'), may hold values from -6 to 6
Outputs:
- out: bfloat16 [1024, 16, 1024], P('heads', 'experts')
- x_grad: float32 [1024, 16, 1024], P('heads', 'experts')
- grad_attn_gain: float32 [1024], replicated
- grad_moe_gain: float32 [1024], replicated
- grad_query_weight: float32 [1024, 1024], P(None, 'heads')
- grad_key_weight: float32 [1024, 512], P(None, 'heads')
- grad_value_weight: float32 [1024, 512], P(None, 'heads')
- grad_output_weight: float32 [1024, 1024], P('heads')
- grad_expert_in: float32 [32, 1024, 1024], P('experts')
- grad_expert_down: float32 [32, 512, 1024], P('experts')
The draws below stay inside these ranges and needn't reach their ends.
Inputs may be any that keep to these rules, and one draw needn't show every extreme that they name: `seq_lengths`: in each group of 2 sequences that one index of experts holds, one sequence has the full length 1024. `priority`: among the tokens of one device (positions of one index of heads in the sequences of one index of experts), each value appears exactly once. `expert_ids`: the 8 experts of a token are different.
All inputs are finite; a program needn't handle non-finite values.
Results may differ from the reference program's by a relative error of at most 0.017.
The reference program's roundings to bfloat16 on the way count: a program that leaves them out, or rounds other values in their place, can miss the bound.
Values may be sent and summed in bfloat16 or wider, within the bound.
A program may use at most 256 MiB of HBM per device.

```python
import math
import jax
import jax.numpy as jnp
from jax import lax

MODEL_WIDTH = 1024
QUERY_HEADS = 16
KEY_VALUE_HEADS = 8
HEAD_SIZE = 64
FF = 512
EXPERTS = 32
TOPK = 8
PADDED_LENGTH = 1024
SEQ_GRP = 2
SEQUENCE_TOTAL = 16
SEG_DEV = 256
TOK_DEV = 512
CAP = 160
N_HEADS = 4
N_EXPERTS = 8


def draw_seq_lengths(key, part):
    key = jax.random.fold_in(key, 3)
    key_base, key_pick = jax.random.split(key)
    groups = SEQUENCE_TOTAL // SEQ_GRP
    base_length = jax.random.randint(key_base, (groups, SEQ_GRP), PADDED_LENGTH // 4, PADDED_LENGTH + 1)
    chosen = jax.random.randint(key_pick, (groups, 1), 0, SEQ_GRP)
    lengths_all = jnp.where(jnp.arange(SEQ_GRP)[None, :] == chosen, PADDED_LENGTH, base_length)
    return lengths_all.reshape(SEQUENCE_TOTAL).astype(jnp.int32)


def draw_priority(key, part):
    key = jax.random.fold_in(key, 7)
    row_blocks = PADDED_LENGTH // SEG_DEV
    seq_blocks = SEQUENCE_TOTAL // SEQ_GRP
    key_list = jax.random.split(key, row_blocks * seq_blocks)
    orders = jax.vmap(lambda single: jax.random.permutation(single, TOK_DEV))(key_list)
    orders = orders.reshape(row_blocks, seq_blocks, SEG_DEV, SEQ_GRP)
    orders = jnp.transpose(orders, (0, 2, 1, 3))
    return orders.reshape(PADDED_LENGTH, SEQUENCE_TOTAL).astype(jnp.int32)


def block_scale(rng, extent, cuts, smallest, high):
    factor_of, own = 1.0, jax.random.fold_in(rng, 6)
    for position, shards_of in cuts:
        heights = jnp.exp(jax.random.uniform(jax.random.fold_in(own, position), (shards_of,), jnp.float32, smallest / len(cuts), high / len(cuts)))
        factor_of = factor_of * jnp.repeat(heights, extent[position] // shards_of).reshape([-1 if axis == position else 1 for axis in range(len(extent))])
    return factor_of


def distinct(key, rows, amount, top, lift):
    ranking = jax.random.permutation(jax.random.fold_in(key, 1), amount)
    pull = ranking
    for power in range(3):
        pull = pull * pull // amount
    pull = pull * lift // amount
    tickets = jax.random.randint(jax.random.fold_in(key, 2), (rows, amount), 0, 4096) + pull
    sure = jax.random.permutation(jax.random.fold_in(key, 3), rows)[jnp.arange(amount) % rows]
    tickets = jnp.where(jnp.arange(rows)[:, None] == sure[None, :], 1 << 14, tickets)
    score = tickets * amount + jnp.arange(amount)
    return lax.top_k(score.astype(jnp.int32), top)[1].astype(jnp.int32)


def bell_draw(stream_key, dims, deviation, reach, cuts=(), kind=jnp.bfloat16):
    values = jax.random.normal(stream_key, dims, jnp.float32) * deviation
    if len(cuts) > 0:
        values = block_scale(stream_key, dims, cuts, -0.22, 0.18) * values
    return jnp.clip(values, min=-reach, max=reach).astype(kind)


def setup_inputs(seed: int = 0) -> dict:
    keys = jax.random.split(jax.random.key(seed), 15)
    return {
        "layer_input": bell_draw(keys[0], (PADDED_LENGTH, SEQUENCE_TOTAL, MODEL_WIDTH), 1.0, 6.0, ((0, 4), (1, 8))),
        "seq_lengths": draw_seq_lengths(jax.random.fold_in(keys[14], 71), 0),
        "expert_ids": distinct(keys[2], PADDED_LENGTH * SEQUENCE_TOTAL, EXPERTS, TOPK, 2048).reshape((PADDED_LENGTH, SEQUENCE_TOTAL, TOPK)),
        "route_weight": jnp.clip(jnp.exp(math.log(0.25) - 1.4271164 * jax.random.uniform(keys[3], (PADDED_LENGTH, SEQUENCE_TOTAL, TOPK), jnp.float32) ** block_scale(keys[3], (PADDED_LENGTH, SEQUENCE_TOTAL, TOPK), ((0, 4), (1, 8)), -0.2, 0.2)), 0.06, 0.25),
        "priority": draw_priority(jax.random.fold_in(keys[14], 71), 0),
        "attn_gain": jnp.clip(1.0 + 0.15 * jax.random.normal(keys[5], (MODEL_WIDTH,), jnp.float32), 0.25, 1.75),
        "moe_gain": jnp.clip(1.0 + 0.15 * jax.random.normal(keys[6], (MODEL_WIDTH,), jnp.float32), 0.25, 1.75),
        "query_matrix": bell_draw(keys[7], (MODEL_WIDTH, QUERY_HEADS * HEAD_SIZE), (MODEL_WIDTH // 4) ** -0.5, 0.375, ((1, 4),)),
        "key_matrix": bell_draw(keys[8], (MODEL_WIDTH, KEY_VALUE_HEADS * HEAD_SIZE), MODEL_WIDTH ** -0.5, 0.1875, ((1, 4),)),
        "value_matrix": bell_draw(keys[9], (MODEL_WIDTH, KEY_VALUE_HEADS * HEAD_SIZE), MODEL_WIDTH ** -0.5, 0.1875, ((1, 4),)),
        "output_matrix": bell_draw(keys[10], (QUERY_HEADS * HEAD_SIZE, MODEL_WIDTH), (QUERY_HEADS * HEAD_SIZE // 16) ** -0.5, 0.75, ((0, 4),)),
        "expert_in": bell_draw(keys[11], (EXPERTS, MODEL_WIDTH, 2 * FF), MODEL_WIDTH ** -0.5, 0.1875, ((0, 8),)),
        "expert_down": bell_draw(keys[12], (EXPERTS, FF, MODEL_WIDTH), (FF // 16) ** -0.5, 1.0, ((0, 8),)),
        "out_grad": bell_draw(keys[13], (PADDED_LENGTH, SEQUENCE_TOTAL, MODEL_WIDTH), 1.0, 6.0, ((0, 4), (1, 8))),
    }


epsilon = 1e-06
highest_precision = lax.Precision.HIGHEST

@jax.custom_vjp
def reduced_type(v):
    return lax.optimization_barrier(v.astype(jnp.bfloat16)).astype(jnp.float32)

@jax.custom_vjp
def reduced_backward(v):
    return v

def low_keep(v):
    return (reduced_type(v), None)

def low_pass(kept, grad):
    return (grad,)

def back_keep(v):
    return (v, None)

def back_low(kept, grad):
    return (reduced_type(grad),)
reduced_type.defvjp(low_keep, low_pass)
reduced_backward.defvjp(back_keep, back_low)

def rms_scale(values):
    return lax.rsqrt(lax.optimization_barrier(jnp.mean(values * values, axis=-1, keepdims=True)) + epsilon)

def rotary_tables(length, head_dim):
    half_dim = head_dim // 2
    frequency = jnp.exp(jnp.arange(half_dim, dtype=jnp.float32) * (-2.0 * math.log(10000.0) / head_dim))
    angles = jnp.arange(length, dtype=jnp.float32)[:, None] * frequency[None, :]
    return (jnp.cos(angles), jnp.sin(angles))

def apply_rotary(values, cosine_table, sine_table):
    half_dim = values.shape[-1] // 2
    lower_half = values[..., :half_dim]
    upper_half = values[..., half_dim:]
    return jnp.concatenate([lower_half * cosine_table - upper_half * sine_table, upper_half * cosine_table + lower_half * sine_table], axis=-1)

def block_slots(block_ids, block_order, block_live, expert_count, capacity):
    token_count, top_count = block_ids.shape
    ranked = jnp.zeros((token_count,), jnp.int32).at[block_order].set(jnp.arange(token_count, dtype=jnp.int32))
    sorted_ids = block_ids[ranked].reshape(-1).astype(jnp.int32)
    sorted_live = jnp.repeat(block_live[ranked], top_count)
    matches = ((sorted_ids[:, None] == jnp.arange(expert_count, dtype=jnp.int32)[None, :]) & sorted_live[:, None]).astype(jnp.int32)
    before = (jnp.cumsum(matches, axis=0) - matches).astype(jnp.int32)
    slot_sorted = lax.optimization_barrier(jnp.sum(before * matches, axis=1)).astype(jnp.int32)
    keep_sorted = sorted_live & (slot_sorted < capacity)
    target_sorted = jnp.where(keep_sorted, sorted_ids * capacity + slot_sorted, expert_count * capacity).astype(jnp.int32)
    target = target_sorted.reshape(token_count, top_count)[block_order]
    owners = jnp.full((expert_count * capacity + 1,), token_count, jnp.int32)
    owners = owners.at[target.reshape(-1)].set(jnp.repeat(jnp.arange(token_count, dtype=jnp.int32), top_count))
    return (target, owners[:expert_count * capacity])

def slot_weights(target, weights, slot_total):
    table = jnp.zeros((slot_total + 1,), weights.dtype).at[target.reshape(-1)].set(weights.reshape(-1))
    return table[:slot_total]

def device_blocks(values):
    tail = values.shape[2:]
    pieces = values.reshape((N_HEADS, PADDED_LENGTH // N_HEADS, N_EXPERTS, SEQ_GRP) + tail)
    pieces = jnp.moveaxis(pieces, 2, 1)
    return pieces.reshape((N_HEADS * N_EXPERTS, TOK_DEV) + tail)

def attend_one(query_seq, key_seq, value_seq, length_one):
    raw = reduced_backward(jnp.einsum('qgrd,kgd->grqk', query_seq, key_seq, precision=highest_precision))
    positions = jnp.arange(PADDED_LENGTH, dtype=jnp.int32)
    allowed = (positions[None, :] <= positions[:, None]) & (positions[None, :] < length_one)
    scores = jnp.where(allowed, raw * HEAD_SIZE ** (-0.5), -1e+30)
    probs = jax.nn.softmax(scores, axis=-1)
    return jnp.einsum('grqk,kgd->qgrd', reduced_type(probs), value_seq, precision=highest_precision)

def expert_rows(flat, index_one, win_one, wdown_one):
    rows_in = reduced_backward(flat[index_one])
    gate_up = reduced_backward(jnp.dot(rows_in, win_one, precision=highest_precision, preferred_element_type=jnp.float32))
    hidden = reduced_type(jax.nn.silu(gate_up[:, :FF]) * gate_up[:, FF:])
    return reduced_backward(reduced_type(jnp.dot(hidden, wdown_one, precision=highest_precision, preferred_element_type=jnp.float32)))

def reference(layer_input, seq_lengths, expert_ids, route_weight, priority, attn_gain, moe_gain, query_matrix, key_matrix, value_matrix, output_matrix, expert_in, expert_down, out_grad):
    group_width = QUERY_HEADS // KEY_VALUE_HEADS
    token_total = PADDED_LENGTH * SEQUENCE_TOTAL
    block_count = N_HEADS * N_EXPERTS
    positions = jnp.arange(PADDED_LENGTH, dtype=jnp.int32)
    live_all = positions[:, None] < seq_lengths[None, :]
    targets, owners = jax.vmap(lambda ids_one, order_one, live_one: block_slots(ids_one, order_one, live_one, EXPERTS, CAP))(device_blocks(expert_ids), device_blocks(priority), device_blocks(live_all))
    token_ids = device_blocks(jnp.arange(token_total, dtype=jnp.int32).reshape(PADDED_LENGTH, SEQUENCE_TOTAL))
    token_ids = jnp.concatenate([token_ids, jnp.full((block_count, 1), token_total, jnp.int32)], axis=1)
    global_owner = jnp.take_along_axis(token_ids, owners, axis=1)
    slot_weight = jax.vmap(lambda target_one, weight_one: slot_weights(target_one, weight_one, EXPERTS * CAP))(targets, device_blocks(route_weight))
    gather_index = global_owner.reshape(block_count, EXPERTS, CAP).transpose(1, 0, 2).reshape(EXPERTS, block_count * CAP)
    gather_weight = slot_weight.reshape(block_count, EXPERTS, CAP).transpose(1, 0, 2).reshape(EXPERTS, block_count * CAP)
    cosine_table, sine_table = rotary_tables(PADDED_LENGTH, HEAD_SIZE)

    def forward(inputs_f, gain_one, gain_two, query_weight_param, key_weight_param, value_weight_param, output_weight_param, w_in, w_down):
        attention_input = reduced_type(inputs_f * rms_scale(inputs_f) * gain_one)
        query_linear = reduced_backward(jnp.einsum('gro,ox->grx', attention_input, query_weight_param, precision=highest_precision))
        key_linear = reduced_backward(jnp.einsum('gro,ox->grx', attention_input, key_weight_param, precision=highest_precision))
        value_linear = reduced_backward(jnp.einsum('gro,ox->grx', attention_input, value_weight_param, precision=highest_precision))
        query_rotated = reduced_type(apply_rotary(query_linear.reshape(PADDED_LENGTH, SEQUENCE_TOTAL, KEY_VALUE_HEADS, group_width, HEAD_SIZE), cosine_table[:, None, None, None, :], sine_table[:, None, None, None, :]))
        key_rotated = reduced_type(apply_rotary(key_linear.reshape(PADDED_LENGTH, SEQUENCE_TOTAL, KEY_VALUE_HEADS, HEAD_SIZE), cosine_table[:, None, None, :], sine_table[:, None, None, :]))
        value_reduced = reduced_type(value_linear.reshape(PADDED_LENGTH, SEQUENCE_TOTAL, KEY_VALUE_HEADS, HEAD_SIZE))
        attended = lax.map(jax.checkpoint(lambda item: attend_one(item[0], item[1], item[2], item[3])), (jnp.moveaxis(query_rotated, 1, 0), jnp.moveaxis(key_rotated, 1, 0), jnp.moveaxis(value_reduced, 1, 0), seq_lengths))
        head_result = reduced_type(reduced_backward(jnp.moveaxis(attended, 0, 1).reshape(PADDED_LENGTH, SEQUENCE_TOTAL, QUERY_HEADS * HEAD_SIZE)))
        attention_path = reduced_backward(jnp.einsum('gwm,mr->gwr', head_result, output_weight_param, precision=highest_precision))
        mid = inputs_f + attention_path
        moe_in = reduced_type(mid * rms_scale(mid) * gain_two)
        flat = jnp.concatenate([moe_in.reshape(token_total, MODEL_WIDTH), jnp.zeros((1, MODEL_WIDTH), jnp.float32)], axis=0)

        def expert_step(running, item):
            index_one, weight_one, win_one, wdown_one = item
            rows = jax.checkpoint(expert_rows)(flat, index_one, win_one, wdown_one)
            return (running.at[index_one].add(weight_one[:, None] * rows), None)
        running, unused = lax.scan(expert_step, jnp.zeros((token_total + 1, MODEL_WIDTH), jnp.float32), (gather_index, gather_weight, w_in, w_down))
        moe_sum = running[:token_total].reshape(PADDED_LENGTH, SEQUENCE_TOTAL, MODEL_WIDTH)
        return mid + moe_sum
    result, pullback = jax.vjp(forward, layer_input.astype(jnp.float32), attn_gain, moe_gain, query_matrix.astype(jnp.float32), key_matrix.astype(jnp.float32), value_matrix.astype(jnp.float32), output_matrix.astype(jnp.float32), expert_in.astype(jnp.float32), expert_down.astype(jnp.float32))
    grads = pullback(out_grad.astype(jnp.float32))
    return (result.astype(jnp.bfloat16), grads[0], grads[1], grads[2], grads[3], grads[4], grads[5], grads[6], grads[7], grads[8])
```

```python
import functools
import math

import jax
import jax.numpy as jnp
from jax import lax
from jax.experimental import pallas as pl
from jax.experimental.pallas import tpu as pltpu
from jax.sharding import PartitionSpec as P

HEAD = 64
EXPERTS = 32
EPS = 1e-06
BF = jnp.bfloat16
F32 = jnp.float32
SCALE = HEAD ** (-0.5)
NEG = -1e30
VMEM = 60 * 1024 * 1024


def dot(a, b):
    return jnp.dot(a, b, preferred_element_type=F32)


def dot_nt(a, b):
    return lax.dot_general(a, b, (((1,), (1,)), ((), ())), preferred_element_type=F32)


def dot_tn(a, b):
    return lax.dot_general(a, b, (((0,), (0,)), ((), ())), preferred_element_type=F32)


def params(n):
    return pltpu.CompilerParams(
        dimension_semantics=("arbitrary",) * n, vmem_limit_bytes=VMEM
    )


def swap_halves(v):
    lane = lax.broadcasted_iota(jnp.int32, v.shape, 1)
    return jnp.where(lane % 64 < 32, pltpu.roll(v, 96, 1), pltpu.roll(v, 32, 1))


def attn_mask(offset, n, block, length):
    key = lax.broadcasted_iota(jnp.int32, (n, 2 * block), 0)
    query = lax.broadcasted_iota(jnp.int32, (n, 2 * block), 1)
    query = jnp.where(query >= block, query - block, query) + offset
    return (key <= query) & (key < length)


def two_heads(v):
    return jnp.concatenate([v[:, :HEAD], v[:, HEAD:]], axis=0)


def untwo(vt, block):
    return jnp.concatenate([vt[:, :block], vt[:, block:]], axis=0).T


def fwd_kernel(len_ref, x_ref, w_ref, cq, sq, ckv, skv, qkv_ref, head_ref, lse_ref):
    nh, _, seg, width = x_ref.shape
    full = nh * seg
    block = seg
    length = len_ref[pl.program_id(0)]
    lin = dot(x_ref[...].reshape(full, width), w_ref[0])
    ql, kvl = lin[:, :128], lin[:, 128:]
    q = (ql * cq[...] + swap_halves(ql) * sq[...]).astype(BF)
    kvr = kvl * ckv[...] + swap_halves(kvl) * skv[...]
    kv = kvr.astype(BF)
    qkv_ref[0, 0, :, :128] = q
    qkv_ref[0, 0, :, 128:] = kv
    k = kv[:, :HEAD]
    vt = kvr.T[HEAD:].astype(BF)
    for i in range(nh):
        n = (i + 1) * block
        q2 = two_heads(q[i * block : n])
        s = dot_nt(k[:n], q2)
        s = jnp.where(attn_mask(i * block, n, block, length), s * SCALE, NEG)
        m = jnp.max(s, axis=0, keepdims=True)
        e = jnp.exp(s - m)
        total = jnp.sum(e, axis=0, keepdims=True)
        p = (e * (1.0 / total)).astype(BF)
        lse_ref[0, 0, i : i + 1, :] = m + jnp.log(total)
        head_ref[i, 0] = untwo(dot(vt[:, :n], p), block).astype(BF)


def attn_forward(x, w, lengths, tables):
    nh, nseq, seg, width = x.shape
    groups = w.shape[0]
    full = nh * seg
    cq, sq, ckv, skv = tables
    tab = pl.BlockSpec((full, 128), lambda s, g: (0, 0))
    return pl.pallas_call(
        fwd_kernel,
        grid=(nseq, groups),
        in_specs=[
            pl.BlockSpec(memory_space=pltpu.SMEM),
            pl.BlockSpec((nh, 1, seg, width), lambda s, g: (0, s, 0, 0)),
            pl.BlockSpec((1, width, 256), lambda s, g: (g, 0, 0)),
            tab,
            tab,
            tab,
            tab,
        ],
        out_specs=[
            pl.BlockSpec((1, 1, full, 256), lambda s, g: (s, g, 0, 0)),
            pl.BlockSpec((nh, 1, seg, 128), lambda s, g: (0, s, 0, g)),
            pl.BlockSpec((1, 1, nh, 2 * seg), lambda s, g: (s, g, 0, 0)),
        ],
        out_shape=[
            jax.ShapeDtypeStruct((nseq, groups, full, 256), BF),
            jax.ShapeDtypeStruct((nh, nseq, seg, groups * 128), BF),
            jax.ShapeDtypeStruct((nseq, groups, nh, 2 * seg), F32),
        ],
        compiler_params=params(2),
        cost_estimate=pl.CostEstimate(flops=6 * 10**9, bytes_accessed=12 * 2**20, transcendentals=10**7),
        name="attn_forward",
    )(lengths, x, w, cq, sq, ckv, skv)


def bwd_kernel(len_ref, qkv_ref, do_ref, lse_ref, cq, sq, ckv, skv, out_ref, dkv_ref):
    nh, _, seg, _ = do_ref.shape
    full = nh * seg
    block = seg
    length = len_ref[pl.program_id(0)]
    q = qkv_ref[0, 0, :, :128]
    kv = qkv_ref[0, 0, :, 128:]
    k, v = kv[:, :HEAD], kv[:, HEAD:]
    kt = kv.astype(F32).T[:HEAD].astype(BF)
    dkv_ref[...] = jnp.zeros_like(dkv_ref)
    for i in range(nh):
        n = (i + 1) * block
        rows = pl.ds(i * block, block)
        q2 = two_heads(q[i * block : n])
        do2 = two_heads(do_ref[i, 0])
        s = dot_nt(k[:n], q2)
        p = jnp.exp(
            jnp.where(
                attn_mask(i * block, n, block, length),
                s * SCALE - lse_ref[0, 0, i : i + 1, :],
                NEG,
            )
        )
        dp = dot_nt(v[:n], do2)
        delta = jnp.sum(p * dp, axis=0, keepdims=True)
        ds = (p * (dp - delta) * SCALE).astype(BF)
        dkv_ref[:n, :HEAD] += dot(ds, q2)
        dkv_ref[:n, HEAD:] += dot(p.astype(BF), do2)
        dq = untwo(dot(kt[:, :n], ds), block)
        dq = dq * cq[rows, :] - swap_halves(dq) * sq[rows, :]
        out_ref[i, 0, :, :128] = dq.astype(BF)
    dkv = dkv_ref[...]
    dkv = (dkv * ckv[...] - swap_halves(dkv) * skv[...]).astype(BF)
    for i in range(nh):
        out_ref[i, 0, :, 128:] = dkv[i * block : (i + 1) * block]


def attn_backward(qkv, d_head, lse, lengths, tables):
    nseq, groups, full, _ = qkv.shape
    nh, _, seg, _ = d_head.shape
    cq, sq, ckv, skv = tables
    tab = pl.BlockSpec((full, 128), lambda s, g: (0, 0))
    return pl.pallas_call(
        bwd_kernel,
        grid=(nseq, groups),
        in_specs=[
            pl.BlockSpec(memory_space=pltpu.SMEM),
            pl.BlockSpec((1, 1, full, 256), lambda s, g: (s, g, 0, 0)),
            pl.BlockSpec((nh, 1, seg, 128), lambda s, g: (0, s, 0, g)),
            pl.BlockSpec((1, 1, nh, 2 * seg), lambda s, g: (s, g, 0, 0)),
            tab,
            tab,
            tab,
            tab,
        ],
        out_specs=pl.BlockSpec((nh, 1, seg, 256), lambda s, g: (0, s, 0, g)),
        out_shape=jax.ShapeDtypeStruct((nh, nseq, seg, groups * 256), BF),
        scratch_shapes=[pltpu.VMEM((full, 128), F32)],
        compiler_params=params(2),
        cost_estimate=pl.CostEstimate(flops=12 * 10**9, bytes_accessed=8 * 2**20, transcendentals=10**7),
        name="attn_backward",
    )(lengths, qkv, d_head, lse, cq, sq, ckv, skv)


def rotary_tables(length):
    half = HEAD // 2
    frequency = jnp.exp(jnp.arange(half, dtype=F32) * (-2.0 * math.log(10000.0) / HEAD))
    angles = jnp.arange(length, dtype=F32)[:, None] * frequency[None, :]
    cos, sin = jnp.cos(angles), jnp.sin(angles)
    c1 = jnp.concatenate([cos, cos], axis=1)
    s1 = jnp.concatenate([-sin, sin], axis=1)
    cq = jnp.concatenate([c1, c1], axis=1)
    sq = jnp.concatenate([s1, s1], axis=1)
    ckv = jnp.concatenate([c1, jnp.ones_like(c1)], axis=1)
    skv = jnp.concatenate([s1, jnp.zeros_like(s1)], axis=1)
    return cq, sq, ckv, skv


def pick_rows(slots, cap):
    tokens = slots.shape[1]
    index = lax.broadcasted_iota(jnp.int32, (cap, tokens), 0)
    return [index == slots[j : j + 1, :] for j in range(slots.shape[0])]


def gather_kernel(weighted, slot_ref, *refs):
    if weighted:
        weight_ref, tok_ref, out_ref = refs
    else:
        tok_ref, out_ref = refs[0], refs[-1]
    cap = out_ref.shape[2]
    hits = pick_rows(slot_ref[0], cap)
    rows = dot(jnp.concatenate([h.astype(F32) for h in hits], axis=0).astype(BF), tok_ref[0])
    for j, hit in enumerate(hits):
        part = rows[j * cap : (j + 1) * cap]
        if weighted:
            part = part * jnp.sum(jnp.where(hit, weight_ref[0, j : j + 1, :], 0.0), axis=1, keepdims=True)
        out_ref[j, 0] = part.astype(BF)


def gather_rows(slots, weights, tokens, cap):
    sources, here, count = slots.shape
    width = tokens.shape[-1]
    small = pl.BlockSpec((1, here, count), lambda s: (s, 0, 0))
    weighted = weights is not None
    return pl.pallas_call(
        functools.partial(gather_kernel, weighted),
        grid=(sources,),
        in_specs=[small] + [small] * weighted + [pl.BlockSpec((1, count, width), lambda s: (s, 0, 0))],
        out_specs=pl.BlockSpec((here, 1, cap, width), lambda s: (0, s, 0, 0)),
        out_shape=jax.ShapeDtypeStruct((here, sources, cap, width), BF),
        compiler_params=params(1),
        cost_estimate=pl.CostEstimate(
            flops=2 * sources * here * cap * count * width,
            bytes_accessed=2 * sources * width * (count + here * cap),
            transcendentals=0,
        ),
        name="gather_rows",
    )(*([slots] + [weights] * weighted + [tokens]))


def expert_kernel(steps, slot_ref, weight_ref, x_ref, d_ref, win_ref, wdown_ref,
                  out_ref, drow_ref, gin_ref, gdown_ref, hid_ref, dgu_ref, *acc):
    _, sources, cap, width = x_ref.shape
    ff = wdown_ref.shape[1]
    per = 2 if sources % 2 == 0 else 1
    win, wdown = win_ref[0], wdown_ref[0]
    for c in range(sources // per):
        rows = slice(c * per * cap, (c + 1) * per * cap)
        x = x_ref[0, c * per : (c + 1) * per].reshape(per * cap, width)
        d = d_ref[0, c * per : (c + 1) * per].reshape(per * cap, width)
        gu = dot(x, win)
        gate, up = gu[:, :ff], gu[:, ff:]
        sig = 1.0 / (1.0 + jnp.exp(-gate))
        act = gate * sig
        hidden = (act * up).astype(BF)
        hid_ref[rows, :] = hidden
        result = dot(hidden, wdown).astype(BF).astype(F32)
        for b in range(per):
            hit = pick_rows(slot_ref[c * per + b, 0], cap)[0]
            w = jnp.sum(jnp.where(hit, weight_ref[c * per + b, 0], 0.0), axis=1, keepdims=True)
            out_ref[0, c * per + b] = (result[b * cap : (b + 1) * cap] * w).astype(BF)
        dh = dot_nt(d, wdown)
        dgu_ref[rows, :ff] = (dh * up * (sig * (1.0 + gate * (1.0 - sig)))).astype(BF)
        dgu_ref[rows, ff:] = (dh * act).astype(BF)
        drow = dot_nt(dgu_ref[rows, :], win).astype(BF)
        for b in range(per):
            drow_ref[0, c * per + b] = drow[b * cap : (b + 1) * cap]
    x = x_ref[0].reshape(sources * cap, width)
    d = d_ref[0].reshape(sources * cap, width)
    gin = dot_tn(x, dgu_ref[...])
    gdown = dot_tn(hid_ref[...], d)
    if steps == 1:
        gin_ref[0] = gin.astype(BF)
        gdown_ref[0] = gdown.astype(BF)
    else:
        ain, adown = acc
        step = pl.program_id(1)

        @pl.when(step == 0)
        def _():
            ain[...] = jnp.zeros_like(ain)
            adown[...] = jnp.zeros_like(adown)

        ain[...] += gin
        adown[...] += gdown

        @pl.when(step == steps - 1)
        def _():
            gin_ref[0] = ain[...].astype(BF)
            gdown_ref[0] = adown[...].astype(BF)


def experts_call(first, count, slots, weights, x, d, win, wdown):
    _, sources, cap, width = x.shape
    tokens = slots.shape[-1]
    ff = wdown.shape[1]
    chunk = min(sources, 8)
    steps = sources // chunk
    small = pl.BlockSpec((chunk, 1, 1, tokens), lambda j, r: (r, first + j, 0, 0))
    rows = pl.BlockSpec((1, chunk, cap, width), lambda j, r: (first + j, r, 0, 0))
    rows_out = pl.BlockSpec((1, chunk, cap, width), lambda j, r: (j, r, 0, 0))
    scratch = [pltpu.VMEM((chunk * cap, ff), BF), pltpu.VMEM((chunk * cap, 2 * ff), BF)]
    if steps > 1:
        scratch += [pltpu.VMEM((width, 2 * ff), F32), pltpu.VMEM((ff, width), F32)]
    shape = jax.ShapeDtypeStruct((count, sources, cap, width), BF)
    return pl.pallas_call(
        functools.partial(expert_kernel, steps),
        grid=(count, steps),
        in_specs=[
            small,
            small,
            rows,
            rows,
            pl.BlockSpec((1, width, 2 * ff), lambda j, r: (first + j, 0, 0)),
            pl.BlockSpec((1, ff, width), lambda j, r: (first + j, 0, 0)),
        ],
        out_specs=[
            rows_out,
            rows_out,
            pl.BlockSpec((1, width, 2 * ff), lambda j, r: (j, 0, 0)),
            pl.BlockSpec((1, ff, width), lambda j, r: (j, 0, 0)),
        ],
        out_shape=[
            shape,
            shape,
            jax.ShapeDtypeStruct((count, width, 2 * ff), BF),
            jax.ShapeDtypeStruct((count, ff, width), BF),
        ],
        scratch_shapes=scratch,
        compiler_params=params(2),
        cost_estimate=pl.CostEstimate(
            flops=2 * count * sources * cap * width * ff * 9,
            bytes_accessed=8 * count * sources * cap * width + 12 * count * width * ff,
            transcendentals=count * sources * cap * ff,
        ),
        name="experts",
    )(slots[:, :, None, :], weights[:, :, None, :], x, d, win, wdown)


def combine_kernel(parts, slot_ref, *refs):
    row_refs, out_refs = refs[: 2 * parts], refs[2 * parts :]
    slots = slot_ref[0]
    count, here = slots.shape
    cap = row_refs[0].shape[2]
    lane = lax.broadcasted_iota(jnp.int32, (count, here * cap), 1)
    hot = None
    for j in range(here):
        col = slots[:, j : j + 1]
        hit = lane == jnp.where(col >= 0, col + j * cap, -1)
        hot = hit if hot is None else hot | hit
    hot = hot.astype(F32).astype(BF)
    for group, out_ref in zip((row_refs[:parts], row_refs[parts:]), out_refs):
        rows = jnp.concatenate([r[j, 0] for r in group for j in range(r.shape[0])], axis=0)
        out_ref[0] = dot(hot, rows).astype(BF)


def combine(slots_t, outs, drows):
    sources, count, here = slots_t.shape
    _, _, cap, width = outs[0].shape
    blocks = [pl.BlockSpec((o.shape[0], 1, cap, width), lambda s: (0, s, 0, 0)) for o in outs]
    shape = jax.ShapeDtypeStruct((sources, count, width), BF)
    spec = pl.BlockSpec((1, count, width), lambda s: (s, 0, 0))
    return pl.pallas_call(
        functools.partial(combine_kernel, len(outs)),
        grid=(sources,),
        in_specs=[pl.BlockSpec((1, count, here), lambda s: (s, 0, 0))] + blocks + blocks,
        out_specs=[spec, spec],
        out_shape=[shape, shape],
        compiler_params=params(1),
        cost_estimate=pl.CostEstimate(
            flops=4 * sources * here * cap * count * width,
            bytes_accessed=4 * sources * width * (count + here * cap),
            transcendentals=0,
        ),
        name="combine",
    )(slots_t, *outs, *drows)


def swap(x, bit, n):
    return lax.ppermute(x, "experts", [(i, i ^ bit) for i in range(n)])


def plane_gather(x, n):
    if n != 8:
        whole = lax.all_gather(x, "experts", axis=0)
        order = lax.axis_index("experts") ^ jnp.arange(n, dtype=jnp.int32)
        return whole[order]
    got = {0: x}
    for r in (2, 4, 6):
        got[r] = swap(x, r, n)
    for r in (0, 2, 4, 6):
        got[r + 1] = swap(got[r], 1, n)
    return jnp.stack([got[r] for r in range(n)], axis=0)


def plane_scatter(parts, n):
    if n != 8:
        order = lax.axis_index("experts") ^ jnp.arange(n, dtype=jnp.int32)
        return lax.psum_scatter(parts[order].astype(F32), "experts", scatter_dimension=0)
    odd = swap(parts[1::2], 1, n)
    both = [parts[2 * i].astype(F32) + odd[i].astype(F32) for i in range(4)]
    total = both[0]
    for i in (1, 2, 3):
        total = total + swap(both[i].astype(BF), 2 * i, n).astype(F32)
    return total


def heads_sum(x, z, nh):
    if nh != 4:
        return lax.psum(x.astype(F32), "heads")
    first = lax.ppermute(x, "heads", [(0, 1), (3, 2)])
    pair = (x.astype(F32) + first.astype(F32)).astype(BF)
    second = lax.ppermute(pair, "heads", [(1, 2), (2, 1)])
    total = (pair.astype(F32) + second.astype(F32)).astype(BF)
    third = lax.ppermute(total, "heads", [(1, 0), (2, 3)])
    return jnp.where((z == 1) | (z == 2), total, third).astype(F32)


def body(layer_input, seq_lengths, expert_ids, route_weight, priority, attn_gain, moe_gain,
         query_matrix, key_matrix, value_matrix, output_matrix, expert_in, expert_down, out_grad):
    seg, nseq, width = layer_input.shape
    nh, ne = lax.axis_size("heads"), lax.axis_size("experts")
    z, me = lax.axis_index("heads"), lax.axis_index("experts")
    top = expert_ids.shape[-1]
    tokens = seg * nseq
    groups = key_matrix.shape[1] // HEAD
    here = expert_in.shape[0]
    cap = (5 * tokens * top + 4 * EXPERTS - 1) // (4 * EXPERTS)

    def local(v):
        return jnp.swapaxes(v, 0, 1).reshape((tokens,) + v.shape[2:])

    def unlocal(v):
        return jnp.swapaxes(v.reshape((nseq, seg) + v.shape[1:]), 0, 1)

    ids = local(expert_ids)
    order = local(priority)
    weight = local(route_weight)
    position = z * seg + jnp.arange(seg, dtype=jnp.int32)
    live = (position[None, :] < seq_lengths[:, None]).reshape(tokens)
    match = ids.T[:, None, :] == jnp.arange(EXPERTS, dtype=jnp.int32)[None, :, None]
    weight_e = jnp.sum(jnp.where(match, weight.T[:, None, :], 0.0), axis=0)
    chosen = jnp.any(match, axis=0) & live[None, :]
    earlier = (order[:, None] < order[None, :]).astype(BF)
    before = dot(chosen.astype(BF), earlier)
    slot = jnp.where(chosen & (before < cap), before, -1.0)
    packed = jnp.stack([slot.reshape(ne, here, tokens), weight_e.reshape(ne, here, tokens)], axis=1)
    packed = lax.all_to_all(packed, "experts", split_axis=0, concat_axis=0, tiled=True)
    packed = packed[me ^ jnp.arange(ne, dtype=jnp.int32)]
    slots = packed[:, 0].astype(jnp.int32)
    weights = packed[:, 1]

    xf = local(layer_input).astype(F32)
    inv_one = lax.rsqrt(jnp.mean(xf * xf, axis=-1, keepdims=True) + EPS)
    attn_in = (xf * inv_one * attn_gain).astype(BF)
    gathered = lax.all_gather(attn_in.reshape(nseq, seg, width), "heads", axis=0)

    wq = query_matrix.reshape(width, groups, 128)
    wk = key_matrix.reshape(width, groups, HEAD)
    wv = value_matrix.reshape(width, groups, HEAD)
    w_local = jnp.concatenate([wq, wk, wv], axis=2)
    w_groups = jnp.transpose(w_local, (1, 0, 2))
    rows_in = width // ne
    rows_out = output_matrix.shape[0] // ne
    w_piece = lax.dynamic_slice_in_dim(w_local.reshape(width, groups * 256), me * rows_in, rows_in, 0)
    o_piece = lax.dynamic_slice_in_dim(output_matrix, me * rows_out, rows_out, 0)
    o_full = lax.all_gather(o_piece, ("heads", "experts"), axis=0, tiled=True)
    w_full = lax.all_gather(w_piece, ("heads", "experts"), axis=0, tiled=True)
    w_full = w_full.reshape(nh, width, groups * 256)

    tables = rotary_tables(nh * seg)
    qkv, heads_out, lse = attn_forward(gathered, w_groups, seq_lengths, tables)
    heads_in = lax.all_to_all(heads_out, "heads", split_axis=0, concat_axis=0, tiled=True)
    heads_in = heads_in.reshape(nh, tokens, groups * 128)
    o_parts = o_full.reshape(nh, groups * 128, width)
    branch = jnp.einsum("ztm,zmw->tw", heads_in, o_parts, preferred_element_type=F32)
    mid = xf + branch
    inv_two = lax.rsqrt(jnp.mean(mid * mid, axis=-1, keepdims=True) + EPS)
    moe_in = (mid * inv_two * moe_gain).astype(BF)

    grad = local(out_grad)
    grads_all = plane_gather(grad, ne)
    d_rows = gather_rows(slots, weights, grads_all, cap)
    tokens_all = plane_gather(moe_in, ne)
    x_rows = gather_rows(slots, None, tokens_all, cap)
    outs, drows, gins, gdowns = [], [], [], []
    for j in range(here):
        o, dr, gi, gd = experts_call(j, 1, slots, weights, x_rows, d_rows, expert_in, expert_down)
        outs.append(o)
        drows.append(dr)
        gins.append(heads_sum(gi, z, nh))
        gdowns.append(heads_sum(gd, z, nh))
    grad_in = jnp.concatenate(gins, axis=0)
    grad_down = jnp.concatenate(gdowns, axis=0)
    moe_parts, d_parts = combine(jnp.swapaxes(slots, 1, 2), outs, drows)
    d_moe = plane_scatter(d_parts, ne)
    moe_sum = plane_scatter(moe_parts, ne)
    out = (mid + moe_sum).astype(BF)

    gf = grad.astype(F32)
    zed = moe_gain * d_moe
    d_mid = gf + inv_two * zed - mid * (inv_two ** 3 * jnp.mean(zed * mid, axis=-1, keepdims=True))
    gain_two = jnp.sum(d_moe * mid * inv_two, axis=0)
    d_branch = d_mid.astype(BF)
    d_heads = jnp.einsum("tw,zmw->ztm", d_branch, o_parts, preferred_element_type=F32).astype(BF)
    d_heads = d_heads.reshape(nh, nseq, seg, groups * 128)
    d_heads = lax.all_to_all(d_heads, "heads", split_axis=0, concat_axis=0, tiled=True)
    o_partial = jnp.einsum("ztm,tw->zmw", heads_in, d_branch, preferred_element_type=F32)
    o_grad = lax.psum_scatter(o_partial, "heads", scatter_dimension=0)
    o_grad = lax.psum(o_grad, "experts")

    dqkv = attn_backward(qkv, d_heads, lse, seq_lengths, tables)
    w_partial = jnp.einsum("zsrm,zsrc->mc", gathered, dqkv, preferred_element_type=F32)
    back = lax.all_to_all(dqkv, "heads", split_axis=0, concat_axis=0, tiled=True)
    back = back.reshape(nh, tokens, groups * 256)
    d_attn = jnp.einsum("ztc,zmc->tm", back, w_full, preferred_element_type=F32)
    w_grad = lax.psum(w_partial, "experts").reshape(width, groups, 256)
    wed = attn_gain * d_attn
    x_grad = d_mid + inv_one * wed - xf * (inv_one ** 3 * jnp.mean(wed * xf, axis=-1, keepdims=True))
    gain_one = jnp.sum(d_attn * xf * inv_one, axis=0)
    gain_one, gain_two = lax.psum((gain_one, gain_two), ("heads", "experts"))
    return (
        unlocal(out),
        unlocal(x_grad),
        gain_one,
        gain_two,
        w_grad[:, :, :128].reshape(query_matrix.shape),
        w_grad[:, :, 128:192].reshape(key_matrix.shape),
        w_grad[:, :, 192:].reshape(value_matrix.shape),
        o_grad,
        grad_in,
        grad_down,
    )


def solution(mesh):
    rows = P("heads", "experts", None)
    in_specs = (
        rows,
        P("experts"),
        rows,
        rows,
        P("heads", "experts"),
        P(),
        P(),
        P(None, "heads"),
        P(None, "heads"),
        P(None, "heads"),
        P("heads", None),
        P("experts", None, None),
        P("experts", None, None),
        rows,
    )
    out_specs = (
        rows,
        rows,
        P(),
        P(),
        P(None, "heads"),
        P(None, "heads"),
        P(None, "heads"),
        P("heads", None),
        P("experts", None, None),
        P("experts", None, None),
    )
    return jax.shard_map(body, mesh=mesh, in_specs=in_specs, out_specs=out_specs, check_vma=False)
```

```python
import functools
import math

import jax
import jax.numpy as jnp
from jax import lax
from jax.experimental import pallas as pl
from jax.experimental.pallas import tpu as pltpu
from jax.sharding import PartitionSpec as P

HEAD = 64
EXPERTS = 32
EPS = 1e-06
BF = jnp.bfloat16
F32 = jnp.float32
SCALE = HEAD ** (-0.5)
NEG = -1e30
VMEM = 60 * 1024 * 1024
MESH = pl.DeviceIdType.MESH
DMA = pltpu.SemaphoreType.DMA


def dot(a, b):
    return jnp.dot(a, b, preferred_element_type=F32)


def dot_nt(a, b):
    return lax.dot_general(a, b, (((1,), (1,)), ((), ())), preferred_element_type=F32)


def dot_tn(a, b):
    return lax.dot_general(a, b, (((0,), (0,)), ((), ())), preferred_element_type=F32)


def params(n):
    return pltpu.CompilerParams(
        dimension_semantics=("arbitrary",) * n, vmem_limit_bytes=VMEM
    )


def swap_halves(v):
    lane = lax.broadcasted_iota(jnp.int32, v.shape, 1)
    return jnp.where(lane % 64 < 32, pltpu.roll(v, 96, 1), pltpu.roll(v, 32, 1))


def attn_mask(offset, n, block, length):
    key = lax.broadcasted_iota(jnp.int32, (n, 2 * block), 0)
    query = lax.broadcasted_iota(jnp.int32, (n, 2 * block), 1)
    query = jnp.where(query >= block, query - block, query) + offset
    return (key <= query) & (key < length)


def two_heads(v):
    return jnp.concatenate([v[:, :HEAD], v[:, HEAD:]], axis=0)


def untwo(vt, block):
    return jnp.concatenate([vt[:, :block], vt[:, block:]], axis=0).T


def fwd_kernel(len_ref, x_ref, w_ref, cq, sq, ckv, skv, qkv_ref, head_ref, lse_ref):
    nh, _, seg, width = x_ref.shape
    full = nh * seg
    block = seg
    length = len_ref[pl.program_id(0)]
    lin = dot(x_ref[...].reshape(full, width), w_ref[0])
    ql, kvl = lin[:, :128], lin[:, 128:]
    q = (ql * cq[...] + swap_halves(ql) * sq[...]).astype(BF)
    kvr = kvl * ckv[...] + swap_halves(kvl) * skv[...]
    kv = kvr.astype(BF)
    qkv_ref[0, 0, :, :128] = q
    qkv_ref[0, 0, :, 128:] = kv
    k = kv[:, :HEAD]
    vt = kvr.T[HEAD:].astype(BF)
    for i in range(nh):
        n = (i + 1) * block
        q2 = two_heads(q[i * block : n])
        s = dot_nt(k[:n], q2)
        s = jnp.where(attn_mask(i * block, n, block, length), s * SCALE, NEG)
        m = jnp.max(s, axis=0, keepdims=True)
        e = jnp.exp(s - m)
        total = jnp.sum(e, axis=0, keepdims=True)
        p = (e * (1.0 / total)).astype(BF)
        lse_ref[0, 0, i : i + 1, :] = m + jnp.log(total)
        head_ref[i, 0] = untwo(dot(vt[:, :n], p), block).astype(BF)


def attn_forward(x, w, lengths, tables):
    nh, nseq, seg, width = x.shape
    groups = w.shape[0]
    full = nh * seg
    cq, sq, ckv, skv = tables
    tab = pl.BlockSpec((full, 128), lambda s, g: (0, 0))
    return pl.pallas_call(
        fwd_kernel,
        grid=(nseq, groups),
        in_specs=[
            pl.BlockSpec(memory_space=pltpu.SMEM),
            pl.BlockSpec((nh, 1, seg, width), lambda s, g: (0, s, 0, 0)),
            pl.BlockSpec((1, width, 256), lambda s, g: (g, 0, 0)),
            tab,
            tab,
            tab,
            tab,
        ],
        out_specs=[
            pl.BlockSpec((1, 1, full, 256), lambda s, g: (s, g, 0, 0)),
            pl.BlockSpec((nh, 1, seg, 128), lambda s, g: (0, s, 0, g)),
            pl.BlockSpec((1, 1, nh, 2 * seg), lambda s, g: (s, g, 0, 0)),
        ],
        out_shape=[
            jax.ShapeDtypeStruct((nseq, groups, full, 256), BF),
            jax.ShapeDtypeStruct((nh, nseq, seg, groups * 128), BF),
            jax.ShapeDtypeStruct((nseq, groups, nh, 2 * seg), F32),
        ],
        compiler_params=params(2),
        cost_estimate=pl.CostEstimate(flops=6 * 10**9, bytes_accessed=12 * 2**20, transcendentals=10**7),
        name="attn_forward",
    )(lengths, x, w, cq, sq, ckv, skv)


def bwd_piece(q, kv, heads, lses, length, tables, dkv_ref, put):
    cq, sq, ckv, skv = tables
    full, block = q.shape[0], lses(0).shape[1] // 2
    k, v = kv[:, :HEAD], kv[:, HEAD:]
    kt = kv.astype(F32).T[:HEAD].astype(BF)
    dkv_ref[...] = jnp.zeros_like(dkv_ref)
    for i in range(full // block):
        n = (i + 1) * block
        rows = pl.ds(i * block, block)
        q2 = two_heads(q[i * block : n])
        do2 = two_heads(heads(i))
        s = dot_nt(k[:n], q2)
        p = jnp.exp(jnp.where(attn_mask(i * block, n, block, length), s * SCALE - lses(i), NEG))
        dp = dot_nt(v[:n], do2)
        delta = jnp.sum(p * dp, axis=0, keepdims=True)
        ds = (p * (dp - delta) * SCALE).astype(BF)
        dkv_ref[:n, :HEAD] += dot(ds, q2)
        dkv_ref[:n, HEAD:] += dot(p.astype(BF), do2)
        dq = untwo(dot(kt[:, :n], ds), block)
        dq = dq * cq[rows, :] - swap_halves(dq) * sq[rows, :]
        put(i, 0, dq.astype(BF))
    dkv = dkv_ref[...]
    dkv = (dkv * ckv[...] - swap_halves(dkv) * skv[...]).astype(BF)
    for i in range(full // block):
        put(i, 128, dkv[i * block : (i + 1) * block])


def bwd_kernel(len_ref, qkv_ref, do_ref, lse_ref, cq, sq, ckv, skv, out_ref, dkv_ref):
    def put(i, lo, v):
        out_ref[i, 0, :, lo : lo + 128] = v

    bwd_piece(
        qkv_ref[0, 0, :, :128],
        qkv_ref[0, 0, :, 128:],
        lambda i: do_ref[i, 0],
        lambda i: lse_ref[0, 0, i : i + 1, :],
        len_ref[pl.program_id(0)],
        (cq, sq, ckv, skv),
        dkv_ref,
        put,
    )


def attn_backward(qkv, d_head, lse, lengths, tables):
    nseq, groups, full, _ = qkv.shape
    nh, _, seg, _ = d_head.shape
    cq, sq, ckv, skv = tables
    tab = pl.BlockSpec((full, 128), lambda s, g: (0, 0))
    return pl.pallas_call(
        bwd_kernel,
        grid=(nseq, groups),
        in_specs=[
            pl.BlockSpec(memory_space=pltpu.SMEM),
            pl.BlockSpec((1, 1, full, 256), lambda s, g: (s, g, 0, 0)),
            pl.BlockSpec((nh, 1, seg, 128), lambda s, g: (0, s, 0, g)),
            pl.BlockSpec((1, 1, nh, 2 * seg), lambda s, g: (s, g, 0, 0)),
            tab,
            tab,
            tab,
            tab,
        ],
        out_specs=pl.BlockSpec((nh, 1, seg, 256), lambda s, g: (0, s, 0, g)),
        out_shape=jax.ShapeDtypeStruct((nh, nseq, seg, groups * 256), BF),
        scratch_shapes=[pltpu.VMEM((full, 128), F32)],
        compiler_params=params(2),
        cost_estimate=pl.CostEstimate(flops=12 * 10**9, bytes_accessed=8 * 2**20, transcendentals=10**7),
        name="attn_backward",
    )(lengths, qkv, d_head, lse, cq, sq, ckv, skv)


def rotary_tables(length):
    half = HEAD // 2
    frequency = jnp.exp(jnp.arange(half, dtype=F32) * (-2.0 * math.log(10000.0) / HEAD))
    angles = jnp.arange(length, dtype=F32)[:, None] * frequency[None, :]
    cos, sin = jnp.cos(angles), jnp.sin(angles)
    c1 = jnp.concatenate([cos, cos], axis=1)
    s1 = jnp.concatenate([-sin, sin], axis=1)
    cq = jnp.concatenate([c1, c1], axis=1)
    sq = jnp.concatenate([s1, s1], axis=1)
    ckv = jnp.concatenate([c1, jnp.ones_like(c1)], axis=1)
    skv = jnp.concatenate([s1, jnp.zeros_like(s1)], axis=1)
    return cq, sq, ckv, skv


def pick_rows(slots, cap):
    tokens = slots.shape[1]
    index = lax.broadcasted_iota(jnp.int32, (cap, tokens), 0)
    return [index == slots[j : j + 1, :] for j in range(slots.shape[0])]


def gather_kernel(weighted, slot_ref, *refs):
    if weighted:
        weight_ref, tok_ref, out_ref = refs
    else:
        tok_ref, out_ref = refs[0], refs[-1]
    cap = out_ref.shape[2]
    hits = pick_rows(slot_ref[0], cap)
    rows = dot(jnp.concatenate([h.astype(F32) for h in hits], axis=0).astype(BF), tok_ref[0])
    for j, hit in enumerate(hits):
        part = rows[j * cap : (j + 1) * cap]
        if weighted:
            part = part * jnp.sum(jnp.where(hit, weight_ref[0, j : j + 1, :], 0.0), axis=1, keepdims=True)
        out_ref[j, 0] = part.astype(BF)


def gather_rows(slots, weights, tokens, cap):
    sources, here, count = slots.shape
    width = tokens.shape[-1]
    small = pl.BlockSpec((1, here, count), lambda s: (s, 0, 0))
    weighted = weights is not None
    return pl.pallas_call(
        functools.partial(gather_kernel, weighted),
        grid=(sources,),
        in_specs=[small] + [small] * weighted + [pl.BlockSpec((1, count, width), lambda s: (s, 0, 0))],
        out_specs=pl.BlockSpec((here, 1, cap, width), lambda s: (0, s, 0, 0)),
        out_shape=jax.ShapeDtypeStruct((here, sources, cap, width), BF),
        compiler_params=params(1),
        cost_estimate=pl.CostEstimate(
            flops=2 * sources * here * cap * count * width,
            bytes_accessed=2 * sources * width * (count + here * cap),
            transcendentals=0,
        ),
        name="gather_rows",
    )(*([slots] + [weights] * weighted + [tokens]))


def expert_kernel(steps, slot_ref, weight_ref, x_ref, d_ref, win_ref, wdown_ref,
                  out_ref, drow_ref, grad_ref, hid_ref, dgu_ref, *acc):
    _, sources, cap, width = x_ref.shape
    ff = wdown_ref.shape[1]
    per = 2 if sources % 2 == 0 else 1
    win, wdown = win_ref[0], wdown_ref[0]
    for c in range(sources // per):
        rows = slice(c * per * cap, (c + 1) * per * cap)
        x = x_ref[0, c * per : (c + 1) * per].reshape(per * cap, width)
        d = d_ref[0, c * per : (c + 1) * per].reshape(per * cap, width)
        gu = dot(x, win)
        gate, up = gu[:, :ff], gu[:, ff:]
        sig = 1.0 / (1.0 + jnp.exp(-gate))
        act = gate * sig
        hidden = (act * up).astype(BF)
        hid_ref[rows, :] = hidden
        result = dot(hidden, wdown).astype(BF).astype(F32)
        for b in range(per):
            hit = pick_rows(slot_ref[c * per + b, 0], cap)[0]
            w = jnp.sum(jnp.where(hit, weight_ref[c * per + b, 0], 0.0), axis=1, keepdims=True)
            out_ref[0, c * per + b] = (result[b * cap : (b + 1) * cap] * w).astype(BF)
        dh = dot_nt(d, wdown)
        dgu_ref[rows, :ff] = (dh * up * (sig * (1.0 + gate * (1.0 - sig)))).astype(BF)
        dgu_ref[rows, ff:] = (dh * act).astype(BF)
        drow = dot_nt(dgu_ref[rows, :], win).astype(BF)
        for b in range(per):
            drow_ref[0, c * per + b] = drow[b * cap : (b + 1) * cap]
    x = x_ref[0].reshape(sources * cap, width)
    d = d_ref[0].reshape(sources * cap, width)
    gin = dot_tn(x, dgu_ref[...])
    gdown = dot_tn(hid_ref[...], d)
    if steps == 1:
        grad_ref[0, :width] = gin.astype(BF)
        grad_ref[0, width:] = gdown.astype(BF)
    else:
        ain, adown = acc
        step = pl.program_id(1)

        @pl.when(step == 0)
        def _():
            ain[...] = jnp.zeros_like(ain)
            adown[...] = jnp.zeros_like(adown)

        ain[...] += gin
        adown[...] += gdown

        @pl.when(step == steps - 1)
        def _():
            grad_ref[0, :width] = ain[...].astype(BF)
            grad_ref[0, width:] = adown[...].astype(BF)


def experts_call(slots, weights, x, d, win, wdown):
    count, sources, cap, width = x.shape
    tokens = slots.shape[-1]
    ff = wdown.shape[1]
    chunk = min(sources, 8)
    steps = sources // chunk
    small = pl.BlockSpec((chunk, 1, 1, tokens), lambda j, r: (r, j, 0, 0))
    rows = pl.BlockSpec((1, chunk, cap, width), lambda j, r: (j, r, 0, 0))
    rows_out = pl.BlockSpec((1, chunk, cap, width), lambda j, r: (j, r, 0, 0))
    scratch = [pltpu.VMEM((chunk * cap, ff), BF), pltpu.VMEM((chunk * cap, 2 * ff), BF)]
    if steps > 1:
        scratch += [pltpu.VMEM((width, 2 * ff), F32), pltpu.VMEM((ff, width), F32)]
    shape = jax.ShapeDtypeStruct((count, sources, cap, width), BF)
    return pl.pallas_call(
        functools.partial(expert_kernel, steps),
        grid=(count, steps),
        in_specs=[
            small,
            small,
            rows,
            rows,
            pl.BlockSpec((1, width, 2 * ff), lambda j, r: (j, 0, 0)),
            pl.BlockSpec((1, ff, width), lambda j, r: (j, 0, 0)),
        ],
        out_specs=[
            rows_out,
            rows_out,
            pl.BlockSpec((1, width + ff, width), lambda j, r: (j, 0, 0)),
        ],
        out_shape=[
            shape,
            shape,
            jax.ShapeDtypeStruct((count, width + ff, width), BF),
        ],
        scratch_shapes=scratch,
        compiler_params=params(2),
        cost_estimate=pl.CostEstimate(
            flops=2 * count * sources * cap * width * ff * 9,
            bytes_accessed=8 * count * sources * cap * width + 12 * count * width * ff,
            transcendentals=count * sources * cap * ff,
        ),
        name="experts",
    )(slots[:, :, None, :], weights[:, :, None, :], x, d, win, wdown)


def combine_kernel(slot_ref, row_ref, out_ref):
    slots = slot_ref[0]
    count, here = slots.shape
    cap = row_ref.shape[2]
    lane = lax.broadcasted_iota(jnp.int32, (count, here * cap), 1)
    hot = None
    for j in range(here):
        col = slots[:, j : j + 1]
        hit = lane == jnp.where(col >= 0, col + j * cap, -1)
        hot = hit if hot is None else hot | hit
    hot = hot.astype(F32).astype(BF)
    out_ref[0] = dot(hot, row_ref[...].reshape(here * cap, row_ref.shape[3])).astype(BF)


def combine(slots_t, rows):
    sources, count, here = slots_t.shape
    _, _, cap, width = rows.shape
    return pl.pallas_call(
        combine_kernel,
        grid=(sources,),
        in_specs=[
            pl.BlockSpec((1, count, here), lambda s: (s, 0, 0)),
            pl.BlockSpec((here, 1, cap, width), lambda s: (0, s, 0, 0)),
        ],
        out_specs=pl.BlockSpec((1, count, width), lambda s: (s, 0, 0)),
        out_shape=jax.ShapeDtypeStruct((sources, count, width), BF),
        compiler_params=params(1),
        cost_estimate=pl.CostEstimate(
            flops=2 * sources * here * cap * count * width,
            bytes_accessed=2 * sources * width * (count + here * cap),
            transcendentals=0,
        ),
        name="combine",
    )(slots_t, rows)


def swap(x, bit, n):
    return lax.ppermute(x, "experts", [(i, i ^ bit) for i in range(n)])


def plane_gather(x, n):
    if n != 8:
        whole = lax.all_gather(x, "experts", axis=0)
        order = lax.axis_index("experts") ^ jnp.arange(n, dtype=jnp.int32)
        return whole[order]
    got = {0: x}
    for r in (2, 4, 6):
        got[r] = swap(x, r, n)
    for r in (0, 2, 4, 6):
        got[r + 1] = swap(got[r], 1, n)
    return jnp.stack([got[r] for r in range(n)], axis=0)


def plane_scatter(parts, n):
    if n != 8:
        order = lax.axis_index("experts") ^ jnp.arange(n, dtype=jnp.int32)
        return lax.psum_scatter(parts[order].astype(F32), "experts", scatter_dimension=0)
    odd = swap(parts[1::2], 1, n)
    both = [parts[2 * i].astype(F32) + odd[i].astype(F32) for i in range(4)]
    total = both[0]
    for i in (1, 2, 3):
        total = total + swap(both[i].astype(BF), 2 * i, n).astype(F32)
    return total


def heads_sum(x, z, nh):
    if nh != 4:
        return lax.psum(x.astype(F32), "heads")
    first = lax.ppermute(x, "heads", [(0, 1), (3, 2)])
    pair = (x.astype(F32) + first.astype(F32)).astype(BF)
    second = lax.ppermute(pair, "heads", [(1, 2), (2, 1)])
    total = (pair.astype(F32) + second.astype(F32)).astype(BF)
    third = lax.ppermute(total, "heads", [(1, 0), (2, 3)])
    return jnp.where((z == 1) | (z == 2), total, third).astype(F32)


CHUNK = 256
LAG = 3


def remote(src, dst, send, recv, axis, index):
    return pltpu.make_async_remote_copy(
        src_ref=src, dst_ref=dst, send_sem=send, recv_sem=recv,
        device_id={axis: index}, device_id_type=MESH,
    )


def greet(nh, masks):
    z, me = lax.axis_index("heads"), lax.axis_index("experts")
    bar = pltpu.get_barrier_semaphore()
    for d in range(1, nh):
        pl.semaphore_signal(bar, inc=1, device_id={"heads": lax.rem(z + d, nh)}, device_id_type=MESH)
    for r in masks:
        pl.semaphore_signal(bar, inc=1, device_id={"experts": me ^ r}, device_id_type=MESH)
    pl.semaphore_wait(bar, nh - 1 + len(masks))


class Chain:
    def __init__(self, src, out, scratch, first, count):
        self.src, self.out, self.first, self.count = src, out, first, count
        self.a, self.b, self.buf, self.s1, self.r1, self.s2, self.r2, self.ls, self.os = scratch
        z = lax.axis_index("heads")
        self.mid = (z == 1) | (z == 2)
        self.outer = jnp.where(z == 0, 1, jnp.where(z == 1, 0, jnp.where(z == 2, 3, 2)))
        self.inner = jnp.where(z == 1, 2, jnp.where(z == 2, 1, z))

    def piece(self, k):
        return self.src.at[pl.ds((self.first + k) * CHUNK, CHUNK)]

    def load(self, k):
        return pltpu.make_async_copy(self.piece(k), self.buf.at[lax.rem(k, 2)], self.ls.at[lax.rem(k, 2)])

    def store(self, ref, k):
        return pltpu.make_async_copy(ref.at[k], self.out.at[pl.ds(k * CHUNK, CHUNK)], self.os.at[k])

    def up(self, k):
        return remote(self.piece(k), self.a.at[k], self.s1.at[k], self.r1.at[k], "heads", self.outer)

    def across(self, k):
        return remote(self.a.at[k], self.b.at[k], self.s2.at[k], self.r2.at[k], "heads", self.inner)

    def down(self, k):
        return remote(self.b.at[k], self.a.at[k], self.s1.at[k], self.r1.at[k], "heads", self.outer)

    def begin(self):
        @pl.when(self.mid)
        def _():
            self.load(0).start()

    def steps(self):
        return self.count + LAG

    def step(self, k):
        n = self.count

        @pl.when(self.mid)
        def _():
            @pl.when(k < n)
            def _():
                @pl.when(k + 1 < n)
                def _():
                    self.load(k + 1).start()

                self.load(k).wait()
                self.up(k).wait_recv()
                own = self.buf[lax.rem(k, 2)].astype(F32)
                self.a[k] = (self.a[k].astype(F32) + own).astype(BF)
                self.across(k).start()

            @pl.when((k >= 1) & (k <= n))
            def _():
                j = k - 1
                self.across(j).wait_recv()
                self.b[j] = (self.a[j].astype(F32) + self.b[j].astype(F32)).astype(BF)
                self.down(j).start()
                self.store(self.b, j).start()

        @pl.when(jnp.logical_not(self.mid))
        def _():
            @pl.when(k < n)
            def _():
                @pl.when(k >= LAG)
                def _():
                    self.up(k - LAG).wait_send()

                self.up(k).start()

            @pl.when(k >= LAG)
            def _():
                j = k - LAG
                self.down(j).wait_recv()
                self.store(self.a, j).start()

    def run(self, first, last):
        @pl.loop(first, last)
        def _(k):
            self.step(k)

    def finish(self):
        n = self.count

        @pl.when(self.mid)
        def _():
            @pl.loop(0, n)
            def _(k):
                self.across(k).wait_send()
                self.down(k).wait_send()
                self.store(self.b, k).wait()

        @pl.when(jnp.logical_not(self.mid))
        def _():
            @pl.loop(n - LAG, n)
            def _(k):
                self.up(k).wait_send()

            @pl.loop(0, n)
            def _(k):
                self.store(self.a, k).wait()


def chain_scratch(count, width):
    return [
        pltpu.VMEM((count, CHUNK, width), BF),
        pltpu.VMEM((count, CHUNK, width), BF),
        pltpu.VMEM((2, CHUNK, width), BF),
        DMA((count,)),
        DMA((count,)),
        DMA((count,)),
        DMA((count,)),
        DMA((2,)),
        DMA((count,)),
    ]


def middle_kernel(count, len_ref, sum_ref, parts_ref, mid_ref, grad_ref, gain_ref, o_ref, qkv_ref, lse_ref,
                  cq, sq, ckv, skv, total_ref, dmid_ref, dbranch_ref, gtwo_ref, dqkv_ref,
                  c_buf, e_buf, f_buf, hs, hr, dmoe, dkv, cs, cr, fs, fr, hss, hrs, *chain):
    nh, nseq, seg, _ = dqkv_ref.shape
    groups = qkv_ref.shape[1]
    tokens = nseq * seg
    z, me = lax.axis_index("heads"), lax.axis_index("experts")
    chain = Chain(sum_ref, total_ref, chain, 0, count)
    greet(nh, (1, 2, 4, 6))

    def core(i):
        return remote(parts_ref.at[2 * i + 1], c_buf.at[i], cs.at[i], cr.at[i], "experts", me ^ 1)

    def chip(i):
        return remote(e_buf.at[i - 1], f_buf.at[i - 1], fs.at[i - 1], fr.at[i - 1], "experts", me ^ (2 * i))

    order = (3, 1, 2)
    for i in order + (0,):
        core(i).start()
    chain.begin()
    chain.run(0, 1)
    for i in order:
        core(i).wait_recv()
        e_buf[i - 1] = (parts_ref[2 * i].astype(F32) + c_buf[i].astype(F32)).astype(BF)
        chip(i).start()
    chain.run(1, 2)
    core(0).wait_recv()
    dmoe[...] = parts_ref[0].astype(F32) + c_buf[0].astype(F32)
    chain.run(2, 5)
    for i in order:
        chip(i).wait_recv()

    gtwo_ref[...] = jnp.zeros_like(gtwo_ref)
    rows_at = 128

    @pl.loop(0, tokens // rows_at)
    def _(i):
        rows = pl.ds(i * rows_at, rows_at)
        d = dmoe[rows]
        for r in range(3):
            d = d + f_buf[r, rows].astype(F32)
        m = mid_ref[rows]
        inv = lax.rsqrt(jnp.mean(m * m, axis=-1, keepdims=True) + EPS)
        zed = gain_ref[...] * d
        dm = grad_ref[rows].astype(F32) + inv * zed - m * (inv * inv * inv * jnp.mean(zed * m, axis=-1, keepdims=True))
        gtwo_ref[...] += jnp.sum(d * m * inv, axis=0, keepdims=True)
        dmid_ref[rows] = dm
        db = dm.astype(BF)
        dbranch_ref[rows] = db
        for h in range(nh):
            hs[h, rows] = dot_nt(db, o_ref[h]).astype(BF)

    def send(d):
        to = lax.rem(z + d, nh)
        return remote(hs.at[to], hr.at[z], hss.at[d], hrs.at[d], "heads", to)

    def arrive(d):
        src = lax.rem(z + nh - d, nh)
        return remote(hs.at[src], hr.at[src], hss.at[d], hrs.at[d], "heads", src)

    for d in range(1, nh):
        send(d).start()
    hr[pl.ds(z, 1)] = hs[pl.ds(z, 1)]
    chain.run(5, 8)
    for d in range(1, nh):
        arrive(d).wait_recv()

    @pl.loop(0, nseq)
    def _(s):
        length = len_ref[s]
        for g in range(groups):
            def put(i, lo, v):
                dqkv_ref[i, s, :, g * 256 + lo : g * 256 + lo + 128] = v

            bwd_piece(
                qkv_ref[s, g, :, :128],
                qkv_ref[s, g, :, 128:],
                lambda i: hr[i, pl.ds(s * seg, seg), g * 128 : (g + 1) * 128],
                lambda i: lse_ref[s, g, i : i + 1, :],
                length,
                (cq, sq, ckv, skv),
                dkv,
                put,
            )
        chain.step(8 + s)

    chain.run(8 + nseq, chain.steps())
    chain.finish()
    for i in range(4):
        core(i).wait_send()
    for i in order:
        chip(i).wait_send()
    for d in range(1, nh):
        send(d).wait_send()


def middle(count, lengths, sums, parts, mid, grad, gain, o_parts, qkv, lse, tables):
    nseq, groups, full, _ = qkv.shape
    nh = o_parts.shape[0]
    tokens, width = mid.shape
    seg = tokens // nseq
    vmem = pl.BlockSpec(memory_space=pltpu.VMEM)
    hbm = pl.BlockSpec(memory_space=pl.ANY)
    heads = (nh, tokens, groups * 128)
    return pl.pallas_call(
        functools.partial(middle_kernel, count),
        in_specs=[pl.BlockSpec(memory_space=pltpu.SMEM), hbm] + [vmem] * 11,
        out_specs=[hbm] + [vmem] * 4,
        out_shape=[
            jax.ShapeDtypeStruct((count * CHUNK, width), BF),
            jax.ShapeDtypeStruct((tokens, width), F32),
            jax.ShapeDtypeStruct((tokens, width), BF),
            jax.ShapeDtypeStruct((1, width), F32),
            jax.ShapeDtypeStruct((nh, nseq, seg, groups * 256), BF),
        ],
        scratch_shapes=[
            pltpu.VMEM((4, tokens, width), BF),
            pltpu.VMEM((3, tokens, width), BF),
            pltpu.VMEM((3, tokens, width), BF),
            pltpu.VMEM(heads, BF),
            pltpu.VMEM(heads, BF),
            pltpu.VMEM((tokens, width), F32),
            pltpu.VMEM((full, 128), F32),
            DMA((4,)),
            DMA((4,)),
            DMA((3,)),
            DMA((3,)),
            DMA((nh,)),
            DMA((nh,)),
        ]
        + chain_scratch(count, width),
        compiler_params=pltpu.CompilerParams(
            collective_id=1, has_side_effects=True, vmem_limit_bytes=VMEM
        ),
        cost_estimate=pl.CostEstimate(flops=10**11, bytes_accessed=30 * 2**20, transcendentals=10**7),
        name="middle",
    )(lengths, sums, parts, mid, grad, gain, o_parts, qkv, lse, *tables)


def last_kernel(first, count, sum_ref, parts_ref, total_ref, got_ref, ps, pr, *chain):
    ne = parts_ref.shape[0]
    me = lax.axis_index("experts")
    chain = Chain(sum_ref, total_ref, chain, first, count)
    greet(lax.axis_size("heads"), tuple(range(1, ne)))

    def part(r):
        return remote(parts_ref.at[r], got_ref.at[r - 1], ps.at[r], pr.at[r], "experts", me ^ r)

    chain.begin()
    for r in range(ne - 1, 0, -1):
        part(r).start()
    chain.run(0, chain.steps())
    chain.finish()
    for r in range(1, ne):
        part(r).wait()


def last(first, count, sums, parts):
    ne, tokens, width = parts.shape
    hbm = pl.BlockSpec(memory_space=pl.ANY)
    return pl.pallas_call(
        functools.partial(last_kernel, first, count),
        in_specs=[hbm, hbm],
        out_specs=[hbm, hbm],
        out_shape=[
            jax.ShapeDtypeStruct((count * CHUNK, width), BF),
            jax.ShapeDtypeStruct((ne - 1, tokens, width), BF),
        ],
        scratch_shapes=[DMA((ne,)), DMA((ne,))] + chain_scratch(count, width),
        compiler_params=pltpu.CompilerParams(
            collective_id=2, has_side_effects=True, vmem_limit_bytes=VMEM
        ),
        cost_estimate=pl.CostEstimate(flops=2 * 10**11, bytes_accessed=30 * 2**20, transcendentals=0),
        name="last",
    )(sums, parts)


def body(layer_input, seq_lengths, expert_ids, route_weight, priority, attn_gain, moe_gain,
         query_matrix, key_matrix, value_matrix, output_matrix, expert_in, expert_down, out_grad):
    seg, nseq, width = layer_input.shape
    nh, ne = lax.axis_size("heads"), lax.axis_size("experts")
    z, me = lax.axis_index("heads"), lax.axis_index("experts")
    top = expert_ids.shape[-1]
    tokens = seg * nseq
    groups = key_matrix.shape[1] // HEAD
    here = expert_in.shape[0]
    cap = (5 * tokens * top + 4 * EXPERTS - 1) // (4 * EXPERTS)

    def local(v):
        return jnp.swapaxes(v, 0, 1).reshape((tokens,) + v.shape[2:])

    def unlocal(v):
        return jnp.swapaxes(v.reshape((nseq, seg) + v.shape[1:]), 0, 1)

    ids = local(expert_ids)
    order = local(priority)
    weight = local(route_weight)
    position = z * seg + jnp.arange(seg, dtype=jnp.int32)
    live = (position[None, :] < seq_lengths[:, None]).reshape(tokens)
    match = ids.T[:, None, :] == jnp.arange(EXPERTS, dtype=jnp.int32)[None, :, None]
    weight_e = jnp.sum(jnp.where(match, weight.T[:, None, :], 0.0), axis=0)
    chosen = jnp.any(match, axis=0) & live[None, :]
    earlier = (order[:, None] < order[None, :]).astype(BF)
    before = dot(chosen.astype(BF), earlier)
    slot = jnp.where(chosen & (before < cap), before, -1.0)
    packed = jnp.stack([slot.reshape(ne, here, tokens), weight_e.reshape(ne, here, tokens)], axis=1)
    packed = lax.all_to_all(packed, "experts", split_axis=0, concat_axis=0, tiled=True)
    packed = packed[me ^ jnp.arange(ne, dtype=jnp.int32)]
    slots = packed[:, 0].astype(jnp.int32)
    weights = packed[:, 1]

    xf = local(layer_input).astype(F32)
    inv_one = lax.rsqrt(jnp.mean(xf * xf, axis=-1, keepdims=True) + EPS)
    attn_in = (xf * inv_one * attn_gain).astype(BF)
    gathered = lax.all_gather(attn_in.reshape(nseq, seg, width), "heads", axis=0)

    wq = query_matrix.reshape(width, groups, 128)
    wk = key_matrix.reshape(width, groups, HEAD)
    wv = value_matrix.reshape(width, groups, HEAD)
    w_local = jnp.concatenate([wq, wk, wv], axis=2)
    w_groups = jnp.transpose(w_local, (1, 0, 2))
    rows_in = width // ne
    rows_out = output_matrix.shape[0] // ne
    w_piece = lax.dynamic_slice_in_dim(w_local.reshape(width, groups * 256), me * rows_in, rows_in, 0)
    o_piece = lax.dynamic_slice_in_dim(output_matrix, me * rows_out, rows_out, 0)
    o_full = lax.all_gather(o_piece, ("heads", "experts"), axis=0, tiled=True)
    w_full = lax.all_gather(w_piece, ("heads", "experts"), axis=0, tiled=True)
    w_full = w_full.reshape(nh, width, groups * 256)

    tables = rotary_tables(nh * seg)
    qkv, heads_out, lse = attn_forward(gathered, w_groups, seq_lengths, tables)
    heads_in = lax.all_to_all(heads_out, "heads", split_axis=0, concat_axis=0, tiled=True)
    heads_in = heads_in.reshape(nh, tokens, groups * 128)
    o_parts = o_full.reshape(nh, groups * 128, width)
    branch = jnp.einsum("ztm,zmw->tw", heads_in, o_parts, preferred_element_type=F32)
    mid = xf + branch
    inv_two = lax.rsqrt(jnp.mean(mid * mid, axis=-1, keepdims=True) + EPS)
    moe_in = (mid * inv_two * moe_gain).astype(BF)

    grad = local(out_grad)
    grads_all = plane_gather(grad, ne)
    d_rows = gather_rows(slots, weights, grads_all, cap)
    tokens_all = plane_gather(moe_in, ne)
    x_rows = gather_rows(slots, None, tokens_all, cap)
    results, drows, sums = experts_call(slots, weights, x_rows, d_rows, expert_in, expert_down)
    slots_t = jnp.swapaxes(slots, 1, 2)
    d_parts = combine(slots_t, drows)
    moe_parts = combine(slots_t, results)
    if nh == 4 and ne == 8:
        flat = sums.reshape(-1, width)
        chunks = flat.shape[0] // CHUNK
        half = chunks // 2
        total_a, d_mid, d_branch, gain_two, dqkv = middle(
            half, seq_lengths, flat, d_parts, mid, grad, moe_gain.reshape(1, width), o_parts, qkv, lse, tables)
        gain_two = gain_two.reshape(width)
        back = lax.all_to_all(dqkv, "heads", split_axis=0, concat_axis=0, tiled=True)
        flat, moe_parts, d_branch = lax.optimization_barrier((flat, moe_parts, d_branch))
        total_b, got = last(half, chunks - half, flat, moe_parts)
        moe_sum = moe_parts[0].astype(F32) + jnp.sum(got.astype(F32), axis=0)
        totals = [t.reshape(here // 2, sums.shape[1], width).astype(F32) for t in (total_a, total_b)]
        grad_in = jnp.concatenate([t[:, :width] for t in totals], axis=0)
        grad_down = jnp.concatenate([t[:, width:] for t in totals], axis=0)
    else:
        totals = heads_sum(sums, z, nh)
        grad_in, grad_down = totals[:, :width], totals[:, width:]
        d_moe = plane_scatter(d_parts, ne)
        moe_sum = plane_scatter(moe_parts, ne)
        zed = moe_gain * d_moe
        d_mid = grad.astype(F32) + inv_two * zed - mid * (inv_two ** 3 * jnp.mean(zed * mid, axis=-1, keepdims=True))
        gain_two = jnp.sum(d_moe * mid * inv_two, axis=0)
        d_branch = d_mid.astype(BF)
        d_heads = jnp.einsum("tw,zmw->ztm", d_branch, o_parts, preferred_element_type=F32).astype(BF)
        d_heads = d_heads.reshape(nh, nseq, seg, groups * 128)
        d_heads = lax.all_to_all(d_heads, "heads", split_axis=0, concat_axis=0, tiled=True)
        dqkv = attn_backward(qkv, d_heads, lse, seq_lengths, tables)
        back = lax.all_to_all(dqkv, "heads", split_axis=0, concat_axis=0, tiled=True)
    out = (mid + moe_sum).astype(BF)

    o_partial = jnp.einsum("ztm,tw->zmw", heads_in, d_branch, preferred_element_type=F32)
    o_grad = lax.psum_scatter(o_partial, "heads", scatter_dimension=0)
    o_grad = lax.psum(o_grad, "experts")
    w_partial = jnp.einsum("zsrm,zsrc->mc", gathered, dqkv, preferred_element_type=F32)
    w_grad = lax.psum(w_partial, "experts").reshape(width, groups, 256)
    back = back.reshape(nh, tokens, groups * 256)
    d_attn = jnp.einsum("ztc,zmc->tm", back, w_full, preferred_element_type=F32)
    wed = attn_gain * d_attn
    x_grad = d_mid + inv_one * wed - xf * (inv_one ** 3 * jnp.mean(wed * xf, axis=-1, keepdims=True))
    gain_one = jnp.sum(d_attn * xf * inv_one, axis=0)
    gain_one, gain_two = lax.psum((gain_one, gain_two), ("heads", "experts"))
    return (
        unlocal(out),
        unlocal(x_grad),
        gain_one,
        gain_two,
        w_grad[:, :, :128].reshape(query_matrix.shape),
        w_grad[:, :, 128:192].reshape(key_matrix.shape),
        w_grad[:, :, 192:].reshape(value_matrix.shape),
        o_grad,
        grad_in,
        grad_down,
    )


def solution(mesh):
    rows = P("heads", "experts", None)
    in_specs = (
        rows,
        P("experts"),
        rows,
        rows,
        P("heads", "experts"),
        P(),
        P(),
        P(None, "heads"),
        P(None, "heads"),
        P(None, "heads"),
        P("heads", None),
        P("experts", None, None),
        P("experts", None, None),
        rows,
    )
    out_specs = (
        rows,
        rows,
        P(),
        P(),
        P(None, "heads"),
        P(None, "heads"),
        P(None, "heads"),
        P("heads", None),
        P("experts", None, None),
        P("experts", None, None),
    )
    return jax.shard_map(body, mesh=mesh, in_specs=in_specs, out_specs=out_specs, check_vma=False)
```

```python
import functools
import math

import jax
import jax.numpy as jnp
from jax import lax
from jax.experimental import pallas as pl
from jax.experimental.pallas import tpu as pltpu
from jax.sharding import PartitionSpec as P

HEAD = 64
EXPERTS = 32
EPS = 1e-06
BF = jnp.bfloat16
F32 = jnp.float32
SCALE = HEAD ** (-0.5)
NEG = -1e30
VMEM = 63 * 1024 * 1024
MESH = pl.DeviceIdType.MESH
DMA = pltpu.SemaphoreType.DMA


def dot(a, b):
    return jnp.dot(a, b, preferred_element_type=F32)


def dot_nt(a, b):
    return lax.dot_general(a, b, (((1,), (1,)), ((), ())), preferred_element_type=F32)


def dot_tn(a, b):
    return lax.dot_general(a, b, (((0,), (0,)), ((), ())), preferred_element_type=F32)


def params(n):
    return pltpu.CompilerParams(
        dimension_semantics=("arbitrary",) * n, vmem_limit_bytes=VMEM
    )


def swap_halves(v):
    lane = lax.broadcasted_iota(jnp.int32, v.shape, 1)
    return jnp.where(lane % 64 < 32, pltpu.roll(v, 96, 1), pltpu.roll(v, 32, 1))


def attn_mask(offset, n, block, length):
    key = lax.broadcasted_iota(jnp.int32, (n, block), 0)
    query = lax.broadcasted_iota(jnp.int32, (n, block), 1) + offset
    return (key <= query) & (key < length)


def two_heads(v):
    return jnp.concatenate([v[:, :HEAD], v[:, HEAD:]], axis=0)


def untwo(vt, block):
    return jnp.concatenate([vt[:, :block], vt[:, block:]], axis=0).T


def fwd_kernel(len_ref, x_ref, w_ref, cq, sq, ckv, skv, qkv_ref, head_ref, lse_ref):
    nh, _, seg, width = x_ref.shape
    full = nh * seg
    block = seg
    length = len_ref[pl.program_id(0)]
    lin = dot(x_ref[...].reshape(full, width), w_ref[0])
    ql, kvl = lin[:, :128], lin[:, 128:]
    q = (ql * cq[...] + swap_halves(ql) * sq[...]).astype(BF)
    kvr = kvl * ckv[...] + swap_halves(kvl) * skv[...]
    kv = kvr.astype(BF)
    qkv_ref[0, 0, :, :128] = q
    qkv_ref[0, 0, :, 128:] = kv
    k = kv[:, :HEAD]
    vt = kvr.T[HEAD:].astype(BF)
    for i in range(nh):
        n = (i + 1) * block
        q2 = two_heads(q[i * block : n])
        s = dot_nt(k[:n], q2)
        mask = attn_mask(i * block, n, block, length)
        s = jnp.where(jnp.concatenate([mask, mask], axis=1), s * SCALE, NEG)
        m = jnp.max(s, axis=0, keepdims=True)
        e = jnp.exp(s - m)
        total = jnp.sum(e, axis=0, keepdims=True)
        p = (e * (1.0 / total)).astype(BF)
        lse_ref[0, 0, i : i + 1, :] = m + jnp.log(total)
        head_ref[i, 0] = untwo(dot(vt[:, :n], p), block).astype(BF)


def attn_forward(x, w, lengths, tables):
    nh, nseq, seg, width = x.shape
    groups = w.shape[0]
    full = nh * seg
    cq, sq, ckv, skv = tables
    tab = pl.BlockSpec((full, 128), lambda s, g: (0, 0))
    return pl.pallas_call(
        fwd_kernel,
        grid=(nseq, groups),
        in_specs=[
            pl.BlockSpec(memory_space=pltpu.SMEM),
            pl.BlockSpec((nh, 1, seg, width), lambda s, g: (0, s, 0, 0)),
            pl.BlockSpec((1, width, 256), lambda s, g: (g, 0, 0)),
            tab,
            tab,
            tab,
            tab,
        ],
        out_specs=[
            pl.BlockSpec((1, 1, full, 256), lambda s, g: (s, g, 0, 0)),
            pl.BlockSpec((nh, 1, seg, 128), lambda s, g: (0, s, 0, g)),
            pl.BlockSpec((1, 1, nh, 2 * seg), lambda s, g: (s, g, 0, 0)),
        ],
        out_shape=[
            jax.ShapeDtypeStruct((nseq, groups, full, 256), BF),
            jax.ShapeDtypeStruct((nh, nseq, seg, groups * 128), BF),
            jax.ShapeDtypeStruct((nseq, groups, nh, 2 * seg), F32),
        ],
        compiler_params=params(2),
        cost_estimate=pl.CostEstimate(flops=6 * 10**9, bytes_accessed=12 * 2**20, transcendentals=10**7),
        name="attn_forward",
    )(lengths, x, w, cq, sq, ckv, skv)


def bwd_piece(q, kv, heads, lses, length, tables, dkv_ref, put):
    cq, sq, ckv, skv = tables
    full, block = q.shape[0], lses(0).shape[1] // 2
    k, v = kv[:, :HEAD], kv[:, HEAD:]
    kt = kv.astype(F32).T[:HEAD].astype(BF)
    dkv_ref[...] = jnp.zeros_like(dkv_ref)
    for i in range(full // block):
        n = (i + 1) * block
        rows = pl.ds(i * block, block)
        mask = attn_mask(i * block, n, block, length)
        grads = []
        for h in range(2):
            qh = q[i * block : n, h * HEAD : (h + 1) * HEAD]
            doh = heads(i)[:, h * HEAD : (h + 1) * HEAD]
            s = dot_nt(k[:n], qh)
            p = jnp.exp(jnp.where(mask, s * SCALE - lses(i)[:, h * block : (h + 1) * block], NEG))
            dp = dot_nt(v[:n], doh)
            delta = jnp.sum(p * dp, axis=0, keepdims=True)
            ds = (p * (dp - delta) * SCALE).astype(BF)
            dkv_ref[:n, :HEAD] += dot(ds, qh)
            dkv_ref[:n, HEAD:] += dot(p.astype(BF), doh)
            grads.append(dot(kt[:, :n], ds))
        dq = jnp.concatenate(grads, axis=0).T
        dq = dq * cq[rows, :] - swap_halves(dq) * sq[rows, :]
        put(i, 0, dq.astype(BF))
    dkv = dkv_ref[...]
    dkv = (dkv * ckv[...] - swap_halves(dkv) * skv[...]).astype(BF)
    for i in range(full // block):
        put(i, 128, dkv[i * block : (i + 1) * block])


def bwd_kernel(len_ref, qkv_ref, do_ref, lse_ref, cq, sq, ckv, skv, out_ref, dkv_ref):
    def put(i, lo, v):
        out_ref[i, 0, :, lo : lo + 128] = v

    bwd_piece(
        qkv_ref[0, 0, :, :128],
        qkv_ref[0, 0, :, 128:],
        lambda i: do_ref[i, 0],
        lambda i: lse_ref[0, 0, i : i + 1, :],
        len_ref[pl.program_id(0)],
        (cq, sq, ckv, skv),
        dkv_ref,
        put,
    )


def attn_backward(qkv, d_head, lse, lengths, tables):
    nseq, groups, full, _ = qkv.shape
    nh, _, seg, _ = d_head.shape
    cq, sq, ckv, skv = tables
    tab = pl.BlockSpec((full, 128), lambda s, g: (0, 0))
    return pl.pallas_call(
        bwd_kernel,
        grid=(nseq, groups),
        in_specs=[
            pl.BlockSpec(memory_space=pltpu.SMEM),
            pl.BlockSpec((1, 1, full, 256), lambda s, g: (s, g, 0, 0)),
            pl.BlockSpec((nh, 1, seg, 128), lambda s, g: (0, s, 0, g)),
            pl.BlockSpec((1, 1, nh, 2 * seg), lambda s, g: (s, g, 0, 0)),
            tab,
            tab,
            tab,
            tab,
        ],
        out_specs=pl.BlockSpec((nh, 1, seg, 256), lambda s, g: (0, s, 0, g)),
        out_shape=jax.ShapeDtypeStruct((nh, nseq, seg, groups * 256), BF),
        scratch_shapes=[pltpu.VMEM((full, 128), F32)],
        compiler_params=params(2),
        cost_estimate=pl.CostEstimate(flops=12 * 10**9, bytes_accessed=8 * 2**20, transcendentals=10**7),
        name="attn_backward",
    )(lengths, qkv, d_head, lse, cq, sq, ckv, skv)


def rotary_tables(length):
    half = HEAD // 2
    frequency = jnp.exp(jnp.arange(half, dtype=F32) * (-2.0 * math.log(10000.0) / HEAD))
    angles = jnp.arange(length, dtype=F32)[:, None] * frequency[None, :]
    cos, sin = jnp.cos(angles), jnp.sin(angles)
    c1 = jnp.concatenate([cos, cos], axis=1)
    s1 = jnp.concatenate([-sin, sin], axis=1)
    cq = jnp.concatenate([c1, c1], axis=1)
    sq = jnp.concatenate([s1, s1], axis=1)
    ckv = jnp.concatenate([c1, jnp.ones_like(c1)], axis=1)
    skv = jnp.concatenate([s1, jnp.zeros_like(s1)], axis=1)
    return cq, sq, ckv, skv


def pick_rows(slots, cap):
    tokens = slots.shape[1]
    index = lax.broadcasted_iota(jnp.int32, (cap, tokens), 0)
    return [index == slots[j : j + 1, :] for j in range(slots.shape[0])]


def gather_kernel(weighted, slot_ref, *refs):
    if weighted:
        weight_ref, tok_ref, out_ref = refs
    else:
        tok_ref, out_ref = refs[0], refs[-1]
    cap = out_ref.shape[2]
    hits = pick_rows(slot_ref[0], cap)
    rows = dot(jnp.concatenate([h.astype(F32) for h in hits], axis=0).astype(BF), tok_ref[0])
    for j, hit in enumerate(hits):
        part = rows[j * cap : (j + 1) * cap]
        if weighted:
            part = part * jnp.sum(jnp.where(hit, weight_ref[0, j : j + 1, :], 0.0), axis=1, keepdims=True)
        out_ref[j, 0] = part.astype(BF)


def gather_rows(slots, weights, tokens, cap):
    sources, here, count = slots.shape
    width = tokens.shape[-1]
    small = pl.BlockSpec((1, here, count), lambda s: (s, 0, 0))
    weighted = weights is not None
    return pl.pallas_call(
        functools.partial(gather_kernel, weighted),
        grid=(sources,),
        in_specs=[small] + [small] * weighted + [pl.BlockSpec((1, count, width), lambda s: (s, 0, 0))],
        out_specs=pl.BlockSpec((here, 1, cap, width), lambda s: (0, s, 0, 0)),
        out_shape=jax.ShapeDtypeStruct((here, sources, cap, width), BF),
        compiler_params=params(1),
        cost_estimate=pl.CostEstimate(
            flops=2 * sources * here * cap * count * width,
            bytes_accessed=2 * sources * width * (count + here * cap),
            transcendentals=0,
        ),
        name="gather_rows",
    )(*([slots] + [weights] * weighted + [tokens]))


def expert_kernel(steps, slot_ref, weight_ref, x_ref, d_ref, win_ref, wdown_ref,
                  out_ref, drow_ref, grad_ref, hid_ref, dgu_ref, *acc):
    _, sources, cap, width = x_ref.shape
    ff = wdown_ref.shape[1]
    per = 2 if sources % 2 == 0 else 1
    win, wdown = win_ref[0], wdown_ref[0]
    for c in range(sources // per):
        rows = slice(c * per * cap, (c + 1) * per * cap)
        x = x_ref[0, c * per : (c + 1) * per].reshape(per * cap, width)
        d = d_ref[0, c * per : (c + 1) * per].reshape(per * cap, width)
        gu = dot(x, win)
        gate, up = gu[:, :ff], gu[:, ff:]
        sig = 1.0 / (1.0 + jnp.exp(-gate))
        act = gate * sig
        hidden = (act * up).astype(BF)
        hid_ref[rows, :] = hidden
        result = dot(hidden, wdown).astype(BF).astype(F32)
        for b in range(per):
            hit = pick_rows(slot_ref[c * per + b, 0], cap)[0]
            w = jnp.sum(jnp.where(hit, weight_ref[c * per + b, 0], 0.0), axis=1, keepdims=True)
            out_ref[0, c * per + b] = (result[b * cap : (b + 1) * cap] * w).astype(BF)
        dh = dot_nt(d, wdown)
        dgu_ref[rows, :ff] = (dh * up * (sig * (1.0 + gate * (1.0 - sig)))).astype(BF)
        dgu_ref[rows, ff:] = (dh * act).astype(BF)
        drow = dot_nt(dgu_ref[rows, :], win).astype(BF)
        for b in range(per):
            drow_ref[0, c * per + b] = drow[b * cap : (b + 1) * cap]
    x = x_ref[0].reshape(sources * cap, width)
    d = d_ref[0].reshape(sources * cap, width)
    gin = dot_tn(x, dgu_ref[...])
    gdown = dot_tn(hid_ref[...], d)
    if steps == 1:
        grad_ref[0, :width] = gin.astype(BF)
        grad_ref[0, width:] = gdown.astype(BF)
    else:
        ain, adown = acc
        step = pl.program_id(1)

        @pl.when(step == 0)
        def _():
            ain[...] = jnp.zeros_like(ain)
            adown[...] = jnp.zeros_like(adown)

        ain[...] += gin
        adown[...] += gdown

        @pl.when(step == steps - 1)
        def _():
            grad_ref[0, :width] = ain[...].astype(BF)
            grad_ref[0, width:] = adown[...].astype(BF)


def experts_call(slots, weights, x, d, win, wdown):
    count, sources, cap, width = x.shape
    tokens = slots.shape[-1]
    ff = wdown.shape[1]
    chunk = min(sources, 8)
    steps = sources // chunk
    small = pl.BlockSpec((chunk, 1, 1, tokens), lambda j, r: (r, j, 0, 0))
    rows = pl.BlockSpec((1, chunk, cap, width), lambda j, r: (j, r, 0, 0))
    rows_out = pl.BlockSpec((1, chunk, cap, width), lambda j, r: (j, r, 0, 0))
    scratch = [pltpu.VMEM((chunk * cap, ff), BF), pltpu.VMEM((chunk * cap, 2 * ff), BF)]
    if steps > 1:
        scratch += [pltpu.VMEM((width, 2 * ff), F32), pltpu.VMEM((ff, width), F32)]
    shape = jax.ShapeDtypeStruct((count, sources, cap, width), BF)
    return pl.pallas_call(
        functools.partial(expert_kernel, steps),
        grid=(count, steps),
        in_specs=[
            small,
            small,
            rows,
            rows,
            pl.BlockSpec((1, width, 2 * ff), lambda j, r: (j, 0, 0)),
            pl.BlockSpec((1, ff, width), lambda j, r: (j, 0, 0)),
        ],
        out_specs=[
            rows_out,
            rows_out,
            pl.BlockSpec((1, width + ff, width), lambda j, r: (j, 0, 0)),
        ],
        out_shape=[
            shape,
            shape,
            jax.ShapeDtypeStruct((count, width + ff, width), BF),
        ],
        scratch_shapes=scratch,
        compiler_params=params(2),
        cost_estimate=pl.CostEstimate(
            flops=2 * count * sources * cap * width * ff * 9,
            bytes_accessed=8 * count * sources * cap * width + 12 * count * width * ff,
            transcendentals=count * sources * cap * ff,
        ),
        name="experts",
    )(slots[:, :, None, :], weights[:, :, None, :], x, d, win, wdown)


def combine_kernel(slot_ref, row_ref, out_ref):
    slots = slot_ref[0]
    count, here = slots.shape
    cap = row_ref.shape[2]
    lane = lax.broadcasted_iota(jnp.int32, (count, here * cap), 1)
    hot = None
    for j in range(here):
        col = slots[:, j : j + 1]
        hit = lane == jnp.where(col >= 0, col + j * cap, -1)
        hot = hit if hot is None else hot | hit
    hot = hot.astype(F32).astype(BF)
    out_ref[0] = dot(hot, row_ref[...].reshape(here * cap, row_ref.shape[3])).astype(BF)


def combine(slots_t, rows):
    sources, count, here = slots_t.shape
    _, _, cap, width = rows.shape
    return pl.pallas_call(
        combine_kernel,
        grid=(sources,),
        in_specs=[
            pl.BlockSpec((1, count, here), lambda s: (s, 0, 0)),
            pl.BlockSpec((here, 1, cap, width), lambda s: (0, s, 0, 0)),
        ],
        out_specs=pl.BlockSpec((1, count, width), lambda s: (s, 0, 0)),
        out_shape=jax.ShapeDtypeStruct((sources, count, width), BF),
        compiler_params=params(1),
        cost_estimate=pl.CostEstimate(
            flops=2 * sources * here * cap * count * width,
            bytes_accessed=2 * sources * width * (count + here * cap),
            transcendentals=0,
        ),
        name="combine",
    )(slots_t, rows)


def swap(x, bit, n):
    return lax.ppermute(x, "experts", [(i, i ^ bit) for i in range(n)])


def plane_gather(x, n):
    if n != 8:
        whole = lax.all_gather(x, "experts", axis=0)
        order = lax.axis_index("experts") ^ jnp.arange(n, dtype=jnp.int32)
        return whole[order]
    got = {0: x}
    for r in (2, 4, 6):
        got[r] = swap(x, r, n)
    for r in (0, 2, 4, 6):
        got[r + 1] = swap(got[r], 1, n)
    return jnp.stack([got[r] for r in range(n)], axis=0)


def plane_scatter(parts, n):
    if n != 8:
        order = lax.axis_index("experts") ^ jnp.arange(n, dtype=jnp.int32)
        return lax.psum_scatter(parts[order].astype(F32), "experts", scatter_dimension=0)
    odd = swap(parts[1::2], 1, n)
    both = [parts[2 * i].astype(F32) + odd[i].astype(F32) for i in range(4)]
    total = both[0]
    for i in (1, 2, 3):
        total = total + swap(both[i].astype(BF), 2 * i, n).astype(F32)
    return total


def heads_sum(x, z, nh):
    if nh != 4:
        return lax.psum(x.astype(F32), "heads")
    first = lax.ppermute(x, "heads", [(0, 1), (3, 2)])
    pair = (x.astype(F32) + first.astype(F32)).astype(BF)
    second = lax.ppermute(pair, "heads", [(1, 2), (2, 1)])
    total = (pair.astype(F32) + second.astype(F32)).astype(BF)
    third = lax.ppermute(total, "heads", [(1, 0), (2, 3)])
    return jnp.where((z == 1) | (z == 2), total, third).astype(F32)


def weight_sums(heads_in, d_branch, gathered, dqkv, ne):
    nh, tokens, part = heads_in.shape
    width, cols = d_branch.shape[1], dqkv.shape[2]
    col, row = width // ne, width // ne
    o = jnp.einsum("ztm,tew->ezmw", heads_in, d_branch.reshape(tokens, ne, col), preferred_element_type=F32)
    w = jnp.einsum("ztm,ztc->mc", gathered.reshape(nh, tokens, width), dqkv, preferred_element_type=F32)
    cut = cols // col
    w = jnp.swapaxes(w.reshape(ne, row, cut, col), 1, 2).reshape(ne, cut * row, col)
    both = jnp.concatenate([o.reshape(ne, nh * part, col), w], axis=1)
    both = lax.psum_scatter(both, "experts", scatter_dimension=0)
    o, w = both[: nh * part], both[nh * part :]
    o = lax.psum_scatter(o.reshape(nh, part, col), "heads", scatter_dimension=0)
    return weight_split(lax.all_gather(jnp.concatenate([o, w], axis=0), "experts", axis=0), part, cols)


def weight_split(both, part, cols):
    ne, _, col = both.shape
    width, row, cut = ne * col, col, cols // col
    o = jnp.swapaxes(both[:, :part], 0, 1).reshape(part, width)
    w = jnp.swapaxes(both[:, part:].reshape(ne, cut, row, col), 1, 2)
    return o, w.reshape(width, cols)


CHUNK = 256
LAG = 3


def remote(src, dst, send, recv, axis, index):
    return pltpu.make_async_remote_copy(
        src_ref=src, dst_ref=dst, send_sem=send, recv_sem=recv,
        device_id={axis: index}, device_id_type=MESH,
    )


def greet(nh, masks):
    z, me = lax.axis_index("heads"), lax.axis_index("experts")
    bar = pltpu.get_barrier_semaphore()
    for d in range(1, nh):
        pl.semaphore_signal(bar, inc=1, device_id={"heads": lax.rem(z + d, nh)}, device_id_type=MESH)
    for r in masks:
        pl.semaphore_signal(bar, inc=1, device_id={"experts": me ^ r}, device_id_type=MESH)
    pl.semaphore_wait(bar, nh - 1 + len(masks))


class Chain:
    def __init__(self, src, out, scratch, first, count):
        self.src, self.out, self.first, self.count = src, out, first, count
        self.a, self.b, self.buf, self.s1, self.r1, self.s2, self.r2, self.ls, self.os = scratch
        z = lax.axis_index("heads")
        self.mid = (z == 1) | (z == 2)
        self.outer = jnp.where(z == 0, 1, jnp.where(z == 1, 0, jnp.where(z == 2, 3, 2)))
        self.inner = jnp.where(z == 1, 2, jnp.where(z == 2, 1, z))

    def piece(self, k):
        return self.src.at[pl.ds((self.first + k) * CHUNK, CHUNK)]

    def load(self, k):
        return pltpu.make_async_copy(self.piece(k), self.buf.at[lax.rem(k, 2)], self.ls.at[lax.rem(k, 2)])

    def store(self, ref, k):
        return pltpu.make_async_copy(ref.at[k], self.out.at[pl.ds((self.first + k) * CHUNK, CHUNK)], self.os.at[k])

    def up(self, k):
        return remote(self.piece(k), self.a.at[k], self.s1.at[k], self.r1.at[k], "heads", self.outer)

    def across(self, k):
        return remote(self.a.at[k], self.b.at[k], self.s2.at[k], self.r2.at[k], "heads", self.inner)

    def down(self, k):
        return remote(self.b.at[k], self.a.at[k], self.s1.at[k], self.r1.at[k], "heads", self.outer)

    def begin(self):
        @pl.when(self.mid)
        def _():
            self.load(0).start()

    def steps(self):
        return self.count + LAG

    def step(self, k):
        n = self.count

        @pl.when(self.mid)
        def _():
            @pl.when(k < n)
            def _():
                @pl.when(k + 1 < n)
                def _():
                    self.load(k + 1).start()

                self.load(k).wait()
                self.up(k).wait_recv()
                own = self.buf[lax.rem(k, 2)].astype(F32)
                self.a[k] = (self.a[k].astype(F32) + own).astype(BF)
                self.across(k).start()

            @pl.when((k >= 1) & (k <= n))
            def _():
                j = k - 1
                self.across(j).wait_recv()
                self.b[j] = (self.a[j].astype(F32) + self.b[j].astype(F32)).astype(BF)
                self.down(j).start()
                self.store(self.b, j).start()

        @pl.when(jnp.logical_not(self.mid))
        def _():
            @pl.when(k < n)
            def _():
                @pl.when(k >= LAG)
                def _():
                    self.up(k - LAG).wait_send()

                self.up(k).start()

            @pl.when(k >= LAG)
            def _():
                j = k - LAG
                self.down(j).wait_recv()
                self.store(self.a, j).start()

    def run(self, first, last):
        @pl.loop(first, last)
        def _(k):
            self.step(k)

    def finish(self):
        n = self.count

        @pl.when(self.mid)
        def _():
            @pl.loop(0, n)
            def _(k):
                self.across(k).wait_send()
                self.down(k).wait_send()
                self.store(self.b, k).wait()

        @pl.when(jnp.logical_not(self.mid))
        def _():
            @pl.loop(n - LAG, n)
            def _(k):
                self.up(k).wait_send()

            @pl.loop(0, n)
            def _(k):
                self.store(self.a, k).wait()


def chain_scratch(count, width):
    return [
        pltpu.VMEM((count, CHUNK, width), BF),
        pltpu.VMEM((count, CHUNK, width), BF),
        pltpu.VMEM((2, CHUNK, width), BF),
        DMA((count,)),
        DMA((count,)),
        DMA((count,)),
        DMA((count,)),
        DMA((2,)),
        DMA((count,)),
    ]


class PlaneSum:
    order = (3, 1, 2)

    def __init__(self, rows, slots, total, scratch):
        self.rows, self.slots, self.total = rows, slots, total
        self.buf, self.odd, self.c, self.e, self.f, self.ls, self.cs, self.cr, self.fs, self.fr = scratch
        self.me = lax.axis_index("experts")
        self.here, _, self.cap, self.width = rows.shape

    def load(self, r, at):
        return [
            pltpu.make_async_copy(self.rows.at[j, r], self.buf.at[at, j], self.ls.at[at, j])
            for j in range(self.here)
        ]

    def core(self, i):
        return remote(self.odd.at[i], self.c.at[i], self.cs.at[i], self.cr.at[i], "experts", self.me ^ 1)

    def chip(self, i):
        return remote(self.e.at[i - 1], self.f.at[i - 1], self.fs.at[i - 1], self.fr.at[i - 1], "experts", self.me ^ (2 * i))

    def part(self, r, at, after, after_at):
        if after is not None:
            for c in self.load(after, after_at):
                c.start()
        slots = self.slots[r].T.astype(jnp.int32)
        lane = lax.broadcasted_iota(jnp.int32, (slots.shape[0], self.here * self.cap), 1)
        hot = None
        for j in range(self.here):
            col = slots[:, j : j + 1]
            hit = lane == jnp.where(col >= 0, col + j * self.cap, -1)
            hot = hit if hot is None else hot | hit
        for c in self.load(r, at):
            c.wait()
        rows = self.buf[at].reshape(self.here * self.cap, self.width)
        return dot(hot.astype(F32).astype(BF), rows)

    def run(self, chain, step):
        turns = [2 * i + 1 for i in self.order + (0,)] + [2 * i for i in self.order + (0,)]
        for c in self.load(turns[0], 0):
            c.start()
        for t, r in enumerate(turns):
            after = turns[t + 1] if t + 1 < len(turns) else None
            value = self.part(r, t % 2, after, (t + 1) % 2)
            i = r // 2
            if r % 2:
                self.odd[i] = value.astype(BF)
                self.core(i).start()
            else:
                self.core(i).wait_recv()
                value = value + self.c[i].astype(F32)
                if i:
                    self.e[i - 1] = value.astype(BF)
                    self.chip(i).start()
                else:
                    self.total[...] = value
            if t == 3:
                chain.run(step, step + 1)
        chain.run(step + 1, step + 4)
        for i in self.order:
            self.chip(i).wait_recv()
        return step + 4

    def rows_total(self, rows):
        d = self.total[rows]
        for r in range(3):
            d = d + self.f[r, rows].astype(F32)
        return d

    def finish(self):
        for i in range(4):
            self.core(i).wait_send()
        for i in self.order:
            self.chip(i).wait_send()


def plane_scratch(here, cap, tokens, width):
    return [
        pltpu.VMEM((2, here, cap, width), BF),
        pltpu.VMEM((4, tokens, width), BF),
        pltpu.VMEM((4, tokens, width), BF),
        pltpu.VMEM((3, tokens, width), BF),
        pltpu.VMEM((3, tokens, width), BF),
        DMA((2, here)),
        DMA((4,)),
        DMA((4,)),
        DMA((3,)),
        DMA((3,)),
    ]


PLANE = 10


class Exchange:
    def __init__(self, src, dst, send, recv, nh):
        self.src, self.dst, self.ss, self.rs, self.nh = src, dst, send, recv, nh
        self.z = lax.axis_index("heads")

    def send(self, d):
        to = lax.rem(self.z + d, self.nh)
        return remote(self.src.at[to], self.dst.at[self.z], self.ss.at[d], self.rs.at[d], "heads", to)

    def start(self):
        for d in range(1, self.nh):
            self.send(d).start()
        own = pl.ds(self.z, 1)
        self.dst[own] = self.src[own]

    def wait_recv(self):
        for d in range(1, self.nh):
            at = lax.rem(self.z + self.nh - d, self.nh)
            remote(self.src.at[at], self.dst.at[at], self.ss.at[d], self.rs.at[d], "heads", at).wait_recv()

    def finish(self):
        for d in range(1, self.nh):
            self.send(d).wait_send()


ROWS = 128


def middle_kernel(count, len_ref, sum_ref, rows_ref, slot_ref, mid_ref, grad_ref, gain_ref, o_ref, qkv_ref, lse_ref,
                  cq, sq, ckv, skv, hin_ref, x_ref, total_ref, dmid_ref, gtwo_ref, dqkv_ref, parts_ref,
                  dbranch_ref, hs, hr, dmoe, dkv, hss, hrs, xs, *scratch):
    nh, tokens, _ = dqkv_ref.shape
    nseq, groups = qkv_ref.shape[:2]
    seg = tokens // nseq
    chain = Chain(sum_ref, total_ref, scratch[PLANE:], 0, count)
    plane = PlaneSum(rows_ref, slot_ref, dmoe, scratch[:PLANE])
    heads = Exchange(hs, hr, hss, hrs, nh)
    greet(nh, (1, 2, 4, 6))
    chain.begin()
    chain.run(0, 1)
    step = plane.run(chain, 1)
    gtwo_ref[...] = jnp.zeros_like(gtwo_ref)

    @pl.loop(0, tokens // ROWS)
    def _(i):
        rows = pl.ds(i * ROWS, ROWS)
        d = plane.rows_total(rows)
        m = mid_ref[rows]
        inv = lax.rsqrt(jnp.mean(m * m, axis=-1, keepdims=True) + EPS)
        zed = gain_ref[...] * d
        dm = grad_ref[rows].astype(F32) + inv * zed - m * (inv * inv * inv * jnp.mean(zed * m, axis=-1, keepdims=True))
        gtwo_ref[...] += jnp.sum(d * m * inv, axis=0, keepdims=True)
        dmid_ref[rows] = dm
        db = dm.astype(BF)
        dbranch_ref[rows] = db
        for h in range(nh):
            hs[h, rows] = dot_nt(db, o_ref[h]).astype(BF)

    heads.start()
    chain.run(step, step + 3)
    step = step + 3
    heads.wait_recv()

    @pl.loop(0, nseq)
    def _(s):
        length = len_ref[s]
        at = pl.ds(s * seg, seg)
        for g in range(groups):
            def put(i, lo, v):
                dqkv_ref[i, at, g * 256 + lo : g * 256 + lo + 128] = v

            bwd_piece(
                qkv_ref[s, g, :, :128],
                qkv_ref[s, g, :, 128:],
                lambda i: hr[i, at, g * 128 : (g + 1) * 128],
                lambda i: lse_ref[s, g, i : i + 1, :],
                length,
                (cq, sq, ckv, skv),
                dkv,
                put,
            )
        chain.step(step + s)

    step = step + nseq
    for i in range(4):
        plane.core(i).wait_send()
    load = pltpu.make_async_copy(x_ref, plane.odd, xs)
    load.start()
    ne, _, col = parts_ref.shape
    part = hin_ref.shape[2]
    db = dbranch_ref[...]
    for h in range(nh):
        o = dot_tn(hin_ref[h], db)
        for e in range(ne):
            parts_ref[e, h * part : (h + 1) * part] = o[:, e * col : (e + 1) * col]
    chain.run(step, step + 1)
    load.wait()
    wsum = dmoe
    wsum[...] = dot_tn(dqkv_ref[0], plane.odd[0])
    for h in range(1, nh):
        wsum[...] += dot_tn(dqkv_ref[h], plane.odd[h])
    row = wsum.shape[1] // ne
    for e in range(ne):
        for c in range(wsum.shape[0] // col):
            at = nh * part + c * row
            parts_ref[e, at : at + row] = wsum[c * col : (c + 1) * col, e * row : (e + 1) * row].T
    chain.run(step + 1, chain.steps())
    chain.finish()
    for i in plane.order:
        plane.chip(i).wait_send()
    heads.finish()


def middle(count, lengths, sums, rows, slots, mid, grad, gain, o_parts, qkv, lse, tables, heads_in, x):
    nseq, groups, full, _ = qkv.shape
    nh = o_parts.shape[0]
    tokens, width = mid.shape
    here, ne, cap, _ = rows.shape
    vmem = pl.BlockSpec(memory_space=pltpu.VMEM)
    hbm = pl.BlockSpec(memory_space=pl.ANY)
    heads = (nh, tokens, groups * 128)
    col = width // ne
    cols = groups * 256
    return pl.pallas_call(
        functools.partial(middle_kernel, count),
        in_specs=[pl.BlockSpec(memory_space=pltpu.SMEM), hbm, hbm] + [vmem] * 12 + [hbm],
        out_specs=[hbm] + [vmem] * 4,
        out_shape=[
            jax.ShapeDtypeStruct(sums.shape, BF),
            jax.ShapeDtypeStruct((tokens, width), F32),
            jax.ShapeDtypeStruct((1, width), F32),
            jax.ShapeDtypeStruct((nh, tokens, cols), BF),
            jax.ShapeDtypeStruct((ne, width + cols * width // (ne * col), col), F32),
        ],
        scratch_shapes=[
            pltpu.VMEM((tokens, width), BF),
            pltpu.VMEM(heads, BF),
            pltpu.VMEM(heads, BF),
            pltpu.VMEM((tokens, width), F32),
            pltpu.VMEM((full, 128), F32),
            DMA((nh,)),
            DMA((nh,)),
            DMA,
        ]
        + plane_scratch(here, cap, tokens, width)
        + chain_scratch(count, width),
        compiler_params=pltpu.CompilerParams(
            collective_id=1, has_side_effects=True, vmem_limit_bytes=VMEM
        ),
        cost_estimate=pl.CostEstimate(flops=10**11, bytes_accessed=30 * 2**20, transcendentals=10**7),
        name="middle",
    )(lengths, sums, rows, slots, mid, grad, gain, o_parts, qkv, lse, *tables, heads_in, x)


def last_kernel(first, count, begun_ref, sum_ref, rows_ref, slot_ref, mid_ref, dqkv_ref, w_ref, x_ref, dmid_ref, gain_ref, gtwo_ref,
                parts_ref, total_ref, out_ref, xgrad_ref, gains_ref, got_ref, wide_ref,
                br, moe, gp, gz, acc, stage, oz, fin, brs, brr, gps, gpr, gzs, gzr, ws, wr, wl, oss, ors, fs, fr, fl, *scratch):
    nh, tokens, _ = dqkv_ref.shape
    dattn = moe
    ne = rows_ref.shape[1]
    z, me = lax.axis_index("heads"), lax.axis_index("experts")
    chain = Chain(sum_ref, total_ref, scratch[PLANE:], first, count)
    plane = PlaneSum(rows_ref, slot_ref, moe, scratch[:PLANE])
    back = Exchange(dqkv_ref, br, brs, brr, nh)
    greet(nh, tuple(range(1, ne)))
    back.start()
    chain.begin()

    def scatter(r, at):
        return remote(parts_ref.at[me ^ r], got_ref.at[at], ws.at[r], wr.at[r], "experts", me ^ r)

    for r in (6, 7, 2, 3, 4, 5, 1):
        scatter(r, me).start()
    chain.run(0, 3)
    step = plane.run(chain, 3)

    @pl.loop(0, tokens // ROWS)
    def _(i):
        rows = pl.ds(i * ROWS, ROWS)
        out_ref[rows] = (mid_ref[rows] + plane.rows_total(rows)).astype(BF)

    def fetch(r):
        ref = got_ref.at[me ^ r] if r else parts_ref.at[me]
        return pltpu.make_async_copy(ref, stage.at[r % 2], wl.at[r % 2])

    for r in range(ne):
        if r:
            scatter(r, me ^ r).wait_recv()
        fetch(r).start()
        if r:
            fetch(r - 1).wait()
            acc[...] = stage[0] if r == 1 else acc[...] + stage[(r - 1) % 2]
    fetch(ne - 1).wait()
    acc[...] += stage[(ne - 1) % 2]
    part = oz.shape[1]

    def strip(d, to, at):
        rows = pl.ds(pl.multiple_of(to * part, part), part)
        return remote(acc.at[rows], oz.at[at], oss.at[d], ors.at[d], "heads", to)

    for d in range(1, nh):
        strip(d, lax.rem(z + d, nh), z).start()
    oz[z] = acc[pl.ds(pl.multiple_of(z * part, part), part)]
    chain.run(step, step + 1)
    step = step + 1
    back.wait_recv()
    dattn[...] = dot_nt(br[0], w_ref[0])
    for h in range(1, nh):
        dattn[...] += dot_nt(br[h], w_ref[h])
    pad = jnp.zeros((6, gtwo_ref.shape[1]), F32)
    own = jnp.zeros_like(gtwo_ref[...])

    def rows_back(i, total):
        rows = pl.ds(i * ROWS, ROWS)
        d = dattn[rows]
        x = x_ref[rows].astype(F32)
        inv = lax.rsqrt(jnp.mean(x * x, axis=-1, keepdims=True) + EPS)
        wed = gain_ref[...] * d
        xgrad_ref[rows] = dmid_ref[rows] + inv * wed - x * (inv * inv * inv * jnp.mean(wed * x, axis=-1, keepdims=True))
        return total + jnp.sum(d * x * inv, axis=0, keepdims=True)

    own = lax.fori_loop(0, tokens // ROWS, rows_back, own)
    gp[me] = jnp.concatenate([own, gtwo_ref[...], pad], axis=0)

    def near(r, at):
        return remote(gp.at[me], gp.at[at], gps.at[r], gpr.at[r], "experts", me ^ r)

    for r in range(1, ne):
        near(r, me).start()
    for d in range(1, nh):
        src = lax.rem(z + nh - d, nh)
        strip(d, src, src).wait_recv()
    fin[:part] = oz[0] + oz[1] + oz[2] + oz[3]
    fin[part:] = acc[nh * part :]

    def spread(r, at):
        return remote(fin, wide_ref.at[at], fs.at[r], fr.at[r], "experts", me ^ r)

    for r in (6, 7, 2, 3, 4, 5, 1):
        spread(r, me).start()
    keep = pltpu.make_async_copy(fin, wide_ref.at[me], fl)
    keep.start()
    chain.run(step, step + 1)
    total = None
    for r in range(1, ne):
        near(r, me ^ r).wait_recv()
    for e in range(ne):
        total = gp[e] if total is None else total + gp[e]
    gz[z] = total

    def far(d, to, at):
        return remote(gz.at[z], gz.at[at], gzs.at[d], gzr.at[d], "heads", to)

    for d in range(1, nh):
        far(d, lax.rem(z + d, nh), z).start()
    chain.run(step + 1, chain.steps())
    total = None
    for d in range(1, nh):
        src = lax.rem(z + nh - d, nh)
        far(d, src, src).wait_recv()
    for h in range(nh):
        total = gz[h] if total is None else total + gz[h]
    gains_ref[...] = total
    chain.finish()
    plane.finish()
    back.finish()
    keep.wait()
    for r in range(1, ne):
        near(r, me).wait_send()
        scatter(r, me).wait_send()
        spread(r, me ^ r).wait_recv()
        spread(r, me).wait_send()
    for d in range(1, nh):
        far(d, lax.rem(z + d, nh), z).wait_send()
        strip(d, lax.rem(z + d, nh), z).wait_send()


def last(first, count, total, sums, rows, slots, mid, dqkv, w_full, x, d_mid, gain, gain_two, parts):
    nh, tokens, cols = dqkv.shape
    here, ne, cap, width = rows.shape
    col = parts.shape[2]
    deep = parts.shape[1] - width + width // nh
    hbm = pl.BlockSpec(memory_space=pl.ANY)
    vmem = pl.BlockSpec(memory_space=pltpu.VMEM)
    return pl.pallas_call(
        functools.partial(last_kernel, first, count),
        in_specs=[hbm, hbm, hbm] + [vmem] * 8 + [hbm],
        input_output_aliases={0: 0},
        out_specs=[hbm] + [vmem] * 3 + [hbm, hbm],
        out_shape=[
            jax.ShapeDtypeStruct(sums.shape, BF),
            jax.ShapeDtypeStruct((tokens, width), BF),
            jax.ShapeDtypeStruct((tokens, width), F32),
            jax.ShapeDtypeStruct((8, width), F32),
            jax.ShapeDtypeStruct(parts.shape, F32),
            jax.ShapeDtypeStruct((ne, deep, col), F32),
        ],
        scratch_shapes=[
            pltpu.VMEM((nh, tokens, cols), BF),
            pltpu.VMEM((tokens, width), F32),
            pltpu.VMEM((ne, 8, width), F32),
            pltpu.VMEM((nh, 8, width), F32),
            pltpu.VMEM(parts.shape[1:], F32),
            pltpu.VMEM((2,) + parts.shape[1:], F32),
            pltpu.VMEM((nh, width // nh, col), F32),
            pltpu.VMEM((deep, col), F32),
            DMA((nh,)),
            DMA((nh,)),
            DMA((ne,)),
            DMA((ne,)),
            DMA((nh,)),
            DMA((nh,)),
            DMA((ne,)),
            DMA((ne,)),
            DMA((2,)),
            DMA((nh,)),
            DMA((nh,)),
            DMA((ne,)),
            DMA((ne,)),
            DMA,
        ]
        + plane_scratch(here, cap, tokens, width)
        + chain_scratch(count, width),
        compiler_params=pltpu.CompilerParams(
            collective_id=2, has_side_effects=True, vmem_limit_bytes=VMEM
        ),
        cost_estimate=pl.CostEstimate(flops=2 * 10**11, bytes_accessed=30 * 2**20, transcendentals=0),
        name="last",
    )(total, sums, rows, slots, mid, dqkv, w_full, x, d_mid, gain, gain_two, parts)


def body(layer_input, seq_lengths, expert_ids, route_weight, priority, attn_gain, moe_gain,
         query_matrix, key_matrix, value_matrix, output_matrix, expert_in, expert_down, out_grad):
    seg, nseq, width = layer_input.shape
    nh, ne = lax.axis_size("heads"), lax.axis_size("experts")
    z, me = lax.axis_index("heads"), lax.axis_index("experts")
    top = expert_ids.shape[-1]
    tokens = seg * nseq
    groups = key_matrix.shape[1] // HEAD
    here = expert_in.shape[0]
    cap = (5 * tokens * top + 4 * EXPERTS - 1) // (4 * EXPERTS)

    def local(v):
        return jnp.swapaxes(v, 0, 1).reshape((tokens,) + v.shape[2:])

    def unlocal(v):
        return jnp.swapaxes(v.reshape((nseq, seg) + v.shape[1:]), 0, 1)

    ids = local(expert_ids)
    order = local(priority)
    weight = local(route_weight)
    position = z * seg + jnp.arange(seg, dtype=jnp.int32)
    live = (position[None, :] < seq_lengths[:, None]).reshape(tokens)
    match = ids.T[:, None, :] == jnp.arange(EXPERTS, dtype=jnp.int32)[None, :, None]
    weight_e = jnp.sum(jnp.where(match, weight.T[:, None, :], 0.0), axis=0)
    chosen = jnp.any(match, axis=0) & live[None, :]
    earlier = (order[:, None] < order[None, :]).astype(BF)
    before = dot(chosen.astype(BF), earlier)
    slot = jnp.where(chosen & (before < cap), before, -1.0)
    packed = jnp.stack([slot.reshape(ne, here, tokens), weight_e.reshape(ne, here, tokens)], axis=1)
    packed = lax.all_to_all(packed, "experts", split_axis=0, concat_axis=0, tiled=True)
    packed = packed[me ^ jnp.arange(ne, dtype=jnp.int32)]
    slots = packed[:, 0].astype(jnp.int32)
    weights = packed[:, 1]

    xf = local(layer_input).astype(F32)
    inv_one = lax.rsqrt(jnp.mean(xf * xf, axis=-1, keepdims=True) + EPS)
    attn_in = (xf * inv_one * attn_gain).astype(BF)
    gathered = lax.all_gather(attn_in.reshape(nseq, seg, width), "heads", axis=0)

    wq = query_matrix.reshape(width, groups, 128)
    wk = key_matrix.reshape(width, groups, HEAD)
    wv = value_matrix.reshape(width, groups, HEAD)
    w_local = jnp.concatenate([wq, wk, wv], axis=2)
    w_groups = jnp.transpose(w_local, (1, 0, 2))
    rows_in = width // ne
    rows_out = output_matrix.shape[0] // ne
    w_local = w_local.reshape(width, groups * 256)
    w_piece = lax.dynamic_slice_in_dim(w_local, me * rows_in, rows_in, 0)
    o_piece = lax.dynamic_slice_in_dim(output_matrix, me * rows_out, rows_out, 0)
    o_full = lax.all_gather(o_piece, ("heads", "experts"), axis=0, tiled=True)

    tables = rotary_tables(nh * seg)
    qkv, heads_out, lse = attn_forward(gathered, w_groups, seq_lengths, tables)
    heads_in = lax.all_to_all(heads_out, "heads", split_axis=0, concat_axis=0, tiled=True)
    heads_in = heads_in.reshape(nh, tokens, groups * 128)
    o_parts = o_full.reshape(nh, groups * 128, width)
    branch = jnp.einsum("ztm,zmw->tw", heads_in, o_parts, preferred_element_type=F32)
    mid = xf + branch
    inv_two = lax.rsqrt(jnp.mean(mid * mid, axis=-1, keepdims=True) + EPS)
    moe_in = (mid * inv_two * moe_gain).astype(BF)

    grad = local(out_grad)
    grads_all = plane_gather(grad, ne)
    d_rows = gather_rows(slots, weights, grads_all, cap)
    moe_in, d_rows = lax.optimization_barrier((moe_in, d_rows))
    tokens_all = plane_gather(moe_in, ne)
    x_rows = gather_rows(slots, None, tokens_all, cap)
    w_piece, x_rows = lax.optimization_barrier((w_piece, x_rows))
    w_full = lax.all_gather(w_piece, ("heads", "experts"), axis=0, tiled=True)
    w_full = w_full.reshape(nh, width, groups * 256)
    results, drows, sums = experts_call(slots, weights, x_rows, d_rows, expert_in, expert_down)
    slots_t = jnp.swapaxes(slots, 1, 2)
    if nh == 4 and ne == 8:
        w_full, drows = lax.optimization_barrier((w_full, drows))
        flat = sums.reshape(-1, width)
        chunks = flat.shape[0] // CHUNK
        half = (3 * chunks) // 8
        slots8 = jnp.pad(packed[:, 0], ((0, 0), (0, 8 - here), (0, 0)), constant_values=-1.0)
        total, d_mid, gain_two, dqkv, parts = middle(
            half, seq_lengths, flat, drows, slots8, mid, grad, moe_gain.reshape(1, width), o_parts, qkv, lse, tables,
            heads_in, gathered.reshape(nh, tokens, width))
        total, out, x_grad, gains, _, wide = last(
            half, chunks - half, total, flat, results, slots8, mid, dqkv, w_full, local(layer_input), d_mid,
            attn_gain.reshape(1, width), gain_two, parts)
        o_grad, w_grad = weight_split(wide, groups * 128, groups * 256)
        gain_one, gain_two = gains[0], gains[1]
        totals = total.reshape(sums.shape).astype(F32)
        grad_in, grad_down = totals[:, :width], totals[:, width:]
    else:
        d_parts = combine(slots_t, drows)
        moe_parts = combine(slots_t, results)
        totals = heads_sum(sums, z, nh)
        grad_in, grad_down = totals[:, :width], totals[:, width:]
        d_moe = plane_scatter(d_parts, ne)
        moe_sum = plane_scatter(moe_parts, ne)
        out = (mid + moe_sum).astype(BF)
        zed = moe_gain * d_moe
        d_mid = grad.astype(F32) + inv_two * zed - mid * (inv_two ** 3 * jnp.mean(zed * mid, axis=-1, keepdims=True))
        gain_two = jnp.sum(d_moe * mid * inv_two, axis=0)
        d_branch = d_mid.astype(BF)
        d_heads = jnp.einsum("tw,zmw->ztm", d_branch, o_parts, preferred_element_type=F32).astype(BF)
        d_heads = d_heads.reshape(nh, nseq, seg, groups * 128)
        d_heads = lax.all_to_all(d_heads, "heads", split_axis=0, concat_axis=0, tiled=True)
        dqkv = attn_backward(qkv, d_heads, lse, seq_lengths, tables)
        dqkv = dqkv.reshape(nh, tokens, groups * 256)
        back = lax.all_to_all(dqkv, "heads", split_axis=0, concat_axis=0, tiled=True)
        d_attn = jnp.einsum("ztc,zmc->tm", back, w_full, preferred_element_type=F32)
        o_grad, w_grad = weight_sums(heads_in, d_branch, gathered, dqkv, ne)
        wed = attn_gain * d_attn
        x_grad = d_mid + inv_one * wed - xf * (inv_one ** 3 * jnp.mean(wed * xf, axis=-1, keepdims=True))
        gain_one = jnp.sum(d_attn * xf * inv_one, axis=0)
        gain_one, gain_two = lax.psum((gain_one, gain_two), ("heads", "experts"))
    w_grad = w_grad.reshape(width, groups, 256)
    return (
        unlocal(out),
        unlocal(x_grad),
        gain_one,
        gain_two,
        w_grad[:, :, :128].reshape(query_matrix.shape),
        w_grad[:, :, 128:192].reshape(key_matrix.shape),
        w_grad[:, :, 192:].reshape(value_matrix.shape),
        o_grad,
        grad_in,
        grad_down,
    )


def solution(mesh):
    rows = P("heads", "experts", None)
    in_specs = (
        rows,
        P("experts"),
        rows,
        rows,
        P("heads", "experts"),
        P(),
        P(),
        P(None, "heads"),
        P(None, "heads"),
        P(None, "heads"),
        P("heads", None),
        P("experts", None, None),
        P("experts", None, None),
        rows,
    )
    out_specs = (
        rows,
        rows,
        P(),
        P(),
        P(None, "heads"),
        P(None, "heads"),
        P(None, "heads"),
        P("heads", None),
        P("experts", None, None),
        P("experts", None, None),
    )
    return jax.shard_map(body, mesh=mesh, in_specs=in_specs, out_specs=out_specs, check_vma=False)
```

```python
import functools
import math

import jax
import jax.numpy as jnp
from jax import lax
from jax.experimental import pallas as pl
from jax.experimental.pallas import tpu as pltpu
from jax.sharding import PartitionSpec as P

HEAD = 64
EXPERTS = 32
EPS = 1e-06
BF = jnp.bfloat16
F32 = jnp.float32
SCALE = HEAD ** (-0.5)
NEG = -1e30
VMEM = 63 * 1024 * 1024
MESH = pl.DeviceIdType.MESH
DMA = pltpu.SemaphoreType.DMA


def dot(a, b):
    return jnp.dot(a, b, preferred_element_type=F32)


def dot_nt(a, b):
    return lax.dot_general(a, b, (((1,), (1,)), ((), ())), preferred_element_type=F32)


def dot_tn(a, b):
    return lax.dot_general(a, b, (((0,), (0,)), ((), ())), preferred_element_type=F32)


def params(n):
    return pltpu.CompilerParams(
        dimension_semantics=("arbitrary",) * n, vmem_limit_bytes=VMEM
    )


def swap_halves(v):
    lane = lax.broadcasted_iota(jnp.int32, v.shape, 1)
    return jnp.where(lane % 64 < 32, pltpu.roll(v, 96, 1), pltpu.roll(v, 32, 1))


def attn_mask(offset, n, block, length):
    key = lax.broadcasted_iota(jnp.int32, (n, block), 0)
    query = lax.broadcasted_iota(jnp.int32, (n, block), 1) + offset
    return (key <= query) & (key < length)


def two_heads(v):
    return jnp.concatenate([v[:, :HEAD], v[:, HEAD:]], axis=0)


def untwo(vt, block):
    return jnp.concatenate([vt[:, :block], vt[:, block:]], axis=0).T


def fwd_kernel(len_ref, x_ref, w_ref, cq, sq, ckv, skv, qkv_ref, head_ref, lse_ref):
    nh, _, seg, width = x_ref.shape
    full = nh * seg
    block = seg
    length = len_ref[pl.program_id(0)]
    lin = dot(x_ref[...].reshape(full, width), w_ref[0])
    ql, kvl = lin[:, :128], lin[:, 128:]
    q = (ql * cq[...] + swap_halves(ql) * sq[...]).astype(BF)
    kvr = kvl * ckv[...] + swap_halves(kvl) * skv[...]
    kv = kvr.astype(BF)
    qkv_ref[0, 0, :, :128] = q
    qkv_ref[0, 0, :, 128:] = kv
    k = kv[:, :HEAD]
    vt = kvr.T[HEAD:].astype(BF)
    for i in range(nh):
        n = (i + 1) * block
        q2 = two_heads(q[i * block : n])
        s = dot_nt(k[:n], q2)
        mask = attn_mask(i * block, n, block, length)
        s = jnp.where(jnp.concatenate([mask, mask], axis=1), s * SCALE, NEG)
        m = jnp.max(s, axis=0, keepdims=True)
        e = jnp.exp(s - m)
        total = jnp.sum(e, axis=0, keepdims=True)
        p = (e * (1.0 / total)).astype(BF)
        lse_ref[0, 0, i : i + 1, :] = m + jnp.log(total)
        head_ref[i, 0] = untwo(dot(vt[:, :n], p), block).astype(BF)


def attn_forward(x, w, lengths, tables):
    nh, nseq, seg, width = x.shape
    groups = w.shape[0]
    full = nh * seg
    cq, sq, ckv, skv = tables
    tab = pl.BlockSpec((full, 128), lambda s, g: (0, 0))
    return pl.pallas_call(
        fwd_kernel,
        grid=(nseq, groups),
        in_specs=[
            pl.BlockSpec(memory_space=pltpu.SMEM),
            pl.BlockSpec((nh, 1, seg, width), lambda s, g: (0, s, 0, 0)),
            pl.BlockSpec((1, width, 256), lambda s, g: (g, 0, 0)),
            tab,
            tab,
            tab,
            tab,
        ],
        out_specs=[
            pl.BlockSpec((1, 1, full, 256), lambda s, g: (s, g, 0, 0)),
            pl.BlockSpec((nh, 1, seg, 128), lambda s, g: (0, s, 0, g)),
            pl.BlockSpec((1, 1, nh, 2 * seg), lambda s, g: (s, g, 0, 0)),
        ],
        out_shape=[
            jax.ShapeDtypeStruct((nseq, groups, full, 256), BF),
            jax.ShapeDtypeStruct((nh, nseq, seg, groups * 128), BF),
            jax.ShapeDtypeStruct((nseq, groups, nh, 2 * seg), F32),
        ],
        compiler_params=params(2),
        cost_estimate=pl.CostEstimate(flops=6 * 10**9, bytes_accessed=12 * 2**20, transcendentals=10**7),
        name="attn_forward",
    )(lengths, x, w, cq, sq, ckv, skv)


def bwd_piece(q, kv, heads, lses, length, tables, dkv_ref, put):
    cq, sq, ckv, skv = tables
    full, block = q.shape[0], lses(0).shape[1] // 2
    k, v = kv[:, :HEAD], kv[:, HEAD:]
    kt = kv.astype(F32).T[:HEAD].astype(BF)
    dkv_ref[...] = jnp.zeros_like(dkv_ref)
    for i in range(full // block):
        n = (i + 1) * block
        rows = pl.ds(i * block, block)
        mask = attn_mask(i * block, n, block, length)
        grads = []
        for h in range(2):
            qh = q[i * block : n, h * HEAD : (h + 1) * HEAD]
            doh = heads(i)[:, h * HEAD : (h + 1) * HEAD]
            s = dot_nt(k[:n], qh)
            p = jnp.exp(jnp.where(mask, s * SCALE - lses(i)[:, h * block : (h + 1) * block], NEG))
            dp = dot_nt(v[:n], doh)
            delta = jnp.sum(p * dp, axis=0, keepdims=True)
            ds = (p * (dp - delta) * SCALE).astype(BF)
            dkv_ref[:n, :HEAD] += dot(ds, qh)
            dkv_ref[:n, HEAD:] += dot(p.astype(BF), doh)
            grads.append(dot(kt[:, :n], ds))
        dq = jnp.concatenate(grads, axis=0).T
        dq = dq * cq[rows, :] - swap_halves(dq) * sq[rows, :]
        put(i, 0, dq.astype(BF))
    dkv = dkv_ref[...]
    dkv = (dkv * ckv[...] - swap_halves(dkv) * skv[...]).astype(BF)
    for i in range(full // block):
        put(i, 128, dkv[i * block : (i + 1) * block])


def bwd_kernel(len_ref, qkv_ref, do_ref, lse_ref, cq, sq, ckv, skv, out_ref, dkv_ref):
    def put(i, lo, v):
        out_ref[i, 0, :, lo : lo + 128] = v

    bwd_piece(
        qkv_ref[0, 0, :, :128],
        qkv_ref[0, 0, :, 128:],
        lambda i: do_ref[i, 0],
        lambda i: lse_ref[0, 0, i : i + 1, :],
        len_ref[pl.program_id(0)],
        (cq, sq, ckv, skv),
        dkv_ref,
        put,
    )


def attn_backward(qkv, d_head, lse, lengths, tables):
    nseq, groups, full, _ = qkv.shape
    nh, _, seg, _ = d_head.shape
    cq, sq, ckv, skv = tables
    tab = pl.BlockSpec((full, 128), lambda s, g: (0, 0))
    return pl.pallas_call(
        bwd_kernel,
        grid=(nseq, groups),
        in_specs=[
            pl.BlockSpec(memory_space=pltpu.SMEM),
            pl.BlockSpec((1, 1, full, 256), lambda s, g: (s, g, 0, 0)),
            pl.BlockSpec((nh, 1, seg, 128), lambda s, g: (0, s, 0, g)),
            pl.BlockSpec((1, 1, nh, 2 * seg), lambda s, g: (s, g, 0, 0)),
            tab,
            tab,
            tab,
            tab,
        ],
        out_specs=pl.BlockSpec((nh, 1, seg, 256), lambda s, g: (0, s, 0, g)),
        out_shape=jax.ShapeDtypeStruct((nh, nseq, seg, groups * 256), BF),
        scratch_shapes=[pltpu.VMEM((full, 128), F32)],
        compiler_params=params(2),
        cost_estimate=pl.CostEstimate(flops=12 * 10**9, bytes_accessed=8 * 2**20, transcendentals=10**7),
        name="attn_backward",
    )(lengths, qkv, d_head, lse, cq, sq, ckv, skv)


def rotary_tables(length):
    half = HEAD // 2
    frequency = jnp.exp(jnp.arange(half, dtype=F32) * (-2.0 * math.log(10000.0) / HEAD))
    angles = jnp.arange(length, dtype=F32)[:, None] * frequency[None, :]
    cos, sin = jnp.cos(angles), jnp.sin(angles)
    c1 = jnp.concatenate([cos, cos], axis=1)
    s1 = jnp.concatenate([-sin, sin], axis=1)
    cq = jnp.concatenate([c1, c1], axis=1)
    sq = jnp.concatenate([s1, s1], axis=1)
    ckv = jnp.concatenate([c1, jnp.ones_like(c1)], axis=1)
    skv = jnp.concatenate([s1, jnp.zeros_like(s1)], axis=1)
    return cq, sq, ckv, skv


def pick_rows(slots, cap):
    tokens = slots.shape[1]
    index = lax.broadcasted_iota(jnp.int32, (cap, tokens), 0)
    return [index == slots[j : j + 1, :] for j in range(slots.shape[0])]


def gather_kernel(weighted, slot_ref, *refs):
    if weighted:
        weight_ref, tok_ref, out_ref = refs
    else:
        tok_ref, out_ref = refs[0], refs[-1]
    cap = out_ref.shape[2]
    hits = pick_rows(slot_ref[0], cap)
    rows = dot(jnp.concatenate([h.astype(F32) for h in hits], axis=0).astype(BF), tok_ref[0])
    for j, hit in enumerate(hits):
        part = rows[j * cap : (j + 1) * cap]
        if weighted:
            part = part * jnp.sum(jnp.where(hit, weight_ref[0, j : j + 1, :], 0.0), axis=1, keepdims=True)
        out_ref[j, 0] = part.astype(BF)


def gather_rows(slots, weights, tokens, cap):
    sources, here, count = slots.shape
    width = tokens.shape[-1]
    small = pl.BlockSpec((1, here, count), lambda s: (s, 0, 0))
    weighted = weights is not None
    return pl.pallas_call(
        functools.partial(gather_kernel, weighted),
        grid=(sources,),
        in_specs=[small] + [small] * weighted + [pl.BlockSpec((1, count, width), lambda s: (s, 0, 0))],
        out_specs=pl.BlockSpec((here, 1, cap, width), lambda s: (0, s, 0, 0)),
        out_shape=jax.ShapeDtypeStruct((here, sources, cap, width), BF),
        compiler_params=params(1),
        cost_estimate=pl.CostEstimate(
            flops=2 * sources * here * cap * count * width,
            bytes_accessed=2 * sources * width * (count + here * cap),
            transcendentals=0,
        ),
        name="gather_rows",
    )(*([slots] + [weights] * weighted + [tokens]))


def expert_kernel(steps, slot_ref, weight_ref, x_ref, d_ref, win_ref, wdown_ref,
                  out_ref, drow_ref, grad_ref, hid_ref, dgu_ref, *acc):
    _, sources, cap, width = x_ref.shape
    ff = wdown_ref.shape[1]
    per = 2 if sources % 2 == 0 else 1
    win, wdown = win_ref[0], wdown_ref[0]
    for c in range(sources // per):
        rows = slice(c * per * cap, (c + 1) * per * cap)
        x = x_ref[0, c * per : (c + 1) * per].reshape(per * cap, width)
        d = d_ref[0, c * per : (c + 1) * per].reshape(per * cap, width)
        gu = dot(x, win)
        gate, up = gu[:, :ff], gu[:, ff:]
        sig = 1.0 / (1.0 + jnp.exp(-gate))
        act = gate * sig
        hidden = (act * up).astype(BF)
        hid_ref[rows, :] = hidden
        result = dot(hidden, wdown).astype(BF).astype(F32)
        for b in range(per):
            hit = pick_rows(slot_ref[c * per + b, 0], cap)[0]
            w = jnp.sum(jnp.where(hit, weight_ref[c * per + b, 0], 0.0), axis=1, keepdims=True)
            out_ref[0, c * per + b] = (result[b * cap : (b + 1) * cap] * w).astype(BF)
        dh = dot_nt(d, wdown)
        dgu_ref[rows, :ff] = (dh * up * (sig * (1.0 + gate * (1.0 - sig)))).astype(BF)
        dgu_ref[rows, ff:] = (dh * act).astype(BF)
        drow = dot_nt(dgu_ref[rows, :], win).astype(BF)
        for b in range(per):
            drow_ref[0, c * per + b] = drow[b * cap : (b + 1) * cap]
    x = x_ref[0].reshape(sources * cap, width)
    d = d_ref[0].reshape(sources * cap, width)
    gin = dot_tn(x, dgu_ref[...])
    gdown = dot_tn(hid_ref[...], d)
    if steps == 1:
        grad_ref[0, :width] = gin.astype(BF)
        grad_ref[0, width:] = gdown.astype(BF)
    else:
        ain, adown = acc
        step = pl.program_id(1)

        @pl.when(step == 0)
        def _():
            ain[...] = jnp.zeros_like(ain)
            adown[...] = jnp.zeros_like(adown)

        ain[...] += gin
        adown[...] += gdown

        @pl.when(step == steps - 1)
        def _():
            grad_ref[0, :width] = ain[...].astype(BF)
            grad_ref[0, width:] = adown[...].astype(BF)


def experts_call(slots, weights, x, d, win, wdown):
    count, sources, cap, width = x.shape
    tokens = slots.shape[-1]
    ff = wdown.shape[1]
    chunk = min(sources, 8)
    steps = sources // chunk
    small = pl.BlockSpec((chunk, 1, 1, tokens), lambda j, r: (r, j, 0, 0))
    rows = pl.BlockSpec((1, chunk, cap, width), lambda j, r: (j, r, 0, 0))
    rows_out = pl.BlockSpec((1, chunk, cap, width), lambda j, r: (j, r, 0, 0))
    scratch = [pltpu.VMEM((chunk * cap, ff), BF), pltpu.VMEM((chunk * cap, 2 * ff), BF)]
    if steps > 1:
        scratch += [pltpu.VMEM((width, 2 * ff), F32), pltpu.VMEM((ff, width), F32)]
    shape = jax.ShapeDtypeStruct((count, sources, cap, width), BF)
    return pl.pallas_call(
        functools.partial(expert_kernel, steps),
        grid=(count, steps),
        in_specs=[
            small,
            small,
            rows,
            rows,
            pl.BlockSpec((1, width, 2 * ff), lambda j, r: (j, 0, 0)),
            pl.BlockSpec((1, ff, width), lambda j, r: (j, 0, 0)),
        ],
        out_specs=[
            rows_out,
            rows_out,
            pl.BlockSpec((1, width + ff, width), lambda j, r: (j, 0, 0)),
        ],
        out_shape=[
            shape,
            shape,
            jax.ShapeDtypeStruct((count, width + ff, width), BF),
        ],
        scratch_shapes=scratch,
        compiler_params=params(2),
        cost_estimate=pl.CostEstimate(
            flops=2 * count * sources * cap * width * ff * 9,
            bytes_accessed=8 * count * sources * cap * width + 12 * count * width * ff,
            transcendentals=count * sources * cap * ff,
        ),
        name="experts",
    )(slots[:, :, None, :], weights[:, :, None, :], x, d, win, wdown)


def combine_kernel(slot_ref, row_ref, out_ref):
    slots = slot_ref[0]
    count, here = slots.shape
    cap = row_ref.shape[2]
    lane = lax.broadcasted_iota(jnp.int32, (count, here * cap), 1)
    hot = None
    for j in range(here):
        col = slots[:, j : j + 1]
        hit = lane == jnp.where(col >= 0, col + j * cap, -1)
        hot = hit if hot is None else hot | hit
    hot = hot.astype(F32).astype(BF)
    out_ref[0] = dot(hot, row_ref[...].reshape(here * cap, row_ref.shape[3])).astype(BF)


def combine(slots_t, rows):
    sources, count, here = slots_t.shape
    _, _, cap, width = rows.shape
    return pl.pallas_call(
        combine_kernel,
        grid=(sources,),
        in_specs=[
            pl.BlockSpec((1, count, here), lambda s: (s, 0, 0)),
            pl.BlockSpec((here, 1, cap, width), lambda s: (0, s, 0, 0)),
        ],
        out_specs=pl.BlockSpec((1, count, width), lambda s: (s, 0, 0)),
        out_shape=jax.ShapeDtypeStruct((sources, count, width), BF),
        compiler_params=params(1),
        cost_estimate=pl.CostEstimate(
            flops=2 * sources * here * cap * count * width,
            bytes_accessed=2 * sources * width * (count + here * cap),
            transcendentals=0,
        ),
        name="combine",
    )(slots_t, rows)


def swap(x, bit, n):
    return lax.ppermute(x, "experts", [(i, i ^ bit) for i in range(n)])


def plane_gather(x, n):
    if n != 8:
        whole = lax.all_gather(x, "experts", axis=0)
        order = lax.axis_index("experts") ^ jnp.arange(n, dtype=jnp.int32)
        return whole[order]
    got = {0: x}
    for r in (2, 4, 6):
        got[r] = swap(x, r, n)
    for r in (0, 2, 4, 6):
        got[r + 1] = swap(got[r], 1, n)
    return jnp.stack([got[r] for r in range(n)], axis=0)


def plane_scatter(parts, n):
    if n != 8:
        order = lax.axis_index("experts") ^ jnp.arange(n, dtype=jnp.int32)
        return lax.psum_scatter(parts[order].astype(F32), "experts", scatter_dimension=0)
    odd = swap(parts[1::2], 1, n)
    both = [parts[2 * i].astype(F32) + odd[i].astype(F32) for i in range(4)]
    total = both[0]
    for i in (1, 2, 3):
        total = total + swap(both[i].astype(BF), 2 * i, n).astype(F32)
    return total


def heads_sum(x, z, nh):
    if nh != 4:
        return lax.psum(x.astype(F32), "heads")
    first = lax.ppermute(x, "heads", [(0, 1), (3, 2)])
    pair = (x.astype(F32) + first.astype(F32)).astype(BF)
    second = lax.ppermute(pair, "heads", [(1, 2), (2, 1)])
    total = (pair.astype(F32) + second.astype(F32)).astype(BF)
    third = lax.ppermute(total, "heads", [(1, 0), (2, 3)])
    return jnp.where((z == 1) | (z == 2), total, third).astype(F32)


def weight_sums(heads_in, d_branch, gathered, dqkv, ne):
    nh, tokens, part = heads_in.shape
    width, cols = d_branch.shape[1], dqkv.shape[2]
    col, row = width // ne, width // ne
    o = jnp.einsum("ztm,tew->ezmw", heads_in, d_branch.reshape(tokens, ne, col), preferred_element_type=F32)
    w = jnp.einsum("ztm,ztc->mc", gathered.reshape(nh, tokens, width), dqkv, preferred_element_type=F32)
    cut = cols // col
    w = jnp.swapaxes(w.reshape(ne, row, cut, col), 1, 2).reshape(ne, cut * row, col)
    both = jnp.concatenate([o.reshape(ne, nh * part, col), w], axis=1)
    both = lax.psum_scatter(both, "experts", scatter_dimension=0)
    o, w = both[: nh * part], both[nh * part :]
    o = lax.psum_scatter(o.reshape(nh, part, col), "heads", scatter_dimension=0)
    return weight_split(lax.all_gather(jnp.concatenate([o, w], axis=0), "experts", axis=0), part, cols)


def weight_split(both, part, cols):
    ne, _, col = both.shape
    width, row, cut = ne * col, col, cols // col
    o = jnp.swapaxes(both[:, :part], 0, 1).reshape(part, width)
    w = jnp.swapaxes(both[:, part:].reshape(ne, cut, row, col), 1, 2)
    return o, w.reshape(width, cols)


CHUNK = 256
LAG = 3


def remote(src, dst, send, recv, axis, index):
    return pltpu.make_async_remote_copy(
        src_ref=src, dst_ref=dst, send_sem=send, recv_sem=recv,
        device_id={axis: index}, device_id_type=MESH,
    )


def greet(nh, masks):
    z, me = lax.axis_index("heads"), lax.axis_index("experts")
    bar = pltpu.get_barrier_semaphore()
    for d in range(1, nh):
        pl.semaphore_signal(bar, inc=1, device_id={"heads": lax.rem(z + d, nh)}, device_id_type=MESH)
    for r in masks:
        pl.semaphore_signal(bar, inc=1, device_id={"experts": me ^ r}, device_id_type=MESH)
    pl.semaphore_wait(bar, nh - 1 + len(masks))


class Chain:
    def __init__(self, src, out, scratch, first, count):
        self.src, self.out, self.first, self.count = src, out, first, count
        self.a, self.b, self.buf, self.s1, self.r1, self.s2, self.r2, self.ls, self.os = scratch
        z = lax.axis_index("heads")
        self.mid = (z == 1) | (z == 2)
        self.outer = jnp.where(z == 0, 1, jnp.where(z == 1, 0, jnp.where(z == 2, 3, 2)))
        self.inner = jnp.where(z == 1, 2, jnp.where(z == 2, 1, z))

    def piece(self, k):
        return self.src.at[pl.ds((self.first + k) * CHUNK, CHUNK)]

    def load(self, k):
        return pltpu.make_async_copy(self.piece(k), self.buf.at[lax.rem(k, 2)], self.ls.at[lax.rem(k, 2)])

    def store(self, ref, k):
        return pltpu.make_async_copy(ref.at[k], self.out.at[pl.ds((self.first + k) * CHUNK, CHUNK)], self.os.at[k])

    def up(self, k):
        return remote(self.piece(k), self.a.at[k], self.s1.at[k], self.r1.at[k], "heads", self.outer)

    def across(self, k):
        return remote(self.a.at[k], self.b.at[k], self.s2.at[k], self.r2.at[k], "heads", self.inner)

    def down(self, k):
        return remote(self.b.at[k], self.a.at[k], self.s1.at[k], self.r1.at[k], "heads", self.outer)

    def begin(self):
        @pl.when(self.mid)
        def _():
            self.load(0).start()

    def steps(self):
        return self.count + LAG

    def step(self, k):
        n = self.count

        @pl.when(self.mid)
        def _():
            @pl.when(k < n)
            def _():
                @pl.when(k + 1 < n)
                def _():
                    self.load(k + 1).start()

                self.load(k).wait()
                self.up(k).wait_recv()
                own = self.buf[lax.rem(k, 2)].astype(F32)
                self.a[k] = (self.a[k].astype(F32) + own).astype(BF)
                self.across(k).start()

            @pl.when((k >= 1) & (k <= n))
            def _():
                j = k - 1
                self.across(j).wait_recv()
                self.b[j] = (self.a[j].astype(F32) + self.b[j].astype(F32)).astype(BF)
                self.down(j).start()
                self.store(self.b, j).start()

        @pl.when(jnp.logical_not(self.mid))
        def _():
            @pl.when(k < n)
            def _():
                @pl.when(k >= LAG)
                def _():
                    self.up(k - LAG).wait_send()

                self.up(k).start()

            @pl.when(k >= LAG)
            def _():
                j = k - LAG
                self.down(j).wait_recv()
                self.store(self.a, j).start()

    def run(self, first, last):
        @pl.loop(first, last)
        def _(k):
            self.step(k)

    def finish(self):
        n = self.count

        @pl.when(self.mid)
        def _():
            @pl.loop(0, n)
            def _(k):
                self.across(k).wait_send()
                self.down(k).wait_send()
                self.store(self.b, k).wait()

        @pl.when(jnp.logical_not(self.mid))
        def _():
            @pl.loop(n - LAG, n)
            def _(k):
                self.up(k).wait_send()

            @pl.loop(0, n)
            def _(k):
                self.store(self.a, k).wait()


def chain_scratch(count, width):
    return [
        pltpu.VMEM((count, CHUNK, width), BF),
        pltpu.VMEM((count, CHUNK, width), BF),
        pltpu.VMEM((2, CHUNK, width), BF),
        DMA((count,)),
        DMA((count,)),
        DMA((count,)),
        DMA((count,)),
        DMA((2,)),
        DMA((count,)),
    ]


class PlaneSum:
    order = (3, 1, 2)

    def __init__(self, rows, slots, total, scratch):
        self.rows, self.slots, self.total = rows, slots, total
        self.buf, self.odd, self.c, self.e, self.f, self.ls, self.cs, self.cr, self.fs, self.fr = scratch
        self.me = lax.axis_index("experts")
        self.here, _, self.cap, self.width = rows.shape

    def load(self, r, at):
        return [
            pltpu.make_async_copy(self.rows.at[j, r], self.buf.at[at, j], self.ls.at[at, j])
            for j in range(self.here)
        ]

    def core(self, i):
        return remote(self.odd.at[i], self.c.at[i], self.cs.at[i], self.cr.at[i], "experts", self.me ^ 1)

    def chip(self, i):
        return remote(self.e.at[i - 1], self.f.at[i - 1], self.fs.at[i - 1], self.fr.at[i - 1], "experts", self.me ^ (2 * i))

    def part(self, r, at, after, after_at):
        if after is not None:
            for c in self.load(after, after_at):
                c.start()
        slots = self.slots[r].T.astype(jnp.int32)
        lane = lax.broadcasted_iota(jnp.int32, (slots.shape[0], self.here * self.cap), 1)
        hot = None
        for j in range(self.here):
            col = slots[:, j : j + 1]
            hit = lane == jnp.where(col >= 0, col + j * self.cap, -1)
            hot = hit if hot is None else hot | hit
        for c in self.load(r, at):
            c.wait()
        rows = self.buf[at].reshape(self.here * self.cap, self.width)
        return dot(hot.astype(F32).astype(BF), rows)

    def run(self, chain, step):
        turns = [2 * i + 1 for i in self.order + (0,)] + [2 * i for i in self.order + (0,)]
        for c in self.load(turns[0], 0):
            c.start()
        for t, r in enumerate(turns):
            after = turns[t + 1] if t + 1 < len(turns) else None
            value = self.part(r, t % 2, after, (t + 1) % 2)
            i = r // 2
            if r % 2:
                self.odd[i] = value.astype(BF)
                self.core(i).start()
            else:
                self.core(i).wait_recv()
                value = value + self.c[i].astype(F32)
                if i:
                    self.e[i - 1] = value.astype(BF)
                    self.chip(i).start()
                else:
                    self.total[...] = value
            if t == 3:
                chain.run(step, step + 1)
        chain.run(step + 1, step + 4)
        for i in self.order:
            self.chip(i).wait_recv()
        return step + 4

    def rows_total(self, rows):
        d = self.total[rows]
        for r in range(3):
            d = d + self.f[r, rows].astype(F32)
        return d

    def finish(self):
        for i in range(4):
            self.core(i).wait_send()
        for i in self.order:
            self.chip(i).wait_send()


def plane_scratch(here, cap, tokens, width):
    return [
        pltpu.VMEM((2, here, cap, width), BF),
        pltpu.VMEM((4, tokens, width), BF),
        pltpu.VMEM((4, tokens, width), BF),
        pltpu.VMEM((3, tokens, width), BF),
        pltpu.VMEM((3, tokens, width), BF),
        DMA((2, here)),
        DMA((4,)),
        DMA((4,)),
        DMA((3,)),
        DMA((3,)),
    ]


PLANE = 10


class Exchange:
    def __init__(self, src, dst, send, recv, nh):
        self.src, self.dst, self.ss, self.rs, self.nh = src, dst, send, recv, nh
        self.z = lax.axis_index("heads")

    def send(self, d):
        to = lax.rem(self.z + d, self.nh)
        return remote(self.src.at[to], self.dst.at[self.z], self.ss.at[d], self.rs.at[d], "heads", to)

    def start(self):
        for d in range(1, self.nh):
            self.send(d).start()
        own = pl.ds(self.z, 1)
        self.dst[own] = self.src[own]

    def wait_recv(self):
        for d in range(1, self.nh):
            at = lax.rem(self.z + self.nh - d, self.nh)
            remote(self.src.at[at], self.dst.at[at], self.ss.at[d], self.rs.at[d], "heads", at).wait_recv()

    def finish(self):
        for d in range(1, self.nh):
            self.send(d).wait_send()


ROWS = 128


class PlaneGather:
    order = (3, 1, 2)

    def __init__(self, own, slot, sems):
        self.own, self.slot = own, slot
        self.cs, self.cr, self.ks, self.kr = sems
        self.me = lax.axis_index("experts")

    def chip(self, i, e):
        return remote(self.own, self.slot(e), self.cs.at[i], self.cr.at[i], "experts", self.me ^ (2 * i))

    def core(self, i, src, e):
        return remote(src, self.slot(e), self.ks.at[i], self.kr.at[i], "experts", self.me ^ 1)

    def start(self):
        self.core(0, self.own, self.me).start()
        for i in self.order:
            self.chip(i, self.me).start()

    def forward(self, i):
        e = self.me ^ (2 * i)
        self.chip(i, e).wait_recv()
        self.core(i, self.slot(e), e).start()

    def core_arrive(self, i):
        e = self.me ^ 1 ^ (2 * i)
        self.core(i, self.slot(e), e).wait_recv()

    def finish(self):
        for i in range(1, 4):
            self.chip(i, self.me).wait_send()
        for i in range(4):
            self.core(i, self.own if i == 0 else self.slot(self.me ^ (2 * i)), self.me).wait_send()


GATHER = 4


def gather_sems():
    return [DMA((4,)), DMA((4,)), DMA((4,)), DMA((4,))]


class Picker:
    def __init__(self, pack, stage, sems, here, cap):
        self.pack, self.stage, self.sems, self.here, self.cap = pack, stage, sems, here, cap
        self.turn, self.pending = 0, {}

    def pick(self, r, tokens, out, weighted):
        at = self.turn % 2
        self.turn += 1
        info = self.pack[r]
        slots = info.astype(jnp.int32)
        index = lax.broadcasted_iota(jnp.int32, (self.cap, slots.shape[1]), 0)
        hits = [index == slots[j : j + 1] for j in range(self.here)]
        rows = dot(jnp.concatenate([h.astype(F32) for h in hits], axis=0).astype(BF), tokens)
        for c in self.pending.get(at, []):
            c.wait()
        for j, hit in enumerate(hits):
            part = rows[j * self.cap : (j + 1) * self.cap]
            if weighted:
                w = info[self.here + j : self.here + j + 1]
                part = part * jnp.sum(jnp.where(hit, w, 0.0), axis=1, keepdims=True)
            self.stage[at, j] = part.astype(BF)
        self.pending[at] = [
            pltpu.make_async_copy(self.stage.at[at, j], out.at[j, r], self.sems.at[at, j])
            for j in range(self.here)
        ]
        for c in self.pending[at]:
            c.start()

    def finish(self):
        for copies in self.pending.values():
            for c in copies:
                c.wait()


def front_kernel(len_ref, x_ref, og_ref, w_ref, om_ref, pk_ref, again_ref, mgain_ref, cq, sq, ckv, skv,
                 xg_ref, qkv_ref, lse_ref, hin_ref, of_ref, wf_ref, mid_ref, pack_ref, drows_ref, xrows_ref,
                 hs, ogb, mt, stage, ls, lr, ps, pr, hss, hrs, os_, or_, ws, wr, ss, *sems):
    nh, tokens, width = xg_ref.shape
    nseq, groups, full, _ = qkv_ref.shape
    ne = ogb.shape[0]
    seg = tokens // nseq
    here, _, cap, _ = drows_ref.shape
    z, me = lax.axis_index("heads"), lax.axis_index("experts")
    og = PlaneGather(og_ref, lambda e: ogb.at[e], sems[:GATHER])
    og_moe = PlaneGather(mt.at[me], lambda e: mt.at[e], sems[GATHER : 2 * GATHER])
    og_o = PlaneGather(of_ref.at[:, me], lambda e: of_ref.at[:, e], sems[2 * GATHER : 3 * GATHER])
    og_w = PlaneGather(wf_ref.at[:, me], lambda e: wf_ref.at[:, e], sems[3 * GATHER : 4 * GATHER])
    heads = Exchange(hs, hin_ref, hss, hrs, nh)
    picker = Picker(pack_ref, stage, ss, here, cap)

    @pl.loop(0, tokens // ROWS)
    def _(i):
        rows = pl.ds(i * ROWS, ROWS)
        x = x_ref[rows].astype(F32)
        inv = lax.rsqrt(jnp.mean(x * x, axis=-1, keepdims=True) + EPS)
        xg_ref[z, rows] = (x * inv * again_ref[...]).astype(BF)

    greet(nh, tuple(range(1, ne)))

    def hop(way, t, p, s, to):
        ref = xg_ref.at[s, pl.ds(p * seg, seg)]
        return remote(ref, ref, ls.at[way, t, p], lr.at[s, p], "heads", to)

    right, left = jnp.minimum(z + 1, nh - 1), jnp.maximum(z - 1, 0)
    for p in range(nseq):
        @pl.when(z < nh - 1)
        def _():
            hop(0, 0, p, z, right).start()

        @pl.when(z > 0)
        def _():
            hop(1, 0, p, z, left).start()

    def info(r):
        return remote(pk_ref.at[me ^ r], pack_ref.at[r], ps.at[r], pr.at[r], "experts", me ^ r)

    for r in range(1, ne):
        info(r).start()
    og.start()
    pack_ref[0] = pk_ref[me]

    def project(s, p):
        x = xg_ref[s, pl.ds(p * seg, seg)]
        at = pl.ds(s * seg, seg)
        for g in range(groups):
            lin = dot(x, w_ref[:, g * 256 : (g + 1) * 256])
            q, kv = lin[:, :128], lin[:, 128:]
            qkv_ref[p, g, at, :128] = (q * cq[at] + swap_halves(q) * sq[at]).astype(BF)
            qkv_ref[p, g, at, 128:] = (kv * ckv[at] + swap_halves(kv) * skv[at]).astype(BF)

    @pl.loop(0, nseq)
    def _(p):
        project(z, p)

    def round_of(t):
        @pl.loop(0, nseq)
        def _(p):
            @pl.when(z >= t)
            def _():
                s = z - t
                hop(0, t, p, s, left).wait_recv()

                @pl.when(z < nh - 1)
                def _():
                    hop(0, t, p, s, right).start()

                project(s, p)

            @pl.when(z + t < nh)
            def _():
                s = z + t
                hop(1, t, p, s, right).wait_recv()

                @pl.when(z > 0)
                def _():
                    hop(1, t, p, s, left).start()

                project(s, p)

    picker.pick(0, og_ref[...], drows_ref, True)
    round_of(1)
    for r in range(1, ne):
        info(r).wait_recv()
    og.core_arrive(0)
    picker.pick(1, ogb[me ^ 1], drows_ref, True)
    round_of(2)
    for i in og.order:
        og.forward(i)
    for i in og.order:
        picker.pick(2 * i, ogb[me ^ (2 * i)], drows_ref, True)
    round_of(3)

    rows_o, rows_w = of_ref.shape[2], wf_ref.shape[2]
    of_ref[z, me] = om_ref[pl.ds(pl.multiple_of(me * rows_o, rows_o), rows_o)]
    wf_ref[z, me] = w_ref[pl.ds(pl.multiple_of(me * rows_w, rows_w), rows_w)]

    def piece(ref, s, r, d, to, h):
        return remote(ref.at[h, me], ref.at[h, me], s.at[d], r.at[d], "heads", to)

    for ref, s, r in ((of_ref, os_, or_), (wf_ref, ws, wr)):
        for d in range(1, nh):
            piece(ref, s, r, d, lax.rem(z + d, nh), z).start()

    @pl.loop(0, nseq)
    def _(p):
        length = len_ref[p]
        at = pl.ds(p * seg, seg)
        for g in range(groups):
            q = qkv_ref[p, g, :, :128]
            kv = qkv_ref[p, g, :, 128:]
            k = kv[:, :HEAD]
            vt = kv.astype(F32).T[HEAD:].astype(BF)
            for i in range(nh):
                n = (i + 1) * seg
                q2 = two_heads(q[i * seg : n])
                s = dot_nt(k[:n], q2)
                mask = attn_mask(i * seg, n, seg, length)
                s = jnp.where(jnp.concatenate([mask, mask], axis=1), s * SCALE, NEG)
                m = jnp.max(s, axis=0, keepdims=True)
                e = jnp.exp(s - m)
                total = jnp.sum(e, axis=0, keepdims=True)
                prob = (e * (1.0 / total)).astype(BF)
                lse_ref[p, g, i : i + 1, :] = m + jnp.log(total)
                hs[i, at, g * 128 : (g + 1) * 128] = untwo(dot(vt[:, :n], prob), seg).astype(BF)

    heads.start()
    for ref, s, r, gather in ((of_ref, os_, or_, og_o), (wf_ref, ws, wr, og_w)):
        for d in range(1, nh):
            src = lax.rem(z + nh - d, nh)
            piece(ref, s, r, d, src, src).wait_recv()
        gather.start()
    for i in (0,) + og.order:
        if i:
            og.core_arrive(i)
            picker.pick(2 * i + 1, ogb[me ^ 1 ^ (2 * i)], drows_ref, True)
    for i in og.order:
        og_o.forward(i)
    for i in range(4):
        og_o.core_arrive(i)
    heads.wait_recv()

    mid_ref[...] = x_ref[...].astype(F32) + dot(hin_ref[0], of_ref[0].reshape(-1, width))
    for h in range(1, nh):
        mid_ref[...] += dot(hin_ref[h], of_ref[h].reshape(-1, width))

    @pl.loop(0, tokens // ROWS)
    def _(i):
        rows = pl.ds(i * ROWS, ROWS)
        m = mid_ref[rows]
        inv = lax.rsqrt(jnp.mean(m * m, axis=-1, keepdims=True) + EPS)
        mt[me, rows] = (m * inv * mgain_ref[...]).astype(BF)

    og_moe.start()
    picker.pick(0, mt[me], xrows_ref, False)
    og_moe.core_arrive(0)
    picker.pick(1, mt[me ^ 1], xrows_ref, False)
    for i in og.order:
        og_w.forward(i)
    for i in (1, 2, 3):
        og_moe.forward(i)
        picker.pick(2 * i, mt[me ^ (2 * i)], xrows_ref, False)
        if i > 1:
            og_moe.core_arrive(i - 1)
            picker.pick(2 * i - 1, mt[me ^ 1 ^ (2 * i - 2)], xrows_ref, False)
    og_moe.core_arrive(3)
    picker.pick(7, mt[me ^ 7], xrows_ref, False)
    picker.finish()
    for i in range(4):
        og_w.core_arrive(i)
    for gather in (og, og_moe, og_o, og_w):
        gather.finish()
    heads.finish()
    for r in range(1, ne):
        info(r).wait_send()
    for ref, s, r in ((of_ref, os_, or_), (wf_ref, ws, wr)):
        for d in range(1, nh):
            piece(ref, s, r, d, lax.rem(z + d, nh), z).wait_send()
    for p in range(nseq):
        for t in range(nh):
            @pl.when((z >= t) & (z < nh - 1))
            def _():
                hop(0, t, p, z - t, right).wait_send()

            @pl.when((z + t < nh) & (z > 0))
            def _():
                hop(1, t, p, z + t, left).wait_send()


def front(lengths, x, og, w_local, o_local, packed, attn_gain, moe_gain, tables, nh, nseq, cap):
    ne, info, _ = packed.shape
    tokens, width = x.shape
    here = info // 2
    cols = w_local.shape[1]
    groups, seg = cols // 256, tokens // nseq
    full = nh * seg
    part = o_local.shape[0]
    vmem = pl.BlockSpec(memory_space=pltpu.VMEM)
    hbm = pl.BlockSpec(memory_space=pl.ANY)
    rows = jax.ShapeDtypeStruct((here, ne, cap, width), BF)
    return pl.pallas_call(
        front_kernel,
        in_specs=[pl.BlockSpec(memory_space=pltpu.SMEM)] + [vmem] * 11,
        out_specs=[vmem] * 8 + [hbm, hbm],
        out_shape=[
            jax.ShapeDtypeStruct((nh, tokens, width), BF),
            jax.ShapeDtypeStruct((nseq, groups, full, 256), BF),
            jax.ShapeDtypeStruct((nseq, groups, nh, 2 * seg), F32),
            jax.ShapeDtypeStruct((nh, tokens, part), BF),
            jax.ShapeDtypeStruct((nh, ne, part // ne, width), BF),
            jax.ShapeDtypeStruct((nh, ne, width // ne, cols), BF),
            jax.ShapeDtypeStruct((tokens, width), F32),
            jax.ShapeDtypeStruct(packed.shape, F32),
            rows,
            rows,
        ],
        scratch_shapes=[
            pltpu.VMEM((nh, tokens, part), BF),
            pltpu.VMEM((ne, tokens, width), BF),
            pltpu.VMEM((ne, tokens, width), BF),
            pltpu.VMEM((2, here, cap, width), BF),
            DMA((2, nh, nseq)),
            DMA((nh, nseq)),
            DMA((ne,)),
            DMA((ne,)),
            DMA((nh,)),
            DMA((nh,)),
            DMA((nh,)),
            DMA((nh,)),
            DMA((nh,)),
            DMA((nh,)),
            DMA((2, here)),
        ]
        + gather_sems() * 4,
        compiler_params=pltpu.CompilerParams(
            collective_id=3, has_side_effects=True, vmem_limit_bytes=VMEM
        ),
        cost_estimate=pl.CostEstimate(flops=10**11, bytes_accessed=60 * 2**20, transcendentals=10**7),
        name="front",
    )(lengths, x, og, w_local, o_local, packed, attn_gain, moe_gain, *tables)


def middle_kernel(count, len_ref, sum_ref, rows_ref, slot_ref, mid_ref, grad_ref, gain_ref, o_ref, qkv_ref, lse_ref,
                  cq, sq, ckv, skv, hin_ref, x_ref, total_ref, dmid_ref, gtwo_ref, dqkv_ref, parts_ref,
                  dbranch_ref, hs, hr, dmoe, dkv, hss, hrs, xs, *scratch):
    nh, tokens, _ = dqkv_ref.shape
    nseq, groups = qkv_ref.shape[:2]
    seg = tokens // nseq
    chain = Chain(sum_ref, total_ref, scratch[PLANE:], 0, count)
    plane = PlaneSum(rows_ref, slot_ref, dmoe, scratch[:PLANE])
    heads = Exchange(hs, hr, hss, hrs, nh)
    greet(nh, (1, 2, 4, 6))
    chain.begin()
    chain.run(0, 1)
    step = plane.run(chain, 1)
    gtwo_ref[...] = jnp.zeros_like(gtwo_ref)

    @pl.loop(0, tokens // ROWS)
    def _(i):
        rows = pl.ds(i * ROWS, ROWS)
        d = plane.rows_total(rows)
        m = mid_ref[rows]
        inv = lax.rsqrt(jnp.mean(m * m, axis=-1, keepdims=True) + EPS)
        zed = gain_ref[...] * d
        dm = grad_ref[rows].astype(F32) + inv * zed - m * (inv * inv * inv * jnp.mean(zed * m, axis=-1, keepdims=True))
        gtwo_ref[...] += jnp.sum(d * m * inv, axis=0, keepdims=True)
        dmid_ref[rows] = dm
        db = dm.astype(BF)
        dbranch_ref[rows] = db
        for h in range(nh):
            hs[h, rows] = dot_nt(db, o_ref[h]).astype(BF)

    heads.start()
    chain.run(step, step + 3)
    step = step + 3
    heads.wait_recv()

    @pl.loop(0, nseq)
    def _(s):
        length = len_ref[s]
        at = pl.ds(s * seg, seg)
        for g in range(groups):
            def put(i, lo, v):
                dqkv_ref[i, at, g * 256 + lo : g * 256 + lo + 128] = v

            bwd_piece(
                qkv_ref[s, g, :, :128],
                qkv_ref[s, g, :, 128:],
                lambda i: hr[i, at, g * 128 : (g + 1) * 128],
                lambda i: lse_ref[s, g, i : i + 1, :],
                length,
                (cq, sq, ckv, skv),
                dkv,
                put,
            )
        chain.step(step + s)

    step = step + nseq
    for i in range(4):
        plane.core(i).wait_send()
    load = pltpu.make_async_copy(x_ref, plane.odd, xs)
    load.start()
    ne, _, col = parts_ref.shape
    part = hin_ref.shape[2]
    db = dbranch_ref[...]
    for h in range(nh):
        o = dot_tn(hin_ref[h], db)
        for e in range(ne):
            parts_ref[e, h * part : (h + 1) * part] = o[:, e * col : (e + 1) * col]
    chain.run(step, step + 1)
    load.wait()
    wsum = dmoe
    wsum[...] = dot_tn(dqkv_ref[0], plane.odd[0])
    for h in range(1, nh):
        wsum[...] += dot_tn(dqkv_ref[h], plane.odd[h])
    row = wsum.shape[1] // ne
    for e in range(ne):
        for c in range(wsum.shape[0] // col):
            at = nh * part + c * row
            parts_ref[e, at : at + row] = wsum[c * col : (c + 1) * col, e * row : (e + 1) * row].T
    chain.run(step + 1, chain.steps())
    chain.finish()
    for i in plane.order:
        plane.chip(i).wait_send()
    heads.finish()


def middle(count, lengths, sums, rows, slots, mid, grad, gain, o_parts, qkv, lse, tables, heads_in, x):
    nseq, groups, full, _ = qkv.shape
    nh = o_parts.shape[0]
    tokens, width = mid.shape
    here, ne, cap, _ = rows.shape
    vmem = pl.BlockSpec(memory_space=pltpu.VMEM)
    hbm = pl.BlockSpec(memory_space=pl.ANY)
    heads = (nh, tokens, groups * 128)
    col = width // ne
    cols = groups * 256
    return pl.pallas_call(
        functools.partial(middle_kernel, count),
        in_specs=[pl.BlockSpec(memory_space=pltpu.SMEM), hbm, hbm] + [vmem] * 12 + [hbm],
        out_specs=[hbm] + [vmem] * 4,
        out_shape=[
            jax.ShapeDtypeStruct(sums.shape, BF),
            jax.ShapeDtypeStruct((tokens, width), F32),
            jax.ShapeDtypeStruct((1, width), F32),
            jax.ShapeDtypeStruct((nh, tokens, cols), BF),
            jax.ShapeDtypeStruct((ne, width + cols * width // (ne * col), col), F32),
        ],
        scratch_shapes=[
            pltpu.VMEM((tokens, width), BF),
            pltpu.VMEM(heads, BF),
            pltpu.VMEM(heads, BF),
            pltpu.VMEM((tokens, width), F32),
            pltpu.VMEM((full, 128), F32),
            DMA((nh,)),
            DMA((nh,)),
            DMA,
        ]
        + plane_scratch(here, cap, tokens, width)
        + chain_scratch(count, width),
        compiler_params=pltpu.CompilerParams(
            collective_id=1, has_side_effects=True, vmem_limit_bytes=VMEM
        ),
        cost_estimate=pl.CostEstimate(flops=10**11, bytes_accessed=30 * 2**20, transcendentals=10**7),
        name="middle",
    )(lengths, sums, rows, slots, mid, grad, gain, o_parts, qkv, lse, *tables, heads_in, x)


def last_kernel(first, count, begun_ref, sum_ref, rows_ref, slot_ref, mid_ref, dqkv_ref, w_ref, x_ref, dmid_ref, gain_ref, gtwo_ref,
                parts_ref, total_ref, out_ref, xgrad_ref, gains_ref, got_ref, wide_ref,
                br, moe, gp, gz, acc, stage, oz, fin, brs, brr, gps, gpr, gzs, gzr, ws, wr, wl, oss, ors, fs, fr, fl, *scratch):
    nh, tokens, _ = dqkv_ref.shape
    dattn = moe
    ne = rows_ref.shape[1]
    z, me = lax.axis_index("heads"), lax.axis_index("experts")
    chain = Chain(sum_ref, total_ref, scratch[PLANE:], first, count)
    plane = PlaneSum(rows_ref, slot_ref, moe, scratch[:PLANE])
    back = Exchange(dqkv_ref, br, brs, brr, nh)
    greet(nh, tuple(range(1, ne)))
    back.start()
    chain.begin()

    def scatter(r, at):
        return remote(parts_ref.at[me ^ r], got_ref.at[at], ws.at[r], wr.at[r], "experts", me ^ r)

    for r in (6, 7, 2, 3, 4, 5, 1):
        scatter(r, me).start()
    chain.run(0, 3)
    step = plane.run(chain, 3)

    @pl.loop(0, tokens // ROWS)
    def _(i):
        rows = pl.ds(i * ROWS, ROWS)
        out_ref[rows] = (mid_ref[rows] + plane.rows_total(rows)).astype(BF)

    def fetch(r):
        ref = got_ref.at[me ^ r] if r else parts_ref.at[me]
        return pltpu.make_async_copy(ref, stage.at[r % 2], wl.at[r % 2])

    for r in range(ne):
        if r:
            scatter(r, me ^ r).wait_recv()
        fetch(r).start()
        if r:
            fetch(r - 1).wait()
            acc[...] = stage[0] if r == 1 else acc[...] + stage[(r - 1) % 2]
    fetch(ne - 1).wait()
    acc[...] += stage[(ne - 1) % 2]
    part = oz.shape[1]

    def strip(d, to, at):
        rows = pl.ds(pl.multiple_of(to * part, part), part)
        return remote(acc.at[rows], oz.at[at], oss.at[d], ors.at[d], "heads", to)

    for d in range(1, nh):
        strip(d, lax.rem(z + d, nh), z).start()
    oz[z] = acc[pl.ds(pl.multiple_of(z * part, part), part)]
    chain.run(step, step + 1)
    step = step + 1
    back.wait_recv()
    dattn[...] = dot_nt(br[0], w_ref[0])
    for h in range(1, nh):
        dattn[...] += dot_nt(br[h], w_ref[h])
    pad = jnp.zeros((6, gtwo_ref.shape[1]), F32)
    own = jnp.zeros_like(gtwo_ref[...])

    def rows_back(i, total):
        rows = pl.ds(i * ROWS, ROWS)
        d = dattn[rows]
        x = x_ref[rows].astype(F32)
        inv = lax.rsqrt(jnp.mean(x * x, axis=-1, keepdims=True) + EPS)
        wed = gain_ref[...] * d
        xgrad_ref[rows] = dmid_ref[rows] + inv * wed - x * (inv * inv * inv * jnp.mean(wed * x, axis=-1, keepdims=True))
        return total + jnp.sum(d * x * inv, axis=0, keepdims=True)

    own = lax.fori_loop(0, tokens // ROWS, rows_back, own)
    gp[me] = jnp.concatenate([own, gtwo_ref[...], pad], axis=0)

    def near(r, at):
        return remote(gp.at[me], gp.at[at], gps.at[r], gpr.at[r], "experts", me ^ r)

    for r in range(1, ne):
        near(r, me).start()
    for d in range(1, nh):
        src = lax.rem(z + nh - d, nh)
        strip(d, src, src).wait_recv()
    fin[:part] = oz[0] + oz[1] + oz[2] + oz[3]
    fin[part:] = acc[nh * part :]

    def spread(r, at):
        return remote(fin, wide_ref.at[at], fs.at[r], fr.at[r], "experts", me ^ r)

    for r in (6, 7, 2, 3, 4, 5, 1):
        spread(r, me).start()
    keep = pltpu.make_async_copy(fin, wide_ref.at[me], fl)
    keep.start()
    chain.run(step, step + 1)
    total = None
    for r in range(1, ne):
        near(r, me ^ r).wait_recv()
    for e in range(ne):
        total = gp[e] if total is None else total + gp[e]
    gz[z] = total

    def far(d, to, at):
        return remote(gz.at[z], gz.at[at], gzs.at[d], gzr.at[d], "heads", to)

    for d in range(1, nh):
        far(d, lax.rem(z + d, nh), z).start()
    chain.run(step + 1, chain.steps())
    total = None
    for d in range(1, nh):
        src = lax.rem(z + nh - d, nh)
        far(d, src, src).wait_recv()
    for h in range(nh):
        total = gz[h] if total is None else total + gz[h]
    gains_ref[...] = total
    chain.finish()
    plane.finish()
    back.finish()
    keep.wait()
    for r in range(1, ne):
        near(r, me).wait_send()
        scatter(r, me).wait_send()
        spread(r, me ^ r).wait_recv()
        spread(r, me).wait_send()
    for d in range(1, nh):
        far(d, lax.rem(z + d, nh), z).wait_send()
        strip(d, lax.rem(z + d, nh), z).wait_send()


def last(first, count, total, sums, rows, slots, mid, dqkv, w_full, x, d_mid, gain, gain_two, parts):
    nh, tokens, cols = dqkv.shape
    here, ne, cap, width = rows.shape
    col = parts.shape[2]
    deep = parts.shape[1] - width + width // nh
    hbm = pl.BlockSpec(memory_space=pl.ANY)
    vmem = pl.BlockSpec(memory_space=pltpu.VMEM)
    return pl.pallas_call(
        functools.partial(last_kernel, first, count),
        in_specs=[hbm, hbm, hbm] + [vmem] * 8 + [hbm],
        input_output_aliases={0: 0},
        out_specs=[hbm] + [vmem] * 3 + [hbm, hbm],
        out_shape=[
            jax.ShapeDtypeStruct(sums.shape, BF),
            jax.ShapeDtypeStruct((tokens, width), BF),
            jax.ShapeDtypeStruct((tokens, width), F32),
            jax.ShapeDtypeStruct((8, width), F32),
            jax.ShapeDtypeStruct(parts.shape, F32),
            jax.ShapeDtypeStruct((ne, deep, col), F32),
        ],
        scratch_shapes=[
            pltpu.VMEM((nh, tokens, cols), BF),
            pltpu.VMEM((tokens, width), F32),
            pltpu.VMEM((ne, 8, width), F32),
            pltpu.VMEM((nh, 8, width), F32),
            pltpu.VMEM(parts.shape[1:], F32),
            pltpu.VMEM((2,) + parts.shape[1:], F32),
            pltpu.VMEM((nh, width // nh, col), F32),
            pltpu.VMEM((deep, col), F32),
            DMA((nh,)),
            DMA((nh,)),
            DMA((ne,)),
            DMA((ne,)),
            DMA((nh,)),
            DMA((nh,)),
            DMA((ne,)),
            DMA((ne,)),
            DMA((2,)),
            DMA((nh,)),
            DMA((nh,)),
            DMA((ne,)),
            DMA((ne,)),
            DMA,
        ]
        + plane_scratch(here, cap, tokens, width)
        + chain_scratch(count, width),
        compiler_params=pltpu.CompilerParams(
            collective_id=2, has_side_effects=True, vmem_limit_bytes=VMEM
        ),
        cost_estimate=pl.CostEstimate(flops=2 * 10**11, bytes_accessed=30 * 2**20, transcendentals=0),
        name="last",
    )(total, sums, rows, slots, mid, dqkv, w_full, x, d_mid, gain, gain_two, parts)


def body(layer_input, seq_lengths, expert_ids, route_weight, priority, attn_gain, moe_gain,
         query_matrix, key_matrix, value_matrix, output_matrix, expert_in, expert_down, out_grad):
    seg, nseq, width = layer_input.shape
    nh, ne = lax.axis_size("heads"), lax.axis_size("experts")
    z, me = lax.axis_index("heads"), lax.axis_index("experts")
    top = expert_ids.shape[-1]
    tokens = seg * nseq
    groups = key_matrix.shape[1] // HEAD
    here = expert_in.shape[0]
    cap = (5 * tokens * top + 4 * EXPERTS - 1) // (4 * EXPERTS)

    def local(v):
        return jnp.swapaxes(v, 0, 1).reshape((tokens,) + v.shape[2:])

    def unlocal(v):
        return jnp.swapaxes(v.reshape((nseq, seg) + v.shape[1:]), 0, 1)

    ids = local(expert_ids)
    order = local(priority)
    weight = local(route_weight)
    position = z * seg + jnp.arange(seg, dtype=jnp.int32)
    live = (position[None, :] < seq_lengths[:, None]).reshape(tokens)
    match = ids.T[:, None, :] == jnp.arange(EXPERTS, dtype=jnp.int32)[None, :, None]
    weight_e = jnp.sum(jnp.where(match, weight.T[:, None, :], 0.0), axis=0)
    chosen = jnp.any(match, axis=0) & live[None, :]
    earlier = (order[:, None] < order[None, :]).astype(BF)
    before = dot(chosen.astype(BF), earlier)
    slot = jnp.where(chosen & (before < cap), before, -1.0)
    packed = jnp.concatenate([slot.reshape(ne, here, tokens), weight_e.reshape(ne, here, tokens)], axis=1)
    wq = query_matrix.reshape(width, groups, 128)
    wk = key_matrix.reshape(width, groups, HEAD)
    wv = value_matrix.reshape(width, groups, HEAD)
    w_local = jnp.concatenate([wq, wk, wv], axis=2).reshape(width, groups * 256)
    tables = rotary_tables(nh * seg)
    x, grad = local(layer_input), local(out_grad)
    xf = x.astype(F32)
    gain_a, gain_m = attn_gain.reshape(1, width), moe_gain.reshape(1, width)
    fast = nh == 4 and ne == 8
    if fast:
        gathered, qkv, lse, heads_in, o_full, w_full, mid, pack, d_rows, x_rows = front(
            seq_lengths, x, grad, w_local, output_matrix, packed, gain_a, gain_m, tables, nh, nseq, cap)
        slots, weights = pack[:, :here].astype(jnp.int32), pack[:, here:]
        w_full = w_full.reshape(nh, width, groups * 256)
        o_parts = o_full.reshape(nh, groups * 128, width)
    else:
        packed = lax.all_to_all(packed, "experts", split_axis=0, concat_axis=0, tiled=True)
        packed = packed[me ^ jnp.arange(ne, dtype=jnp.int32)]
        slots, weights = packed[:, :here].astype(jnp.int32), packed[:, here:]
        inv_one = lax.rsqrt(jnp.mean(xf * xf, axis=-1, keepdims=True) + EPS)
        attn_in = (xf * inv_one * attn_gain).astype(BF)
        gathered = lax.all_gather(attn_in.reshape(nseq, seg, width), "heads", axis=0)
        w_groups = jnp.transpose(w_local.reshape(width, groups, 256), (1, 0, 2))
        rows_in, rows_out = width // ne, output_matrix.shape[0] // ne
        w_piece = lax.dynamic_slice_in_dim(w_local, me * rows_in, rows_in, 0)
        o_piece = lax.dynamic_slice_in_dim(output_matrix, me * rows_out, rows_out, 0)
        o_full = lax.all_gather(o_piece, ("heads", "experts"), axis=0, tiled=True)
        w_full = lax.all_gather(w_piece, ("heads", "experts"), axis=0, tiled=True)
        w_full = w_full.reshape(nh, width, groups * 256)
        qkv, heads_out, lse = attn_forward(gathered, w_groups, seq_lengths, tables)
        heads_in = lax.all_to_all(heads_out, "heads", split_axis=0, concat_axis=0, tiled=True)
        heads_in = heads_in.reshape(nh, tokens, groups * 128)
        o_parts = o_full.reshape(nh, groups * 128, width)
        branch = jnp.einsum("ztm,zmw->tw", heads_in, o_parts, preferred_element_type=F32)
        mid = xf + branch
        inv_two = lax.rsqrt(jnp.mean(mid * mid, axis=-1, keepdims=True) + EPS)
        moe_in = (mid * inv_two * moe_gain).astype(BF)
        d_rows = gather_rows(slots, weights, plane_gather(grad, ne), cap)
        x_rows = gather_rows(slots, None, plane_gather(moe_in, ne), cap)

    results, drows, sums = experts_call(slots, weights, x_rows, d_rows, expert_in, expert_down)
    if fast:
        flat = sums.reshape(-1, width)
        chunks = flat.shape[0] // CHUNK
        half = (3 * chunks) // 8
        total, d_mid, gain_two, dqkv, parts = middle(
            half, seq_lengths, flat, drows, pack, mid, grad, gain_m, o_parts, qkv, lse, tables,
            heads_in, gathered)
        total, out, x_grad, gains, _, wide = last(
            half, chunks - half, total, flat, results, pack, mid, dqkv, w_full, x, d_mid, gain_a, gain_two, parts)
        o_grad, w_grad = weight_split(wide, groups * 128, groups * 256)
        gain_one, gain_two = gains[0], gains[1]
        totals = total.reshape(sums.shape).astype(F32)
        grad_in, grad_down = totals[:, :width], totals[:, width:]
    else:
        slots_t = jnp.swapaxes(slots, 1, 2)
        d_parts = combine(slots_t, drows)
        moe_parts = combine(slots_t, results)
        totals = heads_sum(sums, z, nh)
        grad_in, grad_down = totals[:, :width], totals[:, width:]
        d_moe = plane_scatter(d_parts, ne)
        moe_sum = plane_scatter(moe_parts, ne)
        out = (mid + moe_sum).astype(BF)
        zed = moe_gain * d_moe
        d_mid = grad.astype(F32) + inv_two * zed - mid * (inv_two ** 3 * jnp.mean(zed * mid, axis=-1, keepdims=True))
        gain_two = jnp.sum(d_moe * mid * inv_two, axis=0)
        d_branch = d_mid.astype(BF)
        d_heads = jnp.einsum("tw,zmw->ztm", d_branch, o_parts, preferred_element_type=F32).astype(BF)
        d_heads = d_heads.reshape(nh, nseq, seg, groups * 128)
        d_heads = lax.all_to_all(d_heads, "heads", split_axis=0, concat_axis=0, tiled=True)
        dqkv = attn_backward(qkv, d_heads, lse, seq_lengths, tables)
        dqkv = dqkv.reshape(nh, tokens, groups * 256)
        back = lax.all_to_all(dqkv, "heads", split_axis=0, concat_axis=0, tiled=True)
        d_attn = jnp.einsum("ztc,zmc->tm", back, w_full, preferred_element_type=F32)
        o_grad, w_grad = weight_sums(heads_in, d_branch, gathered, dqkv, ne)
        wed = attn_gain * d_attn
        x_grad = d_mid + inv_one * wed - xf * (inv_one ** 3 * jnp.mean(wed * xf, axis=-1, keepdims=True))
        gain_one = jnp.sum(d_attn * xf * inv_one, axis=0)
        gain_one, gain_two = lax.psum((gain_one, gain_two), ("heads", "experts"))
    w_grad = w_grad.reshape(width, groups, 256)
    return (
        unlocal(out),
        unlocal(x_grad),
        gain_one,
        gain_two,
        w_grad[:, :, :128].reshape(query_matrix.shape),
        w_grad[:, :, 128:192].reshape(key_matrix.shape),
        w_grad[:, :, 192:].reshape(value_matrix.shape),
        o_grad,
        grad_in,
        grad_down,
    )


def solution(mesh):
    rows = P("heads", "experts", None)
    in_specs = (
        rows,
        P("experts"),
        rows,
        rows,
        P("heads", "experts"),
        P(),
        P(),
        P(None, "heads"),
        P(None, "heads"),
        P(None, "heads"),
        P("heads", None),
        P("experts", None, None),
        P("experts", None, None),
        rows,
    )
    out_specs = (
        rows,
        rows,
        P(),
        P(),
        P(None, "heads"),
        P(None, "heads"),
        P(None, "heads"),
        P("heads", None),
        P("experts", None, None),
        P("experts", None, None),
    )
    return jax.shard_map(body, mesh=mesh, in_specs=in_specs, out_specs=out_specs, check_vma=False)
```

```python
import functools
import math

import jax
import jax.numpy as jnp
from jax import lax
from jax.experimental import pallas as pl
from jax.experimental.pallas import tpu as pltpu
from jax.sharding import PartitionSpec as P

HEAD = 64
EXPERTS = 32
EPS = 1e-06
BF = jnp.bfloat16
F32 = jnp.float32
SCALE = HEAD ** (-0.5)
NEG = -1e30
VMEM = 63 * 1024 * 1024
MESH = pl.DeviceIdType.MESH
DMA = pltpu.SemaphoreType.DMA


def dot(a, b):
    return jnp.dot(a, b, preferred_element_type=F32)


def dot_nt(a, b):
    return lax.dot_general(a, b, (((1,), (1,)), ((), ())), preferred_element_type=F32)


def dot_tn(a, b):
    return lax.dot_general(a, b, (((0,), (0,)), ((), ())), preferred_element_type=F32)


def params(n):
    return pltpu.CompilerParams(
        dimension_semantics=("arbitrary",) * n, vmem_limit_bytes=VMEM
    )


def swap_halves(v):
    lane = lax.broadcasted_iota(jnp.int32, v.shape, 1)
    return jnp.where(lane % 64 < 32, pltpu.roll(v, 96, 1), pltpu.roll(v, 32, 1))


def attn_mask(offset, n, block, length):
    key = lax.broadcasted_iota(jnp.int32, (n, block), 0)
    query = lax.broadcasted_iota(jnp.int32, (n, block), 1) + offset
    return (key <= query) & (key < length)


def two_heads(v):
    return jnp.concatenate([v[:, :HEAD], v[:, HEAD:]], axis=0)


def untwo(vt, block):
    return jnp.concatenate([vt[:, :block], vt[:, block:]], axis=0).T


def fwd_kernel(len_ref, x_ref, w_ref, cq, sq, ckv, skv, qkv_ref, head_ref, lse_ref):
    nh, _, seg, width = x_ref.shape
    full = nh * seg
    block = seg
    length = len_ref[pl.program_id(0)]
    lin = dot(x_ref[...].reshape(full, width), w_ref[0])
    ql, kvl = lin[:, :128], lin[:, 128:]
    q = (ql * cq[...] + swap_halves(ql) * sq[...]).astype(BF)
    kvr = kvl * ckv[...] + swap_halves(kvl) * skv[...]
    kv = kvr.astype(BF)
    qkv_ref[0, 0, :, :128] = q
    qkv_ref[0, 0, :, 128:] = kv
    k = kv[:, :HEAD]
    vt = kvr.T[HEAD:].astype(BF)
    for i in range(nh):
        n = (i + 1) * block
        q2 = two_heads(q[i * block : n])
        s = dot_nt(k[:n], q2)
        mask = attn_mask(i * block, n, block, length)
        s = jnp.where(jnp.concatenate([mask, mask], axis=1), s * SCALE, NEG)
        m = jnp.max(s, axis=0, keepdims=True)
        e = jnp.exp(s - m)
        total = jnp.sum(e, axis=0, keepdims=True)
        p = (e * (1.0 / total)).astype(BF)
        lse_ref[0, 0, i : i + 1, :] = m + jnp.log(total)
        head_ref[i, 0] = untwo(dot(vt[:, :n], p), block).astype(BF)


def attn_forward(x, w, lengths, tables):
    nh, nseq, seg, width = x.shape
    groups = w.shape[0]
    full = nh * seg
    cq, sq, ckv, skv = tables
    tab = pl.BlockSpec((full, 128), lambda s, g: (0, 0))
    return pl.pallas_call(
        fwd_kernel,
        grid=(nseq, groups),
        in_specs=[
            pl.BlockSpec(memory_space=pltpu.SMEM),
            pl.BlockSpec((nh, 1, seg, width), lambda s, g: (0, s, 0, 0)),
            pl.BlockSpec((1, width, 256), lambda s, g: (g, 0, 0)),
            tab,
            tab,
            tab,
            tab,
        ],
        out_specs=[
            pl.BlockSpec((1, 1, full, 256), lambda s, g: (s, g, 0, 0)),
            pl.BlockSpec((nh, 1, seg, 128), lambda s, g: (0, s, 0, g)),
            pl.BlockSpec((1, 1, nh, 2 * seg), lambda s, g: (s, g, 0, 0)),
        ],
        out_shape=[
            jax.ShapeDtypeStruct((nseq, groups, full, 256), BF),
            jax.ShapeDtypeStruct((nh, nseq, seg, groups * 128), BF),
            jax.ShapeDtypeStruct((nseq, groups, nh, 2 * seg), F32),
        ],
        compiler_params=params(2),
        cost_estimate=pl.CostEstimate(flops=6 * 10**9, bytes_accessed=12 * 2**20, transcendentals=10**7),
        name="attn_forward",
    )(lengths, x, w, cq, sq, ckv, skv)


def bwd_piece(q, kv, heads, lses, length, tables, dkv_ref, put):
    cq, sq, ckv, skv = tables
    full, block = q.shape[0], lses(0).shape[1] // 2
    k, v = kv[:, :HEAD], kv[:, HEAD:]
    kt = kv.astype(F32).T[:HEAD].astype(BF)
    dkv_ref[...] = jnp.zeros_like(dkv_ref)
    for i in range(full // block):
        n = (i + 1) * block
        rows = pl.ds(i * block, block)
        mask = attn_mask(i * block, n, block, length)
        grads = []
        for h in range(2):
            qh = q[i * block : n, h * HEAD : (h + 1) * HEAD]
            doh = heads(i)[:, h * HEAD : (h + 1) * HEAD]
            s = dot_nt(k[:n], qh)
            p = jnp.exp(jnp.where(mask, s * SCALE - lses(i)[:, h * block : (h + 1) * block], NEG))
            dp = dot_nt(v[:n], doh)
            delta = jnp.sum(p * dp, axis=0, keepdims=True)
            ds = (p * (dp - delta) * SCALE).astype(BF)
            dkv_ref[:n, :HEAD] += dot(ds, qh)
            dkv_ref[:n, HEAD:] += dot(p.astype(BF), doh)
            grads.append(dot(kt[:, :n], ds))
        dq = jnp.concatenate(grads, axis=0).T
        dq = dq * cq[rows, :] - swap_halves(dq) * sq[rows, :]
        put(i, 0, dq.astype(BF))
    dkv = dkv_ref[...]
    dkv = (dkv * ckv[...] - swap_halves(dkv) * skv[...]).astype(BF)
    for i in range(full // block):
        put(i, 128, dkv[i * block : (i + 1) * block])


def bwd_kernel(len_ref, qkv_ref, do_ref, lse_ref, cq, sq, ckv, skv, out_ref, dkv_ref):
    def put(i, lo, v):
        out_ref[i, 0, :, lo : lo + 128] = v

    bwd_piece(
        qkv_ref[0, 0, :, :128],
        qkv_ref[0, 0, :, 128:],
        lambda i: do_ref[i, 0],
        lambda i: lse_ref[0, 0, i : i + 1, :],
        len_ref[pl.program_id(0)],
        (cq, sq, ckv, skv),
        dkv_ref,
        put,
    )


def attn_backward(qkv, d_head, lse, lengths, tables):
    nseq, groups, full, _ = qkv.shape
    nh, _, seg, _ = d_head.shape
    cq, sq, ckv, skv = tables
    tab = pl.BlockSpec((full, 128), lambda s, g: (0, 0))
    return pl.pallas_call(
        bwd_kernel,
        grid=(nseq, groups),
        in_specs=[
            pl.BlockSpec(memory_space=pltpu.SMEM),
            pl.BlockSpec((1, 1, full, 256), lambda s, g: (s, g, 0, 0)),
            pl.BlockSpec((nh, 1, seg, 128), lambda s, g: (0, s, 0, g)),
            pl.BlockSpec((1, 1, nh, 2 * seg), lambda s, g: (s, g, 0, 0)),
            tab,
            tab,
            tab,
            tab,
        ],
        out_specs=pl.BlockSpec((nh, 1, seg, 256), lambda s, g: (0, s, 0, g)),
        out_shape=jax.ShapeDtypeStruct((nh, nseq, seg, groups * 256), BF),
        scratch_shapes=[pltpu.VMEM((full, 128), F32)],
        compiler_params=params(2),
        cost_estimate=pl.CostEstimate(flops=12 * 10**9, bytes_accessed=8 * 2**20, transcendentals=10**7),
        name="attn_backward",
    )(lengths, qkv, d_head, lse, cq, sq, ckv, skv)


def rotary_tables(length):
    half = HEAD // 2
    frequency = jnp.exp(jnp.arange(half, dtype=F32) * (-2.0 * math.log(10000.0) / HEAD))
    angles = jnp.arange(length, dtype=F32)[:, None] * frequency[None, :]
    cos, sin = jnp.cos(angles), jnp.sin(angles)
    c1 = jnp.concatenate([cos, cos], axis=1)
    s1 = jnp.concatenate([-sin, sin], axis=1)
    cq = jnp.concatenate([c1, c1], axis=1)
    sq = jnp.concatenate([s1, s1], axis=1)
    ckv = jnp.concatenate([c1, jnp.ones_like(c1)], axis=1)
    skv = jnp.concatenate([s1, jnp.zeros_like(s1)], axis=1)
    return cq, sq, ckv, skv


def pick_rows(slots, cap):
    tokens = slots.shape[1]
    index = lax.broadcasted_iota(jnp.int32, (cap, tokens), 0)
    return [index == slots[j : j + 1, :] for j in range(slots.shape[0])]


def gather_kernel(weighted, slot_ref, *refs):
    if weighted:
        weight_ref, tok_ref, out_ref = refs
    else:
        tok_ref, out_ref = refs[0], refs[-1]
    cap = out_ref.shape[2]
    hits = pick_rows(slot_ref[0], cap)
    rows = dot(jnp.concatenate([h.astype(F32) for h in hits], axis=0).astype(BF), tok_ref[0])
    for j, hit in enumerate(hits):
        part = rows[j * cap : (j + 1) * cap]
        if weighted:
            part = part * jnp.sum(jnp.where(hit, weight_ref[0, j : j + 1, :], 0.0), axis=1, keepdims=True)
        out_ref[j, 0] = part.astype(BF)


def gather_rows(slots, weights, tokens, cap):
    sources, here, count = slots.shape
    width = tokens.shape[-1]
    small = pl.BlockSpec((1, here, count), lambda s: (s, 0, 0))
    weighted = weights is not None
    return pl.pallas_call(
        functools.partial(gather_kernel, weighted),
        grid=(sources,),
        in_specs=[small] + [small] * weighted + [pl.BlockSpec((1, count, width), lambda s: (s, 0, 0))],
        out_specs=pl.BlockSpec((here, 1, cap, width), lambda s: (0, s, 0, 0)),
        out_shape=jax.ShapeDtypeStruct((here, sources, cap, width), BF),
        compiler_params=params(1),
        cost_estimate=pl.CostEstimate(
            flops=2 * sources * here * cap * count * width,
            bytes_accessed=2 * sources * width * (count + here * cap),
            transcendentals=0,
        ),
        name="gather_rows",
    )(*([slots] + [weights] * weighted + [tokens]))


def expert_kernel(steps, slot_ref, weight_ref, x_ref, d_ref, win_ref, wdown_ref,
                  out_ref, drow_ref, grad_ref, hid_ref, dgu_ref, *acc):
    _, sources, cap, width = x_ref.shape
    ff = wdown_ref.shape[1]
    per = 2 if sources % 2 == 0 else 1
    win, wdown = win_ref[0], wdown_ref[0]
    for c in range(sources // per):
        rows = slice(c * per * cap, (c + 1) * per * cap)
        x = x_ref[0, c * per : (c + 1) * per].reshape(per * cap, width)
        d = d_ref[0, c * per : (c + 1) * per].reshape(per * cap, width)
        gu = dot(x, win)
        gate, up = gu[:, :ff], gu[:, ff:]
        sig = 1.0 / (1.0 + jnp.exp(-gate))
        act = gate * sig
        hidden = (act * up).astype(BF)
        hid_ref[rows, :] = hidden
        result = dot(hidden, wdown).astype(BF).astype(F32)
        for b in range(per):
            hit = pick_rows(slot_ref[c * per + b, 0], cap)[0]
            w = jnp.sum(jnp.where(hit, weight_ref[c * per + b, 0], 0.0), axis=1, keepdims=True)
            out_ref[0, c * per + b] = (result[b * cap : (b + 1) * cap] * w).astype(BF)
        dh = dot_nt(d, wdown)
        dgu_ref[rows, :ff] = (dh * up * (sig * (1.0 + gate * (1.0 - sig)))).astype(BF)
        dgu_ref[rows, ff:] = (dh * act).astype(BF)
        drow = dot_nt(dgu_ref[rows, :], win).astype(BF)
        for b in range(per):
            drow_ref[0, c * per + b] = drow[b * cap : (b + 1) * cap]
    x = x_ref[0].reshape(sources * cap, width)
    d = d_ref[0].reshape(sources * cap, width)
    gin = dot_tn(x, dgu_ref[...])
    gdown = dot_tn(hid_ref[...], d)
    if steps == 1:
        grad_ref[0, :width] = gin.astype(BF)
        grad_ref[0, width:] = gdown.astype(BF)
    else:
        ain, adown = acc
        step = pl.program_id(1)

        @pl.when(step == 0)
        def _():
            ain[...] = jnp.zeros_like(ain)
            adown[...] = jnp.zeros_like(adown)

        ain[...] += gin
        adown[...] += gdown

        @pl.when(step == steps - 1)
        def _():
            grad_ref[0, :width] = ain[...].astype(BF)
            grad_ref[0, width:] = adown[...].astype(BF)


def experts_call(slots, weights, x, d, win, wdown):
    count, sources, cap, width = x.shape
    tokens = slots.shape[-1]
    ff = wdown.shape[1]
    chunk = min(sources, 8)
    steps = sources // chunk
    small = pl.BlockSpec((chunk, 1, 1, tokens), lambda j, r: (r, j, 0, 0))
    rows = pl.BlockSpec((1, chunk, cap, width), lambda j, r: (j, r, 0, 0))
    rows_out = pl.BlockSpec((1, chunk, cap, width), lambda j, r: (j, r, 0, 0))
    scratch = [pltpu.VMEM((chunk * cap, ff), BF), pltpu.VMEM((chunk * cap, 2 * ff), BF)]
    if steps > 1:
        scratch += [pltpu.VMEM((width, 2 * ff), F32), pltpu.VMEM((ff, width), F32)]
    shape = jax.ShapeDtypeStruct((count, sources, cap, width), BF)
    return pl.pallas_call(
        functools.partial(expert_kernel, steps),
        grid=(count, steps),
        in_specs=[
            small,
            small,
            rows,
            rows,
            pl.BlockSpec((1, width, 2 * ff), lambda j, r: (j, 0, 0)),
            pl.BlockSpec((1, ff, width), lambda j, r: (j, 0, 0)),
        ],
        out_specs=[
            rows_out,
            rows_out,
            pl.BlockSpec((1, width + ff, width), lambda j, r: (j, 0, 0)),
        ],
        out_shape=[
            shape,
            shape,
            jax.ShapeDtypeStruct((count, width + ff, width), BF),
        ],
        scratch_shapes=scratch,
        compiler_params=params(2),
        cost_estimate=pl.CostEstimate(
            flops=2 * count * sources * cap * width * ff * 9,
            bytes_accessed=8 * count * sources * cap * width + 12 * count * width * ff,
            transcendentals=count * sources * cap * ff,
        ),
        name="experts",
    )(slots[:, :, None, :], weights[:, :, None, :], x, d, win, wdown)


def combine_kernel(slot_ref, row_ref, out_ref):
    slots = slot_ref[0]
    count, here = slots.shape
    cap = row_ref.shape[2]
    lane = lax.broadcasted_iota(jnp.int32, (count, here * cap), 1)
    hot = None
    for j in range(here):
        col = slots[:, j : j + 1]
        hit = lane == jnp.where(col >= 0, col + j * cap, -1)
        hot = hit if hot is None else hot | hit
    hot = hot.astype(F32).astype(BF)
    out_ref[0] = dot(hot, row_ref[...].reshape(here * cap, row_ref.shape[3])).astype(BF)


def combine(slots_t, rows):
    sources, count, here = slots_t.shape
    _, _, cap, width = rows.shape
    return pl.pallas_call(
        combine_kernel,
        grid=(sources,),
        in_specs=[
            pl.BlockSpec((1, count, here), lambda s: (s, 0, 0)),
            pl.BlockSpec((here, 1, cap, width), lambda s: (0, s, 0, 0)),
        ],
        out_specs=pl.BlockSpec((1, count, width), lambda s: (s, 0, 0)),
        out_shape=jax.ShapeDtypeStruct((sources, count, width), BF),
        compiler_params=params(1),
        cost_estimate=pl.CostEstimate(
            flops=2 * sources * here * cap * count * width,
            bytes_accessed=2 * sources * width * (count + here * cap),
            transcendentals=0,
        ),
        name="combine",
    )(slots_t, rows)


def swap(x, bit, n):
    return lax.ppermute(x, "experts", [(i, i ^ bit) for i in range(n)])


def plane_gather(x, n):
    if n != 8:
        whole = lax.all_gather(x, "experts", axis=0)
        order = lax.axis_index("experts") ^ jnp.arange(n, dtype=jnp.int32)
        return whole[order]
    got = {0: x}
    for r in (2, 4, 6):
        got[r] = swap(x, r, n)
    for r in (0, 2, 4, 6):
        got[r + 1] = swap(got[r], 1, n)
    return jnp.stack([got[r] for r in range(n)], axis=0)


def plane_scatter(parts, n):
    if n != 8:
        order = lax.axis_index("experts") ^ jnp.arange(n, dtype=jnp.int32)
        return lax.psum_scatter(parts[order].astype(F32), "experts", scatter_dimension=0)
    odd = swap(parts[1::2], 1, n)
    both = [parts[2 * i].astype(F32) + odd[i].astype(F32) for i in range(4)]
    total = both[0]
    for i in (1, 2, 3):
        total = total + swap(both[i].astype(BF), 2 * i, n).astype(F32)
    return total


def heads_sum(x, z, nh):
    if nh != 4:
        return lax.psum(x.astype(F32), "heads")
    first = lax.ppermute(x, "heads", [(0, 1), (3, 2)])
    pair = (x.astype(F32) + first.astype(F32)).astype(BF)
    second = lax.ppermute(pair, "heads", [(1, 2), (2, 1)])
    total = (pair.astype(F32) + second.astype(F32)).astype(BF)
    third = lax.ppermute(total, "heads", [(1, 0), (2, 3)])
    return jnp.where((z == 1) | (z == 2), total, third).astype(F32)


def weight_sums(heads_in, d_branch, gathered, dqkv, ne):
    nh, tokens, part = heads_in.shape
    width, cols = d_branch.shape[1], dqkv.shape[2]
    col, row = width // ne, width // ne
    o = jnp.einsum("ztm,tew->ezmw", heads_in, d_branch.reshape(tokens, ne, col), preferred_element_type=F32)
    w = jnp.einsum("ztm,ztc->mc", gathered.reshape(nh, tokens, width), dqkv, preferred_element_type=F32)
    cut = cols // col
    w = jnp.swapaxes(w.reshape(ne, row, cut, col), 1, 2).reshape(ne, cut * row, col)
    both = jnp.concatenate([o.reshape(ne, nh * part, col), w], axis=1)
    both = lax.psum_scatter(both, "experts", scatter_dimension=0)
    o, w = both[: nh * part], both[nh * part :]
    o = lax.psum_scatter(o.reshape(nh, part, col), "heads", scatter_dimension=0)
    return weight_split(lax.all_gather(jnp.concatenate([o, w], axis=0), "experts", axis=0), part, cols)


def weight_split(both, part, cols):
    ne, _, col = both.shape
    width, row, cut = ne * col, col, cols // col
    o = jnp.swapaxes(both[:, :part], 0, 1).reshape(part, width)
    w = jnp.swapaxes(both[:, part:].reshape(ne, cut, row, col), 1, 2)
    return o, w.reshape(width, cols)


CHUNK = 128
LAG = 3
FLIGHT = 6


def remote(src, dst, send, recv, axis, index):
    return pltpu.make_async_remote_copy(
        src_ref=src, dst_ref=dst, send_sem=send, recv_sem=recv,
        device_id={axis: index}, device_id_type=MESH,
    )


def greet(nh, masks):
    z, me = lax.axis_index("heads"), lax.axis_index("experts")
    bar = pltpu.get_barrier_semaphore()
    for d in range(1, nh):
        pl.semaphore_signal(bar, inc=1, device_id={"heads": lax.rem(z + d, nh)}, device_id_type=MESH)
    for r in masks:
        pl.semaphore_signal(bar, inc=1, device_id={"experts": me ^ r}, device_id_type=MESH)
    pl.semaphore_wait(bar, nh - 1 + len(masks))


class Chain:
    def __init__(self, src, out, scratch, first, count):
        self.src, self.out, self.first, self.count = src, out, first, count
        self.a, self.b, self.buf, self.s1, self.r1, self.s2, self.r2, self.ls, self.os = scratch
        z = lax.axis_index("heads")
        self.mid = (z == 1) | (z == 2)
        self.outer = jnp.where(z == 0, 1, jnp.where(z == 1, 0, jnp.where(z == 2, 3, 2)))
        self.inner = jnp.where(z == 1, 2, jnp.where(z == 2, 1, z))

    def piece(self, k):
        return self.src.at[pl.ds((self.first + k) * CHUNK, CHUNK)]

    def load(self, k):
        return pltpu.make_async_copy(self.piece(k), self.buf.at[lax.rem(k, 2)], self.ls.at[lax.rem(k, 2)])

    def store(self, ref, k):
        return pltpu.make_async_copy(ref.at[k], self.out.at[pl.ds((self.first + k) * CHUNK, CHUNK)], self.os.at[k])

    def up(self, k):
        return remote(self.piece(k), self.a.at[k], self.s1.at[k], self.r1.at[k], "heads", self.outer)

    def across(self, k):
        return remote(self.a.at[k], self.b.at[k], self.s2.at[k], self.r2.at[k], "heads", self.inner)

    def down(self, k):
        return remote(self.b.at[k], self.a.at[k], self.s1.at[k], self.r1.at[k], "heads", self.outer)

    def begin(self):
        @pl.when(self.mid)
        def _():
            self.load(0).start()

        @pl.when(jnp.logical_not(self.mid))
        def _():
            @pl.loop(0, FLIGHT)
            def _(k):
                self.up(k).start()

    def pair(self, k):
        @pl.when(k + 1 < self.count)
        def _():
            self.load(k + 1).start()

        self.load(k).wait()
        self.up(k).wait_recv()
        own = self.buf[lax.rem(k, 2)].astype(F32)
        self.a[k] = (self.a[k].astype(F32) + own).astype(BF)
        self.across(k).start()

    def total(self, j):
        self.across(j).wait_recv()
        self.b[j] = (self.a[j].astype(F32) + self.b[j].astype(F32)).astype(BF)
        self.down(j).start()
        self.store(self.b, j).start()

    def take(self, j):
        self.down(j).wait_recv()
        self.store(self.a, j).start()

    def step(self, k, lag=LAG):
        n = self.count

        @pl.when(self.mid)
        def _():
            @pl.when(k < n)
            def _():
                self.pair(k)

            @pl.when((k >= lag) & (k < n + lag))
            def _():
                self.total(k - lag)

        @pl.when(jnp.logical_not(self.mid))
        def _():
            @pl.when(k + FLIGHT < n)
            def _():
                self.up(k).wait_send()
                self.up(k + FLIGHT).start()

            @pl.when((k >= lag + 2) & (k < n + lag + 2))
            def _():
                self.take(k - lag - 2)

    def rest(self, k):
        n = self.count

        @pl.when(self.mid)
        def _():
            @pl.loop(min(max(k - LAG, 0), n), min(max(k - 1, 0), n))
            def _(j):
                self.total(j)

        @pl.when(jnp.logical_not(self.mid))
        def _():
            @pl.loop(min(max(k - LAG - 2, 0), n), min(max(k - 3, 0), n))
            def _(j):
                self.take(j)

        @pl.loop(k, n + 3)
        def _(i):
            self.step(i, 1)

    def run(self, first, last):
        @pl.loop(first, last)
        def _(k):
            self.step(k)

    def finish(self):
        n = self.count

        @pl.when(self.mid)
        def _():
            @pl.loop(0, n)
            def _(k):
                self.across(k).wait_send()
                self.down(k).wait_send()
                self.store(self.b, k).wait()

        @pl.when(jnp.logical_not(self.mid))
        def _():
            @pl.loop(n - FLIGHT, n)
            def _(k):
                self.up(k).wait_send()

            @pl.loop(0, n)
            def _(k):
                self.store(self.a, k).wait()


def chain_scratch(count, width):
    return [
        pltpu.VMEM((count, CHUNK, width), BF),
        pltpu.VMEM((count, CHUNK, width), BF),
        pltpu.VMEM((2, CHUNK, width), BF),
        DMA((count,)),
        DMA((count,)),
        DMA((count,)),
        DMA((count,)),
        DMA((2,)),
        DMA((count,)),
    ]


class PlaneSum:
    order = (3, 1, 2)

    def __init__(self, rows, slots, total, scratch):
        self.rows, self.slots, self.total = rows, slots, total
        self.buf, self.odd, self.c, self.e, self.f, self.ls, self.cs, self.cr, self.fs, self.fr = scratch
        self.me = lax.axis_index("experts")
        self.here, _, self.cap, self.width = rows.shape

    def load(self, r, at):
        return [
            pltpu.make_async_copy(self.rows.at[j, r], self.buf.at[at, j], self.ls.at[at, j])
            for j in range(self.here)
        ]

    def core(self, i):
        return remote(self.odd.at[i], self.c.at[i], self.cs.at[i], self.cr.at[i], "experts", self.me ^ 1)

    def chip(self, i):
        return remote(self.e.at[i - 1], self.f.at[i - 1], self.fs.at[i - 1], self.fr.at[i - 1], "experts", self.me ^ (2 * i))

    def part(self, r, at, after, after_at):
        if after is not None:
            for c in self.load(after, after_at):
                c.start()
        slots = self.slots[r].T.astype(jnp.int32)
        lane = lax.broadcasted_iota(jnp.int32, (slots.shape[0], self.here * self.cap), 1)
        hot = None
        for j in range(self.here):
            col = slots[:, j : j + 1]
            hit = lane == jnp.where(col >= 0, col + j * self.cap, -1)
            hot = hit if hot is None else hot | hit
        for c in self.load(r, at):
            c.wait()
        rows = self.buf[at].reshape(self.here * self.cap, self.width)
        return dot(hot.astype(F32).astype(BF), rows)

    def run(self, chain, step):
        turns = [2 * i + 1 for i in self.order + (0,)] + [2 * i for i in self.order + (0,)]
        for c in self.load(turns[0], 0):
            c.start()
        for t, r in enumerate(turns):
            after = turns[t + 1] if t + 1 < len(turns) else None
            value = self.part(r, t % 2, after, (t + 1) % 2)
            i = r // 2
            if r % 2:
                self.odd[i] = value.astype(BF)
                self.core(i).start()
            else:
                self.core(i).wait_recv()
                value = value + self.c[i].astype(F32)
                if i:
                    self.e[i - 1] = value.astype(BF)
                    self.chip(i).start()
                else:
                    self.total[...] = value
            if t % 2:
                chain.step(step + t // 2)
        return step + 4

    def arrive(self):
        for i in self.order:
            self.chip(i).wait_recv()

    def rows_total(self, rows):
        d = self.total[rows]
        for r in range(3):
            d = d + self.f[r, rows].astype(F32)
        return d

    def finish(self):
        for i in range(4):
            self.core(i).wait_send()
        for i in self.order:
            self.chip(i).wait_send()


def plane_scratch(here, cap, tokens, width):
    return [
        pltpu.VMEM((2, here, cap, width), BF),
        pltpu.VMEM((4, tokens, width), BF),
        pltpu.VMEM((4, tokens, width), BF),
        pltpu.VMEM((3, tokens, width), BF),
        pltpu.VMEM((3, tokens, width), BF),
        DMA((2, here)),
        DMA((4,)),
        DMA((4,)),
        DMA((3,)),
        DMA((3,)),
    ]


PLANE = 10


ROWS = 128


class Exchange:
    def __init__(self, src, dst, send, recv, nh):
        self.src, self.dst, self.ss, self.rs, self.nh = src, dst, send, recv, nh
        self.z = lax.axis_index("heads")

    def send(self, d):
        to = lax.rem(self.z + d, self.nh)
        return remote(self.src(to), self.dst(self.z), self.ss(d), self.rs(d), "heads", to)

    def start(self):
        for d in range(1, self.nh):
            self.send(d).start()

    def wait_recv(self):
        for d in range(1, self.nh):
            at = lax.rem(self.z + self.nh - d, self.nh)
            remote(self.src(at), self.dst(at), self.ss(d), self.rs(d), "heads", at).wait_recv()

    def finish(self):
        for d in range(1, self.nh):
            self.send(d).wait_send()


def whole_exchange(src, dst, send, recv, nh):
    return Exchange(lambda h: src.at[h], lambda h: dst.at[h], lambda d: send.at[d], lambda d: recv.at[d], nh)


class PlaneGather:
    order = (3, 1, 2)

    def __init__(self, own, slot, sems):
        self.own, self.slot = own, slot
        self.cs, self.cr, self.ks, self.kr = sems
        self.me = lax.axis_index("experts")

    def chip(self, i, e):
        return remote(self.own, self.slot(e), self.cs.at[i], self.cr.at[i], "experts", self.me ^ (2 * i))

    def core(self, i, src, e):
        return remote(src, self.slot(e), self.ks.at[i], self.kr.at[i], "experts", self.me ^ 1)

    def start(self):
        self.core(0, self.own, self.me).start()
        for i in self.order:
            self.chip(i, self.me).start()

    def forward(self, i):
        e = self.me ^ (2 * i)
        self.chip(i, e).wait_recv()
        self.core(i, self.slot(e), e).start()

    def core_arrive(self, i):
        e = self.me ^ 1 ^ (2 * i)
        self.core(i, self.slot(e), e).wait_recv()

    def finish(self):
        for i in range(1, 4):
            self.chip(i, self.me).wait_send()
        for i in range(4):
            self.core(i, self.own if i == 0 else self.slot(self.me ^ (2 * i)), self.me).wait_send()


GATHER = 4


def gather_sems():
    return [DMA((4,)), DMA((4,)), DMA((4,)), DMA((4,))]


class Picker:
    def __init__(self, pack, stage, sems, here, cap):
        self.pack, self.stage, self.sems, self.here, self.cap = pack, stage, sems, here, cap
        self.turn, self.pending = 0, {}

    def pick(self, r, tokens, out, weighted):
        at = self.turn % 2
        self.turn += 1
        info = self.pack[r]
        slots = info.astype(jnp.int32)
        index = lax.broadcasted_iota(jnp.int32, (self.cap, slots.shape[1]), 0)
        hits = [index == slots[j : j + 1] for j in range(self.here)]
        rows = dot(jnp.concatenate([h.astype(F32) for h in hits], axis=0).astype(BF), tokens)
        for c in self.pending.get(at, []):
            c.wait()
        for j, hit in enumerate(hits):
            part = rows[j * self.cap : (j + 1) * self.cap]
            if weighted:
                w = info[self.here + j : self.here + j + 1]
                part = part * jnp.sum(jnp.where(hit, w, 0.0), axis=1, keepdims=True)
            self.stage[at, j] = part.astype(BF)
        self.pending[at] = [
            pltpu.make_async_copy(self.stage.at[at, j], out.at[j, r], self.sems.at[at, j])
            for j in range(self.here)
        ]
        for c in self.pending[at]:
            c.start()

    def finish(self):
        for copies in self.pending.values():
            for c in copies:
                c.wait()


def front_kernel(len_ref, x_ref, og_ref, w_ref, om_ref, pk_ref, again_ref, mgain_ref, cq, sq, ckv, skv,
                 xg_ref, qkv_ref, lse_ref, hin_ref, of_ref, wz_ref, mid_ref, pack_ref, drows_ref, xrows_ref,
                 hs, ogb, mt, stage, ls, lr, ps, pr, hss, hrs, os_, or_, ws, wr, ss, *sems):
    nh, tokens, width = xg_ref.shape
    nseq, groups, full, _ = qkv_ref.shape
    ne = ogb.shape[0]
    seg = tokens // nseq
    here, _, cap, _ = drows_ref.shape
    z, me = lax.axis_index("heads"), lax.axis_index("experts")
    og = PlaneGather(og_ref, lambda e: ogb.at[e], sems[:GATHER])
    og_o = PlaneGather(of_ref.at[:, me], lambda e: of_ref.at[:, e], sems[GATHER : 2 * GATHER])

    def moe(p):
        at = pl.ds(p * seg, seg)
        return PlaneGather(mt.at[me, at], lambda e: mt.at[e, at], sems[(2 + p) * GATHER : (3 + p) * GATHER])

    moes = [moe(p) for p in range(nseq)]

    def heads(p):
        at = pl.ds(p * seg, seg)
        return Exchange(
            lambda h: hs.at[h, at], lambda h: hin_ref.at[h, at], lambda d: hss.at[p, d], lambda d: hrs.at[p, d], nh)

    picker = Picker(pack_ref, stage, ss, here, cap)

    @pl.loop(0, tokens // ROWS)
    def _(i):
        rows = pl.ds(i * ROWS, ROWS)
        x = x_ref[rows].astype(F32)
        inv = lax.rsqrt(jnp.mean(x * x, axis=-1, keepdims=True) + EPS)
        xg_ref[z, rows] = (x * inv * again_ref[...]).astype(BF)

    greet(nh, tuple(range(1, ne)))

    def hop(way, t, p, s, to):
        ref = xg_ref.at[s, pl.ds(p * seg, seg)]
        return remote(ref, ref, ls.at[way, t, p], lr.at[s, p], "heads", to)

    right, left = jnp.minimum(z + 1, nh - 1), jnp.maximum(z - 1, 0)
    for p in range(nseq):
        @pl.when(z < nh - 1)
        def _():
            hop(0, 0, p, z, right).start()

        @pl.when(z > 0)
        def _():
            hop(1, 0, p, z, left).start()

    def info(r):
        return remote(pk_ref.at[me ^ r], pack_ref.at[r], ps.at[r], pr.at[r], "experts", me ^ r)

    rows_o, rows_w = of_ref.shape[2], wz_ref.shape[1]
    of_ref[z, me] = om_ref[pl.ds(pl.multiple_of(me * rows_o, rows_o), rows_o)]
    wz_ref[z] = w_ref[pl.ds(pl.multiple_of(me * rows_w, rows_w), rows_w)]
    ofx = Exchange(lambda h: of_ref.at[z, me], lambda h: of_ref.at[h, me], lambda d: os_.at[d], lambda d: or_.at[d], nh)
    wzx = Exchange(lambda h: wz_ref.at[z], lambda h: wz_ref.at[h], lambda d: ws.at[d], lambda d: wr.at[d], nh)
    ofx.start()
    for r in range(1, ne):
        info(r).start()
    og.start()
    pack_ref[0] = pk_ref[me]

    def project(s, p):
        x = xg_ref[s, pl.ds(p * seg, seg)]
        at = pl.ds(s * seg, seg)
        for g in range(groups):
            lin = dot(x, w_ref[:, g * 256 : (g + 1) * 256])
            q, kv = lin[:, :128], lin[:, 128:]
            qkv_ref[p, g, at, :128] = (q * cq[at] + swap_halves(q) * sq[at]).astype(BF)
            qkv_ref[p, g, at, 128:] = (kv * ckv[at] + swap_halves(kv) * skv[at]).astype(BF)

    @pl.loop(0, nseq)
    def _(p):
        project(z, p)

    def round_of(t, then=None):
        @pl.loop(0, nseq)
        def _(p):
            @pl.when(z >= t)
            def _():
                s = z - t
                hop(0, t, p, s, left).wait_recv()

                @pl.when(z < nh - 1)
                def _():
                    hop(0, t, p, s, right).start()

                project(s, p)

            @pl.when(z + t < nh)
            def _():
                s = z + t
                hop(1, t, p, s, right).wait_recv()

                @pl.when(z > 0)
                def _():
                    hop(1, t, p, s, left).start()

                project(s, p)

            if then is not None:
                then(p)

    picker.pick(0, og_ref[...], drows_ref, True)
    round_of(1)
    for r in range(1, ne):
        info(r).wait_recv()
    og.core_arrive(0)
    picker.pick(1, ogb[me ^ 1], drows_ref, True)
    round_of(2)
    for i in og.order:
        og.forward(i)
    for i in og.order:
        picker.pick(2 * i, ogb[me ^ (2 * i)], drows_ref, True)
    ofx.wait_recv()
    og_o.start()

    def attend(p):
        length = len_ref[p]
        at = pl.ds(p * seg, seg)
        for g in range(groups):
            q = qkv_ref[p, g, :, :128]
            kv = qkv_ref[p, g, :, 128:]
            k = kv[:, :HEAD]
            vt = kv.astype(F32).T[HEAD:].astype(BF)
            for i in range(nh):
                n = (i + 1) * seg
                q2 = two_heads(q[i * seg : n])
                s = dot_nt(k[:n], q2)
                mask = attn_mask(i * seg, n, seg, length)
                s = jnp.where(jnp.concatenate([mask, mask], axis=1), s * SCALE, NEG)
                m = jnp.max(s, axis=0, keepdims=True)
                e = jnp.exp(s - m)
                total = jnp.sum(e, axis=0, keepdims=True)
                prob = (e * (1.0 / total)).astype(BF)
                lse_ref[p, g, i : i + 1, :] = m + jnp.log(total)
                hs[i, at, g * 128 : (g + 1) * 128] = untwo(dot(vt[:, :n], prob), seg).astype(BF)
        heads(p).start()
        hin_ref[z, at] = hs[z, at]

    round_of(3, attend)
    wzx.start()
    for i in og.order:
        og_o.forward(i)
    for i in og.order:
        og.core_arrive(i)
        picker.pick(2 * i + 1, ogb[me ^ 1 ^ (2 * i)], drows_ref, True)
    for i in range(4):
        og_o.core_arrive(i)

    for p in range(nseq):
        at = pl.ds(p * seg, seg)
        heads(p).wait_recv()
        mid_ref[at] = x_ref[at].astype(F32) + dot(hin_ref[0, at], of_ref[0].reshape(-1, width))
        for h in range(1, nh):
            mid_ref[at] += dot(hin_ref[h, at], of_ref[h].reshape(-1, width))

        @pl.loop(0, seg // ROWS)
        def _(i):
            rows = pl.ds(p * seg + i * ROWS, ROWS)
            m = mid_ref[rows]
            inv = lax.rsqrt(jnp.mean(m * m, axis=-1, keepdims=True) + EPS)
            mt[me, rows] = (m * inv * mgain_ref[...]).astype(BF)

        moes[p].start()

    picker.pick(0, mt[me], xrows_ref, False)
    for p in range(nseq):
        moes[p].core_arrive(0)
    picker.pick(1, mt[me ^ 1], xrows_ref, False)
    for i in og.order:
        for p in range(nseq - 1):
            moes[p].forward(i)
    for t, i in enumerate(og.order):
        moes[-1].forward(i)
        picker.pick(2 * i, mt[me ^ (2 * i)], xrows_ref, False)
        if t:
            last = og.order[t - 1]
            for p in range(nseq):
                moes[p].core_arrive(last)
            picker.pick(2 * last + 1, mt[me ^ 1 ^ (2 * last)], xrows_ref, False)
    last = og.order[-1]
    for p in range(nseq):
        moes[p].core_arrive(last)
    picker.pick(2 * last + 1, mt[me ^ 1 ^ (2 * last)], xrows_ref, False)
    picker.finish()
    wzx.wait_recv()
    for gather in [og, og_o] + moes:
        gather.finish()
    for exchange in [ofx, wzx] + [heads(p) for p in range(nseq)]:
        exchange.finish()
    for r in range(1, ne):
        info(r).wait_send()
    for p in range(nseq):
        for t in range(nh):
            @pl.when((z >= t) & (z < nh - 1))
            def _():
                hop(0, t, p, z - t, right).wait_send()

            @pl.when((z + t < nh) & (z > 0))
            def _():
                hop(1, t, p, z + t, left).wait_send()


def front(lengths, x, og, w_local, o_local, packed, attn_gain, moe_gain, tables, nh, nseq, cap):
    ne, info, _ = packed.shape
    tokens, width = x.shape
    here = info // 2
    cols = w_local.shape[1]
    groups, seg = cols // 256, tokens // nseq
    full = nh * seg
    part = o_local.shape[0]
    vmem = pl.BlockSpec(memory_space=pltpu.VMEM)
    hbm = pl.BlockSpec(memory_space=pl.ANY)
    rows = jax.ShapeDtypeStruct((here, ne, cap, width), BF)
    return pl.pallas_call(
        front_kernel,
        in_specs=[pl.BlockSpec(memory_space=pltpu.SMEM)] + [vmem] * 11,
        out_specs=[vmem] * 8 + [hbm, hbm],
        out_shape=[
            jax.ShapeDtypeStruct((nh, tokens, width), BF),
            jax.ShapeDtypeStruct((nseq, groups, full, 256), BF),
            jax.ShapeDtypeStruct((nseq, groups, nh, 2 * seg), F32),
            jax.ShapeDtypeStruct((nh, tokens, part), BF),
            jax.ShapeDtypeStruct((nh, ne, part // ne, width), BF),
            jax.ShapeDtypeStruct((nh, width // ne, cols), BF),
            jax.ShapeDtypeStruct((tokens, width), F32),
            jax.ShapeDtypeStruct(packed.shape, F32),
            rows,
            rows,
        ],
        scratch_shapes=[
            pltpu.VMEM((nh, tokens, part), BF),
            pltpu.VMEM((ne, tokens, width), BF),
            pltpu.VMEM((ne, tokens, width), BF),
            pltpu.VMEM((2, here, cap, width), BF),
            DMA((2, nh, nseq)),
            DMA((nh, nseq)),
            DMA((ne,)),
            DMA((ne,)),
            DMA((nseq, nh)),
            DMA((nseq, nh)),
            DMA((nh,)),
            DMA((nh,)),
            DMA((nh,)),
            DMA((nh,)),
            DMA((2, here)),
        ]
        + gather_sems() * (2 + nseq),
        compiler_params=pltpu.CompilerParams(
            collective_id=3, has_side_effects=True, vmem_limit_bytes=VMEM
        ),
        cost_estimate=pl.CostEstimate(flops=10**11, bytes_accessed=60 * 2**20, transcendentals=10**7),
        name="front",
    )(lengths, x, og, w_local, o_local, packed, attn_gain, moe_gain, *tables)


def middle_kernel(count, len_ref, sum_ref, rows_ref, slot_ref, mid_ref, grad_ref, gain_ref, o_ref, qkv_ref, lse_ref,
                  cq, sq, ckv, skv, hin_ref, x_ref, total_ref, dmid_ref, gtwo_ref, dqkv_ref, po_ref, pw_ref,
                  dbranch_ref, wsum, hs, hr, dmoe, dkv, hss, hrs, xs, *scratch):
    nh, tokens, _ = dqkv_ref.shape
    nseq, groups = qkv_ref.shape[:2]
    seg = tokens // nseq
    z = lax.axis_index("heads")
    chain = Chain(sum_ref, total_ref, scratch[PLANE:], 0, count)
    plane = PlaneSum(rows_ref, slot_ref, dmoe, scratch[:PLANE])
    heads = whole_exchange(hs, hr, hss, hrs, nh)
    greet(nh, (1, 2, 4, 6))
    chain.begin()
    chain.run(0, 2)
    step = plane.run(chain, 2)
    chain.run(step, step + 4)
    step = step + 4
    plane.arrive()
    gtwo_ref[...] = jnp.zeros_like(gtwo_ref)

    @pl.loop(0, tokens // ROWS)
    def _(i):
        rows = pl.ds(i * ROWS, ROWS)
        d = plane.rows_total(rows)
        m = mid_ref[rows]
        inv = lax.rsqrt(jnp.mean(m * m, axis=-1, keepdims=True) + EPS)
        zed = gain_ref[...] * d
        dm = grad_ref[rows].astype(F32) + inv * zed - m * (inv * inv * inv * jnp.mean(zed * m, axis=-1, keepdims=True))
        gtwo_ref[...] += jnp.sum(d * m * inv, axis=0, keepdims=True)
        dmid_ref[rows] = dm
        db = dm.astype(BF)
        dbranch_ref[rows] = db
        for h in range(nh):
            hs[h, rows] = dot_nt(db, o_ref[h]).astype(BF)

    heads.start()
    hr[z] = hs[z]
    chain.run(step, step + 4)
    step = step + 4
    heads.wait_recv()

    @pl.loop(0, nseq)
    def _(s):
        length = len_ref[s]
        at = pl.ds(s * seg, seg)
        for g in range(groups):
            def put(i, lo, v):
                dqkv_ref[i, at, g * 256 + lo : g * 256 + lo + 128] = v

            bwd_piece(
                qkv_ref[s, g, :, :128],
                qkv_ref[s, g, :, 128:],
                lambda i: hr[i, at, g * 128 : (g + 1) * 128],
                lambda i: lse_ref[s, g, i : i + 1, :],
                length,
                (cq, sq, ckv, skv),
                dkv,
                put,
            )
            chain.step(step + groups * s + g)

    step = step + groups * nseq
    for i in range(4):
        plane.core(i).wait_send()
    load = pltpu.make_async_copy(x_ref, plane.odd, xs)
    load.start()
    ne, deep, _ = po_ref.shape
    strip, row = deep // nh, pw_ref.shape[1]
    db = dbranch_ref[...]
    for h in range(nh):
        o = dot_tn(hin_ref[h], db).astype(BF)
        for e in range(ne):
            po_ref[e, h * strip : (h + 1) * strip] = o[e * strip : (e + 1) * strip]
    chain.step(step)
    load.wait()
    wsum[...] = dot_tn(plane.odd[0], dqkv_ref[0])
    for h in range(1, nh):
        wsum[...] += dot_tn(plane.odd[h], dqkv_ref[h])
    for e in range(ne):
        pw_ref[e] = wsum[e * row : (e + 1) * row].astype(BF)
    chain.rest(step + 1)
    chain.finish()
    for i in plane.order:
        plane.chip(i).wait_send()
    heads.finish()


def middle(count, lengths, sums, rows, slots, mid, grad, gain, o_parts, qkv, lse, tables, heads_in, x):
    nseq, groups, full, _ = qkv.shape
    nh = o_parts.shape[0]
    tokens, width = mid.shape
    here, ne, cap, _ = rows.shape
    vmem = pl.BlockSpec(memory_space=pltpu.VMEM)
    hbm = pl.BlockSpec(memory_space=pl.ANY)
    heads = (nh, tokens, groups * 128)
    cols = groups * 256
    return pl.pallas_call(
        functools.partial(middle_kernel, count),
        in_specs=[pl.BlockSpec(memory_space=pltpu.SMEM), hbm, hbm] + [vmem] * 12 + [hbm],
        out_specs=[hbm] + [vmem] * 5,
        out_shape=[
            jax.ShapeDtypeStruct(sums.shape, BF),
            jax.ShapeDtypeStruct((tokens, width), F32),
            jax.ShapeDtypeStruct((1, width), F32),
            jax.ShapeDtypeStruct((nh, tokens, cols), BF),
            jax.ShapeDtypeStruct((ne, nh * groups * 128 // ne, width), BF),
            jax.ShapeDtypeStruct((ne, width // ne, cols), BF),
        ],
        scratch_shapes=[
            pltpu.VMEM((tokens, width), BF),
            pltpu.VMEM((width, cols), F32),
            pltpu.VMEM(heads, BF),
            pltpu.VMEM(heads, BF),
            pltpu.VMEM((tokens, width), F32),
            pltpu.VMEM((full, 128), F32),
            DMA((nh,)),
            DMA((nh,)),
            DMA,
        ]
        + plane_scratch(here, cap, tokens, width)
        + chain_scratch(count, width),
        compiler_params=pltpu.CompilerParams(
            collective_id=1, has_side_effects=True, vmem_limit_bytes=VMEM
        ),
        cost_estimate=pl.CostEstimate(flops=10**11, bytes_accessed=30 * 2**20, transcendentals=10**7),
        name="middle",
    )(lengths, sums, rows, slots, mid, grad, gain, o_parts, qkv, lse, *tables, heads_in, x)


class PairSum:
    order = (3, 1, 2)

    def __init__(self, parts, scratch):
        self.parts = parts
        self.c, self.e, self.f, self.cs, self.cr, self.fs, self.fr = scratch
        self.me = lax.axis_index("experts")

    def core(self, i):
        src = self.parts.at[self.me ^ 1 ^ (2 * i)]
        return remote(src, self.c.at[i], self.cs.at[i], self.cr.at[i], "experts", self.me ^ 1)

    def chip(self, i):
        return remote(self.e.at[i - 1], self.f.at[i - 1], self.fs.at[i - 1], self.fr.at[i - 1], "experts", self.me ^ (2 * i))

    def start(self):
        for i in self.order + (0,):
            self.core(i).start()

    def both(self, i):
        return self.parts[self.me ^ (2 * i)].astype(F32) + self.c[i].astype(F32)

    def forward(self):
        for i in self.order:
            self.core(i).wait_recv()
            self.e[i - 1] = self.both(i).astype(BF)
            self.chip(i).start()
        self.core(0).wait_recv()

    def result(self):
        value = self.both(0)
        for i in self.order:
            self.chip(i).wait_recv()
        for r in range(3):
            value = value + self.f[r].astype(F32)
        return value

    def finish(self):
        for i in range(4):
            self.core(i).wait_send()
        for i in self.order:
            self.chip(i).wait_send()


PAIR = 7


def pair_scratch(shape):
    return [pltpu.VMEM((n,) + shape, BF) for n in (4, 3, 3)] + [DMA((4,)), DMA((4,)), DMA((3,)), DMA((3,))]


def last_kernel(first, count, begun_ref, sum_ref, rows_ref, slot_ref, mid_ref, dqkv_ref, wz_ref, x_ref, dmid_ref,
                gain_ref, gtwo_ref, po_ref, pw_ref, total_ref, out_ref, xgrad_ref, gains_ref, ograd_ref, wgrad_ref,
                wf, br, moe, gp, gz, acc, oz, fo, fw, brs, brr, gps, gpr, gzs, gzr, oss, ors, fl, dl, *scratch):
    nh, tokens, _ = dqkv_ref.shape
    dattn = moe
    ne = rows_ref.shape[1]
    z, me = lax.axis_index("heads"), lax.axis_index("experts")
    at = PLANE
    plane = PlaneSum(rows_ref, slot_ref, moe, scratch[:at])
    weights = PlaneGather(wz_ref, lambda e: wf.at[:, e], scratch[at : at + GATHER])
    at += GATHER
    strip, row = fo.shape[0], fw.shape[0]

    def o_rows(e):
        return ograd_ref.at[pl.ds(pl.multiple_of(e * strip, strip), strip)]

    def w_rows(e):
        return wgrad_ref.at[pl.ds(pl.multiple_of(e * row, row), row)]

    spread_o = PlaneGather(fo, o_rows, scratch[at : at + GATHER])
    at += GATHER
    spread_w = PlaneGather(fw, w_rows, scratch[at : at + GATHER])
    at += GATHER
    sum_o = PairSum(po_ref, scratch[at : at + PAIR])
    at += PAIR
    sum_w = PairSum(pw_ref, scratch[at : at + PAIR])
    at += PAIR
    chain = Chain(sum_ref, total_ref, scratch[at:], first, count)
    back = whole_exchange(dqkv_ref, br, brs, brr, nh)
    pieces = Exchange(
        lambda h: acc.at[pl.ds(pl.multiple_of(h * strip, strip), strip)],
        lambda h: oz.at[h], lambda d: oss.at[d], lambda d: ors.at[d], nh)
    first_part = pltpu.make_async_copy(dmid_ref, xgrad_ref, dl)
    first_part.start()
    greet(nh, tuple(range(1, ne)))
    back.start()
    sum_o.start()
    sum_w.start()
    chain.begin()
    br[z] = dqkv_ref[z]
    chain.run(0, 2)
    sum_o.forward()
    sum_w.forward()
    weights.start()
    wf[:, me] = wz_ref[...]
    step = plane.run(chain, 2)
    chain.run(step, step + 2)
    step = step + 2
    acc[...] = sum_o.result()
    pieces.start()
    oz[z] = acc[pl.ds(pl.multiple_of(z * strip, strip), strip)]
    fw[...] = sum_w.result()
    spread_w.start()
    chain.run(step, step + 2)
    step = step + 2
    pieces.wait_recv()
    fo[...] = oz[0] + oz[1] + oz[2] + oz[3]
    spread_o.start()
    keep = [pltpu.make_async_copy(fo, o_rows(me), fl.at[0]), pltpu.make_async_copy(fw, w_rows(me), fl.at[1])]
    for c in keep:
        c.start()
    for i in weights.order:
        weights.forward(i)
    chain.run(step, step + 2)
    step = step + 2
    plane.arrive()

    @pl.loop(0, tokens // ROWS)
    def _(i):
        rows = pl.ds(i * ROWS, ROWS)
        out_ref[rows] = (mid_ref[rows] + plane.rows_total(rows)).astype(BF)

    chain.run(step, step + 2)
    step = step + 2
    for i in range(4):
        weights.core_arrive(i)
    back.wait_recv()
    for h in range(nh):
        term = dot_nt(br[h], wf[h].reshape(-1, wf.shape[3]))
        if h:
            dattn[...] += term
        else:
            dattn[...] = term
    chain.run(step, step + 2)
    step = step + 2
    pad = jnp.zeros((6, gtwo_ref.shape[1]), F32)
    own = jnp.zeros_like(gtwo_ref[...])

    def rows_back(i, total):
        rows = pl.ds(i * ROWS, ROWS)
        d = dattn[rows]
        x = x_ref[rows].astype(F32)
        inv = lax.rsqrt(jnp.mean(x * x, axis=-1, keepdims=True) + EPS)
        wed = gain_ref[...] * d
        xgrad_ref[rows] += inv * wed - x * (inv * inv * inv * jnp.mean(wed * x, axis=-1, keepdims=True))
        return total + jnp.sum(d * x * inv, axis=0, keepdims=True)

    first_part.wait()
    own = lax.fori_loop(0, tokens // ROWS, rows_back, own)
    gp[me] = jnp.concatenate([own, gtwo_ref[...], pad], axis=0)

    def near(r, at):
        return remote(gp.at[me], gp.at[at], gps.at[r], gpr.at[r], "experts", me ^ r)

    for r in range(1, ne):
        near(r, me).start()
    chain.run(step, step + 2)
    step = step + 2
    for spread in (spread_w, spread_o):
        for i in spread.order:
            spread.forward(i)
    for r in range(1, ne):
        near(r, me ^ r).wait_recv()
    total = gp[0]
    for e in range(1, ne):
        total = total + gp[e]
    gz[z] = total
    gains = Exchange(lambda h: gz.at[z], lambda h: gz.at[h], lambda d: gzs.at[d], lambda d: gzr.at[d], nh)
    gains.start()
    chain.rest(step)
    gains.wait_recv()
    total = gz[0]
    for h in range(1, nh):
        total = total + gz[h]
    gains_ref[...] = total
    for spread in (spread_w, spread_o):
        for i in range(4):
            spread.core_arrive(i)
    chain.finish()
    for part in (plane, back, pieces, gains, weights, spread_w, spread_o, sum_o, sum_w):
        part.finish()
    for c in keep:
        c.wait()
    for r in range(1, ne):
        near(r, me).wait_send()


def last(first, count, total, sums, rows, slots, mid, dqkv, w_pieces, x, d_mid, gain, gain_two, po, pw):
    nh, tokens, cols = dqkv.shape
    here, ne, cap, width = rows.shape
    strip = po.shape[1] // nh
    row = pw.shape[1]
    hbm = pl.BlockSpec(memory_space=pl.ANY)
    vmem = pl.BlockSpec(memory_space=pltpu.VMEM)
    return pl.pallas_call(
        functools.partial(last_kernel, first, count),
        in_specs=[hbm, hbm, hbm] + [vmem] * 5 + [hbm] + [vmem] * 4,
        input_output_aliases={0: 0},
        out_specs=[hbm] + [vmem] * 3 + [hbm] * 2,
        out_shape=[
            jax.ShapeDtypeStruct(sums.shape, BF),
            jax.ShapeDtypeStruct((tokens, width), BF),
            jax.ShapeDtypeStruct((tokens, width), F32),
            jax.ShapeDtypeStruct((8, width), F32),
            jax.ShapeDtypeStruct((strip * ne, width), F32),
            jax.ShapeDtypeStruct((row * ne, cols), F32),
        ],
        scratch_shapes=[
            pltpu.VMEM((nh, ne, width // ne, cols), BF),
            pltpu.VMEM((nh, tokens, cols), BF),
            pltpu.VMEM((tokens, width), F32),
            pltpu.VMEM((ne, 8, width), F32),
            pltpu.VMEM((nh, 8, width), F32),
            pltpu.VMEM((nh * strip, width), F32),
            pltpu.VMEM((nh, strip, width), F32),
            pltpu.VMEM((strip, width), F32),
            pltpu.VMEM((row, cols), F32),
            DMA((nh,)),
            DMA((nh,)),
            DMA((ne,)),
            DMA((ne,)),
            DMA((nh,)),
            DMA((nh,)),
            DMA((nh,)),
            DMA((nh,)),
            DMA((2,)),
            DMA,
        ]
        + plane_scratch(here, cap, tokens, width)
        + gather_sems() * 3
        + pair_scratch(po.shape[1:])
        + pair_scratch(pw.shape[1:])
        + chain_scratch(count, width),
        compiler_params=pltpu.CompilerParams(
            collective_id=2, has_side_effects=True, vmem_limit_bytes=VMEM
        ),
        cost_estimate=pl.CostEstimate(flops=2 * 10**11, bytes_accessed=30 * 2**20, transcendentals=0),
        name="last",
    )(total, sums, rows, slots, mid, dqkv, w_pieces, x, d_mid, gain, gain_two, po, pw)


def widen_kernel(x_ref, in_ref, down_ref):
    c = pl.program_id(1)

    @pl.when(c < 2)
    def _():
        in_ref[...] = x_ref[...].astype(F32)

    @pl.when(c == 2)
    def _():
        down_ref[...] = x_ref[...].astype(F32)


def widen(sums, ff):
    here, rows, width = sums.shape
    return pl.pallas_call(
        widen_kernel,
        grid=(here, 3),
        in_specs=[pl.BlockSpec((1, ff, width), lambda j, c: (j, c, 0))],
        out_specs=[
            pl.BlockSpec((1, ff, width), lambda j, c: (j, jnp.minimum(c, 1), 0)),
            pl.BlockSpec((1, ff, width), lambda j, c: (j, 0, 0)),
        ],
        out_shape=[
            jax.ShapeDtypeStruct((here, 2 * ff, width), F32),
            jax.ShapeDtypeStruct((here, ff, width), F32),
        ],
        compiler_params=params(2),
        name="widen",
    )(sums)


def body(layer_input, seq_lengths, expert_ids, route_weight, priority, attn_gain, moe_gain,
         query_matrix, key_matrix, value_matrix, output_matrix, expert_in, expert_down, out_grad):
    seg, nseq, width = layer_input.shape
    nh, ne = lax.axis_size("heads"), lax.axis_size("experts")
    z, me = lax.axis_index("heads"), lax.axis_index("experts")
    top = expert_ids.shape[-1]
    tokens = seg * nseq
    groups = key_matrix.shape[1] // HEAD
    here = expert_in.shape[0]
    cap = (5 * tokens * top + 4 * EXPERTS - 1) // (4 * EXPERTS)

    def local(v):
        return jnp.swapaxes(v, 0, 1).reshape((tokens,) + v.shape[2:])

    def unlocal(v):
        return jnp.swapaxes(v.reshape((nseq, seg) + v.shape[1:]), 0, 1)

    ids = local(expert_ids)
    order = local(priority)
    weight = local(route_weight)
    position = z * seg + jnp.arange(seg, dtype=jnp.int32)
    live = (position[None, :] < seq_lengths[:, None]).reshape(tokens)
    match = ids.T[:, None, :] == jnp.arange(EXPERTS, dtype=jnp.int32)[None, :, None]
    weight_e = jnp.sum(jnp.where(match, weight.T[:, None, :], 0.0), axis=0)
    chosen = jnp.any(match, axis=0) & live[None, :]
    earlier = (order[:, None] < order[None, :]).astype(BF)
    before = dot(chosen.astype(BF), earlier)
    slot = jnp.where(chosen & (before < cap), before, -1.0)
    packed = jnp.concatenate([slot.reshape(ne, here, tokens), weight_e.reshape(ne, here, tokens)], axis=1)
    wq = query_matrix.reshape(width, groups, 128)
    wk = key_matrix.reshape(width, groups, HEAD)
    wv = value_matrix.reshape(width, groups, HEAD)
    w_local = jnp.concatenate([wq, wk, wv], axis=2).reshape(width, groups * 256)
    tables = rotary_tables(nh * seg)
    x, grad = local(layer_input), local(out_grad)
    xf = x.astype(F32)
    gain_a, gain_m = attn_gain.reshape(1, width), moe_gain.reshape(1, width)
    fast = nh == 4 and ne == 8
    if fast:
        gathered, qkv, lse, heads_in, o_full, w_pieces, mid, pack, d_rows, x_rows = front(
            seq_lengths, x, grad, w_local, output_matrix, packed, gain_a, gain_m, tables, nh, nseq, cap)
        slots, weights = pack[:, :here].astype(jnp.int32), pack[:, here:]
        o_parts = o_full.reshape(nh, groups * 128, width)
    else:
        packed = lax.all_to_all(packed, "experts", split_axis=0, concat_axis=0, tiled=True)
        packed = packed[me ^ jnp.arange(ne, dtype=jnp.int32)]
        slots, weights = packed[:, :here].astype(jnp.int32), packed[:, here:]
        inv_one = lax.rsqrt(jnp.mean(xf * xf, axis=-1, keepdims=True) + EPS)
        attn_in = (xf * inv_one * attn_gain).astype(BF)
        gathered = lax.all_gather(attn_in.reshape(nseq, seg, width), "heads", axis=0)
        w_groups = jnp.transpose(w_local.reshape(width, groups, 256), (1, 0, 2))
        rows_in, rows_out = width // ne, output_matrix.shape[0] // ne
        w_piece = lax.dynamic_slice_in_dim(w_local, me * rows_in, rows_in, 0)
        o_piece = lax.dynamic_slice_in_dim(output_matrix, me * rows_out, rows_out, 0)
        o_full = lax.all_gather(o_piece, ("heads", "experts"), axis=0, tiled=True)
        w_full = lax.all_gather(w_piece, ("heads", "experts"), axis=0, tiled=True)
        w_full = w_full.reshape(nh, width, groups * 256)
        qkv, heads_out, lse = attn_forward(gathered, w_groups, seq_lengths, tables)
        heads_in = lax.all_to_all(heads_out, "heads", split_axis=0, concat_axis=0, tiled=True)
        heads_in = heads_in.reshape(nh, tokens, groups * 128)
        o_parts = o_full.reshape(nh, groups * 128, width)
        branch = jnp.einsum("ztm,zmw->tw", heads_in, o_parts, preferred_element_type=F32)
        mid = xf + branch
        inv_two = lax.rsqrt(jnp.mean(mid * mid, axis=-1, keepdims=True) + EPS)
        moe_in = (mid * inv_two * moe_gain).astype(BF)
        d_rows = gather_rows(slots, weights, plane_gather(grad, ne), cap)
        x_rows = gather_rows(slots, None, plane_gather(moe_in, ne), cap)

    results, drows, sums = experts_call(slots, weights, x_rows, d_rows, expert_in, expert_down)
    if fast:
        flat = sums.reshape(-1, width)
        chunks = flat.shape[0] // CHUNK
        half = (5 * chunks) // 12
        total, d_mid, gain_two, dqkv, po, pw = middle(
            half, seq_lengths, flat, drows, pack, mid, grad, gain_m, o_parts, qkv, lse, tables,
            heads_in, gathered)
        total, out, x_grad, gains, o_grad, w_grad = last(
            half, chunks - half, total, flat, results, pack, mid, dqkv, w_pieces, x, d_mid, gain_a, gain_two, po, pw)
        gain_one, gain_two = gains[0], gains[1]
        grad_in, grad_down = widen(total.reshape(sums.shape), expert_down.shape[1])
    else:
        slots_t = jnp.swapaxes(slots, 1, 2)
        d_parts = combine(slots_t, drows)
        moe_parts = combine(slots_t, results)
        totals = heads_sum(sums, z, nh)
        grad_in, grad_down = totals[:, :width], totals[:, width:]
        d_moe = plane_scatter(d_parts, ne)
        moe_sum = plane_scatter(moe_parts, ne)
        out = (mid + moe_sum).astype(BF)
        zed = moe_gain * d_moe
        d_mid = grad.astype(F32) + inv_two * zed - mid * (inv_two ** 3 * jnp.mean(zed * mid, axis=-1, keepdims=True))
        gain_two = jnp.sum(d_moe * mid * inv_two, axis=0)
        d_branch = d_mid.astype(BF)
        d_heads = jnp.einsum("tw,zmw->ztm", d_branch, o_parts, preferred_element_type=F32).astype(BF)
        d_heads = d_heads.reshape(nh, nseq, seg, groups * 128)
        d_heads = lax.all_to_all(d_heads, "heads", split_axis=0, concat_axis=0, tiled=True)
        dqkv = attn_backward(qkv, d_heads, lse, seq_lengths, tables)
        dqkv = dqkv.reshape(nh, tokens, groups * 256)
        back = lax.all_to_all(dqkv, "heads", split_axis=0, concat_axis=0, tiled=True)
        d_attn = jnp.einsum("ztc,zmc->tm", back, w_full, preferred_element_type=F32)
        o_grad, w_grad = weight_sums(heads_in, d_branch, gathered, dqkv, ne)
        wed = attn_gain * d_attn
        x_grad = d_mid + inv_one * wed - xf * (inv_one ** 3 * jnp.mean(wed * xf, axis=-1, keepdims=True))
        gain_one = jnp.sum(d_attn * xf * inv_one, axis=0)
        gain_one, gain_two = lax.psum((gain_one, gain_two), ("heads", "experts"))
    w_grad = w_grad.reshape(width, groups, 256)
    q_grad = w_grad[:, :, :128].reshape(query_matrix.shape)
    k_grad = w_grad[:, :, 128:192].reshape(key_matrix.shape)
    v_grad = w_grad[:, :, 192:].reshape(value_matrix.shape)
    return (
        unlocal(out),
        unlocal(x_grad),
        gain_one,
        gain_two,
        q_grad,
        k_grad,
        v_grad,
        o_grad,
        grad_in,
        grad_down,
    )


def solution(mesh):
    rows = P("heads", "experts", None)
    in_specs = (
        rows,
        P("experts"),
        rows,
        rows,
        P("heads", "experts"),
        P(),
        P(),
        P(None, "heads"),
        P(None, "heads"),
        P(None, "heads"),
        P("heads", None),
        P("experts", None, None),
        P("experts", None, None),
        rows,
    )
    out_specs = (
        rows,
        rows,
        P(),
        P(),
        P(None, "heads"),
        P(None, "heads"),
        P(None, "heads"),
        P("heads", None),
        P("experts", None, None),
        P("experts", None, None),
    )
    return jax.shard_map(body, mesh=mesh, in_specs=in_specs, out_specs=out_specs, check_vma=False)
```

```python
import functools
import math

import jax
import jax.numpy as jnp
from jax import lax
from jax.experimental import pallas as pl
from jax.experimental.pallas import tpu as pltpu
from jax.sharding import PartitionSpec as P

HEAD = 64
EXPERTS = 32
EPS = 1e-06
BF = jnp.bfloat16
F32 = jnp.float32
SCALE = HEAD ** (-0.5)
NEG = -1e30
VMEM = 63 * 1024 * 1024
MESH = pl.DeviceIdType.MESH
DMA = pltpu.SemaphoreType.DMA


def dot(a, b):
    return jnp.dot(a, b, preferred_element_type=F32)


def dot_nt(a, b):
    return lax.dot_general(a, b, (((1,), (1,)), ((), ())), preferred_element_type=F32)


def dot_tn(a, b):
    return lax.dot_general(a, b, (((0,), (0,)), ((), ())), preferred_element_type=F32)


def params(n):
    return pltpu.CompilerParams(
        dimension_semantics=("arbitrary",) * n, vmem_limit_bytes=VMEM
    )


def swap_halves(v):
    lane = lax.broadcasted_iota(jnp.int32, v.shape, 1)
    return jnp.where(lane % 64 < 32, pltpu.roll(v, 96, 1), pltpu.roll(v, 32, 1))


def attn_mask(offset, n, block, length):
    key = lax.broadcasted_iota(jnp.int32, (n, block), 0)
    query = lax.broadcasted_iota(jnp.int32, (n, block), 1) + offset
    return (key <= query) & (key < length)


def two_heads(v):
    return jnp.concatenate([v[:, :HEAD], v[:, HEAD:]], axis=0)


def untwo(vt, block):
    return jnp.concatenate([vt[:, :block], vt[:, block:]], axis=0).T


def fwd_kernel(len_ref, x_ref, w_ref, cq, sq, ckv, skv, qkv_ref, head_ref, lse_ref):
    nh, _, seg, width = x_ref.shape
    full = nh * seg
    block = seg
    length = len_ref[pl.program_id(0)]
    lin = dot(x_ref[...].reshape(full, width), w_ref[0])
    ql, kvl = lin[:, :128], lin[:, 128:]
    q = (ql * cq[...] + swap_halves(ql) * sq[...]).astype(BF)
    kvr = kvl * ckv[...] + swap_halves(kvl) * skv[...]
    kv = kvr.astype(BF)
    qkv_ref[0, 0, :, :128] = q
    qkv_ref[0, 0, :, 128:] = kv
    k = kv[:, :HEAD]
    vt = kvr.T[HEAD:].astype(BF)
    for i in range(nh):
        n = (i + 1) * block
        q2 = two_heads(q[i * block : n])
        s = dot_nt(k[:n], q2)
        mask = attn_mask(i * block, n, block, length)
        s = jnp.where(jnp.concatenate([mask, mask], axis=1), s * SCALE, NEG)
        m = jnp.max(s, axis=0, keepdims=True)
        e = jnp.exp(s - m)
        total = jnp.sum(e, axis=0, keepdims=True)
        p = (e * (1.0 / total)).astype(BF)
        lse_ref[0, 0, i : i + 1, :] = m + jnp.log(total)
        head_ref[i, 0] = untwo(dot(vt[:, :n], p), block).astype(BF)


def attn_forward(x, w, lengths, tables):
    nh, nseq, seg, width = x.shape
    groups = w.shape[0]
    full = nh * seg
    cq, sq, ckv, skv = tables
    tab = pl.BlockSpec((full, 128), lambda s, g: (0, 0))
    return pl.pallas_call(
        fwd_kernel,
        grid=(nseq, groups),
        in_specs=[
            pl.BlockSpec(memory_space=pltpu.SMEM),
            pl.BlockSpec((nh, 1, seg, width), lambda s, g: (0, s, 0, 0)),
            pl.BlockSpec((1, width, 256), lambda s, g: (g, 0, 0)),
            tab,
            tab,
            tab,
            tab,
        ],
        out_specs=[
            pl.BlockSpec((1, 1, full, 256), lambda s, g: (s, g, 0, 0)),
            pl.BlockSpec((nh, 1, seg, 128), lambda s, g: (0, s, 0, g)),
            pl.BlockSpec((1, 1, nh, 2 * seg), lambda s, g: (s, g, 0, 0)),
        ],
        out_shape=[
            jax.ShapeDtypeStruct((nseq, groups, full, 256), BF),
            jax.ShapeDtypeStruct((nh, nseq, seg, groups * 128), BF),
            jax.ShapeDtypeStruct((nseq, groups, nh, 2 * seg), F32),
        ],
        compiler_params=params(2),
        cost_estimate=pl.CostEstimate(flops=6 * 10**9, bytes_accessed=12 * 2**20, transcendentals=10**7),
        name="attn_forward",
    )(lengths, x, w, cq, sq, ckv, skv)


def bwd_piece(q, kv, heads, lses, length, tables, dkv_ref, put):
    cq, sq, ckv, skv = tables
    full, block = q.shape[0], lses(0).shape[1] // 2
    k, v = kv[:, :HEAD], kv[:, HEAD:]
    kt = kv.astype(F32).T[:HEAD].astype(BF)
    dkv_ref[...] = jnp.zeros_like(dkv_ref)
    for i in range(full // block):
        n = (i + 1) * block
        rows = pl.ds(i * block, block)
        mask = attn_mask(i * block, n, block, length)
        grads = []
        for h in range(2):
            qh = q[i * block : n, h * HEAD : (h + 1) * HEAD]
            doh = heads(i)[:, h * HEAD : (h + 1) * HEAD]
            s = dot_nt(k[:n], qh)
            p = jnp.exp(jnp.where(mask, s * SCALE - lses(i)[:, h * block : (h + 1) * block], NEG))
            dp = dot_nt(v[:n], doh)
            delta = jnp.sum(p * dp, axis=0, keepdims=True)
            ds = (p * (dp - delta) * SCALE).astype(BF)
            dkv_ref[:n, :HEAD] += dot(ds, qh)
            dkv_ref[:n, HEAD:] += dot(p.astype(BF), doh)
            grads.append(dot(kt[:, :n], ds))
        dq = jnp.concatenate(grads, axis=0).T
        dq = dq * cq[rows, :] - swap_halves(dq) * sq[rows, :]
        put(i, 0, dq.astype(BF))
    dkv = dkv_ref[...]
    dkv = (dkv * ckv[...] - swap_halves(dkv) * skv[...]).astype(BF)
    for i in range(full // block):
        put(i, 128, dkv[i * block : (i + 1) * block])


def bwd_kernel(len_ref, qkv_ref, do_ref, lse_ref, cq, sq, ckv, skv, out_ref, dkv_ref):
    def put(i, lo, v):
        out_ref[i, 0, :, lo : lo + 128] = v

    bwd_piece(
        qkv_ref[0, 0, :, :128],
        qkv_ref[0, 0, :, 128:],
        lambda i: do_ref[i, 0],
        lambda i: lse_ref[0, 0, i : i + 1, :],
        len_ref[pl.program_id(0)],
        (cq, sq, ckv, skv),
        dkv_ref,
        put,
    )


def attn_backward(qkv, d_head, lse, lengths, tables):
    nseq, groups, full, _ = qkv.shape
    nh, _, seg, _ = d_head.shape
    cq, sq, ckv, skv = tables
    tab = pl.BlockSpec((full, 128), lambda s, g: (0, 0))
    return pl.pallas_call(
        bwd_kernel,
        grid=(nseq, groups),
        in_specs=[
            pl.BlockSpec(memory_space=pltpu.SMEM),
            pl.BlockSpec((1, 1, full, 256), lambda s, g: (s, g, 0, 0)),
            pl.BlockSpec((nh, 1, seg, 128), lambda s, g: (0, s, 0, g)),
            pl.BlockSpec((1, 1, nh, 2 * seg), lambda s, g: (s, g, 0, 0)),
            tab,
            tab,
            tab,
            tab,
        ],
        out_specs=pl.BlockSpec((nh, 1, seg, 256), lambda s, g: (0, s, 0, g)),
        out_shape=jax.ShapeDtypeStruct((nh, nseq, seg, groups * 256), BF),
        scratch_shapes=[pltpu.VMEM((full, 128), F32)],
        compiler_params=params(2),
        cost_estimate=pl.CostEstimate(flops=12 * 10**9, bytes_accessed=8 * 2**20, transcendentals=10**7),
        name="attn_backward",
    )(lengths, qkv, d_head, lse, cq, sq, ckv, skv)


def rotary_tables(length):
    half = HEAD // 2
    frequency = jnp.exp(jnp.arange(half, dtype=F32) * (-2.0 * math.log(10000.0) / HEAD))
    angles = jnp.arange(length, dtype=F32)[:, None] * frequency[None, :]
    cos, sin = jnp.cos(angles), jnp.sin(angles)
    c1 = jnp.concatenate([cos, cos], axis=1)
    s1 = jnp.concatenate([-sin, sin], axis=1)
    cq = jnp.concatenate([c1, c1], axis=1)
    sq = jnp.concatenate([s1, s1], axis=1)
    ckv = jnp.concatenate([c1, jnp.ones_like(c1)], axis=1)
    skv = jnp.concatenate([s1, jnp.zeros_like(s1)], axis=1)
    return cq, sq, ckv, skv


def pick_rows(slots, cap):
    tokens = slots.shape[1]
    index = lax.broadcasted_iota(jnp.int32, (cap, tokens), 0)
    return [index == slots[j : j + 1, :] for j in range(slots.shape[0])]


def gather_kernel(weighted, slot_ref, *refs):
    if weighted:
        weight_ref, tok_ref, out_ref = refs
    else:
        tok_ref, out_ref = refs[0], refs[-1]
    cap = out_ref.shape[2]
    hits = pick_rows(slot_ref[0], cap)
    rows = dot(jnp.concatenate([h.astype(F32) for h in hits], axis=0).astype(BF), tok_ref[0])
    for j, hit in enumerate(hits):
        part = rows[j * cap : (j + 1) * cap]
        if weighted:
            part = part * jnp.sum(jnp.where(hit, weight_ref[0, j : j + 1, :], 0.0), axis=1, keepdims=True)
        out_ref[j, 0] = part.astype(BF)


def gather_rows(slots, weights, tokens, cap):
    sources, here, count = slots.shape
    width = tokens.shape[-1]
    small = pl.BlockSpec((1, here, count), lambda s: (s, 0, 0))
    weighted = weights is not None
    return pl.pallas_call(
        functools.partial(gather_kernel, weighted),
        grid=(sources,),
        in_specs=[small] + [small] * weighted + [pl.BlockSpec((1, count, width), lambda s: (s, 0, 0))],
        out_specs=pl.BlockSpec((here, 1, cap, width), lambda s: (0, s, 0, 0)),
        out_shape=jax.ShapeDtypeStruct((here, sources, cap, width), BF),
        compiler_params=params(1),
        cost_estimate=pl.CostEstimate(
            flops=2 * sources * here * cap * count * width,
            bytes_accessed=2 * sources * width * (count + here * cap),
            transcendentals=0,
        ),
        name="gather_rows",
    )(*([slots] + [weights] * weighted + [tokens]))


def expert_kernel(steps, slot_ref, weight_ref, x_ref, d_ref, win_ref, wdown_ref,
                  out_ref, drow_ref, grad_ref, hid_ref, dgu_ref, *acc):
    _, sources, cap, width = x_ref.shape
    ff = wdown_ref.shape[1]
    per = 2 if sources % 2 == 0 else 1
    win, wdown = win_ref[0], wdown_ref[0]
    for c in range(sources // per):
        rows = slice(c * per * cap, (c + 1) * per * cap)
        x = x_ref[0, c * per : (c + 1) * per].reshape(per * cap, width)
        d = d_ref[0, c * per : (c + 1) * per].reshape(per * cap, width)
        gu = dot(x, win)
        gate, up = gu[:, :ff], gu[:, ff:]
        sig = 1.0 / (1.0 + jnp.exp(-gate))
        act = gate * sig
        hidden = (act * up).astype(BF)
        hid_ref[rows, :] = hidden
        result = dot(hidden, wdown).astype(BF).astype(F32)
        for b in range(per):
            hit = pick_rows(slot_ref[c * per + b, 0], cap)[0]
            w = jnp.sum(jnp.where(hit, weight_ref[c * per + b, 0], 0.0), axis=1, keepdims=True)
            out_ref[0, c * per + b] = (result[b * cap : (b + 1) * cap] * w).astype(BF)
        dh = dot_nt(d, wdown)
        dgu_ref[rows, :ff] = (dh * up * (sig * (1.0 + gate * (1.0 - sig)))).astype(BF)
        dgu_ref[rows, ff:] = (dh * act).astype(BF)
        drow = dot_nt(dgu_ref[rows, :], win).astype(BF)
        for b in range(per):
            drow_ref[0, c * per + b] = drow[b * cap : (b + 1) * cap]
    x = x_ref[0].reshape(sources * cap, width)
    d = d_ref[0].reshape(sources * cap, width)
    gin = dot_tn(x, dgu_ref[...])
    gdown = dot_tn(hid_ref[...], d)
    if steps == 1:
        grad_ref[0, :width] = gin.astype(BF)
        grad_ref[0, width:] = gdown.astype(BF)
    else:
        ain, adown = acc
        step = pl.program_id(1)

        @pl.when(step == 0)
        def _():
            ain[...] = jnp.zeros_like(ain)
            adown[...] = jnp.zeros_like(adown)

        ain[...] += gin
        adown[...] += gdown

        @pl.when(step == steps - 1)
        def _():
            grad_ref[0, :width] = ain[...].astype(BF)
            grad_ref[0, width:] = adown[...].astype(BF)


def experts_call(slots, weights, x, d, win, wdown):
    count, sources, cap, width = x.shape
    tokens = slots.shape[-1]
    ff = wdown.shape[1]
    chunk = min(sources, 8)
    steps = sources // chunk
    small = pl.BlockSpec((chunk, 1, 1, tokens), lambda j, r: (r, j, 0, 0))
    rows = pl.BlockSpec((1, chunk, cap, width), lambda j, r: (j, r, 0, 0))
    rows_out = pl.BlockSpec((1, chunk, cap, width), lambda j, r: (j, r, 0, 0))
    scratch = [pltpu.VMEM((chunk * cap, ff), BF), pltpu.VMEM((chunk * cap, 2 * ff), BF)]
    if steps > 1:
        scratch += [pltpu.VMEM((width, 2 * ff), F32), pltpu.VMEM((ff, width), F32)]
    shape = jax.ShapeDtypeStruct((count, sources, cap, width), BF)
    return pl.pallas_call(
        functools.partial(expert_kernel, steps),
        grid=(count, steps),
        in_specs=[
            small,
            small,
            rows,
            rows,
            pl.BlockSpec((1, width, 2 * ff), lambda j, r: (j, 0, 0)),
            pl.BlockSpec((1, ff, width), lambda j, r: (j, 0, 0)),
        ],
        out_specs=[
            rows_out,
            rows_out,
            pl.BlockSpec((1, width + ff, width), lambda j, r: (j, 0, 0)),
        ],
        out_shape=[
            shape,
            shape,
            jax.ShapeDtypeStruct((count, width + ff, width), BF),
        ],
        scratch_shapes=scratch,
        compiler_params=params(2),
        cost_estimate=pl.CostEstimate(
            flops=2 * count * sources * cap * width * ff * 9,
            bytes_accessed=8 * count * sources * cap * width + 12 * count * width * ff,
            transcendentals=count * sources * cap * ff,
        ),
        name="experts",
    )(slots[:, :, None, :], weights[:, :, None, :], x, d, win, wdown)


def combine_kernel(slot_ref, row_ref, out_ref):
    slots = slot_ref[0]
    count, here = slots.shape
    cap = row_ref.shape[2]
    lane = lax.broadcasted_iota(jnp.int32, (count, here * cap), 1)
    hot = None
    for j in range(here):
        col = slots[:, j : j + 1]
        hit = lane == jnp.where(col >= 0, col + j * cap, -1)
        hot = hit if hot is None else hot | hit
    hot = hot.astype(F32).astype(BF)
    out_ref[0] = dot(hot, row_ref[...].reshape(here * cap, row_ref.shape[3])).astype(BF)


def combine(slots_t, rows):
    sources, count, here = slots_t.shape
    _, _, cap, width = rows.shape
    return pl.pallas_call(
        combine_kernel,
        grid=(sources,),
        in_specs=[
            pl.BlockSpec((1, count, here), lambda s: (s, 0, 0)),
            pl.BlockSpec((here, 1, cap, width), lambda s: (0, s, 0, 0)),
        ],
        out_specs=pl.BlockSpec((1, count, width), lambda s: (s, 0, 0)),
        out_shape=jax.ShapeDtypeStruct((sources, count, width), BF),
        compiler_params=params(1),
        cost_estimate=pl.CostEstimate(
            flops=2 * sources * here * cap * count * width,
            bytes_accessed=2 * sources * width * (count + here * cap),
            transcendentals=0,
        ),
        name="combine",
    )(slots_t, rows)


def swap(x, bit, n):
    return lax.ppermute(x, "experts", [(i, i ^ bit) for i in range(n)])


def plane_gather(x, n):
    if n != 8:
        whole = lax.all_gather(x, "experts", axis=0)
        order = lax.axis_index("experts") ^ jnp.arange(n, dtype=jnp.int32)
        return whole[order]
    got = {0: x}
    for r in (2, 4, 6):
        got[r] = swap(x, r, n)
    for r in (0, 2, 4, 6):
        got[r + 1] = swap(got[r], 1, n)
    return jnp.stack([got[r] for r in range(n)], axis=0)


def plane_scatter(parts, n):
    if n != 8:
        order = lax.axis_index("experts") ^ jnp.arange(n, dtype=jnp.int32)
        return lax.psum_scatter(parts[order].astype(F32), "experts", scatter_dimension=0)
    odd = swap(parts[1::2], 1, n)
    both = [parts[2 * i].astype(F32) + odd[i].astype(F32) for i in range(4)]
    total = both[0]
    for i in (1, 2, 3):
        total = total + swap(both[i].astype(BF), 2 * i, n).astype(F32)
    return total


def heads_sum(x, z, nh):
    if nh != 4:
        return lax.psum(x.astype(F32), "heads")
    first = lax.ppermute(x, "heads", [(0, 1), (3, 2)])
    pair = (x.astype(F32) + first.astype(F32)).astype(BF)
    second = lax.ppermute(pair, "heads", [(1, 2), (2, 1)])
    total = (pair.astype(F32) + second.astype(F32)).astype(BF)
    third = lax.ppermute(total, "heads", [(1, 0), (2, 3)])
    return jnp.where((z == 1) | (z == 2), total, third).astype(F32)


def weight_sums(heads_in, d_branch, gathered, dqkv, ne):
    nh, tokens, part = heads_in.shape
    width, cols = d_branch.shape[1], dqkv.shape[2]
    col, row = width // ne, width // ne
    o = jnp.einsum("ztm,tew->ezmw", heads_in, d_branch.reshape(tokens, ne, col), preferred_element_type=F32)
    w = jnp.einsum("ztm,ztc->mc", gathered.reshape(nh, tokens, width), dqkv, preferred_element_type=F32)
    cut = cols // col
    w = jnp.swapaxes(w.reshape(ne, row, cut, col), 1, 2).reshape(ne, cut * row, col)
    both = jnp.concatenate([o.reshape(ne, nh * part, col), w], axis=1)
    both = lax.psum_scatter(both, "experts", scatter_dimension=0)
    o, w = both[: nh * part], both[nh * part :]
    o = lax.psum_scatter(o.reshape(nh, part, col), "heads", scatter_dimension=0)
    return weight_split(lax.all_gather(jnp.concatenate([o, w], axis=0), "experts", axis=0), part, cols)


def weight_split(both, part, cols):
    ne, _, col = both.shape
    width, row, cut = ne * col, col, cols // col
    o = jnp.swapaxes(both[:, :part], 0, 1).reshape(part, width)
    w = jnp.swapaxes(both[:, part:].reshape(ne, cut, row, col), 1, 2)
    return o, w.reshape(width, cols)


CHUNK = 128
LAG = 3
FLIGHT = 3


def remote(src, dst, send, recv, axis, index):
    return pltpu.make_async_remote_copy(
        src_ref=src, dst_ref=dst, send_sem=send, recv_sem=recv,
        device_id={axis: index}, device_id_type=MESH,
    )


def greet(nh, masks):
    z, me = lax.axis_index("heads"), lax.axis_index("experts")
    bar = pltpu.get_barrier_semaphore()
    for d in range(1, nh):
        pl.semaphore_signal(bar, inc=1, device_id={"heads": lax.rem(z + d, nh)}, device_id_type=MESH)
    for r in masks:
        pl.semaphore_signal(bar, inc=1, device_id={"experts": me ^ r}, device_id_type=MESH)
    pl.semaphore_wait(bar, nh - 1 + len(masks))


class Chain:
    def __init__(self, src, out, scratch, first, count):
        self.src, self.out, self.first, self.count = src, out, first, count
        self.flight = min(FLIGHT, count)
        self.a, self.b, self.buf, self.s1, self.r1, self.s2, self.r2, self.ls, self.os = scratch
        z = lax.axis_index("heads")
        self.mid = (z == 1) | (z == 2)
        self.outer = jnp.where(z == 0, 1, jnp.where(z == 1, 0, jnp.where(z == 2, 3, 2)))
        self.inner = jnp.where(z == 1, 2, jnp.where(z == 2, 1, z))

    def piece(self, k):
        return self.src.at[pl.ds((self.first + k) * CHUNK, CHUNK)]

    def load(self, k):
        return pltpu.make_async_copy(self.piece(k), self.buf.at[lax.rem(k, 2)], self.ls.at[lax.rem(k, 2)])

    def store(self, ref, k):
        return pltpu.make_async_copy(ref.at[k], self.out.at[pl.ds((self.first + k) * CHUNK, CHUNK)], self.os.at[k])

    def up(self, k):
        return remote(self.piece(k), self.a.at[k], self.s1.at[k], self.r1.at[k], "heads", self.outer)

    def across(self, k):
        return remote(self.a.at[k], self.b.at[k], self.s2.at[k], self.r2.at[k], "heads", self.inner)

    def down(self, k):
        return remote(self.b.at[k], self.a.at[k], self.s1.at[k], self.r1.at[k], "heads", self.outer)

    def begin(self):
        @pl.when(self.mid)
        def _():
            self.load(0).start()

        @pl.when(jnp.logical_not(self.mid))
        def _():
            @pl.loop(0, self.flight)
            def _(k):
                self.up(k).start()

    def pair(self, k):
        @pl.when(k + 1 < self.count)
        def _():
            self.load(k + 1).start()

        self.load(k).wait()
        self.up(k).wait_recv()
        own = self.buf[lax.rem(k, 2)].astype(F32)
        self.a[k] = (self.a[k].astype(F32) + own).astype(BF)
        self.across(k).start()

    def total(self, j):
        self.across(j).wait_recv()
        self.b[j] = (self.a[j].astype(F32) + self.b[j].astype(F32)).astype(BF)
        self.down(j).start()
        self.store(self.b, j).start()

    def take(self, j):
        self.down(j).wait_recv()
        self.store(self.a, j).start()

    def step(self, k, lag=LAG):
        n = self.count

        @pl.when(self.mid)
        def _():
            @pl.when(k < n)
            def _():
                self.pair(k)

            @pl.when((k >= lag) & (k < n + lag))
            def _():
                self.total(k - lag)

        @pl.when(jnp.logical_not(self.mid))
        def _():
            @pl.when(k + self.flight < n)
            def _():
                self.up(k).wait_send()
                self.up(k + self.flight).start()

            @pl.when((k >= lag + 2) & (k < n + lag + 2))
            def _():
                self.take(k - lag - 2)

    def rest(self, k):
        n = self.count

        @pl.when(self.mid)
        def _():
            @pl.loop(min(max(k - LAG, 0), n), min(max(k - 1, 0), n))
            def _(j):
                self.total(j)

        @pl.when(jnp.logical_not(self.mid))
        def _():
            @pl.loop(min(max(k - LAG - 2, 0), n), min(max(k - 3, 0), n))
            def _(j):
                self.take(j)

        @pl.loop(k, n + 3)
        def _(i):
            self.step(i, 1)

    def run(self, first, last):
        @pl.loop(first, last)
        def _(k):
            self.step(k)

    def finish(self):
        n = self.count

        @pl.when(self.mid)
        def _():
            @pl.loop(0, n)
            def _(k):
                self.across(k).wait_send()
                self.down(k).wait_send()
                self.store(self.b, k).wait()

        @pl.when(jnp.logical_not(self.mid))
        def _():
            @pl.loop(n - self.flight, n)
            def _(k):
                self.up(k).wait_send()

            @pl.loop(0, n)
            def _(k):
                self.store(self.a, k).wait()


def chain_scratch(count, width):
    return [
        pltpu.VMEM((count, CHUNK, width), BF),
        pltpu.VMEM((count, CHUNK, width), BF),
        pltpu.VMEM((2, CHUNK, width), BF),
        DMA((count,)),
        DMA((count,)),
        DMA((count,)),
        DMA((count,)),
        DMA((2,)),
        DMA((count,)),
    ]


def experts_send_kernel(count, pack_ref, x_ref, d_ref, win_ref, wdown_ref,
                        out_ref, drow_ref, grad_ref, total_ref, hid_ref, dgu_ref, early_ref, *scratch):
    j, last_j = pl.program_id(0), pl.num_programs(0) - 1
    nh = lax.axis_size("heads")
    _, sources, cap, width = x_ref.shape
    here = pack_ref.shape[1] // 2
    ff = wdown_ref.shape[1]
    chain = Chain(early_ref, total_ref, scratch, 0, count)
    per = 2
    parts = sources // per

    def chain_step(t):
        @pl.when(j > 0)
        def _():
            chain.step((j - 1) * 3 + t, 1)

    @pl.when(j == 0)
    def _():
        greet(nh, ())

    win, wdown = win_ref[0], wdown_ref[0]
    for c in range(parts):
        rows = slice(c * per * cap, (c + 1) * per * cap)
        x = x_ref[0, c * per : (c + 1) * per].reshape(per * cap, width)
        d = d_ref[0, c * per : (c + 1) * per].reshape(per * cap, width)
        gu = dot(x, win)
        gate, up = gu[:, :ff], gu[:, ff:]
        sig = 1.0 / (1.0 + jnp.exp(-gate))
        act = gate * sig
        hidden = (act * up).astype(BF)
        hid_ref[rows, :] = hidden
        result = dot(hidden, wdown).astype(BF).astype(F32)
        for b in range(per):
            s = c * per + b
            hit = pick_rows(pack_ref[s, pl.ds(j, 1)].astype(jnp.int32), cap)[0]
            w = jnp.sum(jnp.where(hit, pack_ref[s, pl.ds(here + j, 1)], 0.0), axis=1, keepdims=True)
            out_ref[0, s] = (result[b * cap : (b + 1) * cap] * w).astype(BF)
        dh = dot_nt(d, wdown)
        dgu_ref[rows, :ff] = (dh * up * (sig * (1.0 + gate * (1.0 - sig)))).astype(BF)
        dgu_ref[rows, ff:] = (dh * act).astype(BF)
        drow = dot_nt(dgu_ref[rows, :], win).astype(BF)
        for b in range(per):
            drow_ref[0, c * per + b] = drow[b * cap : (b + 1) * cap]
        if c % 2:
            chain_step(c // 2)
    gin = dot_tn(x_ref[0].reshape(sources * cap, width), dgu_ref[...]).astype(BF)
    grad_ref[0, :width] = gin
    grad_ref[0, width:] = dot_tn(hid_ref[...], d_ref[0].reshape(sources * cap, width)).astype(BF)
    chain_step(2)

    @pl.when(j == 0)
    def _():
        early_ref[...] = gin[: early_ref.shape[0]]
        chain.begin()

    @pl.when(j == last_j)
    def _():
        chain.finish()


def experts_send(count, pack, x, d, win, wdown):
    here, sources, cap, width = x.shape
    ff = wdown.shape[1]
    rows = pl.BlockSpec((1, sources, cap, width), lambda j: (j, 0, 0, 0))
    shape = jax.ShapeDtypeStruct((here, sources, cap, width), BF)
    hbm = pl.BlockSpec(memory_space=pl.ANY)
    return pl.pallas_call(
        functools.partial(experts_send_kernel, count),
        grid=(here,),
        in_specs=[
            pl.BlockSpec(memory_space=pltpu.VMEM),
            rows,
            rows,
            pl.BlockSpec((1, width, 2 * ff), lambda j: (j, 0, 0)),
            pl.BlockSpec((1, ff, width), lambda j: (j, 0, 0)),
        ],
        out_specs=[rows, rows, pl.BlockSpec((1, width + ff, width), lambda j: (j, 0, 0)), hbm],
        out_shape=[
            shape,
            shape,
            jax.ShapeDtypeStruct((here, width + ff, width), BF),
            jax.ShapeDtypeStruct((here * (width + ff), width), BF),
        ],
        scratch_shapes=[
            pltpu.VMEM((sources * cap, ff), BF),
            pltpu.VMEM((sources * cap, 2 * ff), BF),
            pltpu.VMEM((count * CHUNK, width), BF),
        ]
        + chain_scratch(count, width),
        compiler_params=pltpu.CompilerParams(
            dimension_semantics=("arbitrary",), collective_id=4, has_side_effects=True, vmem_limit_bytes=VMEM
        ),
        cost_estimate=pl.CostEstimate(
            flops=18 * here * sources * cap * width * ff,
            bytes_accessed=8 * here * sources * cap * width,
            transcendentals=here * sources * cap * ff,
        ),
        name="experts_send",
    )(pack, x, d, win, wdown)


class PlaneSum:
    order = (3, 1, 2)

    def __init__(self, rows, slots, total, scratch):
        self.rows, self.slots, self.total = rows, slots, total
        self.buf, self.odd, self.c, self.e, self.f, self.ls, self.cs, self.cr, self.fs, self.fr = scratch
        self.me = lax.axis_index("experts")
        self.here, _, self.cap, self.width = rows.shape

    def load(self, r, at):
        return [
            pltpu.make_async_copy(self.rows.at[j, r], self.buf.at[at, j], self.ls.at[at, j])
            for j in range(self.here)
        ]

    def core(self, i):
        return remote(self.odd.at[i], self.c.at[i], self.cs.at[i], self.cr.at[i], "experts", self.me ^ 1)

    def chip(self, i):
        return remote(self.e.at[i - 1], self.f.at[i - 1], self.fs.at[i - 1], self.fr.at[i - 1], "experts", self.me ^ (2 * i))

    def part(self, r, at, after, after_at):
        if after is not None:
            for c in self.load(after, after_at):
                c.start()
        slots = self.slots[r].T.astype(jnp.int32)
        lane = lax.broadcasted_iota(jnp.int32, (slots.shape[0], self.here * self.cap), 1)
        hot = None
        for j in range(self.here):
            col = slots[:, j : j + 1]
            hit = lane == jnp.where(col >= 0, col + j * self.cap, -1)
            hot = hit if hot is None else hot | hit
        for c in self.load(r, at):
            c.wait()
        rows = self.buf[at].reshape(self.here * self.cap, self.width)
        return dot(hot.astype(F32).astype(BF), rows)

    def run(self, chain, step):
        turns = [2 * i + 1 for i in self.order + (0,)] + [2 * i for i in self.order + (0,)]
        for c in self.load(turns[0], 0):
            c.start()
        for t, r in enumerate(turns):
            after = turns[t + 1] if t + 1 < len(turns) else None
            value = self.part(r, t % 2, after, (t + 1) % 2)
            i = r // 2
            if r % 2:
                self.odd[i] = value.astype(BF)
                self.core(i).start()
            else:
                self.core(i).wait_recv()
                value = value + self.c[i].astype(F32)
                if i:
                    self.e[i - 1] = value.astype(BF)
                    self.chip(i).start()
                else:
                    self.total[...] = value
            if t % 2:
                chain.step(step + t // 2)
        return step + 4

    def arrive(self):
        for i in self.order:
            self.chip(i).wait_recv()

    def rows_total(self, rows):
        d = self.total[rows]
        for r in range(3):
            d = d + self.f[r, rows].astype(F32)
        return d

    def finish(self):
        for i in range(4):
            self.core(i).wait_send()
        for i in self.order:
            self.chip(i).wait_send()


def plane_scratch(here, cap, tokens, width):
    return [
        pltpu.VMEM((2, here, cap, width), BF),
        pltpu.VMEM((4, tokens, width), BF),
        pltpu.VMEM((4, tokens, width), BF),
        pltpu.VMEM((3, tokens, width), BF),
        pltpu.VMEM((3, tokens, width), BF),
        DMA((2, here)),
        DMA((4,)),
        DMA((4,)),
        DMA((3,)),
        DMA((3,)),
    ]


PLANE = 10


ROWS = 128


class Exchange:
    def __init__(self, src, dst, send, recv, nh):
        self.src, self.dst, self.ss, self.rs, self.nh = src, dst, send, recv, nh
        self.z = lax.axis_index("heads")

    def send(self, d):
        to = lax.rem(self.z + d, self.nh)
        return remote(self.src(to), self.dst(self.z), self.ss(d), self.rs(d), "heads", to)

    def start(self):
        for k in range(1, self.nh):
            self.send(jnp.where(self.z < self.nh // 2, self.nh - k, k)).start()

    def wait_recv(self):
        for d in range(1, self.nh):
            at = lax.rem(self.z + self.nh - d, self.nh)
            remote(self.src(at), self.dst(at), self.ss(d), self.rs(d), "heads", at).wait_recv()

    def finish(self):
        for d in range(1, self.nh):
            self.send(d).wait_send()


def whole_exchange(src, dst, send, recv, nh):
    return Exchange(lambda h: src.at[h], lambda h: dst.at[h], lambda d: send.at[d], lambda d: recv.at[d], nh)


class PlaneGather:
    order = (3, 1, 2)

    def __init__(self, own, slot, sems):
        self.own, self.slot = own, slot
        self.cs, self.cr, self.ks, self.kr = sems
        self.me = lax.axis_index("experts")

    def chip(self, i, e):
        return remote(self.own, self.slot(e), self.cs.at[i], self.cr.at[i], "experts", self.me ^ (2 * i))

    def core(self, i, src, e):
        return remote(src, self.slot(e), self.ks.at[i], self.kr.at[i], "experts", self.me ^ 1)

    def start(self):
        self.core(0, self.own, self.me).start()
        for i in self.order:
            self.chip(i, self.me).start()

    def forward(self, i):
        e = self.me ^ (2 * i)
        self.chip(i, e).wait_recv()
        self.core(i, self.slot(e), e).start()

    def core_arrive(self, i):
        e = self.me ^ 1 ^ (2 * i)
        self.core(i, self.slot(e), e).wait_recv()

    def finish(self):
        for i in range(1, 4):
            self.chip(i, self.me).wait_send()
        for i in range(4):
            self.core(i, self.own if i == 0 else self.slot(self.me ^ (2 * i)), self.me).wait_send()


GATHER = 4


def gather_sems():
    return [DMA((4,)), DMA((4,)), DMA((4,)), DMA((4,))]


class Picker:
    def __init__(self, pack, stage, sems, here, cap):
        self.pack, self.stage, self.sems, self.here, self.cap = pack, stage, sems, here, cap
        self.turn, self.pending = 0, {}

    def pick(self, r, tokens, out, weighted):
        at = self.turn % 2
        self.turn += 1
        info = self.pack[r]
        slots = info.astype(jnp.int32)
        index = lax.broadcasted_iota(jnp.int32, (self.cap, slots.shape[1]), 0)
        hits = [index == slots[j : j + 1] for j in range(self.here)]
        rows = dot(jnp.concatenate([h.astype(F32) for h in hits], axis=0).astype(BF), tokens)
        for c in self.pending.get(at, []):
            c.wait()
        for j, hit in enumerate(hits):
            part = rows[j * self.cap : (j + 1) * self.cap]
            if weighted:
                w = info[self.here + j : self.here + j + 1]
                part = part * jnp.sum(jnp.where(hit, w, 0.0), axis=1, keepdims=True)
            self.stage[at, j] = part.astype(BF)
        self.pending[at] = [
            pltpu.make_async_copy(self.stage.at[at, j], out.at[j, r], self.sems.at[at, j])
            for j in range(self.here)
        ]
        for c in self.pending[at]:
            c.start()

    def finish(self):
        for copies in self.pending.values():
            for c in copies:
                c.wait()


def front_kernel(len_ref, x_ref, og_ref, wq_ref, wk_ref, wv_ref, om_ref, pk_ref, again_ref, mgain_ref, cq, sq, ckv, skv,
                 xg_ref, qkv_ref, lse_ref, hin_ref, of_ref, wz_ref, mid_ref, pack_ref, drows_ref, xrows_ref,
                 w_ref, hs, ogb, mt, stage, ls, lr, ps, pr, hss, hrs, os_, or_, ws, wr, ss, *sems):
    nh, tokens, width = xg_ref.shape
    nseq, groups, full, _ = qkv_ref.shape
    ne = ogb.shape[0]
    seg = tokens // nseq
    here, _, cap, _ = drows_ref.shape
    z, me = lax.axis_index("heads"), lax.axis_index("experts")
    og = PlaneGather(og_ref, lambda e: ogb.at[e], sems[:GATHER])
    og_o = PlaneGather(of_ref.at[:, me], lambda e: of_ref.at[:, e], sems[GATHER : 2 * GATHER])

    def moe(p):
        at = pl.ds(p * seg, seg)
        return PlaneGather(mt.at[me, at], lambda e: mt.at[e, at], sems[(2 + p) * GATHER : (3 + p) * GATHER])

    moes = [moe(p) for p in range(nseq)]

    def heads(p):
        at = pl.ds(p * seg, seg)
        return Exchange(
            lambda h: hs.at[h, at], lambda h: hin_ref.at[h, at], lambda d: hss.at[p, d], lambda d: hrs.at[p, d], nh)

    picker = Picker(pack_ref, stage, ss, here, cap)

    @pl.loop(0, tokens // ROWS)
    def _(i):
        rows = pl.ds(i * ROWS, ROWS)
        x = x_ref[rows].astype(F32)
        inv = lax.rsqrt(jnp.mean(x * x, axis=-1, keepdims=True) + EPS)
        xg_ref[z, rows] = (x * inv * again_ref[...]).astype(BF)

    greet(nh, tuple(range(1, ne)))
    for g in range(groups):
        head = slice(g * HEAD, (g + 1) * HEAD)
        w_ref[:, g * 256 : g * 256 + 128] = wq_ref[:, g * 128 : (g + 1) * 128]
        w_ref[:, g * 256 + 128 : (g + 1) * 256] = jnp.concatenate([wk_ref[:, head], wv_ref[:, head]], axis=1)

    def hop(way, t, p, s, to):
        ref = xg_ref.at[s, pl.ds(p * seg, seg)]
        return remote(ref, ref, ls.at[way, t, p], lr.at[s, p], "heads", to)

    right, left = jnp.minimum(z + 1, nh - 1), jnp.maximum(z - 1, 0)
    for p in range(nseq):
        @pl.when(z < nh - 1)
        def _():
            hop(0, 0, p, z, right).start()

        @pl.when(z > 0)
        def _():
            hop(1, 0, p, z, left).start()

    def info(r):
        return remote(pk_ref.at[me ^ r], pack_ref.at[r], ps.at[r], pr.at[r], "experts", me ^ r)

    rows_o, rows_w = of_ref.shape[2], wz_ref.shape[1]
    of_ref[z, me] = om_ref[pl.ds(pl.multiple_of(me * rows_o, rows_o), rows_o)]
    wz_ref[z] = w_ref[pl.ds(pl.multiple_of(me * rows_w, rows_w), rows_w)]
    ofx = Exchange(lambda h: of_ref.at[z, me], lambda h: of_ref.at[h, me], lambda d: os_.at[d], lambda d: or_.at[d], nh)
    wzx = Exchange(lambda h: wz_ref.at[z], lambda h: wz_ref.at[h], lambda d: ws.at[d], lambda d: wr.at[d], nh)
    ofx.start()
    for r in range(1, ne):
        info(r).start()
    og.start()
    pack_ref[0] = pk_ref[me]

    def project(s, p):
        x = xg_ref[s, pl.ds(p * seg, seg)]
        at = pl.ds(s * seg, seg)
        for g in range(groups):
            lin = dot(x, w_ref[:, g * 256 : (g + 1) * 256])
            q, kv = lin[:, :128], lin[:, 128:]
            qkv_ref[p, g, at, :128] = (q * cq[at] + swap_halves(q) * sq[at]).astype(BF)
            qkv_ref[p, g, at, 128:] = (kv * ckv[at] + swap_halves(kv) * skv[at]).astype(BF)

    @pl.loop(0, nseq)
    def _(p):
        project(z, p)

    def round_of(t, then=None):
        @pl.loop(0, nseq)
        def _(p):
            @pl.when(z >= t)
            def _():
                s = z - t
                hop(0, t, p, s, left).wait_recv()

                @pl.when(z < nh - 1)
                def _():
                    hop(0, t, p, s, right).start()

                project(s, p)

            @pl.when(z + t < nh)
            def _():
                s = z + t
                hop(1, t, p, s, right).wait_recv()

                @pl.when(z > 0)
                def _():
                    hop(1, t, p, s, left).start()

                project(s, p)

            if then is not None:
                then(p)

    picker.pick(0, og_ref[...], drows_ref, True)
    round_of(1)
    for r in range(1, ne):
        info(r).wait_recv()
    og.core_arrive(0)
    picker.pick(1, ogb[me ^ 1], drows_ref, True)
    round_of(2)
    for i in og.order:
        og.forward(i)
    for i in og.order:
        picker.pick(2 * i, ogb[me ^ (2 * i)], drows_ref, True)
    ofx.wait_recv()
    og_o.start()

    def attend(p):
        length = len_ref[p]
        at = pl.ds(p * seg, seg)
        for g in range(groups):
            q = qkv_ref[p, g, :, :128]
            kv = qkv_ref[p, g, :, 128:]
            k = kv[:, :HEAD]
            vt = kv.astype(F32).T[HEAD:].astype(BF)
            for i in range(nh):
                n = (i + 1) * seg
                q2 = two_heads(q[i * seg : n])
                s = dot_nt(k[:n], q2)
                mask = attn_mask(i * seg, n, seg, length)
                s = jnp.where(jnp.concatenate([mask, mask], axis=1), s * SCALE, NEG)
                m = jnp.max(s, axis=0, keepdims=True)
                e = jnp.exp(s - m)
                total = jnp.sum(e, axis=0, keepdims=True)
                prob = (e * (1.0 / total)).astype(BF)
                lse_ref[p, g, i : i + 1, :] = m + jnp.log(total)
                hs[i, at, g * 128 : (g + 1) * 128] = untwo(dot(vt[:, :n], prob), seg).astype(BF)
        hin_ref[z, at] = hs[z, at]

        @pl.when(at_end)
        def _():
            heads(p).start()

    at_end = (z == 0) | (z == nh - 1)
    round_of(3, attend)
    for p in range(nseq):
        for t in range(nh):
            @pl.when((z >= t) & (z < nh - 1))
            def _():
                hop(0, t, p, z - t, right).wait_send()

            @pl.when((z + t < nh) & (z > 0))
            def _():
                hop(1, t, p, z + t, left).wait_send()

    @pl.when(jnp.logical_not(at_end))
    def _():
        for p in range(nseq):
            heads(p).start()

    for i in og.order:
        og_o.forward(i)
    for i in og.order:
        og.core_arrive(i)
        picker.pick(2 * i + 1, ogb[me ^ 1 ^ (2 * i)], drows_ref, True)
    for i in range(4):
        og_o.core_arrive(i)

    for p in range(nseq):
        at = pl.ds(p * seg, seg)
        heads(p).wait_recv()
        mid_ref[at] = x_ref[at].astype(F32) + dot(hin_ref[0, at], of_ref[0].reshape(-1, width))
        for h in range(1, nh):
            mid_ref[at] += dot(hin_ref[h, at], of_ref[h].reshape(-1, width))

        @pl.loop(0, seg // ROWS)
        def _(i):
            rows = pl.ds(p * seg + i * ROWS, ROWS)
            m = mid_ref[rows]
            inv = lax.rsqrt(jnp.mean(m * m, axis=-1, keepdims=True) + EPS)
            mt[me, rows] = (m * inv * mgain_ref[...]).astype(BF)

        moes[p].start()

    wzx.start()
    picker.pick(0, mt[me], xrows_ref, False)
    for p in range(nseq):
        moes[p].core_arrive(0)
    picker.pick(1, mt[me ^ 1], xrows_ref, False)
    for i in og.order:
        for p in range(nseq - 1):
            moes[p].forward(i)
    for t, i in enumerate(og.order):
        moes[-1].forward(i)
        picker.pick(2 * i, mt[me ^ (2 * i)], xrows_ref, False)
        if t:
            last = og.order[t - 1]
            for p in range(nseq):
                moes[p].core_arrive(last)
            picker.pick(2 * last + 1, mt[me ^ 1 ^ (2 * last)], xrows_ref, False)
    last = og.order[-1]
    for p in range(nseq):
        moes[p].core_arrive(last)
    picker.pick(2 * last + 1, mt[me ^ 1 ^ (2 * last)], xrows_ref, False)
    picker.finish()
    wzx.wait_recv()
    for gather in [og, og_o] + moes:
        gather.finish()
    for exchange in [ofx, wzx] + [heads(p) for p in range(nseq)]:
        exchange.finish()
    for r in range(1, ne):
        info(r).wait_send()


def front(lengths, x, og, wq, wk, wv, o_local, packed, attn_gain, moe_gain, tables, nh, nseq, cap):
    ne, info, _ = packed.shape
    tokens, width = x.shape
    here = info // 2
    cols = 2 * wq.shape[1]
    groups, seg = cols // 256, tokens // nseq
    full = nh * seg
    part = o_local.shape[0]
    vmem = pl.BlockSpec(memory_space=pltpu.VMEM)
    hbm = pl.BlockSpec(memory_space=pl.ANY)
    rows = jax.ShapeDtypeStruct((here, ne, cap, width), BF)
    return pl.pallas_call(
        front_kernel,
        in_specs=[pl.BlockSpec(memory_space=pltpu.SMEM)] + [vmem] * 13,
        out_specs=[vmem] * 8 + [hbm, hbm],
        out_shape=[
            jax.ShapeDtypeStruct((nh, tokens, width), BF),
            jax.ShapeDtypeStruct((nseq, groups, full, 256), BF),
            jax.ShapeDtypeStruct((nseq, groups, nh, 2 * seg), F32),
            jax.ShapeDtypeStruct((nh, tokens, part), BF),
            jax.ShapeDtypeStruct((nh, ne, part // ne, width), BF),
            jax.ShapeDtypeStruct((nh, width // ne, cols), BF),
            jax.ShapeDtypeStruct((tokens, width), F32),
            jax.ShapeDtypeStruct(packed.shape, F32),
            rows,
            rows,
        ],
        scratch_shapes=[
            pltpu.VMEM((width, cols), BF),
            pltpu.VMEM((nh, tokens, part), BF),
            pltpu.VMEM((ne, tokens, width), BF),
            pltpu.VMEM((ne, tokens, width), BF),
            pltpu.VMEM((2, here, cap, width), BF),
            DMA((2, nh, nseq)),
            DMA((nh, nseq)),
            DMA((ne,)),
            DMA((ne,)),
            DMA((nseq, nh)),
            DMA((nseq, nh)),
            DMA((nh,)),
            DMA((nh,)),
            DMA((nh,)),
            DMA((nh,)),
            DMA((2, here)),
        ]
        + gather_sems() * (2 + nseq),
        compiler_params=pltpu.CompilerParams(
            collective_id=3, has_side_effects=True, vmem_limit_bytes=VMEM
        ),
        cost_estimate=pl.CostEstimate(flops=10**11, bytes_accessed=60 * 2**20, transcendentals=10**7),
        name="front",
    )(lengths, x, og, wq, wk, wv, o_local, packed, attn_gain, moe_gain, *tables)


def middle_kernel(first, count, len_ref, begun_ref, sum_ref, rows_ref, slot_ref, mid_ref, grad_ref, gain_ref, o_ref, qkv_ref, lse_ref,
                  cq, sq, ckv, skv, hin_ref, x_ref, total_ref, dmid_ref, gtwo_ref, dqkv_ref, po_ref, pw_ref,
                  dbranch_ref, wsum, hs, hr, dmoe, dkv, hss, hrs, xs, *scratch):
    nh, tokens, _ = dqkv_ref.shape
    nseq, groups = qkv_ref.shape[:2]
    seg = tokens // nseq
    z = lax.axis_index("heads")
    chain = Chain(sum_ref, total_ref, scratch[PLANE:], first, count)
    plane = PlaneSum(rows_ref, slot_ref, dmoe, scratch[:PLANE])
    heads = whole_exchange(hs, hr, hss, hrs, nh)
    greet(nh, (1, 2, 4, 6))
    chain.begin()
    chain.run(0, 2)
    step = plane.run(chain, 2)
    chain.run(step, step + 4)
    step = step + 4
    plane.arrive()
    gtwo_ref[...] = jnp.zeros_like(gtwo_ref)

    @pl.loop(0, tokens // ROWS)
    def _(i):
        rows = pl.ds(i * ROWS, ROWS)
        d = plane.rows_total(rows)
        m = mid_ref[rows]
        inv = lax.rsqrt(jnp.mean(m * m, axis=-1, keepdims=True) + EPS)
        zed = gain_ref[...] * d
        dm = grad_ref[rows].astype(F32) + inv * zed - m * (inv * inv * inv * jnp.mean(zed * m, axis=-1, keepdims=True))
        gtwo_ref[...] += jnp.sum(d * m * inv, axis=0, keepdims=True)
        dmid_ref[rows] = dm
        db = dm.astype(BF)
        dbranch_ref[rows] = db
        for h in range(nh):
            hs[h, rows] = dot_nt(db, o_ref[h]).astype(BF)

    heads.start()
    hr[z] = hs[z]
    chain.run(step, step + 4)
    step = step + 4
    heads.wait_recv()

    @pl.loop(0, nseq)
    def _(s):
        length = len_ref[s]
        at = pl.ds(s * seg, seg)
        for g in range(groups):
            def put(i, lo, v):
                dqkv_ref[i, at, g * 256 + lo : g * 256 + lo + 128] = v

            bwd_piece(
                qkv_ref[s, g, :, :128],
                qkv_ref[s, g, :, 128:],
                lambda i: hr[i, at, g * 128 : (g + 1) * 128],
                lambda i: lse_ref[s, g, i : i + 1, :],
                length,
                (cq, sq, ckv, skv),
                dkv,
                put,
            )
            chain.step(step + groups * s + g)

    step = step + groups * nseq
    for i in range(4):
        plane.core(i).wait_send()
    load = pltpu.make_async_copy(x_ref, plane.odd, xs)
    load.start()
    ne, deep, _ = po_ref.shape
    strip, row = deep // nh, pw_ref.shape[1]
    db = dbranch_ref[...]
    for h in range(nh):
        o = dot_tn(hin_ref[h], db).astype(BF)
        for e in range(ne):
            po_ref[e, h * strip : (h + 1) * strip] = o[e * strip : (e + 1) * strip]
    chain.step(step)
    load.wait()
    wsum[...] = dot_tn(plane.odd[0], dqkv_ref[0])
    for h in range(1, nh):
        wsum[...] += dot_tn(plane.odd[h], dqkv_ref[h])
    for e in range(ne):
        pw_ref[e] = wsum[e * row : (e + 1) * row].astype(BF)
    chain.rest(step + 1)
    chain.finish()
    for i in plane.order:
        plane.chip(i).wait_send()
    heads.finish()


def middle(first, count, lengths, total, sums, rows, slots, mid, grad, gain, o_parts, qkv, lse, tables, heads_in, x):
    nseq, groups, full, _ = qkv.shape
    nh = o_parts.shape[0]
    tokens, width = mid.shape
    here, ne, cap, _ = rows.shape
    vmem = pl.BlockSpec(memory_space=pltpu.VMEM)
    hbm = pl.BlockSpec(memory_space=pl.ANY)
    heads = (nh, tokens, groups * 128)
    cols = groups * 256
    return pl.pallas_call(
        functools.partial(middle_kernel, first, count),
        in_specs=[pl.BlockSpec(memory_space=pltpu.SMEM), hbm, hbm, hbm] + [vmem] * 12 + [hbm],
        input_output_aliases={1: 0},
        out_specs=[hbm] + [vmem] * 5,
        out_shape=[
            jax.ShapeDtypeStruct(sums.shape, BF),
            jax.ShapeDtypeStruct((tokens, width), F32),
            jax.ShapeDtypeStruct((1, width), F32),
            jax.ShapeDtypeStruct((nh, tokens, cols), BF),
            jax.ShapeDtypeStruct((ne, nh * groups * 128 // ne, width), BF),
            jax.ShapeDtypeStruct((ne, width // ne, cols), BF),
        ],
        scratch_shapes=[
            pltpu.VMEM((tokens, width), BF),
            pltpu.VMEM((width, cols), F32),
            pltpu.VMEM(heads, BF),
            pltpu.VMEM(heads, BF),
            pltpu.VMEM((tokens, width), F32),
            pltpu.VMEM((full, 128), F32),
            DMA((nh,)),
            DMA((nh,)),
            DMA,
        ]
        + plane_scratch(here, cap, tokens, width)
        + chain_scratch(count, width),
        compiler_params=pltpu.CompilerParams(
            collective_id=1, has_side_effects=True, vmem_limit_bytes=VMEM
        ),
        cost_estimate=pl.CostEstimate(flops=10**11, bytes_accessed=30 * 2**20, transcendentals=10**7),
        name="middle",
    )(lengths, total, sums, rows, slots, mid, grad, gain, o_parts, qkv, lse, *tables, heads_in, x)


class PairSum:
    order = (3, 1, 2)

    def __init__(self, parts, scratch):
        self.parts = parts
        self.c, self.e, self.f, self.cs, self.cr, self.fs, self.fr = scratch
        self.me = lax.axis_index("experts")

    def core(self, i):
        src = self.parts.at[self.me ^ 1 ^ (2 * i)]
        return remote(src, self.c.at[i], self.cs.at[i], self.cr.at[i], "experts", self.me ^ 1)

    def chip(self, i):
        return remote(self.e.at[i - 1], self.f.at[i - 1], self.fs.at[i - 1], self.fr.at[i - 1], "experts", self.me ^ (2 * i))

    def start(self):
        for i in self.order + (0,):
            self.core(i).start()

    def both(self, i):
        return self.parts[self.me ^ (2 * i)].astype(F32) + self.c[i].astype(F32)

    def forward(self):
        for i in self.order:
            self.core(i).wait_recv()
            self.e[i - 1] = self.both(i).astype(BF)
            self.chip(i).start()
        self.core(0).wait_recv()

    def result(self):
        value = self.both(0)
        for i in self.order:
            self.chip(i).wait_recv()
        for r in range(3):
            value = value + self.f[r].astype(F32)
        return value

    def finish(self):
        for i in range(4):
            self.core(i).wait_send()
        for i in self.order:
            self.chip(i).wait_send()


PAIR = 7


def pair_scratch(shape):
    return [pltpu.VMEM((n,) + shape, BF) for n in (4, 3, 3)] + [DMA((4,)), DMA((4,)), DMA((3,)), DMA((3,))]


def last_kernel(first, count, begun_ref, sum_ref, rows_ref, slot_ref, mid_ref, dqkv_ref, wz_ref, x_ref, dmid_ref,
                gain_ref, gtwo_ref, po_ref, pw_ref, total_ref, out_ref, xgrad_ref, gains_ref, ograd_ref, qgrad_ref, kgrad_ref, vgrad_ref,
                wf, br, moe, gp, gz, acc, oz, fo, fq, fk, fv, brs, brr, gps, gpr, gzs, gzr, oss, ors, fl, dl, *scratch):
    nh, tokens, _ = dqkv_ref.shape
    dattn = moe
    ne = rows_ref.shape[1]
    z, me = lax.axis_index("heads"), lax.axis_index("experts")
    at = PLANE
    plane = PlaneSum(rows_ref, slot_ref, moe, scratch[:at])
    weights = PlaneGather(wz_ref, lambda e: wf.at[:, e], scratch[at : at + GATHER])
    at += GATHER
    strip, row = fo.shape[0], fq.shape[0]

    def o_rows(e):
        return ograd_ref.at[pl.ds(pl.multiple_of(e * strip, strip), strip)]

    def w_rows(ref, e):
        return ref.at[pl.ds(pl.multiple_of(e * row, row), row)]

    spread_o = PlaneGather(fo, o_rows, scratch[at : at + GATHER])
    at += GATHER
    spreads = [spread_o]
    for mine, whole in ((fq, qgrad_ref), (fk, kgrad_ref), (fv, vgrad_ref)):
        spreads.append(PlaneGather(mine, functools.partial(w_rows, whole), scratch[at : at + GATHER]))
        at += GATHER
    sum_o = PairSum(po_ref, scratch[at : at + PAIR])
    at += PAIR
    sum_w = PairSum(pw_ref, scratch[at : at + PAIR])
    at += PAIR
    chain = Chain(sum_ref, total_ref, scratch[at:], first, count)
    back = whole_exchange(dqkv_ref, br, brs, brr, nh)
    pieces = Exchange(
        lambda h: acc.at[pl.ds(pl.multiple_of(h * strip, strip), strip)],
        lambda h: oz.at[h], lambda d: oss.at[d], lambda d: ors.at[d], nh)
    first_part = pltpu.make_async_copy(dmid_ref, xgrad_ref, dl)
    first_part.start()
    greet(nh, tuple(range(1, ne)))
    back.start()
    sum_o.start()
    sum_w.start()
    chain.begin()
    br[z] = dqkv_ref[z]
    chain.run(0, 2)
    sum_o.forward()
    sum_w.forward()
    weights.start()
    wf[:, me] = wz_ref[...]
    step = plane.run(chain, 2)
    chain.run(step, step + 2)
    step = step + 2
    acc[...] = sum_o.result()
    pieces.start()
    oz[z] = acc[pl.ds(pl.multiple_of(z * strip, strip), strip)]
    w = sum_w.result()
    for g in range(fq.shape[1] // 128):
        head = slice(g * HEAD, (g + 1) * HEAD)
        fq[:, g * 128 : (g + 1) * 128] = w[:, g * 256 : g * 256 + 128]
        fk[:, head] = w[:, g * 256 + 128 : g * 256 + 192]
        fv[:, head] = w[:, g * 256 + 192 : (g + 1) * 256]
    for spread in spreads[1:]:
        spread.start()
    chain.run(step, step + 2)
    step = step + 2
    pieces.wait_recv()
    fo[...] = oz[0] + oz[1] + oz[2] + oz[3]
    spread_o.start()
    keep = [pltpu.make_async_copy(g.own, g.slot(me), fl.at[t]) for t, g in enumerate(spreads)]
    for c in keep:
        c.start()
    for i in weights.order:
        weights.forward(i)
    chain.run(step, step + 2)
    step = step + 2
    plane.arrive()

    @pl.loop(0, tokens // ROWS)
    def _(i):
        rows = pl.ds(i * ROWS, ROWS)
        out_ref[rows] = (mid_ref[rows] + plane.rows_total(rows)).astype(BF)

    chain.run(step, step + 2)
    step = step + 2
    for i in range(4):
        weights.core_arrive(i)
    back.wait_recv()
    for h in range(nh):
        term = dot_nt(br[h], wf[h].reshape(-1, wf.shape[3]))
        if h:
            dattn[...] += term
        else:
            dattn[...] = term
    chain.run(step, step + 2)
    step = step + 2
    pad = jnp.zeros((6, gtwo_ref.shape[1]), F32)
    own = jnp.zeros_like(gtwo_ref[...])

    def rows_back(i, total):
        rows = pl.ds(i * ROWS, ROWS)
        d = dattn[rows]
        x = x_ref[rows].astype(F32)
        inv = lax.rsqrt(jnp.mean(x * x, axis=-1, keepdims=True) + EPS)
        wed = gain_ref[...] * d
        xgrad_ref[rows] += inv * wed - x * (inv * inv * inv * jnp.mean(wed * x, axis=-1, keepdims=True))
        return total + jnp.sum(d * x * inv, axis=0, keepdims=True)

    first_part.wait()
    own = lax.fori_loop(0, tokens // ROWS, rows_back, own)
    gp[me] = jnp.concatenate([own, gtwo_ref[...], pad], axis=0)

    def near(r, at):
        return remote(gp.at[me], gp.at[at], gps.at[r], gpr.at[r], "experts", me ^ r)

    for r in range(1, ne):
        near(r, me).start()
    chain.run(step, step + 2)
    step = step + 2
    for spread in spreads[1:] + spreads[:1]:
        for i in spread.order:
            spread.forward(i)
    for r in range(1, ne):
        near(r, me ^ r).wait_recv()
    total = gp[0]
    for e in range(1, ne):
        total = total + gp[e]
    gz[z] = total
    gains = Exchange(lambda h: gz.at[z], lambda h: gz.at[h], lambda d: gzs.at[d], lambda d: gzr.at[d], nh)
    gains.start()
    chain.rest(step)
    gains.wait_recv()
    total = gz[0]
    for h in range(1, nh):
        total = total + gz[h]
    gains_ref[...] = total
    for spread in spreads:
        for i in range(4):
            spread.core_arrive(i)
    chain.finish()
    for part in [plane, back, pieces, gains, weights, sum_o, sum_w] + spreads:
        part.finish()
    for c in keep:
        c.wait()
    for r in range(1, ne):
        near(r, me).wait_send()


def last(first, count, total, sums, rows, slots, mid, dqkv, w_pieces, x, d_mid, gain, gain_two, po, pw):
    nh, tokens, cols = dqkv.shape
    here, ne, cap, width = rows.shape
    strip = po.shape[1] // nh
    row = pw.shape[1]
    hbm = pl.BlockSpec(memory_space=pl.ANY)
    vmem = pl.BlockSpec(memory_space=pltpu.VMEM)
    return pl.pallas_call(
        functools.partial(last_kernel, first, count),
        in_specs=[hbm, hbm, hbm] + [vmem] * 5 + [hbm] + [vmem] * 4,
        input_output_aliases={0: 0},
        out_specs=[hbm] + [vmem] * 3 + [hbm] * 4,
        out_shape=[
            jax.ShapeDtypeStruct(sums.shape, BF),
            jax.ShapeDtypeStruct((tokens, width), BF),
            jax.ShapeDtypeStruct((tokens, width), F32),
            jax.ShapeDtypeStruct((8, width), F32),
            jax.ShapeDtypeStruct((strip * ne, width), F32),
            jax.ShapeDtypeStruct((row * ne, cols // 2), F32),
            jax.ShapeDtypeStruct((row * ne, cols // 4), F32),
            jax.ShapeDtypeStruct((row * ne, cols // 4), F32),
        ],
        scratch_shapes=[
            pltpu.VMEM((nh, ne, width // ne, cols), BF),
            pltpu.VMEM((nh, tokens, cols), BF),
            pltpu.VMEM((tokens, width), F32),
            pltpu.VMEM((ne, 8, width), F32),
            pltpu.VMEM((nh, 8, width), F32),
            pltpu.VMEM((nh * strip, width), F32),
            pltpu.VMEM((nh, strip, width), F32),
            pltpu.VMEM((strip, width), F32),
            pltpu.VMEM((row, cols // 2), F32),
            pltpu.VMEM((row, cols // 4), F32),
            pltpu.VMEM((row, cols // 4), F32),
            DMA((nh,)),
            DMA((nh,)),
            DMA((ne,)),
            DMA((ne,)),
            DMA((nh,)),
            DMA((nh,)),
            DMA((nh,)),
            DMA((nh,)),
            DMA((4,)),
            DMA,
        ]
        + plane_scratch(here, cap, tokens, width)
        + gather_sems() * 5
        + pair_scratch(po.shape[1:])
        + pair_scratch(pw.shape[1:])
        + chain_scratch(count, width),
        compiler_params=pltpu.CompilerParams(
            collective_id=2, has_side_effects=True, vmem_limit_bytes=VMEM
        ),
        cost_estimate=pl.CostEstimate(flops=2 * 10**11, bytes_accessed=30 * 2**20, transcendentals=0),
        name="last",
    )(total, sums, rows, slots, mid, dqkv, w_pieces, x, d_mid, gain, gain_two, po, pw)


def widen_kernel(x_ref, in_ref, down_ref):
    c = pl.program_id(1)

    @pl.when(c < 2)
    def _():
        in_ref[...] = x_ref[...].astype(F32)

    @pl.when(c == 2)
    def _():
        down_ref[...] = x_ref[...].astype(F32)


def widen(sums, ff):
    here, rows, width = sums.shape
    return pl.pallas_call(
        widen_kernel,
        grid=(here, 3),
        in_specs=[pl.BlockSpec((1, ff, width), lambda j, c: (j, c, 0))],
        out_specs=[
            pl.BlockSpec((1, ff, width), lambda j, c: (j, jnp.minimum(c, 1), 0)),
            pl.BlockSpec((1, ff, width), lambda j, c: (j, 0, 0)),
        ],
        out_shape=[
            jax.ShapeDtypeStruct((here, 2 * ff, width), F32),
            jax.ShapeDtypeStruct((here, ff, width), F32),
        ],
        compiler_params=params(2),
        name="widen",
    )(sums)


def body(layer_input, seq_lengths, expert_ids, route_weight, priority, attn_gain, moe_gain,
         query_matrix, key_matrix, value_matrix, output_matrix, expert_in, expert_down, out_grad):
    seg, nseq, width = layer_input.shape
    nh, ne = lax.axis_size("heads"), lax.axis_size("experts")
    z, me = lax.axis_index("heads"), lax.axis_index("experts")
    top = expert_ids.shape[-1]
    tokens = seg * nseq
    groups = key_matrix.shape[1] // HEAD
    here = expert_in.shape[0]
    cap = (5 * tokens * top + 4 * EXPERTS - 1) // (4 * EXPERTS)

    def local(v):
        return jnp.swapaxes(v, 0, 1).reshape((tokens,) + v.shape[2:])

    def unlocal(v):
        return jnp.swapaxes(v.reshape((nseq, seg) + v.shape[1:]), 0, 1)

    ids = local(expert_ids)
    order = local(priority)
    weight = local(route_weight)
    position = z * seg + jnp.arange(seg, dtype=jnp.int32)
    live = (position[None, :] < seq_lengths[:, None]).reshape(tokens)
    match = ids.T[:, None, :] == jnp.arange(EXPERTS, dtype=jnp.int32)[None, :, None]
    weight_e = jnp.sum(jnp.where(match, weight.T[:, None, :], 0.0), axis=0)
    chosen = jnp.any(match, axis=0) & live[None, :]
    earlier = (order[:, None] < order[None, :]).astype(BF)
    before = dot(chosen.astype(BF), earlier)
    slot = jnp.where(chosen & (before < cap), before, -1.0)
    packed = jnp.concatenate([slot.reshape(ne, here, tokens), weight_e.reshape(ne, here, tokens)], axis=1)
    tables = rotary_tables(nh * seg)
    x, grad = local(layer_input), local(out_grad)
    xf = x.astype(F32)
    gain_a, gain_m = attn_gain.reshape(1, width), moe_gain.reshape(1, width)
    fast = nh == 4 and ne == 8
    if fast:
        gathered, qkv, lse, heads_in, o_full, w_pieces, mid, pack, d_rows, x_rows = front(
            seq_lengths, x, grad, query_matrix, key_matrix, value_matrix, output_matrix, packed, gain_a, gain_m, tables, nh, nseq, cap)
        o_parts = o_full.reshape(nh, groups * 128, width)
    else:
        wq = query_matrix.reshape(width, groups, 128)
        wk = key_matrix.reshape(width, groups, HEAD)
        wv = value_matrix.reshape(width, groups, HEAD)
        w_local = jnp.concatenate([wq, wk, wv], axis=2).reshape(width, groups * 256)
        packed = lax.all_to_all(packed, "experts", split_axis=0, concat_axis=0, tiled=True)
        packed = packed[me ^ jnp.arange(ne, dtype=jnp.int32)]
        slots, weights = packed[:, :here].astype(jnp.int32), packed[:, here:]
        inv_one = lax.rsqrt(jnp.mean(xf * xf, axis=-1, keepdims=True) + EPS)
        attn_in = (xf * inv_one * attn_gain).astype(BF)
        gathered = lax.all_gather(attn_in.reshape(nseq, seg, width), "heads", axis=0)
        w_groups = jnp.transpose(w_local.reshape(width, groups, 256), (1, 0, 2))
        rows_in, rows_out = width // ne, output_matrix.shape[0] // ne
        w_piece = lax.dynamic_slice_in_dim(w_local, me * rows_in, rows_in, 0)
        o_piece = lax.dynamic_slice_in_dim(output_matrix, me * rows_out, rows_out, 0)
        o_full = lax.all_gather(o_piece, ("heads", "experts"), axis=0, tiled=True)
        w_full = lax.all_gather(w_piece, ("heads", "experts"), axis=0, tiled=True)
        w_full = w_full.reshape(nh, width, groups * 256)
        qkv, heads_out, lse = attn_forward(gathered, w_groups, seq_lengths, tables)
        heads_in = lax.all_to_all(heads_out, "heads", split_axis=0, concat_axis=0, tiled=True)
        heads_in = heads_in.reshape(nh, tokens, groups * 128)
        o_parts = o_full.reshape(nh, groups * 128, width)
        branch = jnp.einsum("ztm,zmw->tw", heads_in, o_parts, preferred_element_type=F32)
        mid = xf + branch
        inv_two = lax.rsqrt(jnp.mean(mid * mid, axis=-1, keepdims=True) + EPS)
        moe_in = (mid * inv_two * moe_gain).astype(BF)
        d_rows = gather_rows(slots, weights, plane_gather(grad, ne), cap)
        x_rows = gather_rows(slots, None, plane_gather(moe_in, ne), cap)

    if fast:
        chunks = expert_in.shape[0] * (width + expert_down.shape[1]) // CHUNK
        early, half = chunks // 12, (5 * chunks) // 12
        results, drows, sums, total = experts_send(early, pack, x_rows, d_rows, expert_in, expert_down)
        flat = sums.reshape(-1, width)
        total, d_mid, gain_two, dqkv, po, pw = middle(
            early, half, seq_lengths, total, flat, drows, pack, mid, grad, gain_m, o_parts, qkv, lse, tables,
            heads_in, gathered)
        total, out, x_grad, gains, o_grad, q_grad, k_grad, v_grad = last(
            early + half, chunks - early - half, total, flat, results, pack, mid, dqkv, w_pieces, x, d_mid, gain_a, gain_two, po, pw)
        gain_one, gain_two = gains[0], gains[1]
        grad_in, grad_down = widen(total.reshape(sums.shape), expert_down.shape[1])
    else:
        results, drows, sums = experts_call(slots, weights, x_rows, d_rows, expert_in, expert_down)
        slots_t = jnp.swapaxes(slots, 1, 2)
        d_parts = combine(slots_t, drows)
        moe_parts = combine(slots_t, results)
        totals = heads_sum(sums, z, nh)
        grad_in, grad_down = totals[:, :width], totals[:, width:]
        d_moe = plane_scatter(d_parts, ne)
        moe_sum = plane_scatter(moe_parts, ne)
        out = (mid + moe_sum).astype(BF)
        zed = moe_gain * d_moe
        d_mid = grad.astype(F32) + inv_two * zed - mid * (inv_two ** 3 * jnp.mean(zed * mid, axis=-1, keepdims=True))
        gain_two = jnp.sum(d_moe * mid * inv_two, axis=0)
        d_branch = d_mid.astype(BF)
        d_heads = jnp.einsum("tw,zmw->ztm", d_branch, o_parts, preferred_element_type=F32).astype(BF)
        d_heads = d_heads.reshape(nh, nseq, seg, groups * 128)
        d_heads = lax.all_to_all(d_heads, "heads", split_axis=0, concat_axis=0, tiled=True)
        dqkv = attn_backward(qkv, d_heads, lse, seq_lengths, tables)
        dqkv = dqkv.reshape(nh, tokens, groups * 256)
        back = lax.all_to_all(dqkv, "heads", split_axis=0, concat_axis=0, tiled=True)
        d_attn = jnp.einsum("ztc,zmc->tm", back, w_full, preferred_element_type=F32)
        o_grad, w_grad = weight_sums(heads_in, d_branch, gathered, dqkv, ne)
        wed = attn_gain * d_attn
        x_grad = d_mid + inv_one * wed - xf * (inv_one ** 3 * jnp.mean(wed * xf, axis=-1, keepdims=True))
        gain_one = jnp.sum(d_attn * xf * inv_one, axis=0)
        gain_one, gain_two = lax.psum((gain_one, gain_two), ("heads", "experts"))
        w_grad = w_grad.reshape(width, groups, 256)
        q_grad = w_grad[:, :, :128].reshape(query_matrix.shape)
        k_grad = w_grad[:, :, 128:192].reshape(key_matrix.shape)
        v_grad = w_grad[:, :, 192:].reshape(value_matrix.shape)
    return (
        unlocal(out),
        unlocal(x_grad),
        gain_one,
        gain_two,
        q_grad,
        k_grad,
        v_grad,
        o_grad,
        grad_in,
        grad_down,
    )


def solution(mesh):
    rows = P("heads", "experts", None)
    in_specs = (
        rows,
        P("experts"),
        rows,
        rows,
        P("heads", "experts"),
        P(),
        P(),
        P(None, "heads"),
        P(None, "heads"),
        P(None, "heads"),
        P("heads", None),
        P("experts", None, None),
        P("experts", None, None),
        rows,
    )
    out_specs = (
        rows,
        rows,
        P(),
        P(),
        P(None, "heads"),
        P(None, "heads"),
        P(None, "heads"),
        P("heads", None),
        P("experts", None, None),
        P("experts", None, None),
    )
    return jax.shard_map(body, mesh=mesh, in_specs=in_specs, out_specs=out_specs, check_vma=False)
```

```python
import functools
import math

import jax
import jax.numpy as jnp
from jax import lax
from jax.experimental import pallas as pl
from jax.experimental.pallas import tpu as pltpu
from jax.sharding import PartitionSpec as P

HEAD = 64
EXPERTS = 32
EPS = 1e-06
BF = jnp.bfloat16
F32 = jnp.float32
SCALE = HEAD ** (-0.5)
NEG = -1e30
VMEM = 63 * 1024 * 1024
MESH = pl.DeviceIdType.MESH
DMA = pltpu.SemaphoreType.DMA


def dot(a, b):
    return jnp.dot(a, b, preferred_element_type=F32)


def dot_nt(a, b):
    return lax.dot_general(a, b, (((1,), (1,)), ((), ())), preferred_element_type=F32)


def dot_tn(a, b):
    return lax.dot_general(a, b, (((0,), (0,)), ((), ())), preferred_element_type=F32)


def params(n):
    return pltpu.CompilerParams(
        dimension_semantics=("arbitrary",) * n, vmem_limit_bytes=VMEM
    )


def swap_halves(v):
    lane = lax.broadcasted_iota(jnp.int32, v.shape, 1)
    return jnp.where(lane % 64 < 32, pltpu.roll(v, 96, 1), pltpu.roll(v, 32, 1))


def attn_mask(offset, n, block, length):
    key = lax.broadcasted_iota(jnp.int32, (n, block), 0)
    query = lax.broadcasted_iota(jnp.int32, (n, block), 1) + offset
    return (key <= query) & (key < length)


def two_heads(v):
    return jnp.concatenate([v[:, :HEAD], v[:, HEAD:]], axis=0)


def untwo(vt, block):
    return jnp.concatenate([vt[:, :block], vt[:, block:]], axis=0).T


def fwd_kernel(len_ref, x_ref, w_ref, cq, sq, ckv, skv, qkv_ref, head_ref, lse_ref):
    nh, _, seg, width = x_ref.shape
    full = nh * seg
    block = seg
    length = len_ref[pl.program_id(0)]
    lin = dot(x_ref[...].reshape(full, width), w_ref[0])
    ql, kvl = lin[:, :128], lin[:, 128:]
    q = (ql * cq[...] + swap_halves(ql) * sq[...]).astype(BF)
    kvr = kvl * ckv[...] + swap_halves(kvl) * skv[...]
    kv = kvr.astype(BF)
    qkv_ref[0, 0, :, :128] = q
    qkv_ref[0, 0, :, 128:] = kv
    k = kv[:, :HEAD]
    vt = kvr.T[HEAD:].astype(BF)
    for i in range(nh):
        n = (i + 1) * block
        q2 = two_heads(q[i * block : n])
        s = dot_nt(k[:n], q2)
        mask = attn_mask(i * block, n, block, length)
        s = jnp.where(jnp.concatenate([mask, mask], axis=1), s * SCALE, NEG)
        m = jnp.max(s, axis=0, keepdims=True)
        e = jnp.exp(s - m)
        total = jnp.sum(e, axis=0, keepdims=True)
        p = (e * (1.0 / total)).astype(BF)
        lse_ref[0, 0, i : i + 1, :] = m + jnp.log(total)
        head_ref[i, 0] = untwo(dot(vt[:, :n], p), block).astype(BF)


def attn_forward(x, w, lengths, tables):
    nh, nseq, seg, width = x.shape
    groups = w.shape[0]
    full = nh * seg
    cq, sq, ckv, skv = tables
    tab = pl.BlockSpec((full, 128), lambda s, g: (0, 0))
    return pl.pallas_call(
        fwd_kernel,
        grid=(nseq, groups),
        in_specs=[
            pl.BlockSpec(memory_space=pltpu.SMEM),
            pl.BlockSpec((nh, 1, seg, width), lambda s, g: (0, s, 0, 0)),
            pl.BlockSpec((1, width, 256), lambda s, g: (g, 0, 0)),
            tab,
            tab,
            tab,
            tab,
        ],
        out_specs=[
            pl.BlockSpec((1, 1, full, 256), lambda s, g: (s, g, 0, 0)),
            pl.BlockSpec((nh, 1, seg, 128), lambda s, g: (0, s, 0, g)),
            pl.BlockSpec((1, 1, nh, 2 * seg), lambda s, g: (s, g, 0, 0)),
        ],
        out_shape=[
            jax.ShapeDtypeStruct((nseq, groups, full, 256), BF),
            jax.ShapeDtypeStruct((nh, nseq, seg, groups * 128), BF),
            jax.ShapeDtypeStruct((nseq, groups, nh, 2 * seg), F32),
        ],
        compiler_params=params(2),
        cost_estimate=pl.CostEstimate(flops=6 * 10**9, bytes_accessed=12 * 2**20, transcendentals=10**7),
        name="attn_forward",
    )(lengths, x, w, cq, sq, ckv, skv)


def bwd_piece(q, kv, heads, lses, length, tables, dkv_ref, put):
    cq, sq, ckv, skv = tables
    full, block = q.shape[0], lses(0).shape[1] // 2
    k, v = kv[:, :HEAD], kv[:, HEAD:]
    kt = kv.astype(F32).T[:HEAD].astype(BF)
    dkv_ref[...] = jnp.zeros_like(dkv_ref)
    for i in range(full // block):
        n = (i + 1) * block
        rows = pl.ds(i * block, block)
        mask = attn_mask(i * block, n, block, length)
        grads = []
        for h in range(2):
            qh = q[i * block : n, h * HEAD : (h + 1) * HEAD]
            doh = heads(i)[:, h * HEAD : (h + 1) * HEAD]
            s = dot_nt(k[:n], qh)
            p = jnp.exp(jnp.where(mask, s * SCALE - lses(i)[:, h * block : (h + 1) * block], NEG))
            dp = dot_nt(v[:n], doh)
            delta = jnp.sum(p * dp, axis=0, keepdims=True)
            ds = (p * (dp - delta) * SCALE).astype(BF)
            dkv_ref[:n, :HEAD] += dot(ds, qh)
            dkv_ref[:n, HEAD:] += dot(p.astype(BF), doh)
            grads.append(dot(kt[:, :n], ds))
        dq = jnp.concatenate(grads, axis=0).T
        dq = dq * cq[rows, :] - swap_halves(dq) * sq[rows, :]
        put(i, 0, dq.astype(BF))
    dkv = dkv_ref[...]
    dkv = (dkv * ckv[...] - swap_halves(dkv) * skv[...]).astype(BF)
    for i in range(full // block):
        put(i, 128, dkv[i * block : (i + 1) * block])


def bwd_kernel(len_ref, qkv_ref, do_ref, lse_ref, cq, sq, ckv, skv, out_ref, dkv_ref):
    def put(i, lo, v):
        out_ref[i, 0, :, lo : lo + 128] = v

    bwd_piece(
        qkv_ref[0, 0, :, :128],
        qkv_ref[0, 0, :, 128:],
        lambda i: do_ref[i, 0],
        lambda i: lse_ref[0, 0, i : i + 1, :],
        len_ref[pl.program_id(0)],
        (cq, sq, ckv, skv),
        dkv_ref,
        put,
    )


def attn_backward(qkv, d_head, lse, lengths, tables):
    nseq, groups, full, _ = qkv.shape
    nh, _, seg, _ = d_head.shape
    cq, sq, ckv, skv = tables
    tab = pl.BlockSpec((full, 128), lambda s, g: (0, 0))
    return pl.pallas_call(
        bwd_kernel,
        grid=(nseq, groups),
        in_specs=[
            pl.BlockSpec(memory_space=pltpu.SMEM),
            pl.BlockSpec((1, 1, full, 256), lambda s, g: (s, g, 0, 0)),
            pl.BlockSpec((nh, 1, seg, 128), lambda s, g: (0, s, 0, g)),
            pl.BlockSpec((1, 1, nh, 2 * seg), lambda s, g: (s, g, 0, 0)),
            tab,
            tab,
            tab,
            tab,
        ],
        out_specs=pl.BlockSpec((nh, 1, seg, 256), lambda s, g: (0, s, 0, g)),
        out_shape=jax.ShapeDtypeStruct((nh, nseq, seg, groups * 256), BF),
        scratch_shapes=[pltpu.VMEM((full, 128), F32)],
        compiler_params=params(2),
        cost_estimate=pl.CostEstimate(flops=12 * 10**9, bytes_accessed=8 * 2**20, transcendentals=10**7),
        name="attn_backward",
    )(lengths, qkv, d_head, lse, cq, sq, ckv, skv)


def rotary_tables(length):
    half = HEAD // 2
    frequency = jnp.exp(jnp.arange(half, dtype=F32) * (-2.0 * math.log(10000.0) / HEAD))
    angles = jnp.arange(length, dtype=F32)[:, None] * frequency[None, :]
    cos, sin = jnp.cos(angles), jnp.sin(angles)
    c1 = jnp.concatenate([cos, cos], axis=1)
    s1 = jnp.concatenate([-sin, sin], axis=1)
    cq = jnp.concatenate([c1, c1], axis=1)
    sq = jnp.concatenate([s1, s1], axis=1)
    ckv = jnp.concatenate([c1, jnp.ones_like(c1)], axis=1)
    skv = jnp.concatenate([s1, jnp.zeros_like(s1)], axis=1)
    return cq, sq, ckv, skv


def pick_rows(slots, cap):
    tokens = slots.shape[1]
    index = lax.broadcasted_iota(jnp.int32, (cap, tokens), 0)
    return [index == slots[j : j + 1, :] for j in range(slots.shape[0])]


def gather_kernel(weighted, slot_ref, *refs):
    if weighted:
        weight_ref, tok_ref, out_ref = refs
    else:
        tok_ref, out_ref = refs[0], refs[-1]
    cap = out_ref.shape[2]
    hits = pick_rows(slot_ref[0], cap)
    rows = dot(jnp.concatenate([h.astype(F32) for h in hits], axis=0).astype(BF), tok_ref[0])
    for j, hit in enumerate(hits):
        part = rows[j * cap : (j + 1) * cap]
        if weighted:
            part = part * jnp.sum(jnp.where(hit, weight_ref[0, j : j + 1, :], 0.0), axis=1, keepdims=True)
        out_ref[j, 0] = part.astype(BF)


def gather_rows(slots, weights, tokens, cap):
    sources, here, count = slots.shape
    width = tokens.shape[-1]
    small = pl.BlockSpec((1, here, count), lambda s: (s, 0, 0))
    weighted = weights is not None
    return pl.pallas_call(
        functools.partial(gather_kernel, weighted),
        grid=(sources,),
        in_specs=[small] + [small] * weighted + [pl.BlockSpec((1, count, width), lambda s: (s, 0, 0))],
        out_specs=pl.BlockSpec((here, 1, cap, width), lambda s: (0, s, 0, 0)),
        out_shape=jax.ShapeDtypeStruct((here, sources, cap, width), BF),
        compiler_params=params(1),
        cost_estimate=pl.CostEstimate(
            flops=2 * sources * here * cap * count * width,
            bytes_accessed=2 * sources * width * (count + here * cap),
            transcendentals=0,
        ),
        name="gather_rows",
    )(*([slots] + [weights] * weighted + [tokens]))


def expert_kernel(steps, slot_ref, weight_ref, x_ref, d_ref, win_ref, wdown_ref,
                  out_ref, drow_ref, grad_ref, hid_ref, dgu_ref, *acc):
    _, sources, cap, width = x_ref.shape
    ff = wdown_ref.shape[1]
    per = 2 if sources % 2 == 0 else 1
    win, wdown = win_ref[0], wdown_ref[0]
    for c in range(sources // per):
        rows = slice(c * per * cap, (c + 1) * per * cap)
        x = x_ref[0, c * per : (c + 1) * per].reshape(per * cap, width)
        d = d_ref[0, c * per : (c + 1) * per].reshape(per * cap, width)
        gu = dot(x, win)
        gate, up = gu[:, :ff], gu[:, ff:]
        sig = 1.0 / (1.0 + jnp.exp(-gate))
        act = gate * sig
        hidden = (act * up).astype(BF)
        hid_ref[rows, :] = hidden
        result = dot(hidden, wdown).astype(BF).astype(F32)
        for b in range(per):
            hit = pick_rows(slot_ref[c * per + b, 0], cap)[0]
            w = jnp.sum(jnp.where(hit, weight_ref[c * per + b, 0], 0.0), axis=1, keepdims=True)
            out_ref[0, c * per + b] = (result[b * cap : (b + 1) * cap] * w).astype(BF)
        dh = dot_nt(d, wdown)
        dgu_ref[rows, :ff] = (dh * up * (sig * (1.0 + gate * (1.0 - sig)))).astype(BF)
        dgu_ref[rows, ff:] = (dh * act).astype(BF)
        drow = dot_nt(dgu_ref[rows, :], win).astype(BF)
        for b in range(per):
            drow_ref[0, c * per + b] = drow[b * cap : (b + 1) * cap]
    x = x_ref[0].reshape(sources * cap, width)
    d = d_ref[0].reshape(sources * cap, width)
    gin = dot_tn(x, dgu_ref[...])
    gdown = dot_tn(hid_ref[...], d)
    if steps == 1:
        grad_ref[0, :width] = gin.astype(BF)
        grad_ref[0, width:] = gdown.astype(BF)
    else:
        ain, adown = acc
        step = pl.program_id(1)

        @pl.when(step == 0)
        def _():
            ain[...] = jnp.zeros_like(ain)
            adown[...] = jnp.zeros_like(adown)

        ain[...] += gin
        adown[...] += gdown

        @pl.when(step == steps - 1)
        def _():
            grad_ref[0, :width] = ain[...].astype(BF)
            grad_ref[0, width:] = adown[...].astype(BF)


def experts_call(slots, weights, x, d, win, wdown):
    count, sources, cap, width = x.shape
    tokens = slots.shape[-1]
    ff = wdown.shape[1]
    chunk = min(sources, 8)
    steps = sources // chunk
    small = pl.BlockSpec((chunk, 1, 1, tokens), lambda j, r: (r, j, 0, 0))
    rows = pl.BlockSpec((1, chunk, cap, width), lambda j, r: (j, r, 0, 0))
    rows_out = pl.BlockSpec((1, chunk, cap, width), lambda j, r: (j, r, 0, 0))
    scratch = [pltpu.VMEM((chunk * cap, ff), BF), pltpu.VMEM((chunk * cap, 2 * ff), BF)]
    if steps > 1:
        scratch += [pltpu.VMEM((width, 2 * ff), F32), pltpu.VMEM((ff, width), F32)]
    shape = jax.ShapeDtypeStruct((count, sources, cap, width), BF)
    return pl.pallas_call(
        functools.partial(expert_kernel, steps),
        grid=(count, steps),
        in_specs=[
            small,
            small,
            rows,
            rows,
            pl.BlockSpec((1, width, 2 * ff), lambda j, r: (j, 0, 0)),
            pl.BlockSpec((1, ff, width), lambda j, r: (j, 0, 0)),
        ],
        out_specs=[
            rows_out,
            rows_out,
            pl.BlockSpec((1, width + ff, width), lambda j, r: (j, 0, 0)),
        ],
        out_shape=[
            shape,
            shape,
            jax.ShapeDtypeStruct((count, width + ff, width), BF),
        ],
        scratch_shapes=scratch,
        compiler_params=params(2),
        cost_estimate=pl.CostEstimate(
            flops=2 * count * sources * cap * width * ff * 9,
            bytes_accessed=8 * count * sources * cap * width + 12 * count * width * ff,
            transcendentals=count * sources * cap * ff,
        ),
        name="experts",
    )(slots[:, :, None, :], weights[:, :, None, :], x, d, win, wdown)


def combine_kernel(slot_ref, row_ref, out_ref):
    slots = slot_ref[0]
    count, here = slots.shape
    cap = row_ref.shape[2]
    lane = lax.broadcasted_iota(jnp.int32, (count, here * cap), 1)
    hot = None
    for j in range(here):
        col = slots[:, j : j + 1]
        hit = lane == jnp.where(col >= 0, col + j * cap, -1)
        hot = hit if hot is None else hot | hit
    hot = hot.astype(F32).astype(BF)
    out_ref[0] = dot(hot, row_ref[...].reshape(here * cap, row_ref.shape[3])).astype(BF)


def combine(slots_t, rows):
    sources, count, here = slots_t.shape
    _, _, cap, width = rows.shape
    return pl.pallas_call(
        combine_kernel,
        grid=(sources,),
        in_specs=[
            pl.BlockSpec((1, count, here), lambda s: (s, 0, 0)),
            pl.BlockSpec((here, 1, cap, width), lambda s: (0, s, 0, 0)),
        ],
        out_specs=pl.BlockSpec((1, count, width), lambda s: (s, 0, 0)),
        out_shape=jax.ShapeDtypeStruct((sources, count, width), BF),
        compiler_params=params(1),
        cost_estimate=pl.CostEstimate(
            flops=2 * sources * here * cap * count * width,
            bytes_accessed=2 * sources * width * (count + here * cap),
            transcendentals=0,
        ),
        name="combine",
    )(slots_t, rows)


def swap(x, bit, n):
    return lax.ppermute(x, "experts", [(i, i ^ bit) for i in range(n)])


def plane_gather(x, n):
    if n != 8:
        whole = lax.all_gather(x, "experts", axis=0)
        order = lax.axis_index("experts") ^ jnp.arange(n, dtype=jnp.int32)
        return whole[order]
    got = {0: x}
    for r in (2, 4, 6):
        got[r] = swap(x, r, n)
    for r in (0, 2, 4, 6):
        got[r + 1] = swap(got[r], 1, n)
    return jnp.stack([got[r] for r in range(n)], axis=0)


def plane_scatter(parts, n):
    if n != 8:
        order = lax.axis_index("experts") ^ jnp.arange(n, dtype=jnp.int32)
        return lax.psum_scatter(parts[order].astype(F32), "experts", scatter_dimension=0)
    odd = swap(parts[1::2], 1, n)
    both = [parts[2 * i].astype(F32) + odd[i].astype(F32) for i in range(4)]
    total = both[0]
    for i in (1, 2, 3):
        total = total + swap(both[i].astype(BF), 2 * i, n).astype(F32)
    return total


def heads_sum(x, z, nh):
    if nh != 4:
        return lax.psum(x.astype(F32), "heads")
    first = lax.ppermute(x, "heads", [(0, 1), (3, 2)])
    pair = (x.astype(F32) + first.astype(F32)).astype(BF)
    second = lax.ppermute(pair, "heads", [(1, 2), (2, 1)])
    total = (pair.astype(F32) + second.astype(F32)).astype(BF)
    third = lax.ppermute(total, "heads", [(1, 0), (2, 3)])
    return jnp.where((z == 1) | (z == 2), total, third).astype(F32)


def weight_sums(heads_in, d_branch, gathered, dqkv, ne):
    nh, tokens, part = heads_in.shape
    width, cols = d_branch.shape[1], dqkv.shape[2]
    col, row = width // ne, width // ne
    o = jnp.einsum("ztm,tew->ezmw", heads_in, d_branch.reshape(tokens, ne, col), preferred_element_type=F32)
    w = jnp.einsum("ztm,ztc->mc", gathered.reshape(nh, tokens, width), dqkv, preferred_element_type=F32)
    cut = cols // col
    w = jnp.swapaxes(w.reshape(ne, row, cut, col), 1, 2).reshape(ne, cut * row, col)
    both = jnp.concatenate([o.reshape(ne, nh * part, col), w], axis=1)
    both = lax.psum_scatter(both, "experts", scatter_dimension=0)
    o, w = both[: nh * part], both[nh * part :]
    o = lax.psum_scatter(o.reshape(nh, part, col), "heads", scatter_dimension=0)
    return weight_split(lax.all_gather(jnp.concatenate([o, w], axis=0), "experts", axis=0), part, cols)


def weight_split(both, part, cols):
    ne, _, col = both.shape
    width, row, cut = ne * col, col, cols // col
    o = jnp.swapaxes(both[:, :part], 0, 1).reshape(part, width)
    w = jnp.swapaxes(both[:, part:].reshape(ne, cut, row, col), 1, 2)
    return o, w.reshape(width, cols)


CHUNK = 128
LAG = 2
FLIGHT = 3


def remote(src, dst, send, recv, axis, index):
    return pltpu.make_async_remote_copy(
        src_ref=src, dst_ref=dst, send_sem=send, recv_sem=recv,
        device_id={axis: index}, device_id_type=MESH,
    )


def greet(nh, masks):
    z, me = lax.axis_index("heads"), lax.axis_index("experts")
    bar = pltpu.get_barrier_semaphore()
    for d in range(1, nh):
        pl.semaphore_signal(bar, inc=1, device_id={"heads": lax.rem(z + d, nh)}, device_id_type=MESH)
    for r in masks:
        pl.semaphore_signal(bar, inc=1, device_id={"experts": me ^ r}, device_id_type=MESH)
    pl.semaphore_wait(bar, nh - 1 + len(masks))


class Chain:
    def __init__(self, src, out, scratch, first, count):
        self.src, self.out, self.first, self.count = src, out, first, count
        self.flight = min(FLIGHT, count)
        self.a, self.b, self.buf, self.s1, self.r1, self.s2, self.r2, self.ls, self.os = scratch
        z = lax.axis_index("heads")
        self.mid = (z == 1) | (z == 2)
        self.outer = jnp.where(z == 0, 1, jnp.where(z == 1, 0, jnp.where(z == 2, 3, 2)))
        self.inner = jnp.where(z == 1, 2, jnp.where(z == 2, 1, z))

    def piece(self, k):
        return self.src.at[pl.ds((self.first + k) * CHUNK, CHUNK)]

    def load(self, k):
        return pltpu.make_async_copy(self.piece(k), self.buf.at[lax.rem(k, 2)], self.ls.at[lax.rem(k, 2)])

    def store(self, ref, k):
        return pltpu.make_async_copy(ref.at[k], self.out.at[pl.ds((self.first + k) * CHUNK, CHUNK)], self.os.at[k])

    def up(self, k):
        return remote(self.piece(k), self.a.at[k], self.s1.at[k], self.r1.at[k], "heads", self.outer)

    def across(self, k):
        return remote(self.a.at[k], self.b.at[k], self.s2.at[k], self.r2.at[k], "heads", self.inner)

    def down(self, k):
        return remote(self.b.at[k], self.a.at[k], self.s1.at[k], self.r1.at[k], "heads", self.outer)

    def begin(self):
        @pl.when(self.mid)
        def _():
            self.load(0).start()

        @pl.when(jnp.logical_not(self.mid))
        def _():
            @pl.loop(0, self.flight)
            def _(k):
                self.up(k).start()

    def pair(self, k):
        @pl.when(k + 1 < self.count)
        def _():
            self.load(k + 1).start()

        self.load(k).wait()
        self.up(k).wait_recv()
        own = self.buf[lax.rem(k, 2)].astype(F32)
        self.a[k] = (self.a[k].astype(F32) + own).astype(BF)
        self.across(k).start()

    def total(self, j):
        self.across(j).wait_recv()
        self.b[j] = (self.a[j].astype(F32) + self.b[j].astype(F32)).astype(BF)
        self.down(j).start()
        self.store(self.b, j).start()

    def take(self, j):
        self.down(j).wait_recv()
        self.store(self.a, j).start()

    def step(self, k, lag=LAG):
        n = self.count

        @pl.when(self.mid)
        def _():
            @pl.when(k < n)
            def _():
                self.pair(k)

            @pl.when((k >= lag) & (k < n + lag))
            def _():
                self.total(k - lag)

        @pl.when(jnp.logical_not(self.mid))
        def _():
            @pl.when(k + self.flight < n)
            def _():
                self.up(k).wait_send()
                self.up(k + self.flight).start()

            @pl.when((k >= lag + 2) & (k < n + lag + 2))
            def _():
                self.take(k - lag - 2)

    def rest(self, k):
        n = self.count

        @pl.when(self.mid)
        def _():
            @pl.loop(min(max(k - LAG, 0), n), min(max(k - 1, 0), n))
            def _(j):
                self.total(j)

        @pl.when(jnp.logical_not(self.mid))
        def _():
            @pl.loop(min(max(k - LAG - 2, 0), n), min(max(k - 3, 0), n))
            def _(j):
                self.take(j)

        @pl.loop(k, n + 3)
        def _(i):
            self.step(i, 1)

    def run(self, first, last):
        @pl.loop(first, last)
        def _(k):
            self.step(k)

    def finish(self):
        n = self.count

        @pl.when(self.mid)
        def _():
            @pl.loop(0, n)
            def _(k):
                self.across(k).wait_send()
                self.down(k).wait_send()
                self.store(self.b, k).wait()

        @pl.when(jnp.logical_not(self.mid))
        def _():
            @pl.loop(n - self.flight, n)
            def _(k):
                self.up(k).wait_send()

            @pl.loop(0, n)
            def _(k):
                self.store(self.a, k).wait()


def chain_scratch(count, width):
    return [
        pltpu.VMEM((count, CHUNK, width), BF),
        pltpu.VMEM((count, CHUNK, width), BF),
        pltpu.VMEM((2, CHUNK, width), BF),
        DMA((count,)),
        DMA((count,)),
        DMA((count,)),
        DMA((count,)),
        DMA((2,)),
        DMA((count,)),
    ]


def experts_send_kernel(count, pack_ref, x_ref, d_ref, win_ref, wdown_ref,
                        out_ref, drow_ref, grad_ref, total_ref, hid_ref, dgu_ref, early_ref, *scratch):
    j, last_j = pl.program_id(0), pl.num_programs(0) - 1
    nh = lax.axis_size("heads")
    _, sources, cap, width = x_ref.shape
    here = pack_ref.shape[1] // 2
    ff = wdown_ref.shape[1]
    chain = Chain(early_ref, total_ref, scratch, 0, count)
    per = 2
    parts = sources // per

    def chain_step(t):
        @pl.when(j > 0)
        def _():
            chain.step((j - 1) * 3 + t, 1)

    @pl.when(j == 0)
    def _():
        greet(nh, ())

    win, wdown = win_ref[0], wdown_ref[0]
    for c in range(parts):
        rows = slice(c * per * cap, (c + 1) * per * cap)
        x = x_ref[0, c * per : (c + 1) * per].reshape(per * cap, width)
        d = d_ref[0, c * per : (c + 1) * per].reshape(per * cap, width)
        gu = dot(x, win)
        gate, up = gu[:, :ff], gu[:, ff:]
        sig = 1.0 / (1.0 + jnp.exp(-gate))
        act = gate * sig
        hidden = (act * up).astype(BF)
        hid_ref[rows, :] = hidden
        result = dot(hidden, wdown).astype(BF).astype(F32)
        for b in range(per):
            s = c * per + b
            hit = pick_rows(pack_ref[s, pl.ds(j, 1)].astype(jnp.int32), cap)[0]
            w = jnp.sum(jnp.where(hit, pack_ref[s, pl.ds(here + j, 1)], 0.0), axis=1, keepdims=True)
            out_ref[0, s] = (result[b * cap : (b + 1) * cap] * w).astype(BF)
        dh = dot_nt(d, wdown)
        dgu_ref[rows, :ff] = (dh * up * (sig * (1.0 + gate * (1.0 - sig)))).astype(BF)
        dgu_ref[rows, ff:] = (dh * act).astype(BF)
        drow = dot_nt(dgu_ref[rows, :], win).astype(BF)
        for b in range(per):
            drow_ref[0, c * per + b] = drow[b * cap : (b + 1) * cap]
        if c % 2:
            chain_step(c // 2)
    gin = dot_tn(x_ref[0].reshape(sources * cap, width), dgu_ref[...]).astype(BF)
    grad_ref[0, :width] = gin
    grad_ref[0, width:] = dot_tn(hid_ref[...], d_ref[0].reshape(sources * cap, width)).astype(BF)
    chain_step(2)

    @pl.when(j == 0)
    def _():
        early_ref[...] = gin[: early_ref.shape[0]]
        chain.begin()

    @pl.when(j == last_j)
    def _():
        chain.finish()


def experts_send(count, pack, x, d, win, wdown):
    here, sources, cap, width = x.shape
    ff = wdown.shape[1]
    rows = pl.BlockSpec((1, sources, cap, width), lambda j: (j, 0, 0, 0))
    shape = jax.ShapeDtypeStruct((here, sources, cap, width), BF)
    hbm = pl.BlockSpec(memory_space=pl.ANY)
    return pl.pallas_call(
        functools.partial(experts_send_kernel, count),
        grid=(here,),
        in_specs=[
            pl.BlockSpec(memory_space=pltpu.VMEM),
            rows,
            rows,
            pl.BlockSpec((1, width, 2 * ff), lambda j: (j, 0, 0)),
            pl.BlockSpec((1, ff, width), lambda j: (j, 0, 0)),
        ],
        out_specs=[rows, rows, pl.BlockSpec((1, width + ff, width), lambda j: (j, 0, 0)), hbm],
        out_shape=[
            shape,
            shape,
            jax.ShapeDtypeStruct((here, width + ff, width), BF),
            jax.ShapeDtypeStruct((here * (width + ff), width), BF),
        ],
        scratch_shapes=[
            pltpu.VMEM((sources * cap, ff), BF),
            pltpu.VMEM((sources * cap, 2 * ff), BF),
            pltpu.VMEM((count * CHUNK, width), BF),
        ]
        + chain_scratch(count, width),
        compiler_params=pltpu.CompilerParams(
            dimension_semantics=("arbitrary",), collective_id=4, has_side_effects=True, vmem_limit_bytes=VMEM
        ),
        cost_estimate=pl.CostEstimate(
            flops=18 * here * sources * cap * width * ff,
            bytes_accessed=8 * here * sources * cap * width,
            transcendentals=here * sources * cap * ff,
        ),
        name="experts_send",
    )(pack, x, d, win, wdown)


class PlaneSum:
    order = (3, 1, 2)

    def __init__(self, rows, slots, total, scratch):
        self.rows, self.slots, self.total = rows, slots, total
        self.buf, self.odd, self.c, self.e, self.f, self.ls, self.cs, self.cr, self.fs, self.fr = scratch
        self.me = lax.axis_index("experts")
        self.here, _, self.cap, self.width = rows.shape

    def load(self, r, at):
        return [
            pltpu.make_async_copy(self.rows.at[j, r], self.buf.at[at, j], self.ls.at[at, j])
            for j in range(self.here)
        ]

    def core(self, i):
        return remote(self.odd.at[i], self.c.at[i], self.cs.at[i], self.cr.at[i], "experts", self.me ^ 1)

    def chip(self, i):
        return remote(self.e.at[i - 1], self.f.at[i - 1], self.fs.at[i - 1], self.fr.at[i - 1], "experts", self.me ^ (2 * i))

    def part(self, r, at, after, after_at):
        if after is not None:
            for c in self.load(after, after_at):
                c.start()
        slots = self.slots[r].T.astype(jnp.int32)
        lane = lax.broadcasted_iota(jnp.int32, (slots.shape[0], self.here * self.cap), 1)
        hot = None
        for j in range(self.here):
            col = slots[:, j : j + 1]
            hit = lane == jnp.where(col >= 0, col + j * self.cap, -1)
            hot = hit if hot is None else hot | hit
        for c in self.load(r, at):
            c.wait()
        rows = self.buf[at].reshape(self.here * self.cap, self.width)
        return dot(hot.astype(F32).astype(BF), rows)

    def run(self, chain=None, step=0):
        turns = [2 * i + 1 for i in self.order + (0,)] + [2 * i for i in self.order + (0,)]
        for c in self.load(turns[0], 0):
            c.start()
        for t, r in enumerate(turns):
            after = turns[t + 1] if t + 1 < len(turns) else None
            value = self.part(r, t % 2, after, (t + 1) % 2)
            i = r // 2
            if r % 2:
                self.odd[i] = value.astype(BF)
                self.core(i).start()
            else:
                self.core(i).wait_recv()
                value = value + self.c[i].astype(F32)
                if i:
                    self.e[i - 1] = value.astype(BF)
                    self.chip(i).start()
                else:
                    self.total[...] = value
            if chain is not None and t % 2:
                chain.step(step + t // 2)

    def arrive(self):
        for i in self.order:
            self.chip(i).wait_recv()

    def rows_total(self, rows):
        d = self.total[rows]
        for r in range(3):
            d = d + self.f[r, rows].astype(F32)
        return d

    def finish(self):
        for i in range(4):
            self.core(i).wait_send()
        for i in self.order:
            self.chip(i).wait_send()


def plane_scratch(here, cap, tokens, width):
    return [
        pltpu.VMEM((2, here, cap, width), BF),
        pltpu.VMEM((4, tokens, width), BF),
        pltpu.VMEM((4, tokens, width), BF),
        pltpu.VMEM((3, tokens, width), BF),
        pltpu.VMEM((3, tokens, width), BF),
        DMA((2, here)),
        DMA((4,)),
        DMA((4,)),
        DMA((3,)),
        DMA((3,)),
    ]


PLANE = 10


ROWS = 128


class Exchange:
    def __init__(self, src, dst, send, recv, nh):
        self.src, self.dst, self.ss, self.rs, self.nh = src, dst, send, recv, nh
        self.z = lax.axis_index("heads")

    def send(self, d):
        to = lax.rem(self.z + d, self.nh)
        return remote(self.src(to), self.dst(self.z), self.ss(d), self.rs(d), "heads", to)

    def start(self):
        for k in range(1, self.nh):
            self.send(jnp.where(self.z < self.nh // 2, self.nh - k, k)).start()

    def wait_recv(self):
        for d in range(1, self.nh):
            at = lax.rem(self.z + self.nh - d, self.nh)
            remote(self.src(at), self.dst(at), self.ss(d), self.rs(d), "heads", at).wait_recv()

    def finish(self):
        for d in range(1, self.nh):
            self.send(d).wait_send()


def whole_exchange(src, dst, send, recv, nh):
    return Exchange(lambda h: src.at[h], lambda h: dst.at[h], lambda d: send.at[d], lambda d: recv.at[d], nh)


class PlaneGather:
    order = (3, 1, 2)

    def __init__(self, own, slot, sems):
        self.own, self.slot = own, slot
        self.cs, self.cr, self.ks, self.kr = sems
        self.me = lax.axis_index("experts")

    def chip(self, i, e):
        return remote(self.own, self.slot(e), self.cs.at[i], self.cr.at[i], "experts", self.me ^ (2 * i))

    def core(self, i, src, e):
        return remote(src, self.slot(e), self.ks.at[i], self.kr.at[i], "experts", self.me ^ 1)

    def start(self):
        self.core(0, self.own, self.me).start()
        for i in self.order:
            self.chip(i, self.me).start()

    def forward(self, i):
        e = self.me ^ (2 * i)
        self.chip(i, e).wait_recv()
        self.core(i, self.slot(e), e).start()

    def core_arrive(self, i):
        e = self.me ^ 1 ^ (2 * i)
        self.core(i, self.slot(e), e).wait_recv()

    def finish(self):
        for i in range(1, 4):
            self.chip(i, self.me).wait_send()
        for i in range(4):
            self.core(i, self.own if i == 0 else self.slot(self.me ^ (2 * i)), self.me).wait_send()


GATHER = 4


def gather_sems():
    return [DMA((4,)), DMA((4,)), DMA((4,)), DMA((4,))]


class Picker:
    def __init__(self, pack, stage, sems, here, cap):
        self.pack, self.stage, self.sems, self.here, self.cap = pack, stage, sems, here, cap
        self.turn, self.pending = 0, {}

    def pick(self, r, tokens, out, weighted):
        at = self.turn % 2
        self.turn += 1
        info = self.pack[r]
        slots = info.astype(jnp.int32)
        index = lax.broadcasted_iota(jnp.int32, (self.cap, slots.shape[1]), 0)
        hits = [index == slots[j : j + 1] for j in range(self.here)]
        rows = dot(jnp.concatenate([h.astype(F32) for h in hits], axis=0).astype(BF), tokens)
        for c in self.pending.get(at, []):
            c.wait()
        for j, hit in enumerate(hits):
            part = rows[j * self.cap : (j + 1) * self.cap]
            if weighted:
                w = info[self.here + j : self.here + j + 1]
                part = part * jnp.sum(jnp.where(hit, w, 0.0), axis=1, keepdims=True)
            self.stage[at, j] = part.astype(BF)
        self.pending[at] = [
            pltpu.make_async_copy(self.stage.at[at, j], out.at[j, r], self.sems.at[at, j])
            for j in range(self.here)
        ]
        for c in self.pending[at]:
            c.start()

    def finish(self):
        for copies in self.pending.values():
            for c in copies:
                c.wait()


def front_kernel(len_ref, x_ref, og_ref, wq_ref, wk_ref, wv_ref, om_ref, pk_ref, again_ref, mgain_ref, cq, sq, ckv, skv,
                 xg_ref, qkv_ref, lse_ref, hin_ref, of_ref, wz_ref, mid_ref, pack_ref, drows_ref, xrows_ref,
                 w_ref, hs, ogb, mt, stage, ls, lr, ps, pr, hss, hrs, os_, or_, ws, wr, ss, *sems):
    nh, tokens, width = xg_ref.shape
    nseq, groups, full, _ = qkv_ref.shape
    ne = ogb.shape[0]
    seg = tokens // nseq
    here, _, cap, _ = drows_ref.shape
    z, me = lax.axis_index("heads"), lax.axis_index("experts")
    og = PlaneGather(og_ref, lambda e: ogb.at[e], sems[:GATHER])
    og_o = PlaneGather(of_ref.at[:, me], lambda e: of_ref.at[:, e], sems[GATHER : 2 * GATHER])

    def moe(p):
        at = pl.ds(p * seg, seg)
        return PlaneGather(mt.at[me, at], lambda e: mt.at[e, at], sems[(2 + p) * GATHER : (3 + p) * GATHER])

    moes = [moe(p) for p in range(nseq)]

    def heads(p):
        at = pl.ds(p * seg, seg)
        return Exchange(
            lambda h: hs.at[h, at], lambda h: hin_ref.at[h, at], lambda d: hss.at[p, d], lambda d: hrs.at[p, d], nh)

    picker = Picker(pack_ref, stage, ss, here, cap)

    @pl.loop(0, tokens // ROWS)
    def _(i):
        rows = pl.ds(i * ROWS, ROWS)
        x = x_ref[rows].astype(F32)
        inv = lax.rsqrt(jnp.mean(x * x, axis=-1, keepdims=True) + EPS)
        xg_ref[z, rows] = (x * inv * again_ref[...]).astype(BF)

    greet(nh, tuple(range(1, ne)))
    for g in range(groups):
        head = slice(g * HEAD, (g + 1) * HEAD)
        w_ref[:, g * 256 : g * 256 + 128] = wq_ref[:, g * 128 : (g + 1) * 128]
        w_ref[:, g * 256 + 128 : (g + 1) * 256] = jnp.concatenate([wk_ref[:, head], wv_ref[:, head]], axis=1)

    def hop(way, t, p, s, to):
        ref = xg_ref.at[s, pl.ds(p * seg, seg)]
        return remote(ref, ref, ls.at[way, t, p], lr.at[s, p], "heads", to)

    right, left = jnp.minimum(z + 1, nh - 1), jnp.maximum(z - 1, 0)
    for p in range(nseq):
        @pl.when(z < nh - 1)
        def _():
            hop(0, 0, p, z, right).start()

        @pl.when(z > 0)
        def _():
            hop(1, 0, p, z, left).start()

    def info(r):
        return remote(pk_ref.at[me ^ r], pack_ref.at[r], ps.at[r], pr.at[r], "experts", me ^ r)

    rows_o, rows_w = of_ref.shape[2], wz_ref.shape[1]
    of_ref[z, me] = om_ref[pl.ds(pl.multiple_of(me * rows_o, rows_o), rows_o)]
    wz_ref[z] = w_ref[pl.ds(pl.multiple_of(me * rows_w, rows_w), rows_w)]
    ofx = Exchange(lambda h: of_ref.at[z, me], lambda h: of_ref.at[h, me], lambda d: os_.at[d], lambda d: or_.at[d], nh)
    wzx = Exchange(lambda h: wz_ref.at[z], lambda h: wz_ref.at[h], lambda d: ws.at[d], lambda d: wr.at[d], nh)
    ofx.start()
    for r in range(1, ne):
        info(r).start()
    og.start()
    pack_ref[0] = pk_ref[me]

    def project(s, p):
        x = xg_ref[s, pl.ds(p * seg, seg)]
        at = pl.ds(s * seg, seg)
        for g in range(groups):
            lin = dot(x, w_ref[:, g * 256 : (g + 1) * 256])
            q, kv = lin[:, :128], lin[:, 128:]
            qkv_ref[p, g, at, :128] = (q * cq[at] + swap_halves(q) * sq[at]).astype(BF)
            qkv_ref[p, g, at, 128:] = (kv * ckv[at] + swap_halves(kv) * skv[at]).astype(BF)

    @pl.loop(0, nseq)
    def _(p):
        project(z, p)

    def round_of(t, then=None):
        @pl.loop(0, nseq)
        def _(p):
            @pl.when(z >= t)
            def _():
                s = z - t
                hop(0, t, p, s, left).wait_recv()

                @pl.when(z < nh - 1)
                def _():
                    hop(0, t, p, s, right).start()

                project(s, p)

            @pl.when(z + t < nh)
            def _():
                s = z + t
                hop(1, t, p, s, right).wait_recv()

                @pl.when(z > 0)
                def _():
                    hop(1, t, p, s, left).start()

                project(s, p)

            if then is not None:
                then(p)

    picker.pick(0, og_ref[...], drows_ref, True)
    round_of(1)
    for r in range(1, ne):
        info(r).wait_recv()
    og.core_arrive(0)
    picker.pick(1, ogb[me ^ 1], drows_ref, True)
    round_of(2)
    for i in og.order:
        og.forward(i)
    for i in og.order:
        picker.pick(2 * i, ogb[me ^ (2 * i)], drows_ref, True)
    ofx.wait_recv()
    og_o.start()

    def attend(p):
        length = len_ref[p]
        at = pl.ds(p * seg, seg)
        for g in range(groups):
            q = qkv_ref[p, g, :, :128]
            kv = qkv_ref[p, g, :, 128:]
            k = kv[:, :HEAD]
            vt = kv.astype(F32).T[HEAD:].astype(BF)
            for i in range(nh):
                n = (i + 1) * seg
                q2 = two_heads(q[i * seg : n])
                s = dot_nt(k[:n], q2)
                mask = attn_mask(i * seg, n, seg, length)
                s = jnp.where(jnp.concatenate([mask, mask], axis=1), s * SCALE, NEG)
                m = jnp.max(s, axis=0, keepdims=True)
                e = jnp.exp(s - m)
                total = jnp.sum(e, axis=0, keepdims=True)
                prob = (e * (1.0 / total)).astype(BF)
                lse_ref[p, g, i : i + 1, :] = m + jnp.log(total)
                hs[i, at, g * 128 : (g + 1) * 128] = untwo(dot(vt[:, :n], prob), seg).astype(BF)
        hin_ref[z, at] = hs[z, at]

        @pl.when(at_end)
        def _():
            heads(p).start()

    at_end = (z == 0) | (z == nh - 1)
    round_of(3, attend)
    for p in range(nseq):
        for t in range(nh):
            @pl.when((z >= t) & (z < nh - 1))
            def _():
                hop(0, t, p, z - t, right).wait_send()

            @pl.when((z + t < nh) & (z > 0))
            def _():
                hop(1, t, p, z + t, left).wait_send()

    @pl.when(jnp.logical_not(at_end))
    def _():
        for p in range(nseq):
            heads(p).start()

    for i in og.order:
        og_o.forward(i)
    for i in og.order:
        og.core_arrive(i)
        picker.pick(2 * i + 1, ogb[me ^ 1 ^ (2 * i)], drows_ref, True)
    for i in range(4):
        og_o.core_arrive(i)

    for p in range(nseq):
        at = pl.ds(p * seg, seg)
        heads(p).wait_recv()
        mid_ref[at] = x_ref[at].astype(F32) + dot(hin_ref[0, at], of_ref[0].reshape(-1, width))
        for h in range(1, nh):
            mid_ref[at] += dot(hin_ref[h, at], of_ref[h].reshape(-1, width))

        @pl.loop(0, seg // ROWS)
        def _(i):
            rows = pl.ds(p * seg + i * ROWS, ROWS)
            m = mid_ref[rows]
            inv = lax.rsqrt(jnp.mean(m * m, axis=-1, keepdims=True) + EPS)
            mt[me, rows] = (m * inv * mgain_ref[...]).astype(BF)

        moes[p].start()

    wzx.start()
    picker.pick(0, mt[me], xrows_ref, False)
    for p in range(nseq):
        moes[p].core_arrive(0)
    picker.pick(1, mt[me ^ 1], xrows_ref, False)
    for i in og.order:
        for p in range(nseq - 1):
            moes[p].forward(i)
    for t, i in enumerate(og.order):
        moes[-1].forward(i)
        picker.pick(2 * i, mt[me ^ (2 * i)], xrows_ref, False)
        if t:
            last = og.order[t - 1]
            for p in range(nseq):
                moes[p].core_arrive(last)
            picker.pick(2 * last + 1, mt[me ^ 1 ^ (2 * last)], xrows_ref, False)
    last = og.order[-1]
    for p in range(nseq):
        moes[p].core_arrive(last)
    picker.pick(2 * last + 1, mt[me ^ 1 ^ (2 * last)], xrows_ref, False)
    picker.finish()
    wzx.wait_recv()
    for gather in [og, og_o] + moes:
        gather.finish()
    for exchange in [ofx, wzx] + [heads(p) for p in range(nseq)]:
        exchange.finish()
    for r in range(1, ne):
        info(r).wait_send()


def front(lengths, x, og, wq, wk, wv, o_local, packed, attn_gain, moe_gain, tables, nh, nseq, cap):
    ne, info, _ = packed.shape
    tokens, width = x.shape
    here = info // 2
    cols = 2 * wq.shape[1]
    groups, seg = cols // 256, tokens // nseq
    full = nh * seg
    part = o_local.shape[0]
    vmem = pl.BlockSpec(memory_space=pltpu.VMEM)
    hbm = pl.BlockSpec(memory_space=pl.ANY)
    rows = jax.ShapeDtypeStruct((here, ne, cap, width), BF)
    return pl.pallas_call(
        front_kernel,
        in_specs=[pl.BlockSpec(memory_space=pltpu.SMEM)] + [vmem] * 13,
        out_specs=[vmem] * 8 + [hbm, hbm],
        out_shape=[
            jax.ShapeDtypeStruct((nh, tokens, width), BF),
            jax.ShapeDtypeStruct((nseq, groups, full, 256), BF),
            jax.ShapeDtypeStruct((nseq, groups, nh, 2 * seg), F32),
            jax.ShapeDtypeStruct((nh, tokens, part), BF),
            jax.ShapeDtypeStruct((nh, ne, part // ne, width), BF),
            jax.ShapeDtypeStruct((nh, width // ne, cols), BF),
            jax.ShapeDtypeStruct((tokens, width), F32),
            jax.ShapeDtypeStruct(packed.shape, F32),
            rows,
            rows,
        ],
        scratch_shapes=[
            pltpu.VMEM((width, cols), BF),
            pltpu.VMEM((nh, tokens, part), BF),
            pltpu.VMEM((ne, tokens, width), BF),
            pltpu.VMEM((ne, tokens, width), BF),
            pltpu.VMEM((2, here, cap, width), BF),
            DMA((2, nh, nseq)),
            DMA((nh, nseq)),
            DMA((ne,)),
            DMA((ne,)),
            DMA((nseq, nh)),
            DMA((nseq, nh)),
            DMA((nh,)),
            DMA((nh,)),
            DMA((nh,)),
            DMA((nh,)),
            DMA((2, here)),
        ]
        + gather_sems() * (2 + nseq),
        compiler_params=pltpu.CompilerParams(
            collective_id=3, has_side_effects=True, vmem_limit_bytes=VMEM
        ),
        cost_estimate=pl.CostEstimate(flops=10**11, bytes_accessed=60 * 2**20, transcendentals=10**7),
        name="front",
    )(lengths, x, og, wq, wk, wv, o_local, packed, attn_gain, moe_gain, *tables)


def middle_kernel(first, count, len_ref, begun_ref, sum_ref, rows_ref, slot_ref, mid_ref, grad_ref, gain_ref, o_ref, qkv_ref, lse_ref,
                  cq, sq, ckv, skv, hin_ref, x_ref, total_ref, dmid_ref, gtwo_ref, dqkv_ref, po_ref, pw_ref,
                  dbranch_ref, wsum, hs, hr, dmoe, dkv, hss, hrs, xs, *scratch):
    nh, tokens, _ = dqkv_ref.shape
    nseq, groups = qkv_ref.shape[:2]
    seg = tokens // nseq
    z = lax.axis_index("heads")
    chain = Chain(sum_ref, total_ref, scratch[PLANE:], first, count)
    plane = PlaneSum(rows_ref, slot_ref, dmoe, scratch[:PLANE])
    heads = whole_exchange(hs, hr, hss, hrs, nh)
    greet(nh, (1, 2, 4, 6))
    chain.begin()
    plane.run(chain, 0)
    step = 4 + 5
    chain.run(4, step)
    plane.arrive()
    gtwo_ref[...] = jnp.zeros_like(gtwo_ref)

    @pl.loop(0, tokens // ROWS)
    def _(i):
        rows = pl.ds(i * ROWS, ROWS)
        d = plane.rows_total(rows)
        m = mid_ref[rows]
        inv = lax.rsqrt(jnp.mean(m * m, axis=-1, keepdims=True) + EPS)
        zed = gain_ref[...] * d
        dm = grad_ref[rows].astype(F32) + inv * zed - m * (inv * inv * inv * jnp.mean(zed * m, axis=-1, keepdims=True))
        gtwo_ref[...] += jnp.sum(d * m * inv, axis=0, keepdims=True)
        dmid_ref[rows] = dm
        db = dm.astype(BF)
        dbranch_ref[rows] = db
        for h in range(nh):
            hs[h, rows] = dot_nt(db, o_ref[h]).astype(BF)

    heads.start()
    hr[z] = hs[z]
    chain.run(step, step + 4)
    step = step + 4
    heads.wait_recv()

    @pl.loop(0, nseq)
    def _(s):
        length = len_ref[s]
        at = pl.ds(s * seg, seg)
        for g in range(groups):
            def put(i, lo, v):
                dqkv_ref[i, at, g * 256 + lo : g * 256 + lo + 128] = v

            bwd_piece(
                qkv_ref[s, g, :, :128],
                qkv_ref[s, g, :, 128:],
                lambda i: hr[i, at, g * 128 : (g + 1) * 128],
                lambda i: lse_ref[s, g, i : i + 1, :],
                length,
                (cq, sq, ckv, skv),
                dkv,
                put,
            )
            chain.step(step + groups * s + g)

    step = step + groups * nseq
    for i in range(4):
        plane.core(i).wait_send()
    load = pltpu.make_async_copy(x_ref, plane.odd, xs)
    load.start()
    ne, deep, _ = po_ref.shape
    strip, row = deep // nh, pw_ref.shape[1]
    db = dbranch_ref[...]
    for h in range(nh):
        o = dot_tn(hin_ref[h], db).astype(BF)
        for e in range(ne):
            po_ref[e, h * strip : (h + 1) * strip] = o[e * strip : (e + 1) * strip]
    chain.step(step)
    load.wait()
    wsum[...] = dot_tn(plane.odd[0], dqkv_ref[0])
    for h in range(1, nh):
        wsum[...] += dot_tn(plane.odd[h], dqkv_ref[h])
    for e in range(ne):
        pw_ref[e] = wsum[e * row : (e + 1) * row].astype(BF)
    chain.rest(step + 1)
    chain.finish()
    for i in plane.order:
        plane.chip(i).wait_send()
    heads.finish()


def middle(first, count, lengths, total, sums, rows, slots, mid, grad, gain, o_parts, qkv, lse, tables, heads_in, x):
    nseq, groups, full, _ = qkv.shape
    nh = o_parts.shape[0]
    tokens, width = mid.shape
    here, ne, cap, _ = rows.shape
    vmem = pl.BlockSpec(memory_space=pltpu.VMEM)
    hbm = pl.BlockSpec(memory_space=pl.ANY)
    heads = (nh, tokens, groups * 128)
    cols = groups * 256
    return pl.pallas_call(
        functools.partial(middle_kernel, first, count),
        in_specs=[pl.BlockSpec(memory_space=pltpu.SMEM), hbm, hbm, hbm] + [vmem] * 12 + [hbm],
        input_output_aliases={1: 0},
        out_specs=[hbm] + [vmem] * 5,
        out_shape=[
            jax.ShapeDtypeStruct(sums.shape, BF),
            jax.ShapeDtypeStruct((tokens, width), F32),
            jax.ShapeDtypeStruct((1, width), F32),
            jax.ShapeDtypeStruct((nh, tokens, cols), BF),
            jax.ShapeDtypeStruct((ne, nh * groups * 128 // ne, width), BF),
            jax.ShapeDtypeStruct((ne, width // ne, cols), BF),
        ],
        scratch_shapes=[
            pltpu.VMEM((tokens, width), BF),
            pltpu.VMEM((width, cols), F32),
            pltpu.VMEM(heads, BF),
            pltpu.VMEM(heads, BF),
            pltpu.VMEM((tokens, width), F32),
            pltpu.VMEM((full, 128), F32),
            DMA((nh,)),
            DMA((nh,)),
            DMA,
        ]
        + plane_scratch(here, cap, tokens, width)
        + chain_scratch(count, width),
        compiler_params=pltpu.CompilerParams(
            collective_id=1, has_side_effects=True, vmem_limit_bytes=VMEM
        ),
        cost_estimate=pl.CostEstimate(flops=10**11, bytes_accessed=30 * 2**20, transcendentals=10**7),
        name="middle",
    )(lengths, total, sums, rows, slots, mid, grad, gain, o_parts, qkv, lse, *tables, heads_in, x)


class PairSum:
    order = (3, 1, 2)

    def __init__(self, parts, scratch):
        self.parts = parts
        self.c, self.e, self.f, self.cs, self.cr, self.fs, self.fr = scratch
        self.me = lax.axis_index("experts")

    def core(self, i):
        src = self.parts.at[self.me ^ 1 ^ (2 * i)]
        return remote(src, self.c.at[i], self.cs.at[i], self.cr.at[i], "experts", self.me ^ 1)

    def chip(self, i):
        return remote(self.e.at[i - 1], self.f.at[i - 1], self.fs.at[i - 1], self.fr.at[i - 1], "experts", self.me ^ (2 * i))

    def start(self):
        for i in self.order + (0,):
            self.core(i).start()

    def both(self, i):
        return self.parts[self.me ^ (2 * i)].astype(F32) + self.c[i].astype(F32)

    def forward(self):
        for i in self.order:
            self.core(i).wait_recv()
            self.e[i - 1] = self.both(i).astype(BF)
            self.chip(i).start()
        self.core(0).wait_recv()

    def result(self):
        value = self.both(0)
        for i in self.order:
            self.chip(i).wait_recv()
        for r in range(3):
            value = value + self.f[r].astype(F32)
        return value

    def finish(self):
        for i in range(4):
            self.core(i).wait_send()
        for i in self.order:
            self.chip(i).wait_send()


PAIR = 7


def pair_scratch(shape):
    return [pltpu.VMEM((n,) + shape, BF) for n in (4, 3, 3)] + [DMA((4,)), DMA((4,)), DMA((3,)), DMA((3,))]


def last_kernel(first, count, begun_ref, sum_ref, rows_ref, slot_ref, mid_ref, dqkv_ref, wz_ref, x_ref, dmid_ref,
                gain_ref, gtwo_ref, po_ref, pw_ref, total_ref, out_ref, xgrad_ref, gains_ref, ograd_ref, qgrad_ref, kgrad_ref, vgrad_ref,
                wf, br, moe, gp, gz, acc, oz, fo, fq, fk, fv, brs, brr, gps, gpr, gzs, gzr, oss, ors, fl, dl, *scratch):
    nh, tokens, _ = dqkv_ref.shape
    dattn = moe
    ne = rows_ref.shape[1]
    z, me = lax.axis_index("heads"), lax.axis_index("experts")
    at = PLANE
    plane = PlaneSum(rows_ref, slot_ref, moe, scratch[:at])
    weights = PlaneGather(wz_ref, lambda e: wf.at[:, e], scratch[at : at + GATHER])
    at += GATHER
    strip, row = fo.shape[0], fq.shape[0]

    def o_rows(e):
        return ograd_ref.at[pl.ds(pl.multiple_of(e * strip, strip), strip)]

    def w_rows(ref, e):
        return ref.at[pl.ds(pl.multiple_of(e * row, row), row)]

    spread_o = PlaneGather(fo, o_rows, scratch[at : at + GATHER])
    at += GATHER
    spreads = [spread_o]
    for mine, whole in ((fq, qgrad_ref), (fk, kgrad_ref), (fv, vgrad_ref)):
        spreads.append(PlaneGather(mine, functools.partial(w_rows, whole), scratch[at : at + GATHER]))
        at += GATHER
    sum_o = PairSum(po_ref, scratch[at : at + PAIR])
    at += PAIR
    sum_w = PairSum(pw_ref, scratch[at : at + PAIR])
    at += PAIR
    chain = Chain(sum_ref, total_ref, scratch[at:], first, count)
    back = whole_exchange(dqkv_ref, br, brs, brr, nh)
    pieces = Exchange(
        lambda h: acc.at[pl.ds(pl.multiple_of(h * strip, strip), strip)],
        lambda h: oz.at[h], lambda d: oss.at[d], lambda d: ors.at[d], nh)
    first_part = pltpu.make_async_copy(dmid_ref, xgrad_ref, dl)
    first_part.start()
    greet(nh, tuple(range(1, ne)))
    back.start()
    sum_o.start()
    sum_w.start()
    chain.begin()
    br[z] = dqkv_ref[z]
    sum_o.forward()
    sum_w.forward()
    weights.start()
    wf[:, me] = wz_ref[...]
    plane.run()
    acc[...] = sum_o.result()
    pieces.start()
    oz[z] = acc[pl.ds(pl.multiple_of(z * strip, strip), strip)]
    w = sum_w.result()
    for g in range(fq.shape[1] // 128):
        head = slice(g * HEAD, (g + 1) * HEAD)
        fq[:, g * 128 : (g + 1) * 128] = w[:, g * 256 : g * 256 + 128]
        fk[:, head] = w[:, g * 256 + 128 : g * 256 + 192]
        fv[:, head] = w[:, g * 256 + 192 : (g + 1) * 256]
    for spread in spreads[1:]:
        spread.start()
    step = 4
    chain.run(0, step)
    pieces.wait_recv()
    fo[...] = oz[0] + oz[1] + oz[2] + oz[3]
    spread_o.start()
    keep = [pltpu.make_async_copy(g.own, g.slot(me), fl.at[t]) for t, g in enumerate(spreads)]
    for c in keep:
        c.start()
    for i in weights.order:
        weights.forward(i)
    chain.run(step, step + 4)
    step = step + 4
    plane.arrive()

    @pl.loop(0, tokens // ROWS)
    def _(i):
        rows = pl.ds(i * ROWS, ROWS)
        out_ref[rows] = (mid_ref[rows] + plane.rows_total(rows)).astype(BF)

    chain.run(step, step + 2)
    step = step + 2
    for i in range(4):
        weights.core_arrive(i)
    back.wait_recv()
    for h in range(nh):
        term = dot_nt(br[h], wf[h].reshape(-1, wf.shape[3]))
        if h:
            dattn[...] += term
        else:
            dattn[...] = term
    chain.run(step, step + 2)
    step = step + 2
    pad = jnp.zeros((6, gtwo_ref.shape[1]), F32)
    own = jnp.zeros_like(gtwo_ref[...])

    def rows_back(i, total):
        rows = pl.ds(i * ROWS, ROWS)
        d = dattn[rows]
        x = x_ref[rows].astype(F32)
        inv = lax.rsqrt(jnp.mean(x * x, axis=-1, keepdims=True) + EPS)
        wed = gain_ref[...] * d
        xgrad_ref[rows] += inv * wed - x * (inv * inv * inv * jnp.mean(wed * x, axis=-1, keepdims=True))
        return total + jnp.sum(d * x * inv, axis=0, keepdims=True)

    first_part.wait()
    own = lax.fori_loop(0, tokens // ROWS, rows_back, own)
    gp[me] = jnp.concatenate([own, gtwo_ref[...], pad], axis=0)

    def near(r, at):
        return remote(gp.at[me], gp.at[at], gps.at[r], gpr.at[r], "experts", me ^ r)

    for r in range(1, ne):
        near(r, me).start()
    chain.run(step, step + 2)
    step = step + 2
    for spread in spreads[1:] + spreads[:1]:
        for i in spread.order:
            spread.forward(i)
    for r in range(1, ne):
        near(r, me ^ r).wait_recv()
    total = gp[0]
    for e in range(1, ne):
        total = total + gp[e]
    gz[z] = total
    gains = Exchange(lambda h: gz.at[z], lambda h: gz.at[h], lambda d: gzs.at[d], lambda d: gzr.at[d], nh)
    gains.start()
    chain.rest(step)
    gains.wait_recv()
    total = gz[0]
    for h in range(1, nh):
        total = total + gz[h]
    gains_ref[...] = total
    for spread in spreads:
        for i in range(4):
            spread.core_arrive(i)
    chain.finish()
    for part in [plane, back, pieces, gains, weights, sum_o, sum_w] + spreads:
        part.finish()
    for c in keep:
        c.wait()
    for r in range(1, ne):
        near(r, me).wait_send()


def last(first, count, total, sums, rows, slots, mid, dqkv, w_pieces, x, d_mid, gain, gain_two, po, pw):
    nh, tokens, cols = dqkv.shape
    here, ne, cap, width = rows.shape
    strip = po.shape[1] // nh
    row = pw.shape[1]
    hbm = pl.BlockSpec(memory_space=pl.ANY)
    vmem = pl.BlockSpec(memory_space=pltpu.VMEM)
    return pl.pallas_call(
        functools.partial(last_kernel, first, count),
        in_specs=[hbm, hbm, hbm] + [vmem] * 5 + [hbm] + [vmem] * 4,
        input_output_aliases={0: 0},
        out_specs=[hbm] + [vmem] * 3 + [hbm] * 4,
        out_shape=[
            jax.ShapeDtypeStruct(sums.shape, BF),
            jax.ShapeDtypeStruct((tokens, width), BF),
            jax.ShapeDtypeStruct((tokens, width), F32),
            jax.ShapeDtypeStruct((8, width), F32),
            jax.ShapeDtypeStruct((strip * ne, width), F32),
            jax.ShapeDtypeStruct((row * ne, cols // 2), F32),
            jax.ShapeDtypeStruct((row * ne, cols // 4), F32),
            jax.ShapeDtypeStruct((row * ne, cols // 4), F32),
        ],
        scratch_shapes=[
            pltpu.VMEM((nh, ne, width // ne, cols), BF),
            pltpu.VMEM((nh, tokens, cols), BF),
            pltpu.VMEM((tokens, width), F32),
            pltpu.VMEM((ne, 8, width), F32),
            pltpu.VMEM((nh, 8, width), F32),
            pltpu.VMEM((nh * strip, width), F32),
            pltpu.VMEM((nh, strip, width), F32),
            pltpu.VMEM((strip, width), F32),
            pltpu.VMEM((row, cols // 2), F32),
            pltpu.VMEM((row, cols // 4), F32),
            pltpu.VMEM((row, cols // 4), F32),
            DMA((nh,)),
            DMA((nh,)),
            DMA((ne,)),
            DMA((ne,)),
            DMA((nh,)),
            DMA((nh,)),
            DMA((nh,)),
            DMA((nh,)),
            DMA((4,)),
            DMA,
        ]
        + plane_scratch(here, cap, tokens, width)
        + gather_sems() * 5
        + pair_scratch(po.shape[1:])
        + pair_scratch(pw.shape[1:])
        + chain_scratch(count, width),
        compiler_params=pltpu.CompilerParams(
            collective_id=2, has_side_effects=True, vmem_limit_bytes=VMEM
        ),
        cost_estimate=pl.CostEstimate(flops=2 * 10**11, bytes_accessed=30 * 2**20, transcendentals=0),
        name="last",
    )(total, sums, rows, slots, mid, dqkv, w_pieces, x, d_mid, gain, gain_two, po, pw)


def widen_kernel(x_ref, in_ref, down_ref):
    c = pl.program_id(1)

    @pl.when(c < 2)
    def _():
        in_ref[...] = x_ref[...].astype(F32)

    @pl.when(c == 2)
    def _():
        down_ref[...] = x_ref[...].astype(F32)


def widen(sums, ff):
    here, rows, width = sums.shape
    return pl.pallas_call(
        widen_kernel,
        grid=(here, 3),
        in_specs=[pl.BlockSpec((1, ff, width), lambda j, c: (j, c, 0))],
        out_specs=[
            pl.BlockSpec((1, ff, width), lambda j, c: (j, jnp.minimum(c, 1), 0)),
            pl.BlockSpec((1, ff, width), lambda j, c: (j, 0, 0)),
        ],
        out_shape=[
            jax.ShapeDtypeStruct((here, 2 * ff, width), F32),
            jax.ShapeDtypeStruct((here, ff, width), F32),
        ],
        compiler_params=params(2),
        name="widen",
    )(sums)


def body(layer_input, seq_lengths, expert_ids, route_weight, priority, attn_gain, moe_gain,
         query_matrix, key_matrix, value_matrix, output_matrix, expert_in, expert_down, out_grad):
    seg, nseq, width = layer_input.shape
    nh, ne = lax.axis_size("heads"), lax.axis_size("experts")
    z, me = lax.axis_index("heads"), lax.axis_index("experts")
    top = expert_ids.shape[-1]
    tokens = seg * nseq
    groups = key_matrix.shape[1] // HEAD
    here = expert_in.shape[0]
    cap = (5 * tokens * top + 4 * EXPERTS - 1) // (4 * EXPERTS)

    def local(v):
        return jnp.swapaxes(v, 0, 1).reshape((tokens,) + v.shape[2:])

    def unlocal(v):
        return jnp.swapaxes(v.reshape((nseq, seg) + v.shape[1:]), 0, 1)

    ids = local(expert_ids)
    order = local(priority)
    weight = local(route_weight)
    position = z * seg + jnp.arange(seg, dtype=jnp.int32)
    live = (position[None, :] < seq_lengths[:, None]).reshape(tokens)
    match = ids.T[:, None, :] == jnp.arange(EXPERTS, dtype=jnp.int32)[None, :, None]
    weight_e = jnp.sum(jnp.where(match, weight.T[:, None, :], 0.0), axis=0)
    chosen = jnp.any(match, axis=0) & live[None, :]
    earlier = (order[:, None] < order[None, :]).astype(BF)
    before = dot(chosen.astype(BF), earlier)
    slot = jnp.where(chosen & (before < cap), before, -1.0)
    packed = jnp.concatenate([slot.reshape(ne, here, tokens), weight_e.reshape(ne, here, tokens)], axis=1)
    tables = rotary_tables(nh * seg)
    x, grad = local(layer_input), local(out_grad)
    xf = x.astype(F32)
    gain_a, gain_m = attn_gain.reshape(1, width), moe_gain.reshape(1, width)
    fast = nh == 4 and ne == 8
    if fast:
        gathered, qkv, lse, heads_in, o_full, w_pieces, mid, pack, d_rows, x_rows = front(
            seq_lengths, x, grad, query_matrix, key_matrix, value_matrix, output_matrix, packed, gain_a, gain_m, tables, nh, nseq, cap)
        o_parts = o_full.reshape(nh, groups * 128, width)
    else:
        wq = query_matrix.reshape(width, groups, 128)
        wk = key_matrix.reshape(width, groups, HEAD)
        wv = value_matrix.reshape(width, groups, HEAD)
        w_local = jnp.concatenate([wq, wk, wv], axis=2).reshape(width, groups * 256)
        packed = lax.all_to_all(packed, "experts", split_axis=0, concat_axis=0, tiled=True)
        packed = packed[me ^ jnp.arange(ne, dtype=jnp.int32)]
        slots, weights = packed[:, :here].astype(jnp.int32), packed[:, here:]
        inv_one = lax.rsqrt(jnp.mean(xf * xf, axis=-1, keepdims=True) + EPS)
        attn_in = (xf * inv_one * attn_gain).astype(BF)
        gathered = lax.all_gather(attn_in.reshape(nseq, seg, width), "heads", axis=0)
        w_groups = jnp.transpose(w_local.reshape(width, groups, 256), (1, 0, 2))
        rows_in, rows_out = width // ne, output_matrix.shape[0] // ne
        w_piece = lax.dynamic_slice_in_dim(w_local, me * rows_in, rows_in, 0)
        o_piece = lax.dynamic_slice_in_dim(output_matrix, me * rows_out, rows_out, 0)
        o_full = lax.all_gather(o_piece, ("heads", "experts"), axis=0, tiled=True)
        w_full = lax.all_gather(w_piece, ("heads", "experts"), axis=0, tiled=True)
        w_full = w_full.reshape(nh, width, groups * 256)
        qkv, heads_out, lse = attn_forward(gathered, w_groups, seq_lengths, tables)
        heads_in = lax.all_to_all(heads_out, "heads", split_axis=0, concat_axis=0, tiled=True)
        heads_in = heads_in.reshape(nh, tokens, groups * 128)
        o_parts = o_full.reshape(nh, groups * 128, width)
        branch = jnp.einsum("ztm,zmw->tw", heads_in, o_parts, preferred_element_type=F32)
        mid = xf + branch
        inv_two = lax.rsqrt(jnp.mean(mid * mid, axis=-1, keepdims=True) + EPS)
        moe_in = (mid * inv_two * moe_gain).astype(BF)
        d_rows = gather_rows(slots, weights, plane_gather(grad, ne), cap)
        x_rows = gather_rows(slots, None, plane_gather(moe_in, ne), cap)

    if fast:
        chunks = expert_in.shape[0] * (width + expert_down.shape[1]) // CHUNK
        early, half = chunks // 8, (3 * chunks) // 8
        results, drows, sums, total = experts_send(early, pack, x_rows, d_rows, expert_in, expert_down)
        flat = sums.reshape(-1, width)
        total, d_mid, gain_two, dqkv, po, pw = middle(
            early, half, seq_lengths, total, flat, drows, pack, mid, grad, gain_m, o_parts, qkv, lse, tables,
            heads_in, gathered)
        total, out, x_grad, gains, o_grad, q_grad, k_grad, v_grad = last(
            early + half, chunks - early - half, total, flat, results, pack, mid, dqkv, w_pieces, x, d_mid, gain_a, gain_two, po, pw)
        gain_one, gain_two = gains[0], gains[1]
        grad_in, grad_down = widen(total.reshape(sums.shape), expert_down.shape[1])
    else:
        results, drows, sums = experts_call(slots, weights, x_rows, d_rows, expert_in, expert_down)
        slots_t = jnp.swapaxes(slots, 1, 2)
        d_parts = combine(slots_t, drows)
        moe_parts = combine(slots_t, results)
        totals = heads_sum(sums, z, nh)
        grad_in, grad_down = totals[:, :width], totals[:, width:]
        d_moe = plane_scatter(d_parts, ne)
        moe_sum = plane_scatter(moe_parts, ne)
        out = (mid + moe_sum).astype(BF)
        zed = moe_gain * d_moe
        d_mid = grad.astype(F32) + inv_two * zed - mid * (inv_two ** 3 * jnp.mean(zed * mid, axis=-1, keepdims=True))
        gain_two = jnp.sum(d_moe * mid * inv_two, axis=0)
        d_branch = d_mid.astype(BF)
        d_heads = jnp.einsum("tw,zmw->ztm", d_branch, o_parts, preferred_element_type=F32).astype(BF)
        d_heads = d_heads.reshape(nh, nseq, seg, groups * 128)
        d_heads = lax.all_to_all(d_heads, "heads", split_axis=0, concat_axis=0, tiled=True)
        dqkv = attn_backward(qkv, d_heads, lse, seq_lengths, tables)
        dqkv = dqkv.reshape(nh, tokens, groups * 256)
        back = lax.all_to_all(dqkv, "heads", split_axis=0, concat_axis=0, tiled=True)
        d_attn = jnp.einsum("ztc,zmc->tm", back, w_full, preferred_element_type=F32)
        o_grad, w_grad = weight_sums(heads_in, d_branch, gathered, dqkv, ne)
        wed = attn_gain * d_attn
        x_grad = d_mid + inv_one * wed - xf * (inv_one ** 3 * jnp.mean(wed * xf, axis=-1, keepdims=True))
        gain_one = jnp.sum(d_attn * xf * inv_one, axis=0)
        gain_one, gain_two = lax.psum((gain_one, gain_two), ("heads", "experts"))
        w_grad = w_grad.reshape(width, groups, 256)
        q_grad = w_grad[:, :, :128].reshape(query_matrix.shape)
        k_grad = w_grad[:, :, 128:192].reshape(key_matrix.shape)
        v_grad = w_grad[:, :, 192:].reshape(value_matrix.shape)
    return (
        unlocal(out),
        unlocal(x_grad),
        gain_one,
        gain_two,
        q_grad,
        k_grad,
        v_grad,
        o_grad,
        grad_in,
        grad_down,
    )


def solution(mesh):
    rows = P("heads", "experts", None)
    in_specs = (
        rows,
        P("experts"),
        rows,
        rows,
        P("heads", "experts"),
        P(),
        P(),
        P(None, "heads"),
        P(None, "heads"),
        P(None, "heads"),
        P("heads", None),
        P("experts", None, None),
        P("experts", None, None),
        rows,
    )
    out_specs = (
        rows,
        rows,
        P(),
        P(),
        P(None, "heads"),
        P(None, "heads"),
        P(None, "heads"),
        P("heads", None),
        P("experts", None, None),
        P("experts", None, None),
    )
    return jax.shard_map(body, mesh=mesh, in_specs=in_specs, out_specs=out_specs, check_vma=False)
```

```python
import functools
import math

import jax
import jax.numpy as jnp
import numpy as np
from jax import lax
from jax.experimental import pallas as pl
from jax.experimental.pallas import tpu as pltpu
from jax.sharding import PartitionSpec as P

HEAD = 64
EXPERTS = 32
EPS = 1e-06
BF = jnp.bfloat16
F32 = jnp.float32
SCALE = HEAD ** (-0.5)
NEG = -1e30
VMEM = 63 * 1024 * 1024
MESH = pl.DeviceIdType.MESH
DMA = pltpu.SemaphoreType.DMA


def dot(a, b):
    return jnp.dot(a, b, preferred_element_type=F32)


def dot_nt(a, b):
    return lax.dot_general(a, b, (((1,), (1,)), ((), ())), preferred_element_type=F32)


def dot_tn(a, b):
    return lax.dot_general(a, b, (((0,), (0,)), ((), ())), preferred_element_type=F32)


def params(n):
    return pltpu.CompilerParams(
        dimension_semantics=("arbitrary",) * n, vmem_limit_bytes=VMEM
    )


def swap_halves(v):
    lane = lax.broadcasted_iota(jnp.int32, v.shape, 1)
    return jnp.where(lane % 64 < 32, pltpu.roll(v, 96, 1), pltpu.roll(v, 32, 1))


def attn_mask(offset, n, block, length):
    key = lax.broadcasted_iota(jnp.int32, (n, block), 0)
    query = lax.broadcasted_iota(jnp.int32, (n, block), 1) + offset
    return (key <= query) & (key < length)


def two_heads(v):
    return jnp.concatenate([v[:, :HEAD], v[:, HEAD:]], axis=0)


def untwo(vt, block):
    return jnp.concatenate([vt[:, :block], vt[:, block:]], axis=0).T


def fwd_kernel(len_ref, x_ref, w_ref, cq, sq, ckv, skv, qkv_ref, head_ref, lse_ref):
    nh, _, seg, width = x_ref.shape
    full = nh * seg
    block = seg
    length = len_ref[pl.program_id(0)]
    lin = dot(x_ref[...].reshape(full, width), w_ref[0])
    ql, kvl = lin[:, :128], lin[:, 128:]
    q = (ql * cq[...] + swap_halves(ql) * sq[...]).astype(BF)
    kvr = kvl * ckv[...] + swap_halves(kvl) * skv[...]
    kv = kvr.astype(BF)
    qkv_ref[0, 0, :, :128] = q
    qkv_ref[0, 0, :, 128:] = kv
    k = kv[:, :HEAD]
    vt = kvr.T[HEAD:].astype(BF)
    for i in range(nh):
        n = (i + 1) * block
        q2 = two_heads(q[i * block : n])
        s = dot_nt(k[:n], q2)
        mask = attn_mask(i * block, n, block, length)
        s = jnp.where(jnp.concatenate([mask, mask], axis=1), s * SCALE, NEG)
        m = jnp.max(s, axis=0, keepdims=True)
        e = jnp.exp(s - m)
        total = jnp.sum(e, axis=0, keepdims=True)
        p = (e * (1.0 / total)).astype(BF)
        lse_ref[0, 0, i : i + 1, :] = m + jnp.log(total)
        head_ref[i, 0] = untwo(dot(vt[:, :n], p), block).astype(BF)


def attn_forward(x, w, lengths, tables):
    nh, nseq, seg, width = x.shape
    groups = w.shape[0]
    full = nh * seg
    cq, sq, ckv, skv = tables
    tab = pl.BlockSpec((full, 128), lambda s, g: (0, 0))
    return pl.pallas_call(
        fwd_kernel,
        grid=(nseq, groups),
        in_specs=[
            pl.BlockSpec(memory_space=pltpu.SMEM),
            pl.BlockSpec((nh, 1, seg, width), lambda s, g: (0, s, 0, 0)),
            pl.BlockSpec((1, width, 256), lambda s, g: (g, 0, 0)),
            tab,
            tab,
            tab,
            tab,
        ],
        out_specs=[
            pl.BlockSpec((1, 1, full, 256), lambda s, g: (s, g, 0, 0)),
            pl.BlockSpec((nh, 1, seg, 128), lambda s, g: (0, s, 0, g)),
            pl.BlockSpec((1, 1, nh, 2 * seg), lambda s, g: (s, g, 0, 0)),
        ],
        out_shape=[
            jax.ShapeDtypeStruct((nseq, groups, full, 256), BF),
            jax.ShapeDtypeStruct((nh, nseq, seg, groups * 128), BF),
            jax.ShapeDtypeStruct((nseq, groups, nh, 2 * seg), F32),
        ],
        compiler_params=params(2),
        cost_estimate=pl.CostEstimate(flops=6 * 10**9, bytes_accessed=12 * 2**20, transcendentals=10**7),
        name="attn_forward",
    )(lengths, x, w, cq, sq, ckv, skv)


def bwd_piece(q, kv, heads, lses, length, tables, dkv_ref, put):
    cq, sq, ckv, skv = tables
    full, block = q.shape[0], lses(0).shape[1] // 2
    k, v = kv[:, :HEAD], kv[:, HEAD:]
    kt = kv.astype(F32).T[:HEAD].astype(BF)
    dkv_ref[...] = jnp.zeros_like(dkv_ref)
    for i in range(full // block):
        n = (i + 1) * block
        rows = pl.ds(i * block, block)
        mask = attn_mask(i * block, n, block, length)
        grads = []
        for h in range(2):
            qh = q[i * block : n, h * HEAD : (h + 1) * HEAD]
            doh = heads(i)[:, h * HEAD : (h + 1) * HEAD]
            s = dot_nt(k[:n], qh)
            p = jnp.exp(jnp.where(mask, s * SCALE - lses(i)[:, h * block : (h + 1) * block], NEG))
            dp = dot_nt(v[:n], doh)
            delta = jnp.sum(p * dp, axis=0, keepdims=True)
            ds = (p * (dp - delta) * SCALE).astype(BF)
            dkv_ref[:n, :HEAD] += dot(ds, qh)
            dkv_ref[:n, HEAD:] += dot(p.astype(BF), doh)
            grads.append(dot(kt[:, :n], ds))
        dq = jnp.concatenate(grads, axis=0).T
        dq = dq * cq[rows, :] - swap_halves(dq) * sq[rows, :]
        put(i, 0, dq.astype(BF))
    dkv = dkv_ref[...]
    dkv = (dkv * ckv[...] - swap_halves(dkv) * skv[...]).astype(BF)
    for i in range(full // block):
        put(i, 128, dkv[i * block : (i + 1) * block])


def bwd_kernel(len_ref, qkv_ref, do_ref, lse_ref, cq, sq, ckv, skv, out_ref, dkv_ref):
    def put(i, lo, v):
        out_ref[i, 0, :, lo : lo + 128] = v

    bwd_piece(
        qkv_ref[0, 0, :, :128],
        qkv_ref[0, 0, :, 128:],
        lambda i: do_ref[i, 0],
        lambda i: lse_ref[0, 0, i : i + 1, :],
        len_ref[pl.program_id(0)],
        (cq, sq, ckv, skv),
        dkv_ref,
        put,
    )


def attn_backward(qkv, d_head, lse, lengths, tables):
    nseq, groups, full, _ = qkv.shape
    nh, _, seg, _ = d_head.shape
    cq, sq, ckv, skv = tables
    tab = pl.BlockSpec((full, 128), lambda s, g: (0, 0))
    return pl.pallas_call(
        bwd_kernel,
        grid=(nseq, groups),
        in_specs=[
            pl.BlockSpec(memory_space=pltpu.SMEM),
            pl.BlockSpec((1, 1, full, 256), lambda s, g: (s, g, 0, 0)),
            pl.BlockSpec((nh, 1, seg, 128), lambda s, g: (0, s, 0, g)),
            pl.BlockSpec((1, 1, nh, 2 * seg), lambda s, g: (s, g, 0, 0)),
            tab,
            tab,
            tab,
            tab,
        ],
        out_specs=pl.BlockSpec((nh, 1, seg, 256), lambda s, g: (0, s, 0, g)),
        out_shape=jax.ShapeDtypeStruct((nh, nseq, seg, groups * 256), BF),
        scratch_shapes=[pltpu.VMEM((full, 128), F32)],
        compiler_params=params(2),
        cost_estimate=pl.CostEstimate(flops=12 * 10**9, bytes_accessed=8 * 2**20, transcendentals=10**7),
        name="attn_backward",
    )(lengths, qkv, d_head, lse, cq, sq, ckv, skv)


def rotary_tables(length):
    half = HEAD // 2
    exponent = np.arange(half, dtype=np.float32) * np.float32(-2.0 * math.log(10000.0) / HEAD)
    angles = np.arange(length, dtype=np.float32)[:, None] * np.exp(exponent)[None, :]
    cos, sin = np.cos(angles), np.sin(angles)
    c1 = np.concatenate([cos, cos], axis=1)
    s1 = np.concatenate([-sin, sin], axis=1)
    cq = np.concatenate([c1, c1], axis=1)
    sq = np.concatenate([s1, s1], axis=1)
    ckv = np.concatenate([c1, np.ones_like(c1)], axis=1)
    skv = np.concatenate([s1, np.zeros_like(s1)], axis=1)
    return tuple(jnp.asarray(t, F32) for t in (cq, sq, ckv, skv))


def pick_rows(slots, cap):
    tokens = slots.shape[1]
    index = lax.broadcasted_iota(jnp.int32, (cap, tokens), 0)
    return [index == slots[j : j + 1, :] for j in range(slots.shape[0])]


def gather_kernel(weighted, slot_ref, *refs):
    if weighted:
        weight_ref, tok_ref, out_ref = refs
    else:
        tok_ref, out_ref = refs[0], refs[-1]
    cap = out_ref.shape[2]
    hits = pick_rows(slot_ref[0], cap)
    rows = dot(jnp.concatenate([h.astype(F32) for h in hits], axis=0).astype(BF), tok_ref[0])
    for j, hit in enumerate(hits):
        part = rows[j * cap : (j + 1) * cap]
        if weighted:
            part = part * jnp.sum(jnp.where(hit, weight_ref[0, j : j + 1, :], 0.0), axis=1, keepdims=True)
        out_ref[j, 0] = part.astype(BF)


def gather_rows(slots, weights, tokens, cap):
    sources, here, count = slots.shape
    width = tokens.shape[-1]
    small = pl.BlockSpec((1, here, count), lambda s: (s, 0, 0))
    weighted = weights is not None
    return pl.pallas_call(
        functools.partial(gather_kernel, weighted),
        grid=(sources,),
        in_specs=[small] + [small] * weighted + [pl.BlockSpec((1, count, width), lambda s: (s, 0, 0))],
        out_specs=pl.BlockSpec((here, 1, cap, width), lambda s: (0, s, 0, 0)),
        out_shape=jax.ShapeDtypeStruct((here, sources, cap, width), BF),
        compiler_params=params(1),
        cost_estimate=pl.CostEstimate(
            flops=2 * sources * here * cap * count * width,
            bytes_accessed=2 * sources * width * (count + here * cap),
            transcendentals=0,
        ),
        name="gather_rows",
    )(*([slots] + [weights] * weighted + [tokens]))


def expert_kernel(steps, slot_ref, weight_ref, x_ref, d_ref, win_ref, wdown_ref,
                  out_ref, drow_ref, grad_ref, hid_ref, dgu_ref, *acc):
    _, sources, cap, width = x_ref.shape
    ff = wdown_ref.shape[1]
    per = 2 if sources % 2 == 0 else 1
    win, wdown = win_ref[0], wdown_ref[0]
    for c in range(sources // per):
        rows = slice(c * per * cap, (c + 1) * per * cap)
        x = x_ref[0, c * per : (c + 1) * per].reshape(per * cap, width)
        d = d_ref[0, c * per : (c + 1) * per].reshape(per * cap, width)
        gu = dot(x, win)
        gate, up = gu[:, :ff], gu[:, ff:]
        sig = 1.0 / (1.0 + jnp.exp(-gate))
        act = gate * sig
        hidden = (act * up).astype(BF)
        hid_ref[rows, :] = hidden
        result = dot(hidden, wdown).astype(BF).astype(F32)
        for b in range(per):
            hit = pick_rows(slot_ref[c * per + b, 0], cap)[0]
            w = jnp.sum(jnp.where(hit, weight_ref[c * per + b, 0], 0.0), axis=1, keepdims=True)
            out_ref[0, c * per + b] = (result[b * cap : (b + 1) * cap] * w).astype(BF)
        dh = dot_nt(d, wdown)
        dgu_ref[rows, :ff] = (dh * up * (sig * (1.0 + gate * (1.0 - sig)))).astype(BF)
        dgu_ref[rows, ff:] = (dh * act).astype(BF)
        drow = dot_nt(dgu_ref[rows, :], win).astype(BF)
        for b in range(per):
            drow_ref[0, c * per + b] = drow[b * cap : (b + 1) * cap]
    x = x_ref[0].reshape(sources * cap, width)
    d = d_ref[0].reshape(sources * cap, width)
    gin = dot_tn(x, dgu_ref[...])
    gdown = dot_tn(hid_ref[...], d)
    if steps == 1:
        grad_ref[0, :width] = gin.astype(BF)
        grad_ref[0, width:] = gdown.astype(BF)
    else:
        ain, adown = acc
        step = pl.program_id(1)

        @pl.when(step == 0)
        def _():
            ain[...] = jnp.zeros_like(ain)
            adown[...] = jnp.zeros_like(adown)

        ain[...] += gin
        adown[...] += gdown

        @pl.when(step == steps - 1)
        def _():
            grad_ref[0, :width] = ain[...].astype(BF)
            grad_ref[0, width:] = adown[...].astype(BF)


def experts_call(slots, weights, x, d, win, wdown):
    count, sources, cap, width = x.shape
    tokens = slots.shape[-1]
    ff = wdown.shape[1]
    chunk = min(sources, 8)
    steps = sources // chunk
    small = pl.BlockSpec((chunk, 1, 1, tokens), lambda j, r: (r, j, 0, 0))
    rows = pl.BlockSpec((1, chunk, cap, width), lambda j, r: (j, r, 0, 0))
    rows_out = pl.BlockSpec((1, chunk, cap, width), lambda j, r: (j, r, 0, 0))
    scratch = [pltpu.VMEM((chunk * cap, ff), BF), pltpu.VMEM((chunk * cap, 2 * ff), BF)]
    if steps > 1:
        scratch += [pltpu.VMEM((width, 2 * ff), F32), pltpu.VMEM((ff, width), F32)]
    shape = jax.ShapeDtypeStruct((count, sources, cap, width), BF)
    return pl.pallas_call(
        functools.partial(expert_kernel, steps),
        grid=(count, steps),
        in_specs=[
            small,
            small,
            rows,
            rows,
            pl.BlockSpec((1, width, 2 * ff), lambda j, r: (j, 0, 0)),
            pl.BlockSpec((1, ff, width), lambda j, r: (j, 0, 0)),
        ],
        out_specs=[
            rows_out,
            rows_out,
            pl.BlockSpec((1, width + ff, width), lambda j, r: (j, 0, 0)),
        ],
        out_shape=[
            shape,
            shape,
            jax.ShapeDtypeStruct((count, width + ff, width), BF),
        ],
        scratch_shapes=scratch,
        compiler_params=params(2),
        cost_estimate=pl.CostEstimate(
            flops=2 * count * sources * cap * width * ff * 9,
            bytes_accessed=8 * count * sources * cap * width + 12 * count * width * ff,
            transcendentals=count * sources * cap * ff,
        ),
        name="experts",
    )(slots[:, :, None, :], weights[:, :, None, :], x, d, win, wdown)


def combine_kernel(slot_ref, row_ref, out_ref):
    slots = slot_ref[0]
    count, here = slots.shape
    cap = row_ref.shape[2]
    lane = lax.broadcasted_iota(jnp.int32, (count, here * cap), 1)
    hot = None
    for j in range(here):
        col = slots[:, j : j + 1]
        hit = lane == jnp.where(col >= 0, col + j * cap, -1)
        hot = hit if hot is None else hot | hit
    hot = hot.astype(F32).astype(BF)
    out_ref[0] = dot(hot, row_ref[...].reshape(here * cap, row_ref.shape[3])).astype(BF)


def combine(slots_t, rows):
    sources, count, here = slots_t.shape
    _, _, cap, width = rows.shape
    return pl.pallas_call(
        combine_kernel,
        grid=(sources,),
        in_specs=[
            pl.BlockSpec((1, count, here), lambda s: (s, 0, 0)),
            pl.BlockSpec((here, 1, cap, width), lambda s: (0, s, 0, 0)),
        ],
        out_specs=pl.BlockSpec((1, count, width), lambda s: (s, 0, 0)),
        out_shape=jax.ShapeDtypeStruct((sources, count, width), BF),
        compiler_params=params(1),
        cost_estimate=pl.CostEstimate(
            flops=2 * sources * here * cap * count * width,
            bytes_accessed=2 * sources * width * (count + here * cap),
            transcendentals=0,
        ),
        name="combine",
    )(slots_t, rows)


def swap(x, bit, n):
    return lax.ppermute(x, "experts", [(i, i ^ bit) for i in range(n)])


def plane_gather(x, n):
    if n != 8:
        whole = lax.all_gather(x, "experts", axis=0)
        order = lax.axis_index("experts") ^ jnp.arange(n, dtype=jnp.int32)
        return whole[order]
    got = {0: x}
    for r in (2, 4, 6):
        got[r] = swap(x, r, n)
    for r in (0, 2, 4, 6):
        got[r + 1] = swap(got[r], 1, n)
    return jnp.stack([got[r] for r in range(n)], axis=0)


def plane_scatter(parts, n):
    if n != 8:
        order = lax.axis_index("experts") ^ jnp.arange(n, dtype=jnp.int32)
        return lax.psum_scatter(parts[order].astype(F32), "experts", scatter_dimension=0)
    odd = swap(parts[1::2], 1, n)
    both = [parts[2 * i].astype(F32) + odd[i].astype(F32) for i in range(4)]
    total = both[0]
    for i in (1, 2, 3):
        total = total + swap(both[i].astype(BF), 2 * i, n).astype(F32)
    return total


def heads_sum(x, z, nh):
    if nh != 4:
        return lax.psum(x.astype(F32), "heads")
    first = lax.ppermute(x, "heads", [(0, 1), (3, 2)])
    pair = (x.astype(F32) + first.astype(F32)).astype(BF)
    second = lax.ppermute(pair, "heads", [(1, 2), (2, 1)])
    total = (pair.astype(F32) + second.astype(F32)).astype(BF)
    third = lax.ppermute(total, "heads", [(1, 0), (2, 3)])
    return jnp.where((z == 1) | (z == 2), total, third).astype(F32)


def weight_sums(heads_in, d_branch, gathered, dqkv, ne):
    nh, tokens, part = heads_in.shape
    width, cols = d_branch.shape[1], dqkv.shape[2]
    col, row = width // ne, width // ne
    o = jnp.einsum("ztm,tew->ezmw", heads_in, d_branch.reshape(tokens, ne, col), preferred_element_type=F32)
    w = jnp.einsum("ztm,ztc->mc", gathered.reshape(nh, tokens, width), dqkv, preferred_element_type=F32)
    cut = cols // col
    w = jnp.swapaxes(w.reshape(ne, row, cut, col), 1, 2).reshape(ne, cut * row, col)
    both = jnp.concatenate([o.reshape(ne, nh * part, col), w], axis=1)
    both = lax.psum_scatter(both, "experts", scatter_dimension=0)
    o, w = both[: nh * part], both[nh * part :]
    o = lax.psum_scatter(o.reshape(nh, part, col), "heads", scatter_dimension=0)
    return weight_split(lax.all_gather(jnp.concatenate([o, w], axis=0), "experts", axis=0), part, cols)


def weight_split(both, part, cols):
    ne, _, col = both.shape
    width, row, cut = ne * col, col, cols // col
    o = jnp.swapaxes(both[:, :part], 0, 1).reshape(part, width)
    w = jnp.swapaxes(both[:, part:].reshape(ne, cut, row, col), 1, 2)
    return o, w.reshape(width, cols)


CHUNK = 128
LAG = 2
FLIGHT = 3


def remote(src, dst, send, recv, axis, index):
    return pltpu.make_async_remote_copy(
        src_ref=src, dst_ref=dst, send_sem=send, recv_sem=recv,
        device_id={axis: index}, device_id_type=MESH,
    )


def greet(nh, masks):
    z, me = lax.axis_index("heads"), lax.axis_index("experts")
    bar = pltpu.get_barrier_semaphore()
    for d in range(1, nh):
        pl.semaphore_signal(bar, inc=1, device_id={"heads": lax.rem(z + d, nh)}, device_id_type=MESH)
    for r in masks:
        pl.semaphore_signal(bar, inc=1, device_id={"experts": me ^ r}, device_id_type=MESH)
    pl.semaphore_wait(bar, nh - 1 + len(masks))


class Chain:
    def __init__(self, src, out, scratch, first, count):
        self.src, self.out, self.first, self.count = src, out, first, count
        self.flight = min(FLIGHT, count)
        self.a, self.b, self.buf, self.s1, self.r1, self.s2, self.r2, self.ls, self.os = scratch
        z = lax.axis_index("heads")
        self.mid = (z == 1) | (z == 2)
        self.outer = jnp.where(z == 0, 1, jnp.where(z == 1, 0, jnp.where(z == 2, 3, 2)))
        self.inner = jnp.where(z == 1, 2, jnp.where(z == 2, 1, z))

    def piece(self, k):
        return self.src.at[pl.ds((self.first + k) * CHUNK, CHUNK)]

    def load(self, k):
        return pltpu.make_async_copy(self.piece(k), self.buf.at[lax.rem(k, 2)], self.ls.at[lax.rem(k, 2)])

    def store(self, ref, k):
        return pltpu.make_async_copy(ref.at[k], self.out.at[pl.ds((self.first + k) * CHUNK, CHUNK)], self.os.at[k])

    def up(self, k):
        return remote(self.piece(k), self.a.at[k], self.s1.at[k], self.r1.at[k], "heads", self.outer)

    def across(self, k):
        return remote(self.a.at[k], self.b.at[k], self.s2.at[k], self.r2.at[k], "heads", self.inner)

    def down(self, k):
        return remote(self.b.at[k], self.a.at[k], self.s1.at[k], self.r1.at[k], "heads", self.outer)

    def begin(self):
        @pl.when(self.mid)
        def _():
            self.load(0).start()

        @pl.when(jnp.logical_not(self.mid))
        def _():
            @pl.loop(0, self.flight)
            def _(k):
                self.up(k).start()

    def pair(self, k):
        @pl.when(k + 1 < self.count)
        def _():
            self.load(k + 1).start()

        self.load(k).wait()
        self.up(k).wait_recv()
        own = self.buf[lax.rem(k, 2)].astype(F32)
        self.a[k] = (self.a[k].astype(F32) + own).astype(BF)
        self.across(k).start()

    def total(self, j):
        self.across(j).wait_recv()
        self.b[j] = (self.a[j].astype(F32) + self.b[j].astype(F32)).astype(BF)
        self.down(j).start()
        self.store(self.b, j).start()

    def take(self, j):
        self.down(j).wait_recv()
        self.store(self.a, j).start()

    def step(self, k, lag=LAG):
        n = self.count

        @pl.when(self.mid)
        def _():
            @pl.when(k < n)
            def _():
                self.pair(k)

            @pl.when((k >= lag) & (k < n + lag))
            def _():
                self.total(k - lag)

        @pl.when(jnp.logical_not(self.mid))
        def _():
            @pl.when(k + self.flight < n)
            def _():
                self.up(k).wait_send()
                self.up(k + self.flight).start()

            @pl.when((k >= lag + 2) & (k < n + lag + 2))
            def _():
                self.take(k - lag - 2)

    def rest(self, k):
        n = self.count

        @pl.when(self.mid)
        def _():
            @pl.loop(min(max(k - LAG, 0), n), min(max(k - 1, 0), n))
            def _(j):
                self.total(j)

        @pl.when(jnp.logical_not(self.mid))
        def _():
            @pl.loop(min(max(k - LAG - 2, 0), n), min(max(k - 3, 0), n))
            def _(j):
                self.take(j)

        @pl.loop(k, n + 3)
        def _(i):
            self.step(i, 1)

    def run(self, first, last):
        @pl.loop(first, last)
        def _(k):
            self.step(k)

    def finish(self):
        n = self.count

        @pl.when(self.mid)
        def _():
            @pl.loop(0, n)
            def _(k):
                self.across(k).wait_send()
                self.down(k).wait_send()
                self.store(self.b, k).wait()

        @pl.when(jnp.logical_not(self.mid))
        def _():
            @pl.loop(n - self.flight, n)
            def _(k):
                self.up(k).wait_send()

            @pl.loop(0, n)
            def _(k):
                self.store(self.a, k).wait()


def chain_scratch(count, width):
    return [
        pltpu.VMEM((count, CHUNK, width), BF),
        pltpu.VMEM((count, CHUNK, width), BF),
        pltpu.VMEM((2, CHUNK, width), BF),
        DMA((count,)),
        DMA((count,)),
        DMA((count,)),
        DMA((count,)),
        DMA((2,)),
        DMA((count,)),
    ]


def experts_send_kernel(count, pack_ref, x_ref, d_ref, win_ref, wdown_ref,
                        out_ref, drow_ref, grad_ref, total_ref, hid_ref, dgu_ref, early_ref, *scratch):
    j, last_j = pl.program_id(0), pl.num_programs(0) - 1
    nh = lax.axis_size("heads")
    _, sources, cap, width = x_ref.shape
    here = pack_ref.shape[1] // 2
    ff = wdown_ref.shape[1]
    chain = Chain(early_ref, total_ref, scratch, 0, count)
    per = 2
    parts = sources // per

    def chain_step(t):
        @pl.when(j > 0)
        def _():
            chain.step((j - 1) * 3 + t, 1)

    @pl.when(j == 0)
    def _():
        greet(nh, ())

    win, wdown = win_ref[0], wdown_ref[0]
    for c in range(parts):
        rows = slice(c * per * cap, (c + 1) * per * cap)
        x = x_ref[0, c * per : (c + 1) * per].reshape(per * cap, width)
        d = d_ref[0, c * per : (c + 1) * per].reshape(per * cap, width)
        gu = dot(x, win)
        gate, up = gu[:, :ff], gu[:, ff:]
        sig = 1.0 / (1.0 + jnp.exp(-gate))
        act = gate * sig
        hidden = (act * up).astype(BF)
        hid_ref[rows, :] = hidden
        result = dot(hidden, wdown).astype(BF).astype(F32)
        for b in range(per):
            s = c * per + b
            hit = pick_rows(pack_ref[s, pl.ds(j, 1)].astype(jnp.int32), cap)[0]
            w = jnp.sum(jnp.where(hit, pack_ref[s, pl.ds(here + j, 1)], 0.0), axis=1, keepdims=True)
            out_ref[0, s] = (result[b * cap : (b + 1) * cap] * w).astype(BF)
        dh = dot_nt(d, wdown)
        dgu_ref[rows, :ff] = (dh * up * (sig * (1.0 + gate * (1.0 - sig)))).astype(BF)
        dgu_ref[rows, ff:] = (dh * act).astype(BF)
        drow = dot_nt(dgu_ref[rows, :], win).astype(BF)
        for b in range(per):
            drow_ref[0, c * per + b] = drow[b * cap : (b + 1) * cap]
        if c % 2:
            chain_step(c // 2)
    gin = dot_tn(x_ref[0].reshape(sources * cap, width), dgu_ref[...]).astype(BF)
    grad_ref[0, :width] = gin
    grad_ref[0, width:] = dot_tn(hid_ref[...], d_ref[0].reshape(sources * cap, width)).astype(BF)
    chain_step(2)

    @pl.when(j == 0)
    def _():
        early_ref[...] = gin[: early_ref.shape[0]]
        chain.begin()

    @pl.when(j == last_j)
    def _():
        chain.finish()


def experts_send(count, pack, x, d, win, wdown):
    here, sources, cap, width = x.shape
    ff = wdown.shape[1]
    rows = pl.BlockSpec((1, sources, cap, width), lambda j: (j, 0, 0, 0))
    shape = jax.ShapeDtypeStruct((here, sources, cap, width), BF)
    hbm = pl.BlockSpec(memory_space=pl.ANY)
    return pl.pallas_call(
        functools.partial(experts_send_kernel, count),
        grid=(here,),
        in_specs=[
            pl.BlockSpec(memory_space=pltpu.VMEM),
            rows,
            rows,
            pl.BlockSpec((1, width, 2 * ff), lambda j: (j, 0, 0)),
            pl.BlockSpec((1, ff, width), lambda j: (j, 0, 0)),
        ],
        out_specs=[rows, rows, pl.BlockSpec((1, width + ff, width), lambda j: (j, 0, 0)), hbm],
        out_shape=[
            shape,
            shape,
            jax.ShapeDtypeStruct((here, width + ff, width), BF),
            jax.ShapeDtypeStruct((here * (width + ff), width), BF),
        ],
        scratch_shapes=[
            pltpu.VMEM((sources * cap, ff), BF),
            pltpu.VMEM((sources * cap, 2 * ff), BF),
            pltpu.VMEM((count * CHUNK, width), BF),
        ]
        + chain_scratch(count, width),
        compiler_params=pltpu.CompilerParams(
            dimension_semantics=("arbitrary",), collective_id=4, has_side_effects=True, vmem_limit_bytes=VMEM
        ),
        cost_estimate=pl.CostEstimate(
            flops=18 * here * sources * cap * width * ff,
            bytes_accessed=8 * here * sources * cap * width,
            transcendentals=here * sources * cap * ff,
        ),
        name="experts_send",
    )(pack, x, d, win, wdown)


class PlaneSum:
    order = (3, 1, 2)

    def __init__(self, rows, slots, total, scratch):
        self.rows, self.slots, self.total = rows, slots, total
        self.buf, self.odd, self.c, self.e, self.f, self.ls, self.cs, self.cr, self.fs, self.fr = scratch
        self.me = lax.axis_index("experts")
        self.here, _, self.cap, self.width = rows.shape

    def load(self, r, at):
        return [
            pltpu.make_async_copy(self.rows.at[j, r], self.buf.at[at, j], self.ls.at[at, j])
            for j in range(self.here)
        ]

    def core(self, i):
        return remote(self.odd.at[i], self.c.at[i], self.cs.at[i], self.cr.at[i], "experts", self.me ^ 1)

    def chip(self, i):
        return remote(self.e.at[i - 1], self.f.at[i - 1], self.fs.at[i - 1], self.fr.at[i - 1], "experts", self.me ^ (2 * i))

    def part(self, r, at, after, after_at):
        if after is not None:
            for c in self.load(after, after_at):
                c.start()
        slots = self.slots[r].T.astype(jnp.int32)
        lane = lax.broadcasted_iota(jnp.int32, (slots.shape[0], self.here * self.cap), 1)
        hot = None
        for j in range(self.here):
            col = slots[:, j : j + 1]
            hit = lane == jnp.where(col >= 0, col + j * self.cap, -1)
            hot = hit if hot is None else hot | hit
        for c in self.load(r, at):
            c.wait()
        rows = self.buf[at].reshape(self.here * self.cap, self.width)
        return dot(hot.astype(F32).astype(BF), rows)

    def run(self, chain=None, step=0):
        turns = [2 * i + 1 for i in self.order + (0,)] + [2 * i for i in self.order + (0,)]
        for c in self.load(turns[0], 0):
            c.start()
        for t, r in enumerate(turns):
            after = turns[t + 1] if t + 1 < len(turns) else None
            value = self.part(r, t % 2, after, (t + 1) % 2)
            i = r // 2
            if r % 2:
                self.odd[i] = value.astype(BF)
                self.core(i).start()
            else:
                self.core(i).wait_recv()
                value = value + self.c[i].astype(F32)
                if i:
                    self.e[i - 1] = value.astype(BF)
                    self.chip(i).start()
                else:
                    self.total[...] = value
            if chain is not None and t % 2:
                chain.step(step + t // 2)

    def arrive(self):
        for i in self.order:
            self.chip(i).wait_recv()

    def rows_total(self, rows):
        d = self.total[rows]
        for r in range(3):
            d = d + self.f[r, rows].astype(F32)
        return d

    def finish(self):
        for i in range(4):
            self.core(i).wait_send()
        for i in self.order:
            self.chip(i).wait_send()


def plane_scratch(here, cap, tokens, width):
    return [
        pltpu.VMEM((2, here, cap, width), BF),
        pltpu.VMEM((4, tokens, width), BF),
        pltpu.VMEM((4, tokens, width), BF),
        pltpu.VMEM((3, tokens, width), BF),
        pltpu.VMEM((3, tokens, width), BF),
        DMA((2, here)),
        DMA((4,)),
        DMA((4,)),
        DMA((3,)),
        DMA((3,)),
    ]


PLANE = 10


ROWS = 128


class Exchange:
    def __init__(self, src, dst, send, recv, nh):
        self.src, self.dst, self.ss, self.rs, self.nh = src, dst, send, recv, nh
        self.z = lax.axis_index("heads")

    def send(self, d):
        to = lax.rem(self.z + d, self.nh)
        return remote(self.src(to), self.dst(self.z), self.ss(d), self.rs(d), "heads", to)

    def start(self):
        for k in range(1, self.nh):
            self.send(jnp.where(self.z < self.nh // 2, self.nh - k, k)).start()

    def wait_recv(self):
        for d in range(1, self.nh):
            at = lax.rem(self.z + self.nh - d, self.nh)
            remote(self.src(at), self.dst(at), self.ss(d), self.rs(d), "heads", at).wait_recv()

    def finish(self):
        for d in range(1, self.nh):
            self.send(d).wait_send()


def whole_exchange(src, dst, send, recv, nh):
    return Exchange(lambda h: src.at[h], lambda h: dst.at[h], lambda d: send.at[d], lambda d: recv.at[d], nh)


class PlaneGather:
    order = (3, 1, 2)

    def __init__(self, own, slot, sems):
        self.own, self.slot = own, slot
        self.cs, self.cr, self.ks, self.kr = sems
        self.me = lax.axis_index("experts")

    def chip(self, i, e):
        return remote(self.own, self.slot(e), self.cs.at[i], self.cr.at[i], "experts", self.me ^ (2 * i))

    def core(self, i, src, e):
        return remote(src, self.slot(e), self.ks.at[i], self.kr.at[i], "experts", self.me ^ 1)

    def start(self):
        self.core(0, self.own, self.me).start()
        for i in self.order:
            self.chip(i, self.me).start()

    def forward(self, i):
        e = self.me ^ (2 * i)
        self.chip(i, e).wait_recv()
        self.core(i, self.slot(e), e).start()

    def core_arrive(self, i):
        e = self.me ^ 1 ^ (2 * i)
        self.core(i, self.slot(e), e).wait_recv()

    def finish(self):
        for i in range(1, 4):
            self.chip(i, self.me).wait_send()
        for i in range(4):
            self.core(i, self.own if i == 0 else self.slot(self.me ^ (2 * i)), self.me).wait_send()


GATHER = 4


def gather_sems():
    return [DMA((4,)), DMA((4,)), DMA((4,)), DMA((4,))]


class Picker:
    def __init__(self, pack, stage, sems, here, cap):
        self.pack, self.stage, self.sems, self.here, self.cap = pack, stage, sems, here, cap
        self.turn, self.pending = 0, {}

    def pick(self, r, tokens, out, weighted):
        at = self.turn % 2
        self.turn += 1
        info = self.pack[r]
        slots = info.astype(jnp.int32)
        index = lax.broadcasted_iota(jnp.int32, (self.cap, slots.shape[1]), 0)
        hits = [index == slots[j : j + 1] for j in range(self.here)]
        rows = dot(jnp.concatenate([h.astype(F32) for h in hits], axis=0).astype(BF), tokens)
        for c in self.pending.get(at, []):
            c.wait()
        for j, hit in enumerate(hits):
            part = rows[j * self.cap : (j + 1) * self.cap]
            if weighted:
                w = info[self.here + j : self.here + j + 1]
                part = part * jnp.sum(jnp.where(hit, w, 0.0), axis=1, keepdims=True)
            self.stage[at, j] = part.astype(BF)
        self.pending[at] = [
            pltpu.make_async_copy(self.stage.at[at, j], out.at[j, r], self.sems.at[at, j])
            for j in range(self.here)
        ]
        for c in self.pending[at]:
            c.start()

    def finish(self):
        for copies in self.pending.values():
            for c in copies:
                c.wait()


def front_kernel(len_ref, x_ref, og_ref, wq_ref, wk_ref, wv_ref, om_ref, pk_ref, again_ref, mgain_ref, cq, sq, ckv, skv,
                 xg_out, qkv_out, lse_ref, hin_out, of_out, wz_ref, mid_out, pack_ref, drows_ref, xrows_ref,
                 xg_ref, qkv_ref, hin_ref, of_ref, mid_ref, outs, w_ref, hs, ogb, mt, stage, ls, lr, ps, pr, hss, hrs, os_, or_, ws, wr, ss, *sems):
    nh, tokens, width = xg_ref.shape
    nseq, groups, full, _ = qkv_ref.shape
    ne = ogb.shape[0]
    seg = tokens // nseq
    here, _, cap, _ = drows_ref.shape
    z, me = lax.axis_index("heads"), lax.axis_index("experts")
    og = PlaneGather(og_ref, lambda e: ogb.at[e], sems[:GATHER])
    og_o = PlaneGather(of_ref.at[:, me], lambda e: of_ref.at[:, e], sems[GATHER : 2 * GATHER])

    def moe(p):
        at = pl.ds(p * seg, seg)
        return PlaneGather(mt.at[me, at], lambda e: mt.at[e, at], sems[(2 + p) * GATHER : (3 + p) * GATHER])

    moes = [moe(p) for p in range(nseq)]

    def heads(p):
        at = pl.ds(p * seg, seg)
        return Exchange(
            lambda h: hs.at[h, at], lambda h: hin_ref.at[h, at], lambda d: hss.at[p, d], lambda d: hrs.at[p, d], nh)

    picker = Picker(pack_ref, stage, ss, here, cap)

    @pl.loop(0, tokens // ROWS)
    def _(i):
        rows = pl.ds(i * ROWS, ROWS)
        x = x_ref[rows].astype(F32)
        inv = lax.rsqrt(jnp.mean(x * x, axis=-1, keepdims=True) + EPS)
        xg_ref[z, rows] = (x * inv * again_ref[...]).astype(BF)

    greet(nh, tuple(range(1, ne)))
    for g in range(groups):
        head = slice(g * HEAD, (g + 1) * HEAD)
        w_ref[:, g * 256 : g * 256 + 128] = wq_ref[:, g * 128 : (g + 1) * 128]
        w_ref[:, g * 256 + 128 : (g + 1) * 256] = jnp.concatenate([wk_ref[:, head], wv_ref[:, head]], axis=1)

    def hop(way, t, p, s, to):
        ref = xg_ref.at[s, pl.ds(p * seg, seg)]
        return remote(ref, ref, ls.at[way, t, p], lr.at[s, p], "heads", to)

    right, left = jnp.minimum(z + 1, nh - 1), jnp.maximum(z - 1, 0)
    for p in range(nseq):
        @pl.when(z < nh - 1)
        def _():
            hop(0, 0, p, z, right).start()

        @pl.when(z > 0)
        def _():
            hop(1, 0, p, z, left).start()

    def info(r):
        return remote(pk_ref.at[me ^ r], pack_ref.at[r], ps.at[r], pr.at[r], "experts", me ^ r)

    rows_o, rows_w = of_ref.shape[2], wz_ref.shape[1]
    of_ref[z, me] = om_ref[pl.ds(pl.multiple_of(me * rows_o, rows_o), rows_o)]
    wz_ref[z] = w_ref[pl.ds(pl.multiple_of(me * rows_w, rows_w), rows_w)]
    ofx = Exchange(lambda h: of_ref.at[z, me], lambda h: of_ref.at[h, me], lambda d: os_.at[d], lambda d: or_.at[d], nh)
    wzx = Exchange(lambda h: wz_ref.at[z], lambda h: wz_ref.at[h], lambda d: ws.at[d], lambda d: wr.at[d], nh)
    ofx.start()
    for r in range(1, ne):
        info(r).start()
    og.start()
    pack_ref[0] = pk_ref[me]

    def project(s, p):
        x = xg_ref[s, pl.ds(p * seg, seg)]
        at = pl.ds(s * seg, seg)
        for g in range(groups):
            lin = dot(x, w_ref[:, g * 256 : (g + 1) * 256])
            q, kv = lin[:, :128], lin[:, 128:]
            qkv_ref[p, g, at, :128] = (q * cq[at] + swap_halves(q) * sq[at]).astype(BF)
            qkv_ref[p, g, at, 128:] = (kv * ckv[at] + swap_halves(kv) * skv[at]).astype(BF)

    @pl.loop(0, nseq)
    def _(p):
        project(z, p)

    def round_of(t, then=None):
        @pl.loop(0, nseq)
        def _(p):
            @pl.when(z >= t)
            def _():
                s = z - t
                hop(0, t, p, s, left).wait_recv()

                @pl.when(z < nh - 1)
                def _():
                    hop(0, t, p, s, right).start()

                project(s, p)

            @pl.when(z + t < nh)
            def _():
                s = z + t
                hop(1, t, p, s, right).wait_recv()

                @pl.when(z > 0)
                def _():
                    hop(1, t, p, s, left).start()

                project(s, p)

            if then is not None:
                then(p)

    picker.pick(0, og_ref[...], drows_ref, True)
    round_of(1)
    for r in range(1, ne):
        info(r).wait_recv()
    og.core_arrive(0)
    picker.pick(1, ogb[me ^ 1], drows_ref, True)
    round_of(2)
    for i in og.order:
        og.forward(i)
    for i in og.order:
        picker.pick(2 * i, ogb[me ^ (2 * i)], drows_ref, True)
    ofx.wait_recv()
    og_o.start()

    def attend(p):
        length = len_ref[p]
        at = pl.ds(p * seg, seg)
        for g in range(groups):
            q = qkv_ref[p, g, :, :128]
            kv = qkv_ref[p, g, :, 128:]
            k = kv[:, :HEAD]
            vt = kv.astype(F32).T[HEAD:].astype(BF)
            for i in range(nh):
                n = (i + 1) * seg
                q2 = two_heads(q[i * seg : n])
                s = dot_nt(k[:n], q2)
                mask = attn_mask(i * seg, n, seg, length)
                s = jnp.where(jnp.concatenate([mask, mask], axis=1), s * SCALE, NEG)
                m = jnp.max(s, axis=0, keepdims=True)
                e = jnp.exp(s - m)
                total = jnp.sum(e, axis=0, keepdims=True)
                prob = (e * (1.0 / total)).astype(BF)
                lse_ref[p, g, i : i + 1, :] = m + jnp.log(total)
                hs[i, at, g * 128 : (g + 1) * 128] = untwo(dot(vt[:, :n], prob), seg).astype(BF)
        hin_ref[z, at] = hs[z, at]

        @pl.when(at_end)
        def _():
            heads(p).start()

    done = [
        pltpu.make_async_copy(src, dst, outs.at[t])
        for t, (src, dst) in enumerate(
            ((xg_ref, xg_out), (qkv_ref, qkv_out), (of_ref, of_out), (hin_ref, hin_out), (mid_ref, mid_out))
        )
    ]
    at_end = (z == 0) | (z == nh - 1)
    round_of(3, attend)
    for p in range(nseq):
        for t in range(nh):
            @pl.when((z >= t) & (z < nh - 1))
            def _():
                hop(0, t, p, z - t, right).wait_send()

            @pl.when((z + t < nh) & (z > 0))
            def _():
                hop(1, t, p, z + t, left).wait_send()

    @pl.when(jnp.logical_not(at_end))
    def _():
        for p in range(nseq):
            heads(p).start()

    for i in og.order:
        og_o.forward(i)
    for i in og.order:
        og.core_arrive(i)
        picker.pick(2 * i + 1, ogb[me ^ 1 ^ (2 * i)], drows_ref, True)
    for i in range(4):
        og_o.core_arrive(i)
    for c in done[:3]:
        c.start()

    for p in range(nseq):
        at = pl.ds(p * seg, seg)
        heads(p).wait_recv()
        mid_ref[at] = x_ref[at].astype(F32) + dot(hin_ref[0, at], of_ref[0].reshape(-1, width))
        for h in range(1, nh):
            mid_ref[at] += dot(hin_ref[h, at], of_ref[h].reshape(-1, width))

        @pl.loop(0, seg // ROWS)
        def _(i):
            rows = pl.ds(p * seg + i * ROWS, ROWS)
            m = mid_ref[rows]
            inv = lax.rsqrt(jnp.mean(m * m, axis=-1, keepdims=True) + EPS)
            mt[me, rows] = (m * inv * mgain_ref[...]).astype(BF)

        moes[p].start()

    for c in done[3:]:
        c.start()
    wzx.start()
    picker.pick(0, mt[me], xrows_ref, False)
    for p in range(nseq):
        moes[p].core_arrive(0)
    picker.pick(1, mt[me ^ 1], xrows_ref, False)
    for i in og.order:
        for p in range(nseq - 1):
            moes[p].forward(i)
    for t, i in enumerate(og.order):
        moes[-1].forward(i)
        picker.pick(2 * i, mt[me ^ (2 * i)], xrows_ref, False)
        if t:
            last = og.order[t - 1]
            for p in range(nseq):
                moes[p].core_arrive(last)
            picker.pick(2 * last + 1, mt[me ^ 1 ^ (2 * last)], xrows_ref, False)
    last = og.order[-1]
    for p in range(nseq):
        moes[p].core_arrive(last)
    picker.pick(2 * last + 1, mt[me ^ 1 ^ (2 * last)], xrows_ref, False)
    picker.finish()
    for c in done:
        c.wait()
    wzx.wait_recv()
    for gather in [og, og_o] + moes:
        gather.finish()
    for exchange in [ofx, wzx] + [heads(p) for p in range(nseq)]:
        exchange.finish()
    for r in range(1, ne):
        info(r).wait_send()


def front(lengths, x, og, wq, wk, wv, o_local, packed, attn_gain, moe_gain, tables, nh, nseq, cap):
    ne, info, _ = packed.shape
    tokens, width = x.shape
    here = info // 2
    cols = 2 * wq.shape[1]
    groups, seg = cols // 256, tokens // nseq
    full = nh * seg
    part = o_local.shape[0]
    vmem = pl.BlockSpec(memory_space=pltpu.VMEM)
    hbm = pl.BlockSpec(memory_space=pl.ANY)
    rows = jax.ShapeDtypeStruct((here, ne, cap, width), BF)
    return pl.pallas_call(
        front_kernel,
        in_specs=[pl.BlockSpec(memory_space=pltpu.SMEM)] + [vmem] * 13,
        out_specs=[hbm, hbm, vmem, hbm, hbm, vmem, hbm, vmem, hbm, hbm],
        out_shape=[
            jax.ShapeDtypeStruct((nh, tokens, width), BF),
            jax.ShapeDtypeStruct((nseq, groups, full, 256), BF),
            jax.ShapeDtypeStruct((nseq, groups, nh, 2 * seg), F32),
            jax.ShapeDtypeStruct((nh, tokens, part), BF),
            jax.ShapeDtypeStruct((nh, ne, part // ne, width), BF),
            jax.ShapeDtypeStruct((nh, width // ne, cols), BF),
            jax.ShapeDtypeStruct((tokens, width), F32),
            jax.ShapeDtypeStruct(packed.shape, F32),
            rows,
            rows,
        ],
        scratch_shapes=[
            pltpu.VMEM((nh, tokens, width), BF),
            pltpu.VMEM((nseq, groups, full, 256), BF),
            pltpu.VMEM((nh, tokens, part), BF),
            pltpu.VMEM((nh, ne, part // ne, width), BF),
            pltpu.VMEM((tokens, width), F32),
            DMA((5,)),
            pltpu.VMEM((width, cols), BF),
            pltpu.VMEM((nh, tokens, part), BF),
            pltpu.VMEM((ne, tokens, width), BF),
            pltpu.VMEM((ne, tokens, width), BF),
            pltpu.VMEM((2, here, cap, width), BF),
            DMA((2, nh, nseq)),
            DMA((nh, nseq)),
            DMA((ne,)),
            DMA((ne,)),
            DMA((nseq, nh)),
            DMA((nseq, nh)),
            DMA((nh,)),
            DMA((nh,)),
            DMA((nh,)),
            DMA((nh,)),
            DMA((2, here)),
        ]
        + gather_sems() * (2 + nseq),
        compiler_params=pltpu.CompilerParams(
            collective_id=3, has_side_effects=True, vmem_limit_bytes=VMEM
        ),
        cost_estimate=pl.CostEstimate(flops=10**11, bytes_accessed=60 * 2**20, transcendentals=10**7),
        name="front",
    )(lengths, x, og, wq, wk, wv, o_local, packed, attn_gain, moe_gain, *tables)


def middle_kernel(first, count, len_ref, begun_ref, sum_ref, rows_ref, slot_ref, mid_in, grad_in, gain_ref, o_in, qkv_in, lse_ref,
                  cq_in, sq_in, ckv_in, skv_in, hin_in, x_ref, total_ref, dmid_ref, gtwo_ref, dqkv_ref, po_ref, pw_ref,
                  mid_ref, grad_ref, o_ref, qkv_ref, cq, sq, ckv, skv, hin_ref, inputs,
                  dbranch_ref, wsum, hs, hr, dmoe, dkv, hss, hrs, xs, *scratch):
    nh, tokens, _ = dqkv_ref.shape
    nseq, groups = qkv_ref.shape[:2]
    seg = tokens // nseq
    z = lax.axis_index("heads")
    chain = Chain(sum_ref, total_ref, scratch[PLANE:], first, count)
    plane = PlaneSum(rows_ref, slot_ref, dmoe, scratch[:PLANE])
    heads = whole_exchange(hs, hr, hss, hrs, nh)
    late = [
        pltpu.make_async_copy(src, dst, inputs.at[t])
        for t, (src, dst) in enumerate(
            (
                (mid_in, mid_ref),
                (grad_in, grad_ref),
                (o_in, o_ref),
                (qkv_in, qkv_ref),
                (cq_in, cq),
                (sq_in, sq),
                (ckv_in, ckv),
                (skv_in, skv),
                (hin_in, hin_ref),
            )
        )
    ]
    for c in late:
        c.start()
    greet(nh, (1, 2, 4, 6))
    chain.begin()
    plane.run(chain, 0)
    step = 4 + 5
    chain.run(4, step)
    plane.arrive()
    for c in late:
        c.wait()
    gtwo_ref[...] = jnp.zeros_like(gtwo_ref)

    @pl.loop(0, tokens // ROWS)
    def _(i):
        rows = pl.ds(i * ROWS, ROWS)
        d = plane.rows_total(rows)
        m = mid_ref[rows]
        inv = lax.rsqrt(jnp.mean(m * m, axis=-1, keepdims=True) + EPS)
        zed = gain_ref[...] * d
        dm = grad_ref[rows].astype(F32) + inv * zed - m * (inv * inv * inv * jnp.mean(zed * m, axis=-1, keepdims=True))
        gtwo_ref[...] += jnp.sum(d * m * inv, axis=0, keepdims=True)
        dmid_ref[rows] = dm
        db = dm.astype(BF)
        dbranch_ref[rows] = db
        for h in range(nh):
            hs[h, rows] = dot_nt(db, o_ref[h]).astype(BF)

    heads.start()
    hr[z] = hs[z]
    chain.run(step, step + 4)
    step = step + 4
    heads.wait_recv()

    @pl.loop(0, nseq)
    def _(s):
        length = len_ref[s]
        at = pl.ds(s * seg, seg)
        for g in range(groups):
            def put(i, lo, v):
                dqkv_ref[i, at, g * 256 + lo : g * 256 + lo + 128] = v

            bwd_piece(
                qkv_ref[s, g, :, :128],
                qkv_ref[s, g, :, 128:],
                lambda i: hr[i, at, g * 128 : (g + 1) * 128],
                lambda i: lse_ref[s, g, i : i + 1, :],
                length,
                (cq, sq, ckv, skv),
                dkv,
                put,
            )
            chain.step(step + groups * s + g)

    step = step + groups * nseq
    for i in range(4):
        plane.core(i).wait_send()
    load = pltpu.make_async_copy(x_ref, plane.odd, xs)
    load.start()
    ne, deep, _ = po_ref.shape
    strip, row = deep // nh, pw_ref.shape[1]
    db = dbranch_ref[...]
    for h in range(nh):
        o = dot_tn(hin_ref[h], db).astype(BF)
        for e in range(ne):
            po_ref[e, h * strip : (h + 1) * strip] = o[e * strip : (e + 1) * strip]
    chain.step(step)
    load.wait()
    wsum[...] = dot_tn(plane.odd[0], dqkv_ref[0])
    for h in range(1, nh):
        wsum[...] += dot_tn(plane.odd[h], dqkv_ref[h])
    for e in range(ne):
        pw_ref[e] = wsum[e * row : (e + 1) * row].astype(BF)
    chain.rest(step + 1)
    chain.finish()
    for i in plane.order:
        plane.chip(i).wait_send()
    heads.finish()


def middle(first, count, lengths, total, sums, rows, slots, mid, grad, gain, o_parts, qkv, lse, tables, heads_in, x):
    nseq, groups, full, _ = qkv.shape
    nh = o_parts.shape[0]
    tokens, width = mid.shape
    here, ne, cap, _ = rows.shape
    vmem = pl.BlockSpec(memory_space=pltpu.VMEM)
    hbm = pl.BlockSpec(memory_space=pl.ANY)
    heads = (nh, tokens, groups * 128)
    cols = groups * 256
    return pl.pallas_call(
        functools.partial(middle_kernel, first, count),
        in_specs=[pl.BlockSpec(memory_space=pltpu.SMEM), hbm, hbm, hbm, vmem, hbm, hbm, vmem, hbm, hbm, vmem] + [hbm] * 6,
        input_output_aliases={1: 0},
        out_specs=[hbm] + [vmem] * 5,
        out_shape=[
            jax.ShapeDtypeStruct(sums.shape, BF),
            jax.ShapeDtypeStruct((tokens, width), F32),
            jax.ShapeDtypeStruct((1, width), F32),
            jax.ShapeDtypeStruct((nh, tokens, cols), BF),
            jax.ShapeDtypeStruct((ne, nh * groups * 128 // ne, width), BF),
            jax.ShapeDtypeStruct((ne, width // ne, cols), BF),
        ],
        scratch_shapes=[pltpu.VMEM(v.shape, v.dtype) for v in (mid, grad, o_parts, qkv) + tuple(tables) + (heads_in,)]
        + [
            DMA((9,)),
            pltpu.VMEM((tokens, width), BF),
            pltpu.VMEM((width, cols), F32),
            pltpu.VMEM(heads, BF),
            pltpu.VMEM(heads, BF),
            pltpu.VMEM((tokens, width), F32),
            pltpu.VMEM((full, 128), F32),
            DMA((nh,)),
            DMA((nh,)),
            DMA,
        ]
        + plane_scratch(here, cap, tokens, width)
        + chain_scratch(count, width),
        compiler_params=pltpu.CompilerParams(
            collective_id=1, has_side_effects=True, vmem_limit_bytes=VMEM
        ),
        cost_estimate=pl.CostEstimate(flops=10**11, bytes_accessed=30 * 2**20, transcendentals=10**7),
        name="middle",
    )(lengths, total, sums, rows, slots, mid, grad, gain, o_parts, qkv, lse, *tables, heads_in, x)


class PairSum:
    order = (3, 1, 2)

    def __init__(self, parts, scratch):
        self.parts = parts
        self.c, self.e, self.f, self.cs, self.cr, self.fs, self.fr = scratch
        self.me = lax.axis_index("experts")

    def core(self, i):
        src = self.parts.at[self.me ^ 1 ^ (2 * i)]
        return remote(src, self.c.at[i], self.cs.at[i], self.cr.at[i], "experts", self.me ^ 1)

    def chip(self, i):
        return remote(self.e.at[i - 1], self.f.at[i - 1], self.fs.at[i - 1], self.fr.at[i - 1], "experts", self.me ^ (2 * i))

    def start(self):
        for i in self.order + (0,):
            self.core(i).start()

    def both(self, i):
        return self.parts[self.me ^ (2 * i)].astype(F32) + self.c[i].astype(F32)

    def forward(self):
        for i in self.order:
            self.core(i).wait_recv()
            self.e[i - 1] = self.both(i).astype(BF)
            self.chip(i).start()
        self.core(0).wait_recv()

    def result(self):
        value = self.both(0)
        for i in self.order:
            self.chip(i).wait_recv()
        for r in range(3):
            value = value + self.f[r].astype(F32)
        return value

    def finish(self):
        for i in range(4):
            self.core(i).wait_send()
        for i in self.order:
            self.chip(i).wait_send()


PAIR = 7


def pair_scratch(shape):
    return [pltpu.VMEM((n,) + shape, BF) for n in (4, 3, 3)] + [DMA((4,)), DMA((4,)), DMA((3,)), DMA((3,))]


def last_kernel(first, count, begun_ref, sum_ref, rows_ref, slot_ref, mid_in, dqkv_ref, wz_ref, x_in, dmid_ref,
                gain_ref, gtwo_ref, po_ref, pw_ref, total_ref, out_ref, xgrad_ref, gains_ref, ograd_ref, qgrad_ref, kgrad_ref, vgrad_ref,
                mid_ref, x_ref, inputs, wf, br, moe, gp, gz, acc, oz, fo, fq, fk, fv, brs, brr, gps, gpr, gzs, gzr, oss, ors, fl, dl, *scratch):
    nh, tokens, _ = dqkv_ref.shape
    dattn = moe
    ne = rows_ref.shape[1]
    z, me = lax.axis_index("heads"), lax.axis_index("experts")
    at = PLANE
    plane = PlaneSum(rows_ref, slot_ref, moe, scratch[:at])
    weights = PlaneGather(wz_ref, lambda e: wf.at[:, e], scratch[at : at + GATHER])
    at += GATHER
    strip, row = fo.shape[0], fq.shape[0]

    def o_rows(e):
        return ograd_ref.at[pl.ds(pl.multiple_of(e * strip, strip), strip)]

    def w_rows(ref, e):
        return ref.at[pl.ds(pl.multiple_of(e * row, row), row)]

    spread_o = PlaneGather(fo, o_rows, scratch[at : at + GATHER])
    at += GATHER
    spreads = [spread_o]
    for mine, whole in ((fq, qgrad_ref), (fk, kgrad_ref), (fv, vgrad_ref)):
        spreads.append(PlaneGather(mine, functools.partial(w_rows, whole), scratch[at : at + GATHER]))
        at += GATHER
    sum_o = PairSum(po_ref, scratch[at : at + PAIR])
    at += PAIR
    sum_w = PairSum(pw_ref, scratch[at : at + PAIR])
    at += PAIR
    chain = Chain(sum_ref, total_ref, scratch[at:], first, count)
    back = whole_exchange(dqkv_ref, br, brs, brr, nh)
    pieces = Exchange(
        lambda h: acc.at[pl.ds(pl.multiple_of(h * strip, strip), strip)],
        lambda h: oz.at[h], lambda d: oss.at[d], lambda d: ors.at[d], nh)
    first_part = pltpu.make_async_copy(dmid_ref, xgrad_ref, dl)
    first_part.start()
    late = [
        pltpu.make_async_copy(mid_in, mid_ref, inputs.at[0]),
        pltpu.make_async_copy(x_in, x_ref, inputs.at[1]),
        pltpu.make_async_copy(dqkv_ref.at[z], br.at[z], inputs.at[2]),
    ]
    for c in late:
        c.start()
    greet(nh, tuple(range(1, ne)))
    back.start()
    sum_o.start()
    sum_w.start()
    chain.begin()
    sum_o.forward()
    sum_w.forward()
    weights.start()
    wf[:, me] = wz_ref[...]
    plane.run()
    acc[...] = sum_o.result()
    pieces.start()
    oz[z] = acc[pl.ds(pl.multiple_of(z * strip, strip), strip)]
    w = sum_w.result()
    for g in range(fq.shape[1] // 128):
        head = slice(g * HEAD, (g + 1) * HEAD)
        fq[:, g * 128 : (g + 1) * 128] = w[:, g * 256 : g * 256 + 128]
        fk[:, head] = w[:, g * 256 + 128 : g * 256 + 192]
        fv[:, head] = w[:, g * 256 + 192 : (g + 1) * 256]
    for spread in spreads[1:]:
        spread.start()
    step = 4
    chain.run(0, step)
    pieces.wait_recv()
    fo[...] = oz[0] + oz[1] + oz[2] + oz[3]
    spread_o.start()
    keep = [pltpu.make_async_copy(g.own, g.slot(me), fl.at[t]) for t, g in enumerate(spreads)]
    for c in keep:
        c.start()
    for i in weights.order:
        weights.forward(i)
    chain.run(step, step + 4)
    step = step + 4
    plane.arrive()
    for c in late:
        c.wait()

    @pl.loop(0, tokens // ROWS)
    def _(i):
        rows = pl.ds(i * ROWS, ROWS)
        out_ref[rows] = (mid_ref[rows] + plane.rows_total(rows)).astype(BF)

    chain.run(step, step + 2)
    step = step + 2
    for i in range(4):
        weights.core_arrive(i)
    back.wait_recv()
    for h in range(nh):
        term = dot_nt(br[h], wf[h].reshape(-1, wf.shape[3]))
        if h:
            dattn[...] += term
        else:
            dattn[...] = term
    chain.run(step, step + 2)
    step = step + 2
    pad = jnp.zeros((6, gtwo_ref.shape[1]), F32)
    own = jnp.zeros_like(gtwo_ref[...])

    def rows_back(i, total):
        rows = pl.ds(i * ROWS, ROWS)
        d = dattn[rows]
        x = x_ref[rows].astype(F32)
        inv = lax.rsqrt(jnp.mean(x * x, axis=-1, keepdims=True) + EPS)
        wed = gain_ref[...] * d
        xgrad_ref[rows] += inv * wed - x * (inv * inv * inv * jnp.mean(wed * x, axis=-1, keepdims=True))
        return total + jnp.sum(d * x * inv, axis=0, keepdims=True)

    first_part.wait()
    own = lax.fori_loop(0, tokens // ROWS, rows_back, own)
    gp[me] = jnp.concatenate([own, gtwo_ref[...], pad], axis=0)

    def near(r, at):
        return remote(gp.at[me], gp.at[at], gps.at[r], gpr.at[r], "experts", me ^ r)

    for r in range(1, ne):
        near(r, me).start()
    chain.run(step, step + 2)
    step = step + 2
    for spread in spreads[1:] + spreads[:1]:
        for i in spread.order:
            spread.forward(i)
    for r in range(1, ne):
        near(r, me ^ r).wait_recv()
    total = gp[0]
    for e in range(1, ne):
        total = total + gp[e]
    gz[z] = total
    gains = Exchange(lambda h: gz.at[z], lambda h: gz.at[h], lambda d: gzs.at[d], lambda d: gzr.at[d], nh)
    gains.start()
    chain.rest(step)
    gains.wait_recv()
    total = gz[0]
    for h in range(1, nh):
        total = total + gz[h]
    gains_ref[...] = total
    for spread in spreads:
        for i in range(4):
            spread.core_arrive(i)
    chain.finish()
    for part in [plane, back, pieces, gains, weights, sum_o, sum_w] + spreads:
        part.finish()
    for c in keep:
        c.wait()
    for r in range(1, ne):
        near(r, me).wait_send()


def last(first, count, total, sums, rows, slots, mid, dqkv, w_pieces, x, d_mid, gain, gain_two, po, pw):
    nh, tokens, cols = dqkv.shape
    here, ne, cap, width = rows.shape
    strip = po.shape[1] // nh
    row = pw.shape[1]
    hbm = pl.BlockSpec(memory_space=pl.ANY)
    vmem = pl.BlockSpec(memory_space=pltpu.VMEM)
    return pl.pallas_call(
        functools.partial(last_kernel, first, count),
        in_specs=[hbm, hbm, hbm, vmem, hbm, hbm, vmem, hbm, hbm] + [vmem] * 4,
        input_output_aliases={0: 0},
        out_specs=[hbm] + [vmem] * 3 + [hbm] * 4,
        out_shape=[
            jax.ShapeDtypeStruct(sums.shape, BF),
            jax.ShapeDtypeStruct((tokens, width), BF),
            jax.ShapeDtypeStruct((tokens, width), F32),
            jax.ShapeDtypeStruct((8, width), F32),
            jax.ShapeDtypeStruct((strip * ne, width), F32),
            jax.ShapeDtypeStruct((row * ne, cols // 2), F32),
            jax.ShapeDtypeStruct((row * ne, cols // 4), F32),
            jax.ShapeDtypeStruct((row * ne, cols // 4), F32),
        ],
        scratch_shapes=[
            pltpu.VMEM(mid.shape, mid.dtype),
            pltpu.VMEM(x.shape, x.dtype),
            DMA((3,)),
            pltpu.VMEM((nh, ne, width // ne, cols), BF),
            pltpu.VMEM((nh, tokens, cols), BF),
            pltpu.VMEM((tokens, width), F32),
            pltpu.VMEM((ne, 8, width), F32),
            pltpu.VMEM((nh, 8, width), F32),
            pltpu.VMEM((nh * strip, width), F32),
            pltpu.VMEM((nh, strip, width), F32),
            pltpu.VMEM((strip, width), F32),
            pltpu.VMEM((row, cols // 2), F32),
            pltpu.VMEM((row, cols // 4), F32),
            pltpu.VMEM((row, cols // 4), F32),
            DMA((nh,)),
            DMA((nh,)),
            DMA((ne,)),
            DMA((ne,)),
            DMA((nh,)),
            DMA((nh,)),
            DMA((nh,)),
            DMA((nh,)),
            DMA((4,)),
            DMA,
        ]
        + plane_scratch(here, cap, tokens, width)
        + gather_sems() * 5
        + pair_scratch(po.shape[1:])
        + pair_scratch(pw.shape[1:])
        + chain_scratch(count, width),
        compiler_params=pltpu.CompilerParams(
            collective_id=2, has_side_effects=True, vmem_limit_bytes=VMEM
        ),
        cost_estimate=pl.CostEstimate(flops=2 * 10**11, bytes_accessed=30 * 2**20, transcendentals=0),
        name="last",
    )(total, sums, rows, slots, mid, dqkv, w_pieces, x, d_mid, gain, gain_two, po, pw)


def widen_kernel(x_ref, in_ref, down_ref):
    c = pl.program_id(1)

    @pl.when(c < 2)
    def _():
        in_ref[...] = x_ref[...].astype(F32)

    @pl.when(c == 2)
    def _():
        down_ref[...] = x_ref[...].astype(F32)


def widen(sums, ff):
    here, rows, width = sums.shape
    return pl.pallas_call(
        widen_kernel,
        grid=(here, 3),
        in_specs=[pl.BlockSpec((1, ff, width), lambda j, c: (j, c, 0))],
        out_specs=[
            pl.BlockSpec((1, ff, width), lambda j, c: (j, jnp.minimum(c, 1), 0)),
            pl.BlockSpec((1, ff, width), lambda j, c: (j, 0, 0)),
        ],
        out_shape=[
            jax.ShapeDtypeStruct((here, 2 * ff, width), F32),
            jax.ShapeDtypeStruct((here, ff, width), F32),
        ],
        compiler_params=params(2),
        name="widen",
    )(sums)


def body(layer_input, seq_lengths, expert_ids, route_weight, priority, attn_gain, moe_gain,
         query_matrix, key_matrix, value_matrix, output_matrix, expert_in, expert_down, out_grad):
    seg, nseq, width = layer_input.shape
    nh, ne = lax.axis_size("heads"), lax.axis_size("experts")
    z, me = lax.axis_index("heads"), lax.axis_index("experts")
    top = expert_ids.shape[-1]
    tokens = seg * nseq
    groups = key_matrix.shape[1] // HEAD
    here = expert_in.shape[0]
    cap = (5 * tokens * top + 4 * EXPERTS - 1) // (4 * EXPERTS)

    def local(v):
        return jnp.swapaxes(v, 0, 1).reshape((tokens,) + v.shape[2:])

    def unlocal(v):
        return jnp.swapaxes(v.reshape((nseq, seg) + v.shape[1:]), 0, 1)

    ids = local(expert_ids)
    order = local(priority)
    weight = local(route_weight)
    position = z * seg + jnp.arange(seg, dtype=jnp.int32)
    live = (position[None, :] < seq_lengths[:, None]).reshape(tokens)
    match = ids.T[:, None, :] == jnp.arange(EXPERTS, dtype=jnp.int32)[None, :, None]
    weight_e = jnp.sum(jnp.where(match, weight.T[:, None, :], 0.0), axis=0)
    chosen = jnp.any(match, axis=0) & live[None, :]
    earlier = (order[:, None] < order[None, :]).astype(BF)
    before = dot(chosen.astype(BF), earlier)
    slot = jnp.where(chosen & (before < cap), before, -1.0)
    packed = jnp.concatenate([slot.reshape(ne, here, tokens), weight_e.reshape(ne, here, tokens)], axis=1)
    tables = rotary_tables(nh * seg)
    x, grad = local(layer_input), local(out_grad)
    xf = x.astype(F32)
    gain_a, gain_m = attn_gain.reshape(1, width), moe_gain.reshape(1, width)
    fast = nh == 4 and ne == 8
    if fast:
        gathered, qkv, lse, heads_in, o_full, w_pieces, mid, pack, d_rows, x_rows = front(
            seq_lengths, x, grad, query_matrix, key_matrix, value_matrix, output_matrix, packed, gain_a, gain_m, tables, nh, nseq, cap)
        o_parts = o_full.reshape(nh, groups * 128, width)
    else:
        wq = query_matrix.reshape(width, groups, 128)
        wk = key_matrix.reshape(width, groups, HEAD)
        wv = value_matrix.reshape(width, groups, HEAD)
        w_local = jnp.concatenate([wq, wk, wv], axis=2).reshape(width, groups * 256)
        packed = lax.all_to_all(packed, "experts", split_axis=0, concat_axis=0, tiled=True)
        packed = packed[me ^ jnp.arange(ne, dtype=jnp.int32)]
        slots, weights = packed[:, :here].astype(jnp.int32), packed[:, here:]
        inv_one = lax.rsqrt(jnp.mean(xf * xf, axis=-1, keepdims=True) + EPS)
        attn_in = (xf * inv_one * attn_gain).astype(BF)
        gathered = lax.all_gather(attn_in.reshape(nseq, seg, width), "heads", axis=0)
        w_groups = jnp.transpose(w_local.reshape(width, groups, 256), (1, 0, 2))
        rows_in, rows_out = width // ne, output_matrix.shape[0] // ne
        w_piece = lax.dynamic_slice_in_dim(w_local, me * rows_in, rows_in, 0)
        o_piece = lax.dynamic_slice_in_dim(output_matrix, me * rows_out, rows_out, 0)
        o_full = lax.all_gather(o_piece, ("heads", "experts"), axis=0, tiled=True)
        w_full = lax.all_gather(w_piece, ("heads", "experts"), axis=0, tiled=True)
        w_full = w_full.reshape(nh, width, groups * 256)
        qkv, heads_out, lse = attn_forward(gathered, w_groups, seq_lengths, tables)
        heads_in = lax.all_to_all(heads_out, "heads", split_axis=0, concat_axis=0, tiled=True)
        heads_in = heads_in.reshape(nh, tokens, groups * 128)
        o_parts = o_full.reshape(nh, groups * 128, width)
        branch = jnp.einsum("ztm,zmw->tw", heads_in, o_parts, preferred_element_type=F32)
        mid = xf + branch
        inv_two = lax.rsqrt(jnp.mean(mid * mid, axis=-1, keepdims=True) + EPS)
        moe_in = (mid * inv_two * moe_gain).astype(BF)
        d_rows = gather_rows(slots, weights, plane_gather(grad, ne), cap)
        x_rows = gather_rows(slots, None, plane_gather(moe_in, ne), cap)

    if fast:
        chunks = expert_in.shape[0] * (width + expert_down.shape[1]) // CHUNK
        early, half = chunks // 8, (3 * chunks) // 8
        results, drows, sums, total = experts_send(early, pack, x_rows, d_rows, expert_in, expert_down)
        flat = sums.reshape(-1, width)
        total, d_mid, gain_two, dqkv, po, pw = middle(
            early, half, seq_lengths, total, flat, drows, pack, mid, grad, gain_m, o_parts, qkv, lse, tables,
            heads_in, gathered)
        total, out, x_grad, gains, o_grad, q_grad, k_grad, v_grad = last(
            early + half, chunks - early - half, total, flat, results, pack, mid, dqkv, w_pieces, x, d_mid, gain_a, gain_two, po, pw)
        gain_one, gain_two = gains[0], gains[1]
        grad_in, grad_down = widen(total.reshape(sums.shape), expert_down.shape[1])
    else:
        results, drows, sums = experts_call(slots, weights, x_rows, d_rows, expert_in, expert_down)
        slots_t = jnp.swapaxes(slots, 1, 2)
        d_parts = combine(slots_t, drows)
        moe_parts = combine(slots_t, results)
        totals = heads_sum(sums, z, nh)
        grad_in, grad_down = totals[:, :width], totals[:, width:]
        d_moe = plane_scatter(d_parts, ne)
        moe_sum = plane_scatter(moe_parts, ne)
        out = (mid + moe_sum).astype(BF)
        zed = moe_gain * d_moe
        d_mid = grad.astype(F32) + inv_two * zed - mid * (inv_two ** 3 * jnp.mean(zed * mid, axis=-1, keepdims=True))
        gain_two = jnp.sum(d_moe * mid * inv_two, axis=0)
        d_branch = d_mid.astype(BF)
        d_heads = jnp.einsum("tw,zmw->ztm", d_branch, o_parts, preferred_element_type=F32).astype(BF)
        d_heads = d_heads.reshape(nh, nseq, seg, groups * 128)
        d_heads = lax.all_to_all(d_heads, "heads", split_axis=0, concat_axis=0, tiled=True)
        dqkv = attn_backward(qkv, d_heads, lse, seq_lengths, tables)
        dqkv = dqkv.reshape(nh, tokens, groups * 256)
        back = lax.all_to_all(dqkv, "heads", split_axis=0, concat_axis=0, tiled=True)
        d_attn = jnp.einsum("ztc,zmc->tm", back, w_full, preferred_element_type=F32)
        o_grad, w_grad = weight_sums(heads_in, d_branch, gathered, dqkv, ne)
        wed = attn_gain * d_attn
        x_grad = d_mid + inv_one * wed - xf * (inv_one ** 3 * jnp.mean(wed * xf, axis=-1, keepdims=True))
        gain_one = jnp.sum(d_attn * xf * inv_one, axis=0)
        gain_one, gain_two = lax.psum((gain_one, gain_two), ("heads", "experts"))
        w_grad = w_grad.reshape(width, groups, 256)
        q_grad = w_grad[:, :, :128].reshape(query_matrix.shape)
        k_grad = w_grad[:, :, 128:192].reshape(key_matrix.shape)
        v_grad = w_grad[:, :, 192:].reshape(value_matrix.shape)
    return (
        unlocal(out),
        unlocal(x_grad),
        gain_one,
        gain_two,
        q_grad,
        k_grad,
        v_grad,
        o_grad,
        grad_in,
        grad_down,
    )


def solution(mesh):
    rows = P("heads", "experts", None)
    in_specs = (
        rows,
        P("experts"),
        rows,
        rows,
        P("heads", "experts"),
        P(),
        P(),
        P(None, "heads"),
        P(None, "heads"),
        P(None, "heads"),
        P("heads", None),
        P("experts", None, None),
        P("experts", None, None),
        rows,
    )
    out_specs = (
        rows,
        rows,
        P(),
        P(),
        P(None, "heads"),
        P(None, "heads"),
        P(None, "heads"),
        P("heads", None),
        P("experts", None, None),
        P("experts", None, None),
    )
    return jax.shard_map(body, mesh=mesh, in_specs=in_specs, out_specs=out_specs, check_vma=False)
```

```python
import functools
import math

import jax
import jax.numpy as jnp
import numpy as np
from jax import lax
from jax.experimental import pallas as pl
from jax.experimental.pallas import tpu as pltpu
from jax.sharding import PartitionSpec as P

HEAD = 64
EXPERTS = 32
EPS = 1e-06
BF = jnp.bfloat16
F32 = jnp.float32
SCALE = HEAD ** (-0.5)
NEG = -1e30
VMEM = 63 * 1024 * 1024
MESH = pl.DeviceIdType.MESH
DMA = pltpu.SemaphoreType.DMA


def dot(a, b):
    return jnp.dot(a, b, preferred_element_type=F32)


def dot_nt(a, b):
    return lax.dot_general(a, b, (((1,), (1,)), ((), ())), preferred_element_type=F32)


def dot_tn(a, b):
    return lax.dot_general(a, b, (((0,), (0,)), ((), ())), preferred_element_type=F32)


def params(n):
    return pltpu.CompilerParams(
        dimension_semantics=("arbitrary",) * n, vmem_limit_bytes=VMEM
    )


def swap_halves(v):
    lane = lax.broadcasted_iota(jnp.int32, v.shape, 1)
    return jnp.where(lane % 64 < 32, pltpu.roll(v, 96, 1), pltpu.roll(v, 32, 1))


def attn_mask(offset, n, block, length):
    key = lax.broadcasted_iota(jnp.int32, (n, block), 0)
    query = lax.broadcasted_iota(jnp.int32, (n, block), 1) + offset
    return (key <= query) & (key < length)


def two_heads(v):
    return jnp.concatenate([v[:, :HEAD], v[:, HEAD:]], axis=0)


def untwo(vt, block):
    return jnp.concatenate([vt[:, :block], vt[:, block:]], axis=0).T


def fwd_kernel(len_ref, x_ref, w_ref, cq, sq, ckv, skv, qkv_ref, head_ref, lse_ref):
    nh, _, seg, width = x_ref.shape
    full = nh * seg
    block = seg
    length = len_ref[pl.program_id(0)]
    lin = dot(x_ref[...].reshape(full, width), w_ref[0])
    ql, kvl = lin[:, :128], lin[:, 128:]
    q = (ql * cq[...] + swap_halves(ql) * sq[...]).astype(BF)
    kvr = kvl * ckv[...] + swap_halves(kvl) * skv[...]
    kv = kvr.astype(BF)
    qkv_ref[0, 0, :, :128] = q
    qkv_ref[0, 0, :, 128:] = kv
    k = kv[:, :HEAD]
    vt = kvr.T[HEAD:].astype(BF)
    for i in range(nh):
        n = (i + 1) * block
        q2 = two_heads(q[i * block : n])
        s = dot_nt(k[:n], q2)
        mask = attn_mask(i * block, n, block, length)
        s = jnp.where(jnp.concatenate([mask, mask], axis=1), s * SCALE, NEG)
        m = jnp.max(s, axis=0, keepdims=True)
        e = jnp.exp(s - m)
        total = jnp.sum(e, axis=0, keepdims=True)
        p = (e * (1.0 / total)).astype(BF)
        lse_ref[0, 0, i : i + 1, :] = m + jnp.log(total)
        head_ref[i, 0] = untwo(dot(vt[:, :n], p), block).astype(BF)


def attn_forward(x, w, lengths, tables):
    nh, nseq, seg, width = x.shape
    groups = w.shape[0]
    full = nh * seg
    cq, sq, ckv, skv = tables
    tab = pl.BlockSpec((full, 128), lambda s, g: (0, 0))
    return pl.pallas_call(
        fwd_kernel,
        grid=(nseq, groups),
        in_specs=[
            pl.BlockSpec(memory_space=pltpu.SMEM),
            pl.BlockSpec((nh, 1, seg, width), lambda s, g: (0, s, 0, 0)),
            pl.BlockSpec((1, width, 256), lambda s, g: (g, 0, 0)),
            tab,
            tab,
            tab,
            tab,
        ],
        out_specs=[
            pl.BlockSpec((1, 1, full, 256), lambda s, g: (s, g, 0, 0)),
            pl.BlockSpec((nh, 1, seg, 128), lambda s, g: (0, s, 0, g)),
            pl.BlockSpec((1, 1, nh, 2 * seg), lambda s, g: (s, g, 0, 0)),
        ],
        out_shape=[
            jax.ShapeDtypeStruct((nseq, groups, full, 256), BF),
            jax.ShapeDtypeStruct((nh, nseq, seg, groups * 128), BF),
            jax.ShapeDtypeStruct((nseq, groups, nh, 2 * seg), F32),
        ],
        compiler_params=params(2),
        cost_estimate=pl.CostEstimate(flops=6 * 10**9, bytes_accessed=12 * 2**20, transcendentals=10**7),
        name="attn_forward",
    )(lengths, x, w, cq, sq, ckv, skv)


def bwd_piece(q, kv, heads, lses, length, tables, dkv_ref, put):
    cq, sq, ckv, skv = tables
    full, block = q.shape[0], lses(0).shape[1] // 2
    k, v = kv[:, :HEAD], kv[:, HEAD:]
    kt = kv.astype(F32).T[:HEAD].astype(BF)
    dkv_ref[...] = jnp.zeros_like(dkv_ref)
    for i in range(full // block):
        n = (i + 1) * block
        rows = pl.ds(i * block, block)
        mask = attn_mask(i * block, n, block, length)
        grads = []
        for h in range(2):
            qh = q[i * block : n, h * HEAD : (h + 1) * HEAD]
            doh = heads(i)[:, h * HEAD : (h + 1) * HEAD]
            s = dot_nt(k[:n], qh)
            p = jnp.exp(jnp.where(mask, s * SCALE - lses(i)[:, h * block : (h + 1) * block], NEG))
            dp = dot_nt(v[:n], doh)
            delta = jnp.sum(p * dp, axis=0, keepdims=True)
            ds = (p * (dp - delta) * SCALE).astype(BF)
            dkv_ref[:n, :HEAD] += dot(ds, qh)
            dkv_ref[:n, HEAD:] += dot(p.astype(BF), doh)
            grads.append(dot(kt[:, :n], ds))
        dq = jnp.concatenate(grads, axis=0).T
        dq = dq * cq[rows, :] - swap_halves(dq) * sq[rows, :]
        put(i, 0, dq.astype(BF))
    dkv = dkv_ref[...]
    dkv = (dkv * ckv[...] - swap_halves(dkv) * skv[...]).astype(BF)
    for i in range(full // block):
        put(i, 128, dkv[i * block : (i + 1) * block])


def bwd_kernel(len_ref, qkv_ref, do_ref, lse_ref, cq, sq, ckv, skv, out_ref, dkv_ref):
    def put(i, lo, v):
        out_ref[i, 0, :, lo : lo + 128] = v

    bwd_piece(
        qkv_ref[0, 0, :, :128],
        qkv_ref[0, 0, :, 128:],
        lambda i: do_ref[i, 0],
        lambda i: lse_ref[0, 0, i : i + 1, :],
        len_ref[pl.program_id(0)],
        (cq, sq, ckv, skv),
        dkv_ref,
        put,
    )


def attn_backward(qkv, d_head, lse, lengths, tables):
    nseq, groups, full, _ = qkv.shape
    nh, _, seg, _ = d_head.shape
    cq, sq, ckv, skv = tables
    tab = pl.BlockSpec((full, 128), lambda s, g: (0, 0))
    return pl.pallas_call(
        bwd_kernel,
        grid=(nseq, groups),
        in_specs=[
            pl.BlockSpec(memory_space=pltpu.SMEM),
            pl.BlockSpec((1, 1, full, 256), lambda s, g: (s, g, 0, 0)),
            pl.BlockSpec((nh, 1, seg, 128), lambda s, g: (0, s, 0, g)),
            pl.BlockSpec((1, 1, nh, 2 * seg), lambda s, g: (s, g, 0, 0)),
            tab,
            tab,
            tab,
            tab,
        ],
        out_specs=pl.BlockSpec((nh, 1, seg, 256), lambda s, g: (0, s, 0, g)),
        out_shape=jax.ShapeDtypeStruct((nh, nseq, seg, groups * 256), BF),
        scratch_shapes=[pltpu.VMEM((full, 128), F32)],
        compiler_params=params(2),
        cost_estimate=pl.CostEstimate(flops=12 * 10**9, bytes_accessed=8 * 2**20, transcendentals=10**7),
        name="attn_backward",
    )(lengths, qkv, d_head, lse, cq, sq, ckv, skv)


def rotary_tables(length):
    half = HEAD // 2
    exponent = np.arange(half, dtype=np.float32) * np.float32(-2.0 * math.log(10000.0) / HEAD)
    angles = np.arange(length, dtype=np.float32)[:, None] * np.exp(exponent)[None, :]
    cos, sin = np.cos(angles), np.sin(angles)
    c1 = np.concatenate([cos, cos], axis=1)
    s1 = np.concatenate([-sin, sin], axis=1)
    cq = np.concatenate([c1, c1], axis=1)
    sq = np.concatenate([s1, s1], axis=1)
    ckv = np.concatenate([c1, np.ones_like(c1)], axis=1)
    skv = np.concatenate([s1, np.zeros_like(s1)], axis=1)
    return tuple(jnp.asarray(t, F32) for t in (cq, sq, ckv, skv))


def pick_rows(slots, cap):
    tokens = slots.shape[1]
    index = lax.broadcasted_iota(jnp.int32, (cap, tokens), 0)
    return [index == slots[j : j + 1, :] for j in range(slots.shape[0])]


def gather_kernel(weighted, slot_ref, *refs):
    if weighted:
        weight_ref, tok_ref, out_ref = refs
    else:
        tok_ref, out_ref = refs[0], refs[-1]
    cap = out_ref.shape[2]
    hits = pick_rows(slot_ref[0], cap)
    rows = dot(jnp.concatenate([h.astype(F32) for h in hits], axis=0).astype(BF), tok_ref[0])
    for j, hit in enumerate(hits):
        part = rows[j * cap : (j + 1) * cap]
        if weighted:
            part = part * jnp.sum(jnp.where(hit, weight_ref[0, j : j + 1, :], 0.0), axis=1, keepdims=True)
        out_ref[j, 0] = part.astype(BF)


def gather_rows(slots, weights, tokens, cap):
    sources, here, count = slots.shape
    width = tokens.shape[-1]
    small = pl.BlockSpec((1, here, count), lambda s: (s, 0, 0))
    weighted = weights is not None
    return pl.pallas_call(
        functools.partial(gather_kernel, weighted),
        grid=(sources,),
        in_specs=[small] + [small] * weighted + [pl.BlockSpec((1, count, width), lambda s: (s, 0, 0))],
        out_specs=pl.BlockSpec((here, 1, cap, width), lambda s: (0, s, 0, 0)),
        out_shape=jax.ShapeDtypeStruct((here, sources, cap, width), BF),
        compiler_params=params(1),
        cost_estimate=pl.CostEstimate(
            flops=2 * sources * here * cap * count * width,
            bytes_accessed=2 * sources * width * (count + here * cap),
            transcendentals=0,
        ),
        name="gather_rows",
    )(*([slots] + [weights] * weighted + [tokens]))


def expert_kernel(steps, slot_ref, weight_ref, x_ref, d_ref, win_ref, wdown_ref,
                  out_ref, drow_ref, grad_ref, hid_ref, dgu_ref, *acc):
    _, sources, cap, width = x_ref.shape
    ff = wdown_ref.shape[1]
    per = 2 if sources % 2 == 0 else 1
    win, wdown = win_ref[0], wdown_ref[0]
    for c in range(sources // per):
        rows = slice(c * per * cap, (c + 1) * per * cap)
        x = x_ref[0, c * per : (c + 1) * per].reshape(per * cap, width)
        d = d_ref[0, c * per : (c + 1) * per].reshape(per * cap, width)
        gu = dot(x, win)
        gate, up = gu[:, :ff], gu[:, ff:]
        sig = 1.0 / (1.0 + jnp.exp(-gate))
        act = gate * sig
        hidden = (act * up).astype(BF)
        hid_ref[rows, :] = hidden
        result = dot(hidden, wdown).astype(BF).astype(F32)
        for b in range(per):
            hit = pick_rows(slot_ref[c * per + b, 0], cap)[0]
            w = jnp.sum(jnp.where(hit, weight_ref[c * per + b, 0], 0.0), axis=1, keepdims=True)
            out_ref[0, c * per + b] = (result[b * cap : (b + 1) * cap] * w).astype(BF)
        dh = dot_nt(d, wdown)
        dgu_ref[rows, :ff] = (dh * up * (sig * (1.0 + gate * (1.0 - sig)))).astype(BF)
        dgu_ref[rows, ff:] = (dh * act).astype(BF)
        drow = dot_nt(dgu_ref[rows, :], win).astype(BF)
        for b in range(per):
            drow_ref[0, c * per + b] = drow[b * cap : (b + 1) * cap]
    x = x_ref[0].reshape(sources * cap, width)
    d = d_ref[0].reshape(sources * cap, width)
    gin = dot_tn(x, dgu_ref[...])
    gdown = dot_tn(hid_ref[...], d)
    if steps == 1:
        grad_ref[0, :width] = gin.astype(BF)
        grad_ref[0, width:] = gdown.astype(BF)
    else:
        ain, adown = acc
        step = pl.program_id(1)

        @pl.when(step == 0)
        def _():
            ain[...] = jnp.zeros_like(ain)
            adown[...] = jnp.zeros_like(adown)

        ain[...] += gin
        adown[...] += gdown

        @pl.when(step == steps - 1)
        def _():
            grad_ref[0, :width] = ain[...].astype(BF)
            grad_ref[0, width:] = adown[...].astype(BF)


def experts_call(slots, weights, x, d, win, wdown):
    count, sources, cap, width = x.shape
    tokens = slots.shape[-1]
    ff = wdown.shape[1]
    chunk = min(sources, 8)
    steps = sources // chunk
    small = pl.BlockSpec((chunk, 1, 1, tokens), lambda j, r: (r, j, 0, 0))
    rows = pl.BlockSpec((1, chunk, cap, width), lambda j, r: (j, r, 0, 0))
    rows_out = pl.BlockSpec((1, chunk, cap, width), lambda j, r: (j, r, 0, 0))
    scratch = [pltpu.VMEM((chunk * cap, ff), BF), pltpu.VMEM((chunk * cap, 2 * ff), BF)]
    if steps > 1:
        scratch += [pltpu.VMEM((width, 2 * ff), F32), pltpu.VMEM((ff, width), F32)]
    shape = jax.ShapeDtypeStruct((count, sources, cap, width), BF)
    return pl.pallas_call(
        functools.partial(expert_kernel, steps),
        grid=(count, steps),
        in_specs=[
            small,
            small,
            rows,
            rows,
            pl.BlockSpec((1, width, 2 * ff), lambda j, r: (j, 0, 0)),
            pl.BlockSpec((1, ff, width), lambda j, r: (j, 0, 0)),
        ],
        out_specs=[
            rows_out,
            rows_out,
            pl.BlockSpec((1, width + ff, width), lambda j, r: (j, 0, 0)),
        ],
        out_shape=[
            shape,
            shape,
            jax.ShapeDtypeStruct((count, width + ff, width), BF),
        ],
        scratch_shapes=scratch,
        compiler_params=params(2),
        cost_estimate=pl.CostEstimate(
            flops=2 * count * sources * cap * width * ff * 9,
            bytes_accessed=8 * count * sources * cap * width + 12 * count * width * ff,
            transcendentals=count * sources * cap * ff,
        ),
        name="experts",
    )(slots[:, :, None, :], weights[:, :, None, :], x, d, win, wdown)


def combine_kernel(slot_ref, row_ref, out_ref):
    slots = slot_ref[0]
    count, here = slots.shape
    cap = row_ref.shape[2]
    lane = lax.broadcasted_iota(jnp.int32, (count, here * cap), 1)
    hot = None
    for j in range(here):
        col = slots[:, j : j + 1]
        hit = lane == jnp.where(col >= 0, col + j * cap, -1)
        hot = hit if hot is None else hot | hit
    hot = hot.astype(F32).astype(BF)
    out_ref[0] = dot(hot, row_ref[...].reshape(here * cap, row_ref.shape[3])).astype(BF)


def combine(slots_t, rows):
    sources, count, here = slots_t.shape
    _, _, cap, width = rows.shape
    return pl.pallas_call(
        combine_kernel,
        grid=(sources,),
        in_specs=[
            pl.BlockSpec((1, count, here), lambda s: (s, 0, 0)),
            pl.BlockSpec((here, 1, cap, width), lambda s: (0, s, 0, 0)),
        ],
        out_specs=pl.BlockSpec((1, count, width), lambda s: (s, 0, 0)),
        out_shape=jax.ShapeDtypeStruct((sources, count, width), BF),
        compiler_params=params(1),
        cost_estimate=pl.CostEstimate(
            flops=2 * sources * here * cap * count * width,
            bytes_accessed=2 * sources * width * (count + here * cap),
            transcendentals=0,
        ),
        name="combine",
    )(slots_t, rows)


def swap(x, bit, n):
    return lax.ppermute(x, "experts", [(i, i ^ bit) for i in range(n)])


def plane_gather(x, n):
    if n != 8:
        whole = lax.all_gather(x, "experts", axis=0)
        order = lax.axis_index("experts") ^ jnp.arange(n, dtype=jnp.int32)
        return whole[order]
    got = {0: x}
    for r in (2, 4, 6):
        got[r] = swap(x, r, n)
    for r in (0, 2, 4, 6):
        got[r + 1] = swap(got[r], 1, n)
    return jnp.stack([got[r] for r in range(n)], axis=0)


def plane_scatter(parts, n):
    if n != 8:
        order = lax.axis_index("experts") ^ jnp.arange(n, dtype=jnp.int32)
        return lax.psum_scatter(parts[order].astype(F32), "experts", scatter_dimension=0)
    odd = swap(parts[1::2], 1, n)
    both = [parts[2 * i].astype(F32) + odd[i].astype(F32) for i in range(4)]
    total = both[0]
    for i in (1, 2, 3):
        total = total + swap(both[i].astype(BF), 2 * i, n).astype(F32)
    return total


def heads_sum(x, z, nh):
    if nh != 4:
        return lax.psum(x.astype(F32), "heads")
    first = lax.ppermute(x, "heads", [(0, 1), (3, 2)])
    pair = (x.astype(F32) + first.astype(F32)).astype(BF)
    second = lax.ppermute(pair, "heads", [(1, 2), (2, 1)])
    total = (pair.astype(F32) + second.astype(F32)).astype(BF)
    third = lax.ppermute(total, "heads", [(1, 0), (2, 3)])
    return jnp.where((z == 1) | (z == 2), total, third).astype(F32)


def weight_sums(heads_in, d_branch, gathered, dqkv, ne):
    nh, tokens, part = heads_in.shape
    width, cols = d_branch.shape[1], dqkv.shape[2]
    col, row = width // ne, width // ne
    o = jnp.einsum("ztm,tew->ezmw", heads_in, d_branch.reshape(tokens, ne, col), preferred_element_type=F32)
    w = jnp.einsum("ztm,ztc->mc", gathered.reshape(nh, tokens, width), dqkv, preferred_element_type=F32)
    cut = cols // col
    w = jnp.swapaxes(w.reshape(ne, row, cut, col), 1, 2).reshape(ne, cut * row, col)
    both = jnp.concatenate([o.reshape(ne, nh * part, col), w], axis=1)
    both = lax.psum_scatter(both, "experts", scatter_dimension=0)
    o, w = both[: nh * part], both[nh * part :]
    o = lax.psum_scatter(o.reshape(nh, part, col), "heads", scatter_dimension=0)
    return weight_split(lax.all_gather(jnp.concatenate([o, w], axis=0), "experts", axis=0), part, cols)


def weight_split(both, part, cols):
    ne, _, col = both.shape
    width, row, cut = ne * col, col, cols // col
    o = jnp.swapaxes(both[:, :part], 0, 1).reshape(part, width)
    w = jnp.swapaxes(both[:, part:].reshape(ne, cut, row, col), 1, 2)
    return o, w.reshape(width, cols)


CHUNK = 128
LAG = 2
FLIGHT = 3


def remote(src, dst, send, recv, axis, index):
    return pltpu.make_async_remote_copy(
        src_ref=src, dst_ref=dst, send_sem=send, recv_sem=recv,
        device_id={axis: index}, device_id_type=MESH,
    )


def greet(nh, masks):
    z, me = lax.axis_index("heads"), lax.axis_index("experts")
    bar = pltpu.get_barrier_semaphore()
    for d in range(1, nh):
        pl.semaphore_signal(bar, inc=1, device_id={"heads": lax.rem(z + d, nh)}, device_id_type=MESH)
    for r in masks:
        pl.semaphore_signal(bar, inc=1, device_id={"experts": me ^ r}, device_id_type=MESH)
    pl.semaphore_wait(bar, nh - 1 + len(masks))


class Chain:
    def __init__(self, src, out, scratch, first, count):
        self.src, self.out, self.first, self.count = src, out, first, count
        self.flight = min(FLIGHT, count)
        self.a, self.b, self.buf, self.s1, self.r1, self.s2, self.r2, self.ls, self.os = scratch
        z = lax.axis_index("heads")
        self.mid = (z == 1) | (z == 2)
        self.outer = jnp.where(z == 0, 1, jnp.where(z == 1, 0, jnp.where(z == 2, 3, 2)))
        self.inner = jnp.where(z == 1, 2, jnp.where(z == 2, 1, z))

    def piece(self, k):
        return self.src.at[pl.ds((self.first + k) * CHUNK, CHUNK)]

    def load(self, k):
        return pltpu.make_async_copy(self.piece(k), self.buf.at[lax.rem(k, 2)], self.ls.at[lax.rem(k, 2)])

    def store(self, ref, k):
        return pltpu.make_async_copy(ref.at[k], self.out.at[pl.ds((self.first + k) * CHUNK, CHUNK)], self.os.at[k])

    def up(self, k):
        return remote(self.piece(k), self.a.at[k], self.s1.at[k], self.r1.at[k], "heads", self.outer)

    def across(self, k):
        return remote(self.a.at[k], self.b.at[k], self.s2.at[k], self.r2.at[k], "heads", self.inner)

    def down(self, k):
        return remote(self.b.at[k], self.a.at[k], self.s1.at[k], self.r1.at[k], "heads", self.outer)

    def begin(self):
        @pl.when(self.mid)
        def _():
            self.load(0).start()

        @pl.when(jnp.logical_not(self.mid))
        def _():
            @pl.loop(0, self.flight)
            def _(k):
                self.up(k).start()

    def pair(self, k):
        @pl.when(k + 1 < self.count)
        def _():
            self.load(k + 1).start()

        self.load(k).wait()
        self.up(k).wait_recv()
        own = self.buf[lax.rem(k, 2)].astype(F32)
        self.a[k] = (self.a[k].astype(F32) + own).astype(BF)
        self.across(k).start()

    def total(self, j):
        self.across(j).wait_recv()
        self.b[j] = (self.a[j].astype(F32) + self.b[j].astype(F32)).astype(BF)
        self.down(j).start()
        self.store(self.b, j).start()

    def take(self, j):
        self.down(j).wait_recv()
        self.store(self.a, j).start()

    def step(self, k, lag=LAG):
        n = self.count

        @pl.when(self.mid)
        def _():
            @pl.when(k < n)
            def _():
                self.pair(k)

            @pl.when((k >= lag) & (k < n + lag))
            def _():
                self.total(k - lag)

        @pl.when(jnp.logical_not(self.mid))
        def _():
            @pl.when(k + self.flight < n)
            def _():
                self.up(k).wait_send()
                self.up(k + self.flight).start()

            @pl.when((k >= lag + 2) & (k < n + lag + 2))
            def _():
                self.take(k - lag - 2)

    def rest(self, k):
        n = self.count

        @pl.when(self.mid)
        def _():
            @pl.loop(min(max(k - LAG, 0), n), min(max(k - 1, 0), n))
            def _(j):
                self.total(j)

        @pl.when(jnp.logical_not(self.mid))
        def _():
            @pl.loop(min(max(k - LAG - 2, 0), n), min(max(k - 3, 0), n))
            def _(j):
                self.take(j)

        @pl.loop(k, n + 3)
        def _(i):
            self.step(i, 1)

    def run(self, first, last):
        @pl.loop(first, last)
        def _(k):
            self.step(k)

    def finish(self):
        n = self.count

        @pl.when(self.mid)
        def _():
            @pl.loop(0, n)
            def _(k):
                self.across(k).wait_send()
                self.down(k).wait_send()
                self.store(self.b, k).wait()

        @pl.when(jnp.logical_not(self.mid))
        def _():
            @pl.loop(n - self.flight, n)
            def _(k):
                self.up(k).wait_send()

            @pl.loop(0, n)
            def _(k):
                self.store(self.a, k).wait()


def chain_scratch(count, width):
    return [
        pltpu.VMEM((count, CHUNK, width), BF),
        pltpu.VMEM((count, CHUNK, width), BF),
        pltpu.VMEM((2, CHUNK, width), BF),
        DMA((count,)),
        DMA((count,)),
        DMA((count,)),
        DMA((count,)),
        DMA((2,)),
        DMA((count,)),
    ]


def experts_send_kernel(count, pack_ref, x_ref, d_ref, win_ref, wdown_ref,
                        out_ref, drow_ref, grad_ref, total_ref, hid_ref, dgu_ref, early_ref, *scratch):
    j, last_j = pl.program_id(0), pl.num_programs(0) - 1
    nh = lax.axis_size("heads")
    _, sources, cap, width = x_ref.shape
    here = pack_ref.shape[1] // 2
    ff = wdown_ref.shape[1]
    chain = Chain(early_ref, total_ref, scratch, 0, count)
    per = 2
    parts = sources // per

    def chain_step(t):
        @pl.when(j > 0)
        def _():
            chain.step((j - 1) * 3 + t, 1)

    @pl.when(j == 0)
    def _():
        greet(nh, ())

    win, wdown = win_ref[0], wdown_ref[0]
    for c in range(parts):
        rows = slice(c * per * cap, (c + 1) * per * cap)
        x = x_ref[0, c * per : (c + 1) * per].reshape(per * cap, width)
        d = d_ref[0, c * per : (c + 1) * per].reshape(per * cap, width)
        gu = dot(x, win)
        gate, up = gu[:, :ff], gu[:, ff:]
        sig = 1.0 / (1.0 + jnp.exp(-gate))
        act = gate * sig
        hidden = (act * up).astype(BF)
        hid_ref[rows, :] = hidden
        result = dot(hidden, wdown).astype(BF).astype(F32)
        for b in range(per):
            s = c * per + b
            hit = pick_rows(pack_ref[s, pl.ds(j, 1)].astype(jnp.int32), cap)[0]
            w = jnp.sum(jnp.where(hit, pack_ref[s, pl.ds(here + j, 1)], 0.0), axis=1, keepdims=True)
            out_ref[0, s] = (result[b * cap : (b + 1) * cap] * w).astype(BF)
        dh = dot_nt(d, wdown)
        dgu_ref[rows, :ff] = (dh * up * (sig * (1.0 + gate * (1.0 - sig)))).astype(BF)
        dgu_ref[rows, ff:] = (dh * act).astype(BF)
        drow = dot_nt(dgu_ref[rows, :], win).astype(BF)
        for b in range(per):
            drow_ref[0, c * per + b] = drow[b * cap : (b + 1) * cap]
        if c % 2:
            chain_step(c // 2)
    gin = dot_tn(x_ref[0].reshape(sources * cap, width), dgu_ref[...]).astype(BF)
    grad_ref[0, :width] = gin
    grad_ref[0, width:] = dot_tn(hid_ref[...], d_ref[0].reshape(sources * cap, width)).astype(BF)
    chain_step(2)

    @pl.when(j == 0)
    def _():
        early_ref[...] = gin[: early_ref.shape[0]]
        chain.begin()

    @pl.when(j == last_j)
    def _():
        chain.finish()


def experts_send(count, pack, x, d, win, wdown):
    here, sources, cap, width = x.shape
    ff = wdown.shape[1]
    rows = pl.BlockSpec((1, sources, cap, width), lambda j: (j, 0, 0, 0))
    shape = jax.ShapeDtypeStruct((here, sources, cap, width), BF)
    hbm = pl.BlockSpec(memory_space=pl.ANY)
    return pl.pallas_call(
        functools.partial(experts_send_kernel, count),
        grid=(here,),
        in_specs=[
            pl.BlockSpec(memory_space=pltpu.VMEM),
            rows,
            rows,
            pl.BlockSpec((1, width, 2 * ff), lambda j: (j, 0, 0)),
            pl.BlockSpec((1, ff, width), lambda j: (j, 0, 0)),
        ],
        out_specs=[rows, rows, pl.BlockSpec((1, width + ff, width), lambda j: (j, 0, 0)), hbm],
        out_shape=[
            shape,
            shape,
            jax.ShapeDtypeStruct((here, width + ff, width), BF),
            jax.ShapeDtypeStruct((here * (width + ff), width), BF),
        ],
        scratch_shapes=[
            pltpu.VMEM((sources * cap, ff), BF),
            pltpu.VMEM((sources * cap, 2 * ff), BF),
            pltpu.VMEM((count * CHUNK, width), BF),
        ]
        + chain_scratch(count, width),
        compiler_params=pltpu.CompilerParams(
            dimension_semantics=("arbitrary",), collective_id=4, has_side_effects=True, vmem_limit_bytes=VMEM
        ),
        cost_estimate=pl.CostEstimate(
            flops=18 * here * sources * cap * width * ff,
            bytes_accessed=8 * here * sources * cap * width,
            transcendentals=here * sources * cap * ff,
        ),
        name="experts_send",
    )(pack, x, d, win, wdown)


class PlaneSum:
    order = (3, 1, 2)

    def __init__(self, rows, slots, total, scratch):
        self.rows, self.slots, self.total = rows, slots, total
        self.buf, self.odd, self.c, self.e, self.f, self.ls, self.cs, self.cr, self.fs, self.fr = scratch
        self.me = lax.axis_index("experts")
        self.here, _, self.cap, self.width = rows.shape

    def load(self, r, at):
        return [
            pltpu.make_async_copy(self.rows.at[j, r], self.buf.at[at, j], self.ls.at[at, j])
            for j in range(self.here)
        ]

    def core(self, i):
        return remote(self.odd.at[i], self.c.at[i], self.cs.at[i], self.cr.at[i], "experts", self.me ^ 1)

    def chip(self, i):
        return remote(self.e.at[i - 1], self.f.at[i - 1], self.fs.at[i - 1], self.fr.at[i - 1], "experts", self.me ^ (2 * i))

    def part(self, r, at, after, after_at):
        if after is not None:
            for c in self.load(after, after_at):
                c.start()
        slots = self.slots[r].T.astype(jnp.int32)
        lane = lax.broadcasted_iota(jnp.int32, (slots.shape[0], self.here * self.cap), 1)
        hot = None
        for j in range(self.here):
            col = slots[:, j : j + 1]
            hit = lane == jnp.where(col >= 0, col + j * self.cap, -1)
            hot = hit if hot is None else hot | hit
        for c in self.load(r, at):
            c.wait()
        rows = self.buf[at].reshape(self.here * self.cap, self.width)
        return dot(hot.astype(F32).astype(BF), rows)

    def run(self, chain=None, step=0):
        turns = [2 * i + 1 for i in self.order + (0,)] + [2 * i for i in self.order + (0,)]
        for c in self.load(turns[0], 0):
            c.start()
        for t, r in enumerate(turns):
            after = turns[t + 1] if t + 1 < len(turns) else None
            value = self.part(r, t % 2, after, (t + 1) % 2)
            i = r // 2
            if r % 2:
                self.odd[i] = value.astype(BF)
                self.core(i).start()
            else:
                self.core(i).wait_recv()
                value = value + self.c[i].astype(F32)
                if i:
                    self.e[i - 1] = value.astype(BF)
                    self.chip(i).start()
                else:
                    self.total[...] = value
            if chain is not None and t % 2:
                chain.step(step + t // 2)

    def arrive(self):
        for i in self.order:
            self.chip(i).wait_recv()

    def rows_total(self, rows):
        d = self.total[rows]
        for r in range(3):
            d = d + self.f[r, rows].astype(F32)
        return d

    def finish(self):
        for i in range(4):
            self.core(i).wait_send()
        for i in self.order:
            self.chip(i).wait_send()


def plane_scratch(here, cap, tokens, width):
    return [
        pltpu.VMEM((2, here, cap, width), BF),
        pltpu.VMEM((4, tokens, width), BF),
        pltpu.VMEM((4, tokens, width), BF),
        pltpu.VMEM((3, tokens, width), BF),
        pltpu.VMEM((3, tokens, width), BF),
        DMA((2, here)),
        DMA((4,)),
        DMA((4,)),
        DMA((3,)),
        DMA((3,)),
    ]


PLANE = 10


ROWS = 128


class Exchange:
    def __init__(self, src, dst, send, recv, nh):
        self.src, self.dst, self.ss, self.rs, self.nh = src, dst, send, recv, nh
        self.z = lax.axis_index("heads")

    def send(self, d):
        to = lax.rem(self.z + d, self.nh)
        return remote(self.src(to), self.dst(self.z), self.ss(d), self.rs(d), "heads", to)

    def start(self):
        for k in range(1, self.nh):
            self.send(jnp.where(self.z < self.nh // 2, self.nh - k, k)).start()

    def wait_recv(self):
        for d in range(1, self.nh):
            at = lax.rem(self.z + self.nh - d, self.nh)
            remote(self.src(at), self.dst(at), self.ss(d), self.rs(d), "heads", at).wait_recv()

    def finish(self):
        for d in range(1, self.nh):
            self.send(d).wait_send()


def whole_exchange(src, dst, send, recv, nh):
    return Exchange(lambda h: src.at[h], lambda h: dst.at[h], lambda d: send.at[d], lambda d: recv.at[d], nh)


class PlaneGather:
    order = (3, 1, 2)

    def __init__(self, own, slot, sems):
        self.own, self.slot = own, slot
        self.cs, self.cr, self.ks, self.kr = sems
        self.me = lax.axis_index("experts")

    def chip(self, i, e):
        return remote(self.own, self.slot(e), self.cs.at[i], self.cr.at[i], "experts", self.me ^ (2 * i))

    def core(self, i, src, e):
        return remote(src, self.slot(e), self.ks.at[i], self.kr.at[i], "experts", self.me ^ 1)

    def start(self):
        self.core(0, self.own, self.me).start()
        for i in self.order:
            self.chip(i, self.me).start()

    def forward(self, i):
        e = self.me ^ (2 * i)
        self.chip(i, e).wait_recv()
        self.core(i, self.slot(e), e).start()

    def core_arrive(self, i):
        e = self.me ^ 1 ^ (2 * i)
        self.core(i, self.slot(e), e).wait_recv()

    def finish(self):
        for i in range(1, 4):
            self.chip(i, self.me).wait_send()
        for i in range(4):
            self.core(i, self.own if i == 0 else self.slot(self.me ^ (2 * i)), self.me).wait_send()


GATHER = 4


def gather_sems():
    return [DMA((4,)), DMA((4,)), DMA((4,)), DMA((4,))]


class Picker:
    def __init__(self, pack, stage, sems, here, cap):
        self.pack, self.stage, self.sems, self.here, self.cap = pack, stage, sems, here, cap
        self.turn, self.pending = 0, {}

    def pick(self, r, tokens, out, weighted):
        at = self.turn % 2
        self.turn += 1
        info = self.pack[r]
        slots = info.astype(jnp.int32)
        index = lax.broadcasted_iota(jnp.int32, (self.cap, slots.shape[1]), 0)
        hits = [index == slots[j : j + 1] for j in range(self.here)]
        rows = dot(jnp.concatenate([h.astype(F32) for h in hits], axis=0).astype(BF), tokens)
        for c in self.pending.get(at, []):
            c.wait()
        for j, hit in enumerate(hits):
            part = rows[j * self.cap : (j + 1) * self.cap]
            if weighted:
                w = info[self.here + j : self.here + j + 1]
                part = part * jnp.sum(jnp.where(hit, w, 0.0), axis=1, keepdims=True)
            self.stage[at, j] = part.astype(BF)
        self.pending[at] = [
            pltpu.make_async_copy(self.stage.at[at, j], out.at[j, r], self.sems.at[at, j])
            for j in range(self.here)
        ]
        for c in self.pending[at]:
            c.start()

    def finish(self):
        for copies in self.pending.values():
            for c in copies:
                c.wait()


def front_kernel(len_ref, x_ref, og_ref, wq_ref, wk_ref, wv_ref, om_ref, pk_ref, again_ref, mgain_ref, cq, sq, ckv, skv,
                 xg_out, qkv_out, lse_ref, hin_out, of_out, wz_ref, mid_out, pack_ref, drows_ref, xrows_ref,
                 xg_ref, qkv_ref, hin_ref, of_ref, mid_ref, outs, w_ref, hs, ogb, mt, stage, ls, lr, ps, pr, hss, hrs, os_, or_, ws, wr, ss, *sems):
    nh, tokens, width = xg_ref.shape
    nseq, groups, full, _ = qkv_ref.shape
    ne = ogb.shape[0]
    seg = tokens // nseq
    here, _, cap, _ = drows_ref.shape
    z, me = lax.axis_index("heads"), lax.axis_index("experts")
    og = PlaneGather(og_ref, lambda e: ogb.at[e], sems[:GATHER])
    og_o = PlaneGather(of_ref.at[:, me], lambda e: of_ref.at[:, e], sems[GATHER : 2 * GATHER])

    def moe(p):
        at = pl.ds(p * seg, seg)
        return PlaneGather(mt.at[me, at], lambda e: mt.at[e, at], sems[(2 + p) * GATHER : (3 + p) * GATHER])

    moes = [moe(p) for p in range(nseq)]

    def heads(p):
        at = pl.ds(p * seg, seg)
        return Exchange(
            lambda h: hs.at[h, at], lambda h: hin_ref.at[h, at], lambda d: hss.at[p, d], lambda d: hrs.at[p, d], nh)

    picker = Picker(pack_ref, stage, ss, here, cap)

    @pl.loop(0, tokens // ROWS)
    def _(i):
        rows = pl.ds(i * ROWS, ROWS)
        x = x_ref[rows].astype(F32)
        inv = lax.rsqrt(jnp.mean(x * x, axis=-1, keepdims=True) + EPS)
        xg_ref[z, rows] = (x * inv * again_ref[...]).astype(BF)

    greet(nh, tuple(range(1, ne)))
    for g in range(groups):
        head = slice(g * HEAD, (g + 1) * HEAD)
        w_ref[:, g * 256 : g * 256 + 128] = wq_ref[:, g * 128 : (g + 1) * 128]
        w_ref[:, g * 256 + 128 : (g + 1) * 256] = jnp.concatenate([wk_ref[:, head], wv_ref[:, head]], axis=1)

    def hop(way, t, p, s, to):
        ref = xg_ref.at[s, pl.ds(p * seg, seg)]
        return remote(ref, ref, ls.at[way, t, p], lr.at[s, p], "heads", to)

    right, left = jnp.minimum(z + 1, nh - 1), jnp.maximum(z - 1, 0)
    for p in range(nseq):
        @pl.when(z < nh - 1)
        def _():
            hop(0, 0, p, z, right).start()

        @pl.when(z > 0)
        def _():
            hop(1, 0, p, z, left).start()

    def info(r):
        return remote(pk_ref.at[me ^ r], pack_ref.at[r], ps.at[r], pr.at[r], "experts", me ^ r)

    rows_o, rows_w = of_ref.shape[2], wz_ref.shape[1]
    of_ref[z, me] = om_ref[pl.ds(pl.multiple_of(me * rows_o, rows_o), rows_o)]
    wz_ref[z] = w_ref[pl.ds(pl.multiple_of(me * rows_w, rows_w), rows_w)]
    ofx = Exchange(lambda h: of_ref.at[z, me], lambda h: of_ref.at[h, me], lambda d: os_.at[d], lambda d: or_.at[d], nh)
    wzx = Exchange(lambda h: wz_ref.at[z], lambda h: wz_ref.at[h], lambda d: ws.at[d], lambda d: wr.at[d], nh)
    ofx.start()
    for r in range(1, ne):
        info(r).start()
    og.start()
    pack_ref[0] = pk_ref[me]

    def project(s, p):
        x = xg_ref[s, pl.ds(p * seg, seg)]
        at = pl.ds(s * seg, seg)
        for g in range(groups):
            lin = dot(x, w_ref[:, g * 256 : (g + 1) * 256])
            q, kv = lin[:, :128], lin[:, 128:]
            qkv_ref[p, g, at, :128] = (q * cq[at] + swap_halves(q) * sq[at]).astype(BF)
            qkv_ref[p, g, at, 128:] = (kv * ckv[at] + swap_halves(kv) * skv[at]).astype(BF)

    @pl.loop(0, nseq)
    def _(p):
        project(z, p)

    def round_of(t, then=None):
        @pl.loop(0, nseq)
        def _(p):
            @pl.when(z >= t)
            def _():
                s = z - t
                hop(0, t, p, s, left).wait_recv()

                @pl.when(z < nh - 1)
                def _():
                    hop(0, t, p, s, right).start()

                project(s, p)

            @pl.when(z + t < nh)
            def _():
                s = z + t
                hop(1, t, p, s, right).wait_recv()

                @pl.when(z > 0)
                def _():
                    hop(1, t, p, s, left).start()

                project(s, p)

            if then is not None:
                then(p)

    picker.pick(0, og_ref[...], drows_ref, True)
    round_of(1)
    for r in range(1, ne):
        info(r).wait_recv()
    og.core_arrive(0)
    picker.pick(1, ogb[me ^ 1], drows_ref, True)
    round_of(2)
    for i in og.order:
        og.forward(i)
    for i in og.order:
        picker.pick(2 * i, ogb[me ^ (2 * i)], drows_ref, True)
    ofx.wait_recv()
    og_o.start()

    def attend(p):
        length = len_ref[p]
        at = pl.ds(p * seg, seg)
        for g in range(groups):
            q = qkv_ref[p, g, :, :128]
            kv = qkv_ref[p, g, :, 128:]
            k = kv[:, :HEAD]
            vt = kv.astype(F32).T[HEAD:].astype(BF)
            for i in range(nh):
                n = (i + 1) * seg
                q2 = two_heads(q[i * seg : n])
                s = dot_nt(k[:n], q2)
                mask = attn_mask(i * seg, n, seg, length)
                s = jnp.where(jnp.concatenate([mask, mask], axis=1), s * SCALE, NEG)
                m = jnp.max(s, axis=0, keepdims=True)
                e = jnp.exp(s - m)
                total = jnp.sum(e, axis=0, keepdims=True)
                prob = (e * (1.0 / total)).astype(BF)
                lse_ref[p, g, i : i + 1, :] = m + jnp.log(total)
                hs[i, at, g * 128 : (g + 1) * 128] = untwo(dot(vt[:, :n], prob), seg).astype(BF)
        hin_ref[z, at] = hs[z, at]

        @pl.when(at_end)
        def _():
            heads(p).start()

    done = [
        pltpu.make_async_copy(src, dst, outs.at[t])
        for t, (src, dst) in enumerate(
            ((xg_ref, xg_out), (qkv_ref, qkv_out), (of_ref, of_out), (hin_ref, hin_out), (mid_ref, mid_out))
        )
    ]
    at_end = (z == 0) | (z == nh - 1)
    round_of(3, attend)
    for p in range(nseq):
        for t in range(nh):
            @pl.when((z >= t) & (z < nh - 1))
            def _():
                hop(0, t, p, z - t, right).wait_send()

            @pl.when((z + t < nh) & (z > 0))
            def _():
                hop(1, t, p, z + t, left).wait_send()

    @pl.when(jnp.logical_not(at_end))
    def _():
        for p in range(nseq):
            heads(p).start()

    for i in og.order:
        og_o.forward(i)
    for i in og.order:
        og.core_arrive(i)
        picker.pick(2 * i + 1, ogb[me ^ 1 ^ (2 * i)], drows_ref, True)
    for i in range(4):
        og_o.core_arrive(i)
    for c in done[:3]:
        c.start()

    for p in range(nseq):
        at = pl.ds(p * seg, seg)
        heads(p).wait_recv()
        mid_ref[at] = x_ref[at].astype(F32) + dot(hin_ref[0, at], of_ref[0].reshape(-1, width))
        for h in range(1, nh):
            mid_ref[at] += dot(hin_ref[h, at], of_ref[h].reshape(-1, width))

        @pl.loop(0, seg // ROWS)
        def _(i):
            rows = pl.ds(p * seg + i * ROWS, ROWS)
            m = mid_ref[rows]
            inv = lax.rsqrt(jnp.mean(m * m, axis=-1, keepdims=True) + EPS)
            mt[me, rows] = (m * inv * mgain_ref[...]).astype(BF)

        moes[p].start()

    for c in done[3:]:
        c.start()
    wzx.start()
    picker.pick(0, mt[me], xrows_ref, False)
    for p in range(nseq):
        moes[p].core_arrive(0)
    picker.pick(1, mt[me ^ 1], xrows_ref, False)
    for i in og.order:
        for p in range(nseq - 1):
            moes[p].forward(i)
    for t, i in enumerate(og.order):
        moes[-1].forward(i)
        picker.pick(2 * i, mt[me ^ (2 * i)], xrows_ref, False)
        if t:
            last = og.order[t - 1]
            for p in range(nseq):
                moes[p].core_arrive(last)
            picker.pick(2 * last + 1, mt[me ^ 1 ^ (2 * last)], xrows_ref, False)
    last = og.order[-1]
    for p in range(nseq):
        moes[p].core_arrive(last)
    picker.pick(2 * last + 1, mt[me ^ 1 ^ (2 * last)], xrows_ref, False)
    picker.finish()
    for c in done:
        c.wait()
    wzx.wait_recv()
    for gather in [og, og_o] + moes:
        gather.finish()
    for exchange in [ofx, wzx] + [heads(p) for p in range(nseq)]:
        exchange.finish()
    for r in range(1, ne):
        info(r).wait_send()


def front(lengths, x, og, wq, wk, wv, o_local, packed, attn_gain, moe_gain, tables, nh, nseq, cap):
    ne, info, _ = packed.shape
    tokens, width = x.shape
    here = info // 2
    cols = 2 * wq.shape[1]
    groups, seg = cols // 256, tokens // nseq
    full = nh * seg
    part = o_local.shape[0]
    vmem = pl.BlockSpec(memory_space=pltpu.VMEM)
    hbm = pl.BlockSpec(memory_space=pl.ANY)
    rows = jax.ShapeDtypeStruct((here, ne, cap, width), BF)
    return pl.pallas_call(
        front_kernel,
        in_specs=[pl.BlockSpec(memory_space=pltpu.SMEM)] + [vmem] * 13,
        out_specs=[hbm, hbm, vmem, hbm, hbm, vmem, hbm, vmem, hbm, hbm],
        out_shape=[
            jax.ShapeDtypeStruct((nh, tokens, width), BF),
            jax.ShapeDtypeStruct((nseq, groups, full, 256), BF),
            jax.ShapeDtypeStruct((nseq, groups, nh, 2 * seg), F32),
            jax.ShapeDtypeStruct((nh, tokens, part), BF),
            jax.ShapeDtypeStruct((nh, ne, part // ne, width), BF),
            jax.ShapeDtypeStruct((nh, width // ne, cols), BF),
            jax.ShapeDtypeStruct((tokens, width), F32),
            jax.ShapeDtypeStruct(packed.shape, F32),
            rows,
            rows,
        ],
        scratch_shapes=[
            pltpu.VMEM((nh, tokens, width), BF),
            pltpu.VMEM((nseq, groups, full, 256), BF),
            pltpu.VMEM((nh, tokens, part), BF),
            pltpu.VMEM((nh, ne, part // ne, width), BF),
            pltpu.VMEM((tokens, width), F32),
            DMA((5,)),
            pltpu.VMEM((width, cols), BF),
            pltpu.VMEM((nh, tokens, part), BF),
            pltpu.VMEM((ne, tokens, width), BF),
            pltpu.VMEM((ne, tokens, width), BF),
            pltpu.VMEM((2, here, cap, width), BF),
            DMA((2, nh, nseq)),
            DMA((nh, nseq)),
            DMA((ne,)),
            DMA((ne,)),
            DMA((nseq, nh)),
            DMA((nseq, nh)),
            DMA((nh,)),
            DMA((nh,)),
            DMA((nh,)),
            DMA((nh,)),
            DMA((2, here)),
        ]
        + gather_sems() * (2 + nseq),
        compiler_params=pltpu.CompilerParams(
            collective_id=3, has_side_effects=True, vmem_limit_bytes=VMEM
        ),
        cost_estimate=pl.CostEstimate(flops=10**11, bytes_accessed=60 * 2**20, transcendentals=10**7),
        name="front",
    )(lengths, x, og, wq, wk, wv, o_local, packed, attn_gain, moe_gain, *tables)


def middle_kernel(first, count, len_ref, begun_ref, sum_ref, rows_ref, slot_ref, mid_in, grad_in, gain_ref, o_in, qkv_in, lse_ref,
                  cq_in, sq_in, ckv_in, skv_in, hin_in, x_ref, total_ref, dmid_out, gtwo_ref, dqkv_out, po_out, pw_ref,
                  dmid_ref, dqkv_ref, po_ref, outs, mid_ref, grad_ref, o_ref, qkv_ref, cq, sq, ckv, skv, hin_ref, inputs,
                  dbranch_ref, wsum, hs, hr, dmoe, dkv, hss, hrs, xs, *scratch):
    nh, tokens, _ = dqkv_ref.shape
    nseq, groups = qkv_ref.shape[:2]
    seg = tokens // nseq
    z = lax.axis_index("heads")
    chain = Chain(sum_ref, total_ref, scratch[PLANE:], first, count)
    plane = PlaneSum(rows_ref, slot_ref, dmoe, scratch[:PLANE])
    heads = whole_exchange(hs, hr, hss, hrs, nh)
    late = [
        pltpu.make_async_copy(src, dst, inputs.at[t])
        for t, (src, dst) in enumerate(
            (
                (mid_in, mid_ref),
                (grad_in, grad_ref),
                (o_in, o_ref),
                (qkv_in, qkv_ref),
                (cq_in, cq),
                (sq_in, sq),
                (ckv_in, ckv),
                (skv_in, skv),
                (hin_in, hin_ref),
            )
        )
    ]
    for c in late:
        c.start()
    greet(nh, (1, 2, 4, 6))
    chain.begin()
    plane.run(chain, 0)
    step = 4 + 5
    chain.run(4, step)
    plane.arrive()
    for c in late:
        c.wait()
    gtwo_ref[...] = jnp.zeros_like(gtwo_ref)

    @pl.loop(0, tokens // ROWS)
    def _(i):
        rows = pl.ds(i * ROWS, ROWS)
        d = plane.rows_total(rows)
        m = mid_ref[rows]
        inv = lax.rsqrt(jnp.mean(m * m, axis=-1, keepdims=True) + EPS)
        zed = gain_ref[...] * d
        dm = grad_ref[rows].astype(F32) + inv * zed - m * (inv * inv * inv * jnp.mean(zed * m, axis=-1, keepdims=True))
        gtwo_ref[...] += jnp.sum(d * m * inv, axis=0, keepdims=True)
        dmid_ref[rows] = dm
        db = dm.astype(BF)
        dbranch_ref[rows] = db
        for h in range(nh):
            hs[h, rows] = dot_nt(db, o_ref[h]).astype(BF)

    done = [
        pltpu.make_async_copy(src, dst, outs.at[t])
        for t, (src, dst) in enumerate(((dmid_ref, dmid_out), (dqkv_ref, dqkv_out), (po_ref, po_out)))
    ]
    heads.start()
    done[0].start()
    hr[z] = hs[z]
    chain.run(step, step + 4)
    step = step + 4
    heads.wait_recv()

    @pl.loop(0, nseq)
    def _(s):
        length = len_ref[s]
        at = pl.ds(s * seg, seg)
        for g in range(groups):
            def put(i, lo, v):
                dqkv_ref[i, at, g * 256 + lo : g * 256 + lo + 128] = v

            bwd_piece(
                qkv_ref[s, g, :, :128],
                qkv_ref[s, g, :, 128:],
                lambda i: hr[i, at, g * 128 : (g + 1) * 128],
                lambda i: lse_ref[s, g, i : i + 1, :],
                length,
                (cq, sq, ckv, skv),
                dkv,
                put,
            )
            chain.step(step + groups * s + g)

    step = step + groups * nseq
    for i in range(4):
        plane.core(i).wait_send()
    load = pltpu.make_async_copy(x_ref, plane.odd, xs)
    load.start()
    done[1].start()
    ne, deep, _ = po_ref.shape
    strip, row = deep // nh, pw_ref.shape[1]
    db = dbranch_ref[...]
    for h in range(nh):
        o = dot_tn(hin_ref[h], db).astype(BF)
        for e in range(ne):
            po_ref[e, h * strip : (h + 1) * strip] = o[e * strip : (e + 1) * strip]
    done[2].start()
    chain.step(step)
    load.wait()
    wsum[...] = dot_tn(plane.odd[0], dqkv_ref[0])
    for h in range(1, nh):
        wsum[...] += dot_tn(plane.odd[h], dqkv_ref[h])
    for e in range(ne):
        pw_ref[e] = wsum[e * row : (e + 1) * row].astype(BF)
    chain.rest(step + 1)
    chain.finish()
    for i in plane.order:
        plane.chip(i).wait_send()
    heads.finish()
    for c in done:
        c.wait()


def middle(first, count, lengths, total, sums, rows, slots, mid, grad, gain, o_parts, qkv, lse, tables, heads_in, x):
    nseq, groups, full, _ = qkv.shape
    nh = o_parts.shape[0]
    tokens, width = mid.shape
    here, ne, cap, _ = rows.shape
    vmem = pl.BlockSpec(memory_space=pltpu.VMEM)
    hbm = pl.BlockSpec(memory_space=pl.ANY)
    heads = (nh, tokens, groups * 128)
    cols = groups * 256
    return pl.pallas_call(
        functools.partial(middle_kernel, first, count),
        in_specs=[pl.BlockSpec(memory_space=pltpu.SMEM), hbm, hbm, hbm, vmem, hbm, hbm, vmem, hbm, hbm, vmem] + [hbm] * 6,
        input_output_aliases={1: 0},
        out_specs=[hbm, hbm, vmem, hbm, hbm, vmem],
        out_shape=[
            jax.ShapeDtypeStruct(sums.shape, BF),
            jax.ShapeDtypeStruct((tokens, width), F32),
            jax.ShapeDtypeStruct((1, width), F32),
            jax.ShapeDtypeStruct((nh, tokens, cols), BF),
            jax.ShapeDtypeStruct((ne, nh * groups * 128 // ne, width), BF),
            jax.ShapeDtypeStruct((ne, width // ne, cols), BF),
        ],
        scratch_shapes=[
            pltpu.VMEM((tokens, width), F32),
            pltpu.VMEM((nh, tokens, cols), BF),
            pltpu.VMEM((ne, nh * groups * 128 // ne, width), BF),
            DMA((3,)),
        ]
        + [pltpu.VMEM(v.shape, v.dtype) for v in (mid, grad, o_parts, qkv) + tuple(tables) + (heads_in,)]
        + [
            DMA((9,)),
            pltpu.VMEM((tokens, width), BF),
            pltpu.VMEM((width, cols), F32),
            pltpu.VMEM(heads, BF),
            pltpu.VMEM(heads, BF),
            pltpu.VMEM((tokens, width), F32),
            pltpu.VMEM((full, 128), F32),
            DMA((nh,)),
            DMA((nh,)),
            DMA,
        ]
        + plane_scratch(here, cap, tokens, width)
        + chain_scratch(count, width),
        compiler_params=pltpu.CompilerParams(
            collective_id=1, has_side_effects=True, vmem_limit_bytes=VMEM
        ),
        cost_estimate=pl.CostEstimate(flops=10**11, bytes_accessed=30 * 2**20, transcendentals=10**7),
        name="middle",
    )(lengths, total, sums, rows, slots, mid, grad, gain, o_parts, qkv, lse, *tables, heads_in, x)


class PairSum:
    order = (3, 1, 2)

    def __init__(self, parts, scratch):
        self.parts = parts
        self.c, self.e, self.f, self.cs, self.cr, self.fs, self.fr = scratch
        self.me = lax.axis_index("experts")

    def core(self, i):
        src = self.parts.at[self.me ^ 1 ^ (2 * i)]
        return remote(src, self.c.at[i], self.cs.at[i], self.cr.at[i], "experts", self.me ^ 1)

    def chip(self, i):
        return remote(self.e.at[i - 1], self.f.at[i - 1], self.fs.at[i - 1], self.fr.at[i - 1], "experts", self.me ^ (2 * i))

    def start(self):
        for i in self.order + (0,):
            self.core(i).start()

    def both(self, i):
        return self.parts[self.me ^ (2 * i)].astype(F32) + self.c[i].astype(F32)

    def forward(self):
        for i in self.order:
            self.core(i).wait_recv()
            self.e[i - 1] = self.both(i).astype(BF)
            self.chip(i).start()
        self.core(0).wait_recv()

    def result(self):
        value = self.both(0)
        for i in self.order:
            self.chip(i).wait_recv()
        for r in range(3):
            value = value + self.f[r].astype(F32)
        return value

    def finish(self):
        for i in range(4):
            self.core(i).wait_send()
        for i in self.order:
            self.chip(i).wait_send()


PAIR = 7


def pair_scratch(shape):
    return [pltpu.VMEM((n,) + shape, BF) for n in (4, 3, 3)] + [DMA((4,)), DMA((4,)), DMA((3,)), DMA((3,))]


def last_kernel(first, count, begun_ref, sum_ref, rows_ref, slot_ref, mid_in, dqkv_ref, wz_ref, x_in, dmid_ref,
                gain_ref, gtwo_ref, po_ref, pw_ref, total_ref, out_out, xgrad_out, gains_ref, ograd_ref, qgrad_ref, kgrad_ref, vgrad_ref,
                out_ref, xgrad_ref, outs, mid_ref, x_ref, inputs, wf, br, moe, gp, gz, acc, oz, fo, fq, fk, fv, brs, brr, gps, gpr, gzs, gzr, oss, ors, fl, dl, *scratch):
    nh, tokens, _ = dqkv_ref.shape
    dattn = moe
    ne = rows_ref.shape[1]
    z, me = lax.axis_index("heads"), lax.axis_index("experts")
    at = PLANE
    plane = PlaneSum(rows_ref, slot_ref, moe, scratch[:at])
    weights = PlaneGather(wz_ref, lambda e: wf.at[:, e], scratch[at : at + GATHER])
    at += GATHER
    strip, row = fo.shape[0], fq.shape[0]

    def o_rows(e):
        return ograd_ref.at[pl.ds(pl.multiple_of(e * strip, strip), strip)]

    def w_rows(ref, e):
        return ref.at[pl.ds(pl.multiple_of(e * row, row), row)]

    spread_o = PlaneGather(fo, o_rows, scratch[at : at + GATHER])
    at += GATHER
    spreads = [spread_o]
    for mine, whole in ((fq, qgrad_ref), (fk, kgrad_ref), (fv, vgrad_ref)):
        spreads.append(PlaneGather(mine, functools.partial(w_rows, whole), scratch[at : at + GATHER]))
        at += GATHER
    sum_o = PairSum(po_ref, scratch[at : at + PAIR])
    at += PAIR
    sum_w = PairSum(pw_ref, scratch[at : at + PAIR])
    at += PAIR
    chain = Chain(sum_ref, total_ref, scratch[at:], first, count)
    back = whole_exchange(dqkv_ref, br, brs, brr, nh)
    pieces = Exchange(
        lambda h: acc.at[pl.ds(pl.multiple_of(h * strip, strip), strip)],
        lambda h: oz.at[h], lambda d: oss.at[d], lambda d: ors.at[d], nh)
    first_part = pltpu.make_async_copy(dmid_ref, xgrad_ref, dl)
    first_part.start()
    late = [
        pltpu.make_async_copy(mid_in, mid_ref, inputs.at[0]),
        pltpu.make_async_copy(x_in, x_ref, inputs.at[1]),
        pltpu.make_async_copy(dqkv_ref.at[z], br.at[z], inputs.at[2]),
    ]
    for c in late:
        c.start()
    greet(nh, tuple(range(1, ne)))
    back.start()
    sum_o.start()
    sum_w.start()
    chain.begin()
    sum_o.forward()
    sum_w.forward()
    weights.start()
    wf[:, me] = wz_ref[...]
    plane.run()
    acc[...] = sum_o.result()
    pieces.start()
    oz[z] = acc[pl.ds(pl.multiple_of(z * strip, strip), strip)]
    w = sum_w.result()
    for g in range(fq.shape[1] // 128):
        head = slice(g * HEAD, (g + 1) * HEAD)
        fq[:, g * 128 : (g + 1) * 128] = w[:, g * 256 : g * 256 + 128]
        fk[:, head] = w[:, g * 256 + 128 : g * 256 + 192]
        fv[:, head] = w[:, g * 256 + 192 : (g + 1) * 256]
    for spread in spreads[1:]:
        spread.start()
    step = 4
    chain.run(0, step)
    pieces.wait_recv()
    fo[...] = oz[0] + oz[1] + oz[2] + oz[3]
    spread_o.start()
    keep = [pltpu.make_async_copy(g.own, g.slot(me), fl.at[t]) for t, g in enumerate(spreads)]
    for c in keep:
        c.start()
    for i in weights.order:
        weights.forward(i)
    chain.run(step, step + 4)
    step = step + 4
    plane.arrive()
    for c in late:
        c.wait()

    @pl.loop(0, tokens // ROWS)
    def _(i):
        rows = pl.ds(i * ROWS, ROWS)
        out_ref[rows] = (mid_ref[rows] + plane.rows_total(rows)).astype(BF)

    done = [pltpu.make_async_copy(out_ref, out_out, outs.at[0]), pltpu.make_async_copy(xgrad_ref, xgrad_out, outs.at[1])]
    done[0].start()
    chain.run(step, step + 2)
    step = step + 2
    for i in range(4):
        weights.core_arrive(i)
    back.wait_recv()
    for h in range(nh):
        term = dot_nt(br[h], wf[h].reshape(-1, wf.shape[3]))
        if h:
            dattn[...] += term
        else:
            dattn[...] = term
    chain.run(step, step + 2)
    step = step + 2
    pad = jnp.zeros((6, gtwo_ref.shape[1]), F32)
    own = jnp.zeros_like(gtwo_ref[...])

    def rows_back(i, total):
        rows = pl.ds(i * ROWS, ROWS)
        d = dattn[rows]
        x = x_ref[rows].astype(F32)
        inv = lax.rsqrt(jnp.mean(x * x, axis=-1, keepdims=True) + EPS)
        wed = gain_ref[...] * d
        xgrad_ref[rows] += inv * wed - x * (inv * inv * inv * jnp.mean(wed * x, axis=-1, keepdims=True))
        return total + jnp.sum(d * x * inv, axis=0, keepdims=True)

    first_part.wait()
    own = lax.fori_loop(0, tokens // ROWS, rows_back, own)
    done[1].start()
    gp[me] = jnp.concatenate([own, gtwo_ref[...], pad], axis=0)

    def near(r, at):
        return remote(gp.at[me], gp.at[at], gps.at[r], gpr.at[r], "experts", me ^ r)

    for r in range(1, ne):
        near(r, me).start()
    chain.run(step, step + 2)
    step = step + 2
    for spread in spreads[1:] + spreads[:1]:
        for i in spread.order:
            spread.forward(i)
    for r in range(1, ne):
        near(r, me ^ r).wait_recv()
    total = gp[0]
    for e in range(1, ne):
        total = total + gp[e]
    gz[z] = total
    gains = Exchange(lambda h: gz.at[z], lambda h: gz.at[h], lambda d: gzs.at[d], lambda d: gzr.at[d], nh)
    gains.start()
    chain.rest(step)
    gains.wait_recv()
    total = gz[0]
    for h in range(1, nh):
        total = total + gz[h]
    gains_ref[...] = total
    for spread in spreads:
        for i in range(4):
            spread.core_arrive(i)
    chain.finish()
    for part in [plane, back, pieces, gains, weights, sum_o, sum_w] + spreads:
        part.finish()
    for c in keep + done:
        c.wait()
    for r in range(1, ne):
        near(r, me).wait_send()


def last(first, count, total, sums, rows, slots, mid, dqkv, w_pieces, x, d_mid, gain, gain_two, po, pw):
    nh, tokens, cols = dqkv.shape
    here, ne, cap, width = rows.shape
    strip = po.shape[1] // nh
    row = pw.shape[1]
    hbm = pl.BlockSpec(memory_space=pl.ANY)
    vmem = pl.BlockSpec(memory_space=pltpu.VMEM)
    return pl.pallas_call(
        functools.partial(last_kernel, first, count),
        in_specs=[hbm, hbm, hbm, vmem, hbm, hbm, vmem, hbm, hbm] + [vmem] * 4,
        input_output_aliases={0: 0},
        out_specs=[hbm] * 3 + [vmem] + [hbm] * 4,
        out_shape=[
            jax.ShapeDtypeStruct(sums.shape, BF),
            jax.ShapeDtypeStruct((tokens, width), BF),
            jax.ShapeDtypeStruct((tokens, width), F32),
            jax.ShapeDtypeStruct((8, width), F32),
            jax.ShapeDtypeStruct((strip * ne, width), F32),
            jax.ShapeDtypeStruct((row * ne, cols // 2), F32),
            jax.ShapeDtypeStruct((row * ne, cols // 4), F32),
            jax.ShapeDtypeStruct((row * ne, cols // 4), F32),
        ],
        scratch_shapes=[
            pltpu.VMEM((tokens, width), BF),
            pltpu.VMEM((tokens, width), F32),
            DMA((2,)),
            pltpu.VMEM(mid.shape, mid.dtype),
            pltpu.VMEM(x.shape, x.dtype),
            DMA((3,)),
            pltpu.VMEM((nh, ne, width // ne, cols), BF),
            pltpu.VMEM((nh, tokens, cols), BF),
            pltpu.VMEM((tokens, width), F32),
            pltpu.VMEM((ne, 8, width), F32),
            pltpu.VMEM((nh, 8, width), F32),
            pltpu.VMEM((nh * strip, width), F32),
            pltpu.VMEM((nh, strip, width), F32),
            pltpu.VMEM((strip, width), F32),
            pltpu.VMEM((row, cols // 2), F32),
            pltpu.VMEM((row, cols // 4), F32),
            pltpu.VMEM((row, cols // 4), F32),
            DMA((nh,)),
            DMA((nh,)),
            DMA((ne,)),
            DMA((ne,)),
            DMA((nh,)),
            DMA((nh,)),
            DMA((nh,)),
            DMA((nh,)),
            DMA((4,)),
            DMA,
        ]
        + plane_scratch(here, cap, tokens, width)
        + gather_sems() * 5
        + pair_scratch(po.shape[1:])
        + pair_scratch(pw.shape[1:])
        + chain_scratch(count, width),
        compiler_params=pltpu.CompilerParams(
            collective_id=2, has_side_effects=True, vmem_limit_bytes=VMEM
        ),
        cost_estimate=pl.CostEstimate(flops=2 * 10**11, bytes_accessed=30 * 2**20, transcendentals=0),
        name="last",
    )(total, sums, rows, slots, mid, dqkv, w_pieces, x, d_mid, gain, gain_two, po, pw)


def widen_kernel(x_ref, *refs):
    c = pl.program_id(1)
    count = (len(refs) - 2) // 2
    in_ref, down_ref = refs[count : count + 2]

    @pl.when(c < 2)
    def _():
        in_ref[...] = x_ref[...].astype(F32)

    @pl.when(c == 2)
    def _():
        down_ref[...] = x_ref[...].astype(F32)

    @pl.when(c == 0)
    def _():
        for src, dst in zip(refs[:count], refs[count + 2 :]):
            dst[...] = src[...]


def widen(sums, ff, others):
    here, rows, width = sums.shape
    blocks = [pl.BlockSpec((v.shape[0] // here, v.shape[1]), lambda j, c: (j, 0)) for v in others]
    return pl.pallas_call(
        widen_kernel,
        grid=(here, 3),
        in_specs=[pl.BlockSpec((1, ff, width), lambda j, c: (j, c, 0))] + blocks,
        out_specs=[
            pl.BlockSpec((1, ff, width), lambda j, c: (j, jnp.minimum(c, 1), 0)),
            pl.BlockSpec((1, ff, width), lambda j, c: (j, 0, 0)),
        ]
        + blocks,
        out_shape=[
            jax.ShapeDtypeStruct((here, 2 * ff, width), F32),
            jax.ShapeDtypeStruct((here, ff, width), F32),
        ]
        + [jax.ShapeDtypeStruct(v.shape, v.dtype) for v in others],
        compiler_params=params(2),
        name="widen",
    )(sums, *others)


def body(layer_input, seq_lengths, expert_ids, route_weight, priority, attn_gain, moe_gain,
         query_matrix, key_matrix, value_matrix, output_matrix, expert_in, expert_down, out_grad):
    seg, nseq, width = layer_input.shape
    nh, ne = lax.axis_size("heads"), lax.axis_size("experts")
    z, me = lax.axis_index("heads"), lax.axis_index("experts")
    top = expert_ids.shape[-1]
    tokens = seg * nseq
    groups = key_matrix.shape[1] // HEAD
    here = expert_in.shape[0]
    cap = (5 * tokens * top + 4 * EXPERTS - 1) // (4 * EXPERTS)

    def local(v):
        return jnp.swapaxes(v, 0, 1).reshape((tokens,) + v.shape[2:])

    def unlocal(v):
        return jnp.swapaxes(v.reshape((nseq, seg) + v.shape[1:]), 0, 1)

    ids = local(expert_ids)
    order = local(priority)
    weight = local(route_weight)
    position = z * seg + jnp.arange(seg, dtype=jnp.int32)
    live = (position[None, :] < seq_lengths[:, None]).reshape(tokens)
    match = ids.T[:, None, :] == jnp.arange(EXPERTS, dtype=jnp.int32)[None, :, None]
    weight_e = jnp.sum(jnp.where(match, weight.T[:, None, :], 0.0), axis=0)
    chosen = jnp.any(match, axis=0) & live[None, :]
    earlier = (order[:, None] < order[None, :]).astype(BF)
    before = dot(chosen.astype(BF), earlier)
    slot = jnp.where(chosen & (before < cap), before, -1.0)
    packed = jnp.concatenate([slot.reshape(ne, here, tokens), weight_e.reshape(ne, here, tokens)], axis=1)
    tables = rotary_tables(nh * seg)
    x, grad = local(layer_input), local(out_grad)
    xf = x.astype(F32)
    gain_a, gain_m = attn_gain.reshape(1, width), moe_gain.reshape(1, width)
    fast = nh == 4 and ne == 8
    if fast:
        gathered, qkv, lse, heads_in, o_full, w_pieces, mid, pack, d_rows, x_rows = front(
            seq_lengths, x, grad, query_matrix, key_matrix, value_matrix, output_matrix, packed, gain_a, gain_m, tables, nh, nseq, cap)
        o_parts = o_full.reshape(nh, groups * 128, width)
    else:
        wq = query_matrix.reshape(width, groups, 128)
        wk = key_matrix.reshape(width, groups, HEAD)
        wv = value_matrix.reshape(width, groups, HEAD)
        w_local = jnp.concatenate([wq, wk, wv], axis=2).reshape(width, groups * 256)
        packed = lax.all_to_all(packed, "experts", split_axis=0, concat_axis=0, tiled=True)
        packed = packed[me ^ jnp.arange(ne, dtype=jnp.int32)]
        slots, weights = packed[:, :here].astype(jnp.int32), packed[:, here:]
        inv_one = lax.rsqrt(jnp.mean(xf * xf, axis=-1, keepdims=True) + EPS)
        attn_in = (xf * inv_one * attn_gain).astype(BF)
        gathered = lax.all_gather(attn_in.reshape(nseq, seg, width), "heads", axis=0)
        w_groups = jnp.transpose(w_local.reshape(width, groups, 256), (1, 0, 2))
        rows_in, rows_out = width // ne, output_matrix.shape[0] // ne
        w_piece = lax.dynamic_slice_in_dim(w_local, me * rows_in, rows_in, 0)
        o_piece = lax.dynamic_slice_in_dim(output_matrix, me * rows_out, rows_out, 0)
        o_full = lax.all_gather(o_piece, ("heads", "experts"), axis=0, tiled=True)
        w_full = lax.all_gather(w_piece, ("heads", "experts"), axis=0, tiled=True)
        w_full = w_full.reshape(nh, width, groups * 256)
        qkv, heads_out, lse = attn_forward(gathered, w_groups, seq_lengths, tables)
        heads_in = lax.all_to_all(heads_out, "heads", split_axis=0, concat_axis=0, tiled=True)
        heads_in = heads_in.reshape(nh, tokens, groups * 128)
        o_parts = o_full.reshape(nh, groups * 128, width)
        branch = jnp.einsum("ztm,zmw->tw", heads_in, o_parts, preferred_element_type=F32)
        mid = xf + branch
        inv_two = lax.rsqrt(jnp.mean(mid * mid, axis=-1, keepdims=True) + EPS)
        moe_in = (mid * inv_two * moe_gain).astype(BF)
        d_rows = gather_rows(slots, weights, plane_gather(grad, ne), cap)
        x_rows = gather_rows(slots, None, plane_gather(moe_in, ne), cap)

    if fast:
        chunks = expert_in.shape[0] * (width + expert_down.shape[1]) // CHUNK
        early, half = chunks // 8, (3 * chunks) // 8
        results, drows, sums, total = experts_send(early, pack, x_rows, d_rows, expert_in, expert_down)
        flat = sums.reshape(-1, width)
        total, d_mid, gain_two, dqkv, po, pw = middle(
            early, half, seq_lengths, total, flat, drows, pack, mid, grad, gain_m, o_parts, qkv, lse, tables,
            heads_in, gathered)
        total, out, x_grad, gains, o_grad, q_grad, k_grad, v_grad = last(
            early + half, chunks - early - half, total, flat, results, pack, mid, dqkv, w_pieces, x, d_mid, gain_a, gain_two, po, pw)
        gain_one, gain_two = gains[0], gains[1]
        grad_in, grad_down, o_grad, q_grad, k_grad, v_grad = widen(
            total.reshape(sums.shape), expert_down.shape[1], (o_grad, q_grad, k_grad, v_grad))
    else:
        results, drows, sums = experts_call(slots, weights, x_rows, d_rows, expert_in, expert_down)
        slots_t = jnp.swapaxes(slots, 1, 2)
        d_parts = combine(slots_t, drows)
        moe_parts = combine(slots_t, results)
        totals = heads_sum(sums, z, nh)
        grad_in, grad_down = totals[:, :width], totals[:, width:]
        d_moe = plane_scatter(d_parts, ne)
        moe_sum = plane_scatter(moe_parts, ne)
        out = (mid + moe_sum).astype(BF)
        zed = moe_gain * d_moe
        d_mid = grad.astype(F32) + inv_two * zed - mid * (inv_two ** 3 * jnp.mean(zed * mid, axis=-1, keepdims=True))
        gain_two = jnp.sum(d_moe * mid * inv_two, axis=0)
        d_branch = d_mid.astype(BF)
        d_heads = jnp.einsum("tw,zmw->ztm", d_branch, o_parts, preferred_element_type=F32).astype(BF)
        d_heads = d_heads.reshape(nh, nseq, seg, groups * 128)
        d_heads = lax.all_to_all(d_heads, "heads", split_axis=0, concat_axis=0, tiled=True)
        dqkv = attn_backward(qkv, d_heads, lse, seq_lengths, tables)
        dqkv = dqkv.reshape(nh, tokens, groups * 256)
        back = lax.all_to_all(dqkv, "heads", split_axis=0, concat_axis=0, tiled=True)
        d_attn = jnp.einsum("ztc,zmc->tm", back, w_full, preferred_element_type=F32)
        o_grad, w_grad = weight_sums(heads_in, d_branch, gathered, dqkv, ne)
        wed = attn_gain * d_attn
        x_grad = d_mid + inv_one * wed - xf * (inv_one ** 3 * jnp.mean(wed * xf, axis=-1, keepdims=True))
        gain_one = jnp.sum(d_attn * xf * inv_one, axis=0)
        gain_one, gain_two = lax.psum((gain_one, gain_two), ("heads", "experts"))
        w_grad = w_grad.reshape(width, groups, 256)
        q_grad = w_grad[:, :, :128].reshape(query_matrix.shape)
        k_grad = w_grad[:, :, 128:192].reshape(key_matrix.shape)
        v_grad = w_grad[:, :, 192:].reshape(value_matrix.shape)
    return (
        unlocal(out),
        unlocal(x_grad),
        gain_one,
        gain_two,
        q_grad,
        k_grad,
        v_grad,
        o_grad,
        grad_in,
        grad_down,
    )


def solution(mesh):
    rows = P("heads", "experts", None)
    in_specs = (
        rows,
        P("experts"),
        rows,
        rows,
        P("heads", "experts"),
        P(),
        P(),
        P(None, "heads"),
        P(None, "heads"),
        P(None, "heads"),
        P("heads", None),
        P("experts", None, None),
        P("experts", None, None),
        rows,
    )
    out_specs = (
        rows,
        rows,
        P(),
        P(),
        P(None, "heads"),
        P(None, "heads"),
        P(None, "heads"),
        P("heads", None),
        P("experts", None, None),
        P("experts", None, None),
    )
    return jax.shard_map(body, mesh=mesh, in_specs=in_specs, out_specs=out_specs, check_vma=False)
```

```python
import functools
import math

import jax
import jax.numpy as jnp
import numpy as np
from jax import lax
from jax.experimental import pallas as pl
from jax.experimental.pallas import tpu as pltpu
from jax.sharding import PartitionSpec as P

HEAD = 64
EXPERTS = 32
EPS = 1e-06
BF = jnp.bfloat16
F32 = jnp.float32
SCALE = HEAD ** (-0.5)
NEG = -1e30
VMEM = 63 * 1024 * 1024
MESH = pl.DeviceIdType.MESH
DMA = pltpu.SemaphoreType.DMA


def dot(a, b):
    return jnp.dot(a, b, preferred_element_type=F32)


def dot_nt(a, b):
    return lax.dot_general(a, b, (((1,), (1,)), ((), ())), preferred_element_type=F32)


def dot_tn(a, b):
    return lax.dot_general(a, b, (((0,), (0,)), ((), ())), preferred_element_type=F32)


def params(n):
    return pltpu.CompilerParams(
        dimension_semantics=("arbitrary",) * n, vmem_limit_bytes=VMEM
    )


def swap_halves(v):
    lane = lax.broadcasted_iota(jnp.int32, v.shape, 1)
    return jnp.where(lane % 64 < 32, pltpu.roll(v, 96, 1), pltpu.roll(v, 32, 1))


def attn_mask(offset, n, block, length):
    key = lax.broadcasted_iota(jnp.int32, (n, block), 0)
    query = lax.broadcasted_iota(jnp.int32, (n, block), 1) + offset
    return (key <= query) & (key < length)


def two_heads(v):
    return jnp.concatenate([v[:, :HEAD], v[:, HEAD:]], axis=0)


def untwo(vt, block):
    return jnp.concatenate([vt[:, :block], vt[:, block:]], axis=0).T


def fwd_kernel(len_ref, x_ref, w_ref, cq, sq, ckv, skv, qkv_ref, head_ref, lse_ref):
    nh, _, seg, width = x_ref.shape
    full = nh * seg
    block = seg
    length = len_ref[pl.program_id(0)]
    lin = dot(x_ref[...].reshape(full, width), w_ref[0])
    ql, kvl = lin[:, :128], lin[:, 128:]
    q = (ql * cq[...] + swap_halves(ql) * sq[...]).astype(BF)
    kvr = kvl * ckv[...] + swap_halves(kvl) * skv[...]
    kv = kvr.astype(BF)
    qkv_ref[0, 0, :, :128] = q
    qkv_ref[0, 0, :, 128:] = kv
    k = kv[:, :HEAD]
    vt = kvr.T[HEAD:].astype(BF)
    for i in range(nh):
        n = (i + 1) * block
        q2 = two_heads(q[i * block : n])
        s = dot_nt(k[:n], q2)
        mask = attn_mask(i * block, n, block, length)
        s = jnp.where(jnp.concatenate([mask, mask], axis=1), s * SCALE, NEG)
        m = jnp.max(s, axis=0, keepdims=True)
        e = jnp.exp(s - m)
        total = jnp.sum(e, axis=0, keepdims=True)
        p = (e * (1.0 / total)).astype(BF)
        lse_ref[0, 0, i : i + 1, :] = m + jnp.log(total)
        head_ref[i, 0] = untwo(dot(vt[:, :n], p), block).astype(BF)


def attn_forward(x, w, lengths, tables):
    nh, nseq, seg, width = x.shape
    groups = w.shape[0]
    full = nh * seg
    cq, sq, ckv, skv = tables
    tab = pl.BlockSpec((full, 128), lambda s, g: (0, 0))
    return pl.pallas_call(
        fwd_kernel,
        grid=(nseq, groups),
        in_specs=[
            pl.BlockSpec(memory_space=pltpu.SMEM),
            pl.BlockSpec((nh, 1, seg, width), lambda s, g: (0, s, 0, 0)),
            pl.BlockSpec((1, width, 256), lambda s, g: (g, 0, 0)),
            tab,
            tab,
            tab,
            tab,
        ],
        out_specs=[
            pl.BlockSpec((1, 1, full, 256), lambda s, g: (s, g, 0, 0)),
            pl.BlockSpec((nh, 1, seg, 128), lambda s, g: (0, s, 0, g)),
            pl.BlockSpec((1, 1, nh, 2 * seg), lambda s, g: (s, g, 0, 0)),
        ],
        out_shape=[
            jax.ShapeDtypeStruct((nseq, groups, full, 256), BF),
            jax.ShapeDtypeStruct((nh, nseq, seg, groups * 128), BF),
            jax.ShapeDtypeStruct((nseq, groups, nh, 2 * seg), F32),
        ],
        compiler_params=params(2),
        cost_estimate=pl.CostEstimate(flops=6 * 10**9, bytes_accessed=12 * 2**20, transcendentals=10**7),
        name="attn_forward",
    )(lengths, x, w, cq, sq, ckv, skv)


def bwd_piece(q, kv, heads, lses, length, tables, dkv_ref, put):
    cq, sq, ckv, skv = tables
    full, block = q.shape[0], lses(0).shape[1] // 2
    k, v = kv[:, :HEAD], kv[:, HEAD:]
    kt = kv.astype(F32).T[:HEAD].astype(BF)
    dkv_ref[...] = jnp.zeros_like(dkv_ref)
    for i in range(full // block):
        n = (i + 1) * block
        rows = pl.ds(i * block, block)
        mask = attn_mask(i * block, n, block, length)
        grads = []
        for h in range(2):
            qh = q[i * block : n, h * HEAD : (h + 1) * HEAD]
            doh = heads(i)[:, h * HEAD : (h + 1) * HEAD]
            s = dot_nt(k[:n], qh)
            p = jnp.exp(jnp.where(mask, s * SCALE - lses(i)[:, h * block : (h + 1) * block], NEG))
            dp = dot_nt(v[:n], doh)
            delta = jnp.sum(p * dp, axis=0, keepdims=True)
            ds = (p * (dp - delta) * SCALE).astype(BF)
            dkv_ref[:n, :HEAD] += dot(ds, qh)
            dkv_ref[:n, HEAD:] += dot(p.astype(BF), doh)
            grads.append(dot(kt[:, :n], ds))
        dq = jnp.concatenate(grads, axis=0).T
        dq = dq * cq[rows, :] - swap_halves(dq) * sq[rows, :]
        put(i, 0, dq.astype(BF))
    dkv = dkv_ref[...]
    dkv = (dkv * ckv[...] - swap_halves(dkv) * skv[...]).astype(BF)
    for i in range(full // block):
        put(i, 128, dkv[i * block : (i + 1) * block])


def bwd_kernel(len_ref, qkv_ref, do_ref, lse_ref, cq, sq, ckv, skv, out_ref, dkv_ref):
    def put(i, lo, v):
        out_ref[i, 0, :, lo : lo + 128] = v

    bwd_piece(
        qkv_ref[0, 0, :, :128],
        qkv_ref[0, 0, :, 128:],
        lambda i: do_ref[i, 0],
        lambda i: lse_ref[0, 0, i : i + 1, :],
        len_ref[pl.program_id(0)],
        (cq, sq, ckv, skv),
        dkv_ref,
        put,
    )


def attn_backward(qkv, d_head, lse, lengths, tables):
    nseq, groups, full, _ = qkv.shape
    nh, _, seg, _ = d_head.shape
    cq, sq, ckv, skv = tables
    tab = pl.BlockSpec((full, 128), lambda s, g: (0, 0))
    return pl.pallas_call(
        bwd_kernel,
        grid=(nseq, groups),
        in_specs=[
            pl.BlockSpec(memory_space=pltpu.SMEM),
            pl.BlockSpec((1, 1, full, 256), lambda s, g: (s, g, 0, 0)),
            pl.BlockSpec((nh, 1, seg, 128), lambda s, g: (0, s, 0, g)),
            pl.BlockSpec((1, 1, nh, 2 * seg), lambda s, g: (s, g, 0, 0)),
            tab,
            tab,
            tab,
            tab,
        ],
        out_specs=pl.BlockSpec((nh, 1, seg, 256), lambda s, g: (0, s, 0, g)),
        out_shape=jax.ShapeDtypeStruct((nh, nseq, seg, groups * 256), BF),
        scratch_shapes=[pltpu.VMEM((full, 128), F32)],
        compiler_params=params(2),
        cost_estimate=pl.CostEstimate(flops=12 * 10**9, bytes_accessed=8 * 2**20, transcendentals=10**7),
        name="attn_backward",
    )(lengths, qkv, d_head, lse, cq, sq, ckv, skv)


def rotary_tables(length):
    half = HEAD // 2
    exponent = np.arange(half, dtype=np.float32) * np.float32(-2.0 * math.log(10000.0) / HEAD)
    angles = np.arange(length, dtype=np.float32)[:, None] * np.exp(exponent)[None, :]
    cos, sin = np.cos(angles), np.sin(angles)
    c1 = np.concatenate([cos, cos], axis=1)
    s1 = np.concatenate([-sin, sin], axis=1)
    cq = np.concatenate([c1, c1], axis=1)
    sq = np.concatenate([s1, s1], axis=1)
    ckv = np.concatenate([c1, np.ones_like(c1)], axis=1)
    skv = np.concatenate([s1, np.zeros_like(s1)], axis=1)
    return tuple(jnp.asarray(t, F32) for t in (cq, sq, ckv, skv))


def pick_rows(slots, cap):
    tokens = slots.shape[1]
    index = lax.broadcasted_iota(jnp.int32, (cap, tokens), 0)
    return [index == slots[j : j + 1, :] for j in range(slots.shape[0])]


def gather_kernel(weighted, slot_ref, *refs):
    if weighted:
        weight_ref, tok_ref, out_ref = refs
    else:
        tok_ref, out_ref = refs[0], refs[-1]
    cap = out_ref.shape[2]
    hits = pick_rows(slot_ref[0], cap)
    rows = dot(jnp.concatenate([h.astype(F32) for h in hits], axis=0).astype(BF), tok_ref[0])
    for j, hit in enumerate(hits):
        part = rows[j * cap : (j + 1) * cap]
        if weighted:
            part = part * jnp.sum(jnp.where(hit, weight_ref[0, j : j + 1, :], 0.0), axis=1, keepdims=True)
        out_ref[j, 0] = part.astype(BF)


def gather_rows(slots, weights, tokens, cap):
    sources, here, count = slots.shape
    width = tokens.shape[-1]
    small = pl.BlockSpec((1, here, count), lambda s: (s, 0, 0))
    weighted = weights is not None
    return pl.pallas_call(
        functools.partial(gather_kernel, weighted),
        grid=(sources,),
        in_specs=[small] + [small] * weighted + [pl.BlockSpec((1, count, width), lambda s: (s, 0, 0))],
        out_specs=pl.BlockSpec((here, 1, cap, width), lambda s: (0, s, 0, 0)),
        out_shape=jax.ShapeDtypeStruct((here, sources, cap, width), BF),
        compiler_params=params(1),
        cost_estimate=pl.CostEstimate(
            flops=2 * sources * here * cap * count * width,
            bytes_accessed=2 * sources * width * (count + here * cap),
            transcendentals=0,
        ),
        name="gather_rows",
    )(*([slots] + [weights] * weighted + [tokens]))


def expert_kernel(steps, slot_ref, weight_ref, x_ref, d_ref, win_ref, wdown_ref,
                  out_ref, drow_ref, grad_ref, hid_ref, dgu_ref, *acc):
    _, sources, cap, width = x_ref.shape
    ff = wdown_ref.shape[1]
    per = 2 if sources % 2 == 0 else 1
    win, wdown = win_ref[0], wdown_ref[0]
    for c in range(sources // per):
        rows = slice(c * per * cap, (c + 1) * per * cap)
        x = x_ref[0, c * per : (c + 1) * per].reshape(per * cap, width)
        d = d_ref[0, c * per : (c + 1) * per].reshape(per * cap, width)
        gu = dot(x, win)
        gate, up = gu[:, :ff], gu[:, ff:]
        sig = 1.0 / (1.0 + jnp.exp(-gate))
        act = gate * sig
        hidden = (act * up).astype(BF)
        hid_ref[rows, :] = hidden
        result = dot(hidden, wdown).astype(BF).astype(F32)
        for b in range(per):
            hit = pick_rows(slot_ref[c * per + b, 0], cap)[0]
            w = jnp.sum(jnp.where(hit, weight_ref[c * per + b, 0], 0.0), axis=1, keepdims=True)
            out_ref[0, c * per + b] = (result[b * cap : (b + 1) * cap] * w).astype(BF)
        dh = dot_nt(d, wdown)
        dgu_ref[rows, :ff] = (dh * up * (sig * (1.0 + gate * (1.0 - sig)))).astype(BF)
        dgu_ref[rows, ff:] = (dh * act).astype(BF)
        drow = dot_nt(dgu_ref[rows, :], win).astype(BF)
        for b in range(per):
            drow_ref[0, c * per + b] = drow[b * cap : (b + 1) * cap]
    x = x_ref[0].reshape(sources * cap, width)
    d = d_ref[0].reshape(sources * cap, width)
    gin = dot_tn(x, dgu_ref[...])
    gdown = dot_tn(hid_ref[...], d)
    if steps == 1:
        grad_ref[0, :width] = gin.astype(BF)
        grad_ref[0, width:] = gdown.astype(BF)
    else:
        ain, adown = acc
        step = pl.program_id(1)

        @pl.when(step == 0)
        def _():
            ain[...] = jnp.zeros_like(ain)
            adown[...] = jnp.zeros_like(adown)

        ain[...] += gin
        adown[...] += gdown

        @pl.when(step == steps - 1)
        def _():
            grad_ref[0, :width] = ain[...].astype(BF)
            grad_ref[0, width:] = adown[...].astype(BF)


def experts_call(slots, weights, x, d, win, wdown):
    count, sources, cap, width = x.shape
    tokens = slots.shape[-1]
    ff = wdown.shape[1]
    chunk = min(sources, 8)
    steps = sources // chunk
    small = pl.BlockSpec((chunk, 1, 1, tokens), lambda j, r: (r, j, 0, 0))
    rows = pl.BlockSpec((1, chunk, cap, width), lambda j, r: (j, r, 0, 0))
    rows_out = pl.BlockSpec((1, chunk, cap, width), lambda j, r: (j, r, 0, 0))
    scratch = [pltpu.VMEM((chunk * cap, ff), BF), pltpu.VMEM((chunk * cap, 2 * ff), BF)]
    if steps > 1:
        scratch += [pltpu.VMEM((width, 2 * ff), F32), pltpu.VMEM((ff, width), F32)]
    shape = jax.ShapeDtypeStruct((count, sources, cap, width), BF)
    return pl.pallas_call(
        functools.partial(expert_kernel, steps),
        grid=(count, steps),
        in_specs=[
            small,
            small,
            rows,
            rows,
            pl.BlockSpec((1, width, 2 * ff), lambda j, r: (j, 0, 0)),
            pl.BlockSpec((1, ff, width), lambda j, r: (j, 0, 0)),
        ],
        out_specs=[
            rows_out,
            rows_out,
            pl.BlockSpec((1, width + ff, width), lambda j, r: (j, 0, 0)),
        ],
        out_shape=[
            shape,
            shape,
            jax.ShapeDtypeStruct((count, width + ff, width), BF),
        ],
        scratch_shapes=scratch,
        compiler_params=params(2),
        cost_estimate=pl.CostEstimate(
            flops=2 * count * sources * cap * width * ff * 9,
            bytes_accessed=8 * count * sources * cap * width + 12 * count * width * ff,
            transcendentals=count * sources * cap * ff,
        ),
        name="experts",
    )(slots[:, :, None, :], weights[:, :, None, :], x, d, win, wdown)


def combine_kernel(slot_ref, row_ref, out_ref):
    slots = slot_ref[0]
    count, here = slots.shape
    cap = row_ref.shape[2]
    lane = lax.broadcasted_iota(jnp.int32, (count, here * cap), 1)
    hot = None
    for j in range(here):
        col = slots[:, j : j + 1]
        hit = lane == jnp.where(col >= 0, col + j * cap, -1)
        hot = hit if hot is None else hot | hit
    hot = hot.astype(F32).astype(BF)
    out_ref[0] = dot(hot, row_ref[...].reshape(here * cap, row_ref.shape[3])).astype(BF)


def combine(slots_t, rows):
    sources, count, here = slots_t.shape
    _, _, cap, width = rows.shape
    return pl.pallas_call(
        combine_kernel,
        grid=(sources,),
        in_specs=[
            pl.BlockSpec((1, count, here), lambda s: (s, 0, 0)),
            pl.BlockSpec((here, 1, cap, width), lambda s: (0, s, 0, 0)),
        ],
        out_specs=pl.BlockSpec((1, count, width), lambda s: (s, 0, 0)),
        out_shape=jax.ShapeDtypeStruct((sources, count, width), BF),
        compiler_params=params(1),
        cost_estimate=pl.CostEstimate(
            flops=2 * sources * here * cap * count * width,
            bytes_accessed=2 * sources * width * (count + here * cap),
            transcendentals=0,
        ),
        name="combine",
    )(slots_t, rows)


def swap(x, bit, n):
    return lax.ppermute(x, "experts", [(i, i ^ bit) for i in range(n)])


def plane_gather(x, n):
    if n != 8:
        whole = lax.all_gather(x, "experts", axis=0)
        order = lax.axis_index("experts") ^ jnp.arange(n, dtype=jnp.int32)
        return whole[order]
    got = {0: x}
    for r in (2, 4, 6):
        got[r] = swap(x, r, n)
    for r in (0, 2, 4, 6):
        got[r + 1] = swap(got[r], 1, n)
    return jnp.stack([got[r] for r in range(n)], axis=0)


def plane_scatter(parts, n):
    if n != 8:
        order = lax.axis_index("experts") ^ jnp.arange(n, dtype=jnp.int32)
        return lax.psum_scatter(parts[order].astype(F32), "experts", scatter_dimension=0)
    odd = swap(parts[1::2], 1, n)
    both = [parts[2 * i].astype(F32) + odd[i].astype(F32) for i in range(4)]
    total = both[0]
    for i in (1, 2, 3):
        total = total + swap(both[i].astype(BF), 2 * i, n).astype(F32)
    return total


def heads_sum(x, z, nh):
    if nh != 4:
        return lax.psum(x.astype(F32), "heads")
    first = lax.ppermute(x, "heads", [(0, 1), (3, 2)])
    pair = (x.astype(F32) + first.astype(F32)).astype(BF)
    second = lax.ppermute(pair, "heads", [(1, 2), (2, 1)])
    total = (pair.astype(F32) + second.astype(F32)).astype(BF)
    third = lax.ppermute(total, "heads", [(1, 0), (2, 3)])
    return jnp.where((z == 1) | (z == 2), total, third).astype(F32)


def weight_sums(heads_in, d_branch, gathered, dqkv, ne):
    nh, tokens, part = heads_in.shape
    width, cols = d_branch.shape[1], dqkv.shape[2]
    col, row = width // ne, width // ne
    o = jnp.einsum("ztm,tew->ezmw", heads_in, d_branch.reshape(tokens, ne, col), preferred_element_type=F32)
    w = jnp.einsum("ztm,ztc->mc", gathered.reshape(nh, tokens, width), dqkv, preferred_element_type=F32)
    cut = cols // col
    w = jnp.swapaxes(w.reshape(ne, row, cut, col), 1, 2).reshape(ne, cut * row, col)
    both = jnp.concatenate([o.reshape(ne, nh * part, col), w], axis=1)
    both = lax.psum_scatter(both, "experts", scatter_dimension=0)
    o, w = both[: nh * part], both[nh * part :]
    o = lax.psum_scatter(o.reshape(nh, part, col), "heads", scatter_dimension=0)
    return weight_split(lax.all_gather(jnp.concatenate([o, w], axis=0), "experts", axis=0), part, cols)


def weight_split(both, part, cols):
    ne, _, col = both.shape
    width, row, cut = ne * col, col, cols // col
    o = jnp.swapaxes(both[:, :part], 0, 1).reshape(part, width)
    w = jnp.swapaxes(both[:, part:].reshape(ne, cut, row, col), 1, 2)
    return o, w.reshape(width, cols)


CHUNK = 128
LAG = 2
FLIGHT = 3


def remote(src, dst, send, recv, axis, index):
    return pltpu.make_async_remote_copy(
        src_ref=src, dst_ref=dst, send_sem=send, recv_sem=recv,
        device_id={axis: index}, device_id_type=MESH,
    )


def greet(nh, masks):
    z, me = lax.axis_index("heads"), lax.axis_index("experts")
    bar = pltpu.get_barrier_semaphore()
    for d in range(1, nh):
        pl.semaphore_signal(bar, inc=1, device_id={"heads": lax.rem(z + d, nh)}, device_id_type=MESH)
    for r in masks:
        pl.semaphore_signal(bar, inc=1, device_id={"experts": me ^ r}, device_id_type=MESH)
    pl.semaphore_wait(bar, nh - 1 + len(masks))


class Chain:
    def __init__(self, src, out, scratch, first, count):
        self.src, self.out, self.first, self.count = src, out, first, count
        self.flight = min(FLIGHT, count)
        self.a, self.b, self.buf, self.s1, self.r1, self.s2, self.r2, self.ls, self.os = scratch
        z = lax.axis_index("heads")
        self.mid = (z == 1) | (z == 2)
        self.outer = jnp.where(z == 0, 1, jnp.where(z == 1, 0, jnp.where(z == 2, 3, 2)))
        self.inner = jnp.where(z == 1, 2, jnp.where(z == 2, 1, z))

    def piece(self, k):
        return self.src.at[pl.ds((self.first + k) * CHUNK, CHUNK)]

    def load(self, k):
        return pltpu.make_async_copy(self.piece(k), self.buf.at[lax.rem(k, 2)], self.ls.at[lax.rem(k, 2)])

    def store(self, ref, k):
        return pltpu.make_async_copy(ref.at[k], self.out.at[pl.ds((self.first + k) * CHUNK, CHUNK)], self.os.at[k])

    def up(self, k):
        return remote(self.piece(k), self.a.at[k], self.s1.at[k], self.r1.at[k], "heads", self.outer)

    def across(self, k):
        return remote(self.a.at[k], self.b.at[k], self.s2.at[k], self.r2.at[k], "heads", self.inner)

    def down(self, k):
        return remote(self.b.at[k], self.a.at[k], self.s1.at[k], self.r1.at[k], "heads", self.outer)

    def begin(self):
        @pl.when(self.mid)
        def _():
            self.load(0).start()

        @pl.when(jnp.logical_not(self.mid))
        def _():
            @pl.loop(0, self.flight)
            def _(k):
                self.up(k).start()

    def pair(self, k):
        @pl.when(k + 1 < self.count)
        def _():
            self.load(k + 1).start()

        self.load(k).wait()
        self.up(k).wait_recv()
        own = self.buf[lax.rem(k, 2)].astype(F32)
        self.a[k] = (self.a[k].astype(F32) + own).astype(BF)
        self.across(k).start()

    def total(self, j):
        self.across(j).wait_recv()
        self.b[j] = (self.a[j].astype(F32) + self.b[j].astype(F32)).astype(BF)
        self.down(j).start()
        self.store(self.b, j).start()

    def take(self, j):
        self.down(j).wait_recv()
        self.store(self.a, j).start()

    def step(self, k, lag=LAG):
        n = self.count

        @pl.when(self.mid)
        def _():
            @pl.when(k < n)
            def _():
                self.pair(k)

            @pl.when((k >= lag) & (k < n + lag))
            def _():
                self.total(k - lag)

        @pl.when(jnp.logical_not(self.mid))
        def _():
            @pl.when(k + self.flight < n)
            def _():
                self.up(k).wait_send()
                self.up(k + self.flight).start()

            @pl.when((k >= lag + 2) & (k < n + lag + 2))
            def _():
                self.take(k - lag - 2)

    def rest(self, k):
        n = self.count

        @pl.when(self.mid)
        def _():
            @pl.loop(min(max(k - LAG, 0), n), min(max(k - 1, 0), n))
            def _(j):
                self.total(j)

        @pl.when(jnp.logical_not(self.mid))
        def _():
            @pl.loop(min(max(k - LAG - 2, 0), n), min(max(k - 3, 0), n))
            def _(j):
                self.take(j)

        @pl.loop(k, n + 3)
        def _(i):
            self.step(i, 1)

    def run(self, first, last):
        @pl.loop(first, last)
        def _(k):
            self.step(k)

    def finish(self):
        n = self.count

        @pl.when(self.mid)
        def _():
            @pl.loop(0, n)
            def _(k):
                self.across(k).wait_send()
                self.down(k).wait_send()
                self.store(self.b, k).wait()

        @pl.when(jnp.logical_not(self.mid))
        def _():
            @pl.loop(n - self.flight, n)
            def _(k):
                self.up(k).wait_send()

            @pl.loop(0, n)
            def _(k):
                self.store(self.a, k).wait()


def chain_scratch(count, width):
    return [
        pltpu.VMEM((count, CHUNK, width), BF),
        pltpu.VMEM((count, CHUNK, width), BF),
        pltpu.VMEM((2, CHUNK, width), BF),
        DMA((count,)),
        DMA((count,)),
        DMA((count,)),
        DMA((count,)),
        DMA((2,)),
        DMA((count,)),
    ]


def experts_send_kernel(count, pack_ref, x_ref, d_ref, win_ref, wdown_ref,
                        out_ref, drow_ref, grad_ref, total_ref, hid_ref, dgu_ref, early_ref, *scratch):
    j, last_j = pl.program_id(0), pl.num_programs(0) - 1
    nh = lax.axis_size("heads")
    _, sources, cap, width = x_ref.shape
    here = pack_ref.shape[1] // 2
    ff = wdown_ref.shape[1]
    chain = Chain(early_ref, total_ref, scratch, 0, count)
    per = 2
    parts = sources // per

    def chain_step(t):
        @pl.when(j > 0)
        def _():
            chain.step((j - 1) * 3 + t, 1)

    @pl.when(j == 0)
    def _():
        greet(nh, ())

    win, wdown = win_ref[0], wdown_ref[0]
    for c in range(parts):
        rows = slice(c * per * cap, (c + 1) * per * cap)
        x = x_ref[0, c * per : (c + 1) * per].reshape(per * cap, width)
        d = d_ref[0, c * per : (c + 1) * per].reshape(per * cap, width)
        gu = dot(x, win)
        gate, up = gu[:, :ff], gu[:, ff:]
        sig = 1.0 / (1.0 + jnp.exp(-gate))
        act = gate * sig
        hidden = (act * up).astype(BF)
        hid_ref[rows, :] = hidden
        result = dot(hidden, wdown).astype(BF).astype(F32)
        for b in range(per):
            s = c * per + b
            hit = pick_rows(pack_ref[s, pl.ds(j, 1)].astype(jnp.int32), cap)[0]
            w = jnp.sum(jnp.where(hit, pack_ref[s, pl.ds(here + j, 1)], 0.0), axis=1, keepdims=True)
            out_ref[0, s] = (result[b * cap : (b + 1) * cap] * w).astype(BF)
        dh = dot_nt(d, wdown)
        dgu_ref[rows, :ff] = (dh * up * (sig * (1.0 + gate * (1.0 - sig)))).astype(BF)
        dgu_ref[rows, ff:] = (dh * act).astype(BF)
        drow = dot_nt(dgu_ref[rows, :], win).astype(BF)
        for b in range(per):
            drow_ref[0, c * per + b] = drow[b * cap : (b + 1) * cap]
        if c % 2:
            chain_step(c // 2)
    gin = dot_tn(x_ref[0].reshape(sources * cap, width), dgu_ref[...]).astype(BF)
    grad_ref[0, :width] = gin
    grad_ref[0, width:] = dot_tn(hid_ref[...], d_ref[0].reshape(sources * cap, width)).astype(BF)
    chain_step(2)

    @pl.when(j == 0)
    def _():
        early_ref[...] = gin[: early_ref.shape[0]]
        chain.begin()

    @pl.when(j == last_j)
    def _():
        chain.finish()


def experts_send(count, pack, x, d, win, wdown):
    here, sources, cap, width = x.shape
    ff = wdown.shape[1]
    rows = pl.BlockSpec((1, sources, cap, width), lambda j: (j, 0, 0, 0))
    shape = jax.ShapeDtypeStruct((here, sources, cap, width), BF)
    hbm = pl.BlockSpec(memory_space=pl.ANY)
    return pl.pallas_call(
        functools.partial(experts_send_kernel, count),
        grid=(here,),
        in_specs=[
            pl.BlockSpec(memory_space=pltpu.VMEM),
            rows,
            rows,
            pl.BlockSpec((1, width, 2 * ff), lambda j: (j, 0, 0)),
            pl.BlockSpec((1, ff, width), lambda j: (j, 0, 0)),
        ],
        out_specs=[rows, rows, pl.BlockSpec((1, width + ff, width), lambda j: (j, 0, 0)), hbm],
        out_shape=[
            shape,
            shape,
            jax.ShapeDtypeStruct((here, width + ff, width), BF),
            jax.ShapeDtypeStruct((here * (width + ff), width), BF),
        ],
        scratch_shapes=[
            pltpu.VMEM((sources * cap, ff), BF),
            pltpu.VMEM((sources * cap, 2 * ff), BF),
            pltpu.VMEM((count * CHUNK, width), BF),
        ]
        + chain_scratch(count, width),
        compiler_params=pltpu.CompilerParams(
            dimension_semantics=("arbitrary",), collective_id=4, has_side_effects=True, vmem_limit_bytes=VMEM
        ),
        cost_estimate=pl.CostEstimate(
            flops=18 * here * sources * cap * width * ff,
            bytes_accessed=8 * here * sources * cap * width,
            transcendentals=here * sources * cap * ff,
        ),
        name="experts_send",
    )(pack, x, d, win, wdown)


class PlaneSum:
    order = (3, 1, 2)

    def __init__(self, rows, slots, total, scratch):
        self.rows, self.slots, self.total = rows, slots, total
        self.buf, self.odd, self.c, self.e, self.f, self.ls, self.cs, self.cr, self.fs, self.fr = scratch
        self.me = lax.axis_index("experts")
        self.here, _, self.cap, self.width = rows.shape

    def load(self, r, at):
        return [
            pltpu.make_async_copy(self.rows.at[j, r], self.buf.at[at, j], self.ls.at[at, j])
            for j in range(self.here)
        ]

    def core(self, i):
        return remote(self.odd.at[i], self.c.at[i], self.cs.at[i], self.cr.at[i], "experts", self.me ^ 1)

    def chip(self, i):
        return remote(self.e.at[i - 1], self.f.at[i - 1], self.fs.at[i - 1], self.fr.at[i - 1], "experts", self.me ^ (2 * i))

    def part(self, r, at, after, after_at):
        if after is not None:
            for c in self.load(after, after_at):
                c.start()
        slots = self.slots[r].T.astype(jnp.int32)
        lane = lax.broadcasted_iota(jnp.int32, (slots.shape[0], self.here * self.cap), 1)
        hot = None
        for j in range(self.here):
            col = slots[:, j : j + 1]
            hit = lane == jnp.where(col >= 0, col + j * self.cap, -1)
            hot = hit if hot is None else hot | hit
        for c in self.load(r, at):
            c.wait()
        rows = self.buf[at].reshape(self.here * self.cap, self.width)
        return dot(hot.astype(F32).astype(BF), rows)

    def run(self, chain=None, step=0):
        turns = [2 * i + 1 for i in self.order + (0,)] + [2 * i for i in self.order + (0,)]
        for c in self.load(turns[0], 0):
            c.start()
        for t, r in enumerate(turns):
            after = turns[t + 1] if t + 1 < len(turns) else None
            value = self.part(r, t % 2, after, (t + 1) % 2)
            i = r // 2
            if r % 2:
                self.odd[i] = value.astype(BF)
                self.core(i).start()
            else:
                self.core(i).wait_recv()
                value = value + self.c[i].astype(F32)
                if i:
                    self.e[i - 1] = value.astype(BF)
                    self.chip(i).start()
                else:
                    self.total[...] = value
            if chain is not None and t % 2:
                chain.step(step + t // 2)

    def arrive(self):
        for i in self.order:
            self.chip(i).wait_recv()

    def rows_total(self, rows):
        d = self.total[rows]
        for r in range(3):
            d = d + self.f[r, rows].astype(F32)
        return d

    def finish(self):
        for i in range(4):
            self.core(i).wait_send()
        for i in self.order:
            self.chip(i).wait_send()


def plane_scratch(here, cap, tokens, width):
    return [
        pltpu.VMEM((2, here, cap, width), BF),
        pltpu.VMEM((4, tokens, width), BF),
        pltpu.VMEM((4, tokens, width), BF),
        pltpu.VMEM((3, tokens, width), BF),
        pltpu.VMEM((3, tokens, width), BF),
        DMA((2, here)),
        DMA((4,)),
        DMA((4,)),
        DMA((3,)),
        DMA((3,)),
    ]


PLANE = 10


ROWS = 128


class Exchange:
    def __init__(self, src, dst, send, recv, nh):
        self.src, self.dst, self.ss, self.rs, self.nh = src, dst, send, recv, nh
        self.z = lax.axis_index("heads")

    def send(self, d):
        to = lax.rem(self.z + d, self.nh)
        return remote(self.src(to), self.dst(self.z), self.ss(d), self.rs(d), "heads", to)

    def start(self):
        for k in range(1, self.nh):
            self.send(jnp.where(self.z < self.nh // 2, self.nh - k, k)).start()

    def wait_recv(self):
        for d in range(1, self.nh):
            at = lax.rem(self.z + self.nh - d, self.nh)
            remote(self.src(at), self.dst(at), self.ss(d), self.rs(d), "heads", at).wait_recv()

    def finish(self):
        for d in range(1, self.nh):
            self.send(d).wait_send()


def whole_exchange(src, dst, send, recv, nh):
    return Exchange(lambda h: src.at[h], lambda h: dst.at[h], lambda d: send.at[d], lambda d: recv.at[d], nh)


class PlaneGather:
    order = (3, 1, 2)

    def __init__(self, own, slot, sems):
        self.own, self.slot = own, slot
        self.cs, self.cr, self.ks, self.kr = sems
        self.me = lax.axis_index("experts")

    def chip(self, i, e):
        return remote(self.own, self.slot(e), self.cs.at[i], self.cr.at[i], "experts", self.me ^ (2 * i))

    def core(self, i, src, e):
        return remote(src, self.slot(e), self.ks.at[i], self.kr.at[i], "experts", self.me ^ 1)

    def start(self):
        self.core(0, self.own, self.me).start()
        for i in self.order:
            self.chip(i, self.me).start()

    def forward(self, i):
        e = self.me ^ (2 * i)
        self.chip(i, e).wait_recv()
        self.core(i, self.slot(e), e).start()

    def core_arrive(self, i):
        e = self.me ^ 1 ^ (2 * i)
        self.core(i, self.slot(e), e).wait_recv()

    def finish(self):
        for i in range(1, 4):
            self.chip(i, self.me).wait_send()
        for i in range(4):
            self.core(i, self.own if i == 0 else self.slot(self.me ^ (2 * i)), self.me).wait_send()


GATHER = 4


def gather_sems():
    return [DMA((4,)), DMA((4,)), DMA((4,)), DMA((4,))]


class Picker:
    def __init__(self, pack, stage, sems, here, cap):
        self.pack, self.stage, self.sems, self.here, self.cap = pack, stage, sems, here, cap
        self.turn, self.pending = 0, {}

    def pick(self, r, tokens, out, weighted):
        at = self.turn % 2
        self.turn += 1
        info = self.pack[r]
        slots = info.astype(jnp.int32)
        index = lax.broadcasted_iota(jnp.int32, (self.cap, slots.shape[1]), 0)
        hits = [index == slots[j : j + 1] for j in range(self.here)]
        rows = dot(jnp.concatenate([h.astype(F32) for h in hits], axis=0).astype(BF), tokens)
        for c in self.pending.get(at, []):
            c.wait()
        for j, hit in enumerate(hits):
            part = rows[j * self.cap : (j + 1) * self.cap]
            if weighted:
                w = info[self.here + j : self.here + j + 1]
                part = part * jnp.sum(jnp.where(hit, w, 0.0), axis=1, keepdims=True)
            self.stage[at, j] = part.astype(BF)
        self.pending[at] = [
            pltpu.make_async_copy(self.stage.at[at, j], out.at[j, r], self.sems.at[at, j])
            for j in range(self.here)
        ]
        for c in self.pending[at]:
            c.start()

    def finish(self):
        for copies in self.pending.values():
            for c in copies:
                c.wait()


def front_kernel(len_ref, x_ref, og_ref, wq_ref, wk_ref, wv_ref, om_ref, pk_ref, again_ref, mgain_ref, cq, sq, ckv, skv,
                 xg_out, qkv_out, lse_ref, hin_out, of_out, wz_ref, mid_out, pack_ref, drows_ref, xrows_ref,
                 xg_ref, qkv_ref, hin_ref, of_ref, mid_ref, outs, w_ref, hs, ogb, mt, stage, ls, lr, ps, pr, hss, hrs, os_, or_, ws, wr, ss, *sems):
    nh, tokens, width = xg_ref.shape
    nseq, groups, full, _ = qkv_ref.shape
    ne = ogb.shape[0]
    seg = tokens // nseq
    here, _, cap, _ = drows_ref.shape
    z, me = lax.axis_index("heads"), lax.axis_index("experts")
    og = PlaneGather(og_ref, lambda e: ogb.at[e], sems[:GATHER])
    og_o = PlaneGather(of_ref.at[:, me], lambda e: of_ref.at[:, e], sems[GATHER : 2 * GATHER])

    def moe(p):
        at = pl.ds(p * seg, seg)
        return PlaneGather(mt.at[me, at], lambda e: mt.at[e, at], sems[(2 + p) * GATHER : (3 + p) * GATHER])

    moes = [moe(p) for p in range(nseq)]

    def heads(p):
        at = pl.ds(p * seg, seg)
        return Exchange(
            lambda h: hs.at[h, at], lambda h: hin_ref.at[h, at], lambda d: hss.at[p, d], lambda d: hrs.at[p, d], nh)

    picker = Picker(pack_ref, stage, ss, here, cap)

    @pl.loop(0, tokens // ROWS)
    def _(i):
        rows = pl.ds(i * ROWS, ROWS)
        x = x_ref[rows].astype(F32)
        inv = lax.rsqrt(jnp.mean(x * x, axis=-1, keepdims=True) + EPS)
        xg_ref[z, rows] = (x * inv * again_ref[...]).astype(BF)

    greet(nh, tuple(range(1, ne)))
    for g in range(groups):
        head = slice(g * HEAD, (g + 1) * HEAD)
        w_ref[:, g * 256 : g * 256 + 128] = wq_ref[:, g * 128 : (g + 1) * 128]
        w_ref[:, g * 256 + 128 : (g + 1) * 256] = jnp.concatenate([wk_ref[:, head], wv_ref[:, head]], axis=1)

    def hop(way, t, p, s, to):
        ref = xg_ref.at[s, pl.ds(p * seg, seg)]
        return remote(ref, ref, ls.at[way, t, p], lr.at[s, p], "heads", to)

    right, left = jnp.minimum(z + 1, nh - 1), jnp.maximum(z - 1, 0)
    for p in range(nseq):
        @pl.when(z < nh - 1)
        def _():
            hop(0, 0, p, z, right).start()

        @pl.when(z > 0)
        def _():
            hop(1, 0, p, z, left).start()

    def info(r):
        return remote(pk_ref.at[me ^ r], pack_ref.at[r], ps.at[r], pr.at[r], "experts", me ^ r)

    rows_o, rows_w = of_ref.shape[2], wz_ref.shape[1]
    of_ref[z, me] = om_ref[pl.ds(pl.multiple_of(me * rows_o, rows_o), rows_o)]
    wz_ref[z] = w_ref[pl.ds(pl.multiple_of(me * rows_w, rows_w), rows_w)]
    ofx = Exchange(lambda h: of_ref.at[z, me], lambda h: of_ref.at[h, me], lambda d: os_.at[d], lambda d: or_.at[d], nh)
    wzx = Exchange(lambda h: wz_ref.at[z], lambda h: wz_ref.at[h], lambda d: ws.at[d], lambda d: wr.at[d], nh)
    ofx.start()
    for r in range(1, ne):
        info(r).start()
    og.start()
    pack_ref[0] = pk_ref[me]

    def project(s, p):
        x = xg_ref[s, pl.ds(p * seg, seg)]
        at = pl.ds(s * seg, seg)
        for g in range(groups):
            lin = dot(x, w_ref[:, g * 256 : (g + 1) * 256])
            q, kv = lin[:, :128], lin[:, 128:]
            qkv_ref[p, g, at, :128] = (q * cq[at] + swap_halves(q) * sq[at]).astype(BF)
            qkv_ref[p, g, at, 128:] = (kv * ckv[at] + swap_halves(kv) * skv[at]).astype(BF)

    @pl.loop(0, nseq)
    def _(p):
        project(z, p)

    def round_of(t, then=None):
        @pl.loop(0, nseq)
        def _(p):
            @pl.when(z >= t)
            def _():
                s = z - t
                hop(0, t, p, s, left).wait_recv()

                @pl.when(z < nh - 1)
                def _():
                    hop(0, t, p, s, right).start()

                project(s, p)

            @pl.when(z + t < nh)
            def _():
                s = z + t
                hop(1, t, p, s, right).wait_recv()

                @pl.when(z > 0)
                def _():
                    hop(1, t, p, s, left).start()

                project(s, p)

            if then is not None:
                then(p)

    picker.pick(0, og_ref[...], drows_ref, True)
    round_of(1)
    for r in range(1, ne):
        info(r).wait_recv()
    og.core_arrive(0)
    picker.pick(1, ogb[me ^ 1], drows_ref, True)
    round_of(2)
    for i in og.order:
        og.forward(i)
    for i in og.order:
        picker.pick(2 * i, ogb[me ^ (2 * i)], drows_ref, True)
    ofx.wait_recv()
    og_o.start()

    def attend(p):
        length = len_ref[p]
        at = pl.ds(p * seg, seg)
        for g in range(groups):
            q = qkv_ref[p, g, :, :128]
            kv = qkv_ref[p, g, :, 128:]
            k = kv[:, :HEAD]
            vt = kv.astype(F32).T[HEAD:].astype(BF)
            for i in range(nh):
                n = (i + 1) * seg
                q2 = two_heads(q[i * seg : n])
                s = dot_nt(k[:n], q2)
                mask = attn_mask(i * seg, n, seg, length)
                s = jnp.where(jnp.concatenate([mask, mask], axis=1), s * SCALE, NEG)
                m = jnp.max(s, axis=0, keepdims=True)
                e = jnp.exp(s - m)
                total = jnp.sum(e, axis=0, keepdims=True)
                prob = (e * (1.0 / total)).astype(BF)
                lse_ref[p, g, i : i + 1, :] = m + jnp.log(total)
                hs[i, at, g * 128 : (g + 1) * 128] = untwo(dot(vt[:, :n], prob), seg).astype(BF)
        hin_ref[z, at] = hs[z, at]

        @pl.when(at_end)
        def _():
            heads(p).start()

    done = [
        pltpu.make_async_copy(src, dst, outs.at[t])
        for t, (src, dst) in enumerate(
            ((xg_ref, xg_out), (qkv_ref, qkv_out), (of_ref, of_out), (hin_ref, hin_out), (mid_ref, mid_out))
        )
    ]
    at_end = (z == 0) | (z == nh - 1)
    round_of(3, attend)
    for p in range(nseq):
        for t in range(nh):
            @pl.when((z >= t) & (z < nh - 1))
            def _():
                hop(0, t, p, z - t, right).wait_send()

            @pl.when((z + t < nh) & (z > 0))
            def _():
                hop(1, t, p, z + t, left).wait_send()

    @pl.when(jnp.logical_not(at_end))
    def _():
        for p in range(nseq):
            heads(p).start()

    for i in og.order:
        og_o.forward(i)
    for i in og.order:
        og.core_arrive(i)
        picker.pick(2 * i + 1, ogb[me ^ 1 ^ (2 * i)], drows_ref, True)
    for i in range(4):
        og_o.core_arrive(i)
    for c in done[:3]:
        c.start()

    for p in range(nseq):
        at = pl.ds(p * seg, seg)
        heads(p).wait_recv()
        mid_ref[at] = x_ref[at].astype(F32) + dot(hin_ref[0, at], of_ref[0].reshape(-1, width))
        for h in range(1, nh):
            mid_ref[at] += dot(hin_ref[h, at], of_ref[h].reshape(-1, width))

        @pl.loop(0, seg // ROWS)
        def _(i):
            rows = pl.ds(p * seg + i * ROWS, ROWS)
            m = mid_ref[rows]
            inv = lax.rsqrt(jnp.mean(m * m, axis=-1, keepdims=True) + EPS)
            mt[me, rows] = (m * inv * mgain_ref[...]).astype(BF)

        moes[p].start()

    for c in done[3:]:
        c.start()
    wzx.start()
    picker.pick(0, mt[me], xrows_ref, False)
    for p in range(nseq):
        moes[p].core_arrive(0)
    picker.pick(1, mt[me ^ 1], xrows_ref, False)
    for i in og.order:
        for p in range(nseq - 1):
            moes[p].forward(i)
    for t, i in enumerate(og.order):
        moes[-1].forward(i)
        picker.pick(2 * i, mt[me ^ (2 * i)], xrows_ref, False)
        if t:
            last = og.order[t - 1]
            for p in range(nseq):
                moes[p].core_arrive(last)
            picker.pick(2 * last + 1, mt[me ^ 1 ^ (2 * last)], xrows_ref, False)
    last = og.order[-1]
    for p in range(nseq):
        moes[p].core_arrive(last)
    picker.pick(2 * last + 1, mt[me ^ 1 ^ (2 * last)], xrows_ref, False)
    picker.finish()
    for c in done:
        c.wait()
    wzx.wait_recv()
    for gather in [og, og_o] + moes:
        gather.finish()
    for exchange in [ofx, wzx] + [heads(p) for p in range(nseq)]:
        exchange.finish()
    for r in range(1, ne):
        info(r).wait_send()


def front(lengths, x, og, wq, wk, wv, o_local, packed, attn_gain, moe_gain, tables, nh, nseq, cap):
    ne, info, _ = packed.shape
    tokens, width = x.shape
    here = info // 2
    cols = 2 * wq.shape[1]
    groups, seg = cols // 256, tokens // nseq
    full = nh * seg
    part = o_local.shape[0]
    vmem = pl.BlockSpec(memory_space=pltpu.VMEM)
    hbm = pl.BlockSpec(memory_space=pl.ANY)
    rows = jax.ShapeDtypeStruct((here, ne, cap, width), BF)
    return pl.pallas_call(
        front_kernel,
        in_specs=[pl.BlockSpec(memory_space=pltpu.SMEM)] + [vmem] * 13,
        out_specs=[hbm, hbm, vmem, hbm, hbm, vmem, hbm, vmem, hbm, hbm],
        out_shape=[
            jax.ShapeDtypeStruct((nh, tokens, width), BF),
            jax.ShapeDtypeStruct((nseq, groups, full, 256), BF),
            jax.ShapeDtypeStruct((nseq, groups, nh, 2 * seg), F32),
            jax.ShapeDtypeStruct((nh, tokens, part), BF),
            jax.ShapeDtypeStruct((nh, ne, part // ne, width), BF),
            jax.ShapeDtypeStruct((nh, width // ne, cols), BF),
            jax.ShapeDtypeStruct((tokens, width), F32),
            jax.ShapeDtypeStruct(packed.shape, F32),
            rows,
            rows,
        ],
        scratch_shapes=[
            pltpu.VMEM((nh, tokens, width), BF),
            pltpu.VMEM((nseq, groups, full, 256), BF),
            pltpu.VMEM((nh, tokens, part), BF),
            pltpu.VMEM((nh, ne, part // ne, width), BF),
            pltpu.VMEM((tokens, width), F32),
            DMA((5,)),
            pltpu.VMEM((width, cols), BF),
            pltpu.VMEM((nh, tokens, part), BF),
            pltpu.VMEM((ne, tokens, width), BF),
            pltpu.VMEM((ne, tokens, width), BF),
            pltpu.VMEM((2, here, cap, width), BF),
            DMA((2, nh, nseq)),
            DMA((nh, nseq)),
            DMA((ne,)),
            DMA((ne,)),
            DMA((nseq, nh)),
            DMA((nseq, nh)),
            DMA((nh,)),
            DMA((nh,)),
            DMA((nh,)),
            DMA((nh,)),
            DMA((2, here)),
        ]
        + gather_sems() * (2 + nseq),
        compiler_params=pltpu.CompilerParams(
            collective_id=3, has_side_effects=True, vmem_limit_bytes=VMEM
        ),
        cost_estimate=pl.CostEstimate(flops=10**11, bytes_accessed=60 * 2**20, transcendentals=10**7),
        name="front",
    )(lengths, x, og, wq, wk, wv, o_local, packed, attn_gain, moe_gain, *tables)


def middle_kernel(first, count, len_ref, begun_ref, sum_ref, rows_ref, slot_ref, mid_in, grad_in, gain_ref, o_in, qkv_in, lse_ref,
                  cq_in, sq_in, ckv_in, skv_in, hin_in, x_ref, total_ref, dmid_out, gtwo_ref, dqkv_out, po_out, pw_ref,
                  dmid_ref, dqkv_ref, po_ref, outs, mid_ref, grad_ref, o_ref, qkv_ref, cq, sq, ckv, skv, hin_ref, inputs,
                  dbranch_ref, wsum, hs, hr, dmoe, dkv, hss, hrs, xs, *scratch):
    nh, tokens, _ = dqkv_ref.shape
    nseq, groups = qkv_ref.shape[:2]
    seg = tokens // nseq
    z = lax.axis_index("heads")
    chain = Chain(sum_ref, total_ref, scratch[PLANE:], first, count)
    plane = PlaneSum(rows_ref, slot_ref, dmoe, scratch[:PLANE])
    heads = whole_exchange(hs, hr, hss, hrs, nh)
    late = [
        pltpu.make_async_copy(src, dst, inputs.at[t])
        for t, (src, dst) in enumerate(
            (
                (mid_in, mid_ref),
                (grad_in, grad_ref),
                (o_in, o_ref),
                (qkv_in, qkv_ref),
                (cq_in, cq),
                (sq_in, sq),
                (ckv_in, ckv),
                (skv_in, skv),
                (hin_in, hin_ref),
            )
        )
    ]
    for c in late:
        c.start()
    greet(nh, (1, 2, 4, 6))
    chain.begin()
    plane.run(chain, 0)
    step = 4 + 5
    chain.run(4, step)
    plane.arrive()
    for c in late:
        c.wait()
    gtwo_ref[...] = jnp.zeros_like(gtwo_ref)

    @pl.loop(0, tokens // ROWS)
    def _(i):
        rows = pl.ds(i * ROWS, ROWS)
        d = plane.rows_total(rows)
        m = mid_ref[rows]
        inv = lax.rsqrt(jnp.mean(m * m, axis=-1, keepdims=True) + EPS)
        zed = gain_ref[...] * d
        dm = grad_ref[rows].astype(F32) + inv * zed - m * (inv * inv * inv * jnp.mean(zed * m, axis=-1, keepdims=True))
        gtwo_ref[...] += jnp.sum(d * m * inv, axis=0, keepdims=True)
        dmid_ref[rows] = dm
        db = dm.astype(BF)
        dbranch_ref[rows] = db
        for h in range(nh):
            hs[h, rows] = dot_nt(db, o_ref[h]).astype(BF)

    done = [
        pltpu.make_async_copy(src, dst, outs.at[t])
        for t, (src, dst) in enumerate(((dmid_ref, dmid_out), (dqkv_ref, dqkv_out), (po_ref, po_out)))
    ]
    heads.start()
    done[0].start()
    hr[z] = hs[z]
    chain.run(step, step + 4)
    step = step + 4
    heads.wait_recv()

    @pl.loop(0, nseq)
    def _(s):
        length = len_ref[s]
        at = pl.ds(s * seg, seg)
        for g in range(groups):
            def put(i, lo, v):
                dqkv_ref[i, at, g * 256 + lo : g * 256 + lo + 128] = v

            bwd_piece(
                qkv_ref[s, g, :, :128],
                qkv_ref[s, g, :, 128:],
                lambda i: hr[i, at, g * 128 : (g + 1) * 128],
                lambda i: lse_ref[s, g, i : i + 1, :],
                length,
                (cq, sq, ckv, skv),
                dkv,
                put,
            )
            chain.step(step + groups * s + g)

    step = step + groups * nseq
    for i in range(4):
        plane.core(i).wait_send()
    load = pltpu.make_async_copy(x_ref, plane.odd, xs)
    load.start()
    done[1].start()
    ne, deep, _ = po_ref.shape
    strip, row = deep // nh, pw_ref.shape[1]
    db = dbranch_ref[...]
    for h in range(nh):
        o = dot_tn(hin_ref[h], db).astype(BF)
        for e in range(ne):
            po_ref[e, h * strip : (h + 1) * strip] = o[e * strip : (e + 1) * strip]
    done[2].start()
    chain.step(step)
    load.wait()
    wsum[...] = dot_tn(plane.odd[0], dqkv_ref[0])
    for h in range(1, nh):
        wsum[...] += dot_tn(plane.odd[h], dqkv_ref[h])
    for e in range(ne):
        pw_ref[e] = wsum[e * row : (e + 1) * row].astype(BF)
    chain.rest(step + 1)
    chain.finish()
    for i in plane.order:
        plane.chip(i).wait_send()
    heads.finish()
    for c in done:
        c.wait()


def middle(first, count, lengths, total, sums, rows, slots, mid, grad, gain, o_parts, qkv, lse, tables, heads_in, x):
    nseq, groups, full, _ = qkv.shape
    nh = o_parts.shape[0]
    tokens, width = mid.shape
    here, ne, cap, _ = rows.shape
    vmem = pl.BlockSpec(memory_space=pltpu.VMEM)
    hbm = pl.BlockSpec(memory_space=pl.ANY)
    heads = (nh, tokens, groups * 128)
    cols = groups * 256
    return pl.pallas_call(
        functools.partial(middle_kernel, first, count),
        in_specs=[pl.BlockSpec(memory_space=pltpu.SMEM), hbm, hbm, hbm, vmem, hbm, hbm, vmem, hbm, hbm, vmem] + [hbm] * 6,
        input_output_aliases={1: 0},
        out_specs=[hbm, hbm, vmem, hbm, hbm, vmem],
        out_shape=[
            jax.ShapeDtypeStruct(sums.shape, BF),
            jax.ShapeDtypeStruct((tokens, width), F32),
            jax.ShapeDtypeStruct((1, width), F32),
            jax.ShapeDtypeStruct((nh, tokens, cols), BF),
            jax.ShapeDtypeStruct((ne, nh * groups * 128 // ne, width), BF),
            jax.ShapeDtypeStruct((ne, width // ne, cols), BF),
        ],
        scratch_shapes=[
            pltpu.VMEM((tokens, width), F32),
            pltpu.VMEM((nh, tokens, cols), BF),
            pltpu.VMEM((ne, nh * groups * 128 // ne, width), BF),
            DMA((3,)),
        ]
        + [pltpu.VMEM(v.shape, v.dtype) for v in (mid, grad, o_parts, qkv) + tuple(tables) + (heads_in,)]
        + [
            DMA((9,)),
            pltpu.VMEM((tokens, width), BF),
            pltpu.VMEM((width, cols), F32),
            pltpu.VMEM(heads, BF),
            pltpu.VMEM(heads, BF),
            pltpu.VMEM((tokens, width), F32),
            pltpu.VMEM((full, 128), F32),
            DMA((nh,)),
            DMA((nh,)),
            DMA,
        ]
        + plane_scratch(here, cap, tokens, width)
        + chain_scratch(count, width),
        compiler_params=pltpu.CompilerParams(
            collective_id=1, has_side_effects=True, vmem_limit_bytes=VMEM
        ),
        cost_estimate=pl.CostEstimate(flops=10**11, bytes_accessed=30 * 2**20, transcendentals=10**7),
        name="middle",
    )(lengths, total, sums, rows, slots, mid, grad, gain, o_parts, qkv, lse, *tables, heads_in, x)


class PairSum:
    order = (3, 1, 2)

    def __init__(self, parts, scratch):
        self.parts = parts
        self.c, self.e, self.f, self.cs, self.cr, self.fs, self.fr = scratch
        self.me = lax.axis_index("experts")

    def core(self, i):
        src = self.parts.at[self.me ^ 1 ^ (2 * i)]
        return remote(src, self.c.at[i], self.cs.at[i], self.cr.at[i], "experts", self.me ^ 1)

    def chip(self, i):
        return remote(self.e.at[i - 1], self.f.at[i - 1], self.fs.at[i - 1], self.fr.at[i - 1], "experts", self.me ^ (2 * i))

    def start(self):
        for i in self.order + (0,):
            self.core(i).start()

    def both(self, i):
        return self.parts[self.me ^ (2 * i)].astype(F32) + self.c[i].astype(F32)

    def forward(self):
        for i in self.order:
            self.core(i).wait_recv()
            self.e[i - 1] = self.both(i).astype(BF)
            self.chip(i).start()
        self.core(0).wait_recv()

    def result(self):
        value = self.both(0)
        for i in self.order:
            self.chip(i).wait_recv()
        for r in range(3):
            value = value + self.f[r].astype(F32)
        return value

    def finish(self):
        for i in range(4):
            self.core(i).wait_send()
        for i in self.order:
            self.chip(i).wait_send()


PAIR = 7


def pair_scratch(shape):
    return [pltpu.VMEM((n,) + shape, BF) for n in (4, 3, 3)] + [DMA((4,)), DMA((4,)), DMA((3,)), DMA((3,))]


def last_kernel(first, count, begun_ref, sum_ref, rows_ref, slot_ref, mid_in, dqkv_ref, wz_ref, x_in, dmid_ref,
                gain_ref, gtwo_ref, po_ref, pw_ref, total_ref, out_out, xgrad_out, gains_ref, ograd_ref, qgrad_ref, kgrad_ref, vgrad_ref,
                out_ref, xgrad_ref, outs, mid_ref, x_ref, inputs, wf, br, moe, gp, gz, acc, oz, fo, fq, fk, fv, brs, brr, gps, gpr, gzs, gzr, oss, ors, fl, dl, *scratch):
    nh, tokens, _ = dqkv_ref.shape
    dattn = moe
    ne = rows_ref.shape[1]
    z, me = lax.axis_index("heads"), lax.axis_index("experts")
    at = PLANE
    plane = PlaneSum(rows_ref, slot_ref, moe, scratch[:at])
    weights = PlaneGather(wz_ref, lambda e: wf.at[:, e], scratch[at : at + GATHER])
    at += GATHER
    strip, row = fo.shape[0], fq.shape[0]

    def o_rows(e):
        return ograd_ref.at[pl.ds(pl.multiple_of(e * strip, strip), strip)]

    def w_rows(ref, e):
        return ref.at[pl.ds(pl.multiple_of(e * row, row), row)]

    spread_o = PlaneGather(fo, o_rows, scratch[at : at + GATHER])
    at += GATHER
    spreads = [spread_o]
    for mine, whole in ((fq, qgrad_ref), (fk, kgrad_ref), (fv, vgrad_ref)):
        spreads.append(PlaneGather(mine, functools.partial(w_rows, whole), scratch[at : at + GATHER]))
        at += GATHER
    sum_o = PairSum(po_ref, scratch[at : at + PAIR])
    at += PAIR
    sum_w = PairSum(pw_ref, scratch[at : at + PAIR])
    at += PAIR
    chain = Chain(sum_ref, total_ref, scratch[at:], first, count)
    back = whole_exchange(dqkv_ref, br, brs, brr, nh)
    pieces = Exchange(
        lambda h: acc.at[pl.ds(pl.multiple_of(h * strip, strip), strip)],
        lambda h: oz.at[h], lambda d: oss.at[d], lambda d: ors.at[d], nh)
    first_part = pltpu.make_async_copy(dmid_ref, xgrad_ref, dl)
    first_part.start()
    late = [
        pltpu.make_async_copy(mid_in, mid_ref, inputs.at[0]),
        pltpu.make_async_copy(x_in, x_ref, inputs.at[1]),
        pltpu.make_async_copy(dqkv_ref.at[z], br.at[z], inputs.at[2]),
    ]
    for c in late:
        c.start()
    greet(nh, tuple(range(1, ne)))
    back.start()
    sum_o.start()
    sum_w.start()
    chain.begin()
    sum_o.forward()
    sum_w.forward()
    weights.start()
    wf[:, me] = wz_ref[...]
    plane.run()
    acc[...] = sum_o.result()
    pieces.start()
    oz[z] = acc[pl.ds(pl.multiple_of(z * strip, strip), strip)]
    w = sum_w.result()
    for g in range(fq.shape[1] // 128):
        head = slice(g * HEAD, (g + 1) * HEAD)
        fq[:, g * 128 : (g + 1) * 128] = w[:, g * 256 : g * 256 + 128]
        fk[:, head] = w[:, g * 256 + 128 : g * 256 + 192]
        fv[:, head] = w[:, g * 256 + 192 : (g + 1) * 256]
    for spread in spreads[1:]:
        spread.start()
    step = 4
    chain.run(0, step)
    pieces.wait_recv()
    fo[...] = oz[0] + oz[1] + oz[2] + oz[3]
    spread_o.start()
    keep = [pltpu.make_async_copy(g.own, g.slot(me), fl.at[t]) for t, g in enumerate(spreads)]
    for c in keep:
        c.start()
    for i in weights.order:
        weights.forward(i)
    chain.run(step, step + 4)
    step = step + 4
    plane.arrive()
    for c in late:
        c.wait()

    @pl.loop(0, tokens // ROWS)
    def _(i):
        rows = pl.ds(i * ROWS, ROWS)
        out_ref[rows] = (mid_ref[rows] + plane.rows_total(rows)).astype(BF)

    done = [pltpu.make_async_copy(out_ref, out_out, outs.at[0]), pltpu.make_async_copy(xgrad_ref, xgrad_out, outs.at[1])]
    done[0].start()
    chain.run(step, step + 2)
    step = step + 2
    for i in range(4):
        weights.core_arrive(i)
    back.wait_recv()
    for h in range(nh):
        term = dot_nt(br[h], wf[h].reshape(-1, wf.shape[3]))
        if h:
            dattn[...] += term
        else:
            dattn[...] = term
    chain.run(step, step + 2)
    step = step + 2
    pad = jnp.zeros((6, gtwo_ref.shape[1]), F32)
    own = jnp.zeros_like(gtwo_ref[...])

    def rows_back(i, total):
        rows = pl.ds(i * ROWS, ROWS)
        d = dattn[rows]
        x = x_ref[rows].astype(F32)
        inv = lax.rsqrt(jnp.mean(x * x, axis=-1, keepdims=True) + EPS)
        wed = gain_ref[...] * d
        xgrad_ref[rows] += inv * wed - x * (inv * inv * inv * jnp.mean(wed * x, axis=-1, keepdims=True))
        return total + jnp.sum(d * x * inv, axis=0, keepdims=True)

    first_part.wait()
    own = lax.fori_loop(0, tokens // ROWS, rows_back, own)
    done[1].start()
    gp[me] = jnp.concatenate([own, gtwo_ref[...], pad], axis=0)

    def near(r, at):
        return remote(gp.at[me], gp.at[at], gps.at[r], gpr.at[r], "experts", me ^ r)

    for r in range(1, ne):
        near(r, me).start()
    chain.run(step, step + 2)
    step = step + 2
    for spread in spreads[1:] + spreads[:1]:
        for i in spread.order:
            spread.forward(i)
    for r in range(1, ne):
        near(r, me ^ r).wait_recv()
    total = gp[0]
    for e in range(1, ne):
        total = total + gp[e]
    gz[z] = total
    gains = Exchange(lambda h: gz.at[z], lambda h: gz.at[h], lambda d: gzs.at[d], lambda d: gzr.at[d], nh)
    gains.start()
    chain.rest(step)
    gains.wait_recv()
    total = gz[0]
    for h in range(1, nh):
        total = total + gz[h]
    gains_ref[...] = total
    for spread in spreads:
        for i in range(4):
            spread.core_arrive(i)
    chain.finish()
    for part in [plane, back, pieces, gains, weights, sum_o, sum_w] + spreads:
        part.finish()
    for c in keep + done:
        c.wait()
    for r in range(1, ne):
        near(r, me).wait_send()


def last(first, count, total, sums, rows, slots, mid, dqkv, w_pieces, x, d_mid, gain, gain_two, po, pw):
    nh, tokens, cols = dqkv.shape
    here, ne, cap, width = rows.shape
    strip = po.shape[1] // nh
    row = pw.shape[1]
    hbm = pl.BlockSpec(memory_space=pl.ANY)
    vmem = pl.BlockSpec(memory_space=pltpu.VMEM)
    return pl.pallas_call(
        functools.partial(last_kernel, first, count),
        in_specs=[hbm, hbm, hbm, vmem, hbm, hbm, vmem, hbm, hbm] + [vmem] * 4,
        input_output_aliases={0: 0},
        out_specs=[hbm] * 3 + [vmem] + [hbm] * 4,
        out_shape=[
            jax.ShapeDtypeStruct(sums.shape, BF),
            jax.ShapeDtypeStruct((tokens, width), BF),
            jax.ShapeDtypeStruct((tokens, width), F32),
            jax.ShapeDtypeStruct((8, width), F32),
            jax.ShapeDtypeStruct((strip * ne, width), F32),
            jax.ShapeDtypeStruct((row * ne, cols // 2), F32),
            jax.ShapeDtypeStruct((row * ne, cols // 4), F32),
            jax.ShapeDtypeStruct((row * ne, cols // 4), F32),
        ],
        scratch_shapes=[
            pltpu.VMEM((tokens, width), BF),
            pltpu.VMEM((tokens, width), F32),
            DMA((2,)),
            pltpu.VMEM(mid.shape, mid.dtype),
            pltpu.VMEM(x.shape, x.dtype),
            DMA((3,)),
            pltpu.VMEM((nh, ne, width // ne, cols), BF),
            pltpu.VMEM((nh, tokens, cols), BF),
            pltpu.VMEM((tokens, width), F32),
            pltpu.VMEM((ne, 8, width), F32),
            pltpu.VMEM((nh, 8, width), F32),
            pltpu.VMEM((nh * strip, width), F32),
            pltpu.VMEM((nh, strip, width), F32),
            pltpu.VMEM((strip, width), F32),
            pltpu.VMEM((row, cols // 2), F32),
            pltpu.VMEM((row, cols // 4), F32),
            pltpu.VMEM((row, cols // 4), F32),
            DMA((nh,)),
            DMA((nh,)),
            DMA((ne,)),
            DMA((ne,)),
            DMA((nh,)),
            DMA((nh,)),
            DMA((nh,)),
            DMA((nh,)),
            DMA((4,)),
            DMA,
        ]
        + plane_scratch(here, cap, tokens, width)
        + gather_sems() * 5
        + pair_scratch(po.shape[1:])
        + pair_scratch(pw.shape[1:])
        + chain_scratch(count, width),
        compiler_params=pltpu.CompilerParams(
            collective_id=2, has_side_effects=True, vmem_limit_bytes=VMEM
        ),
        cost_estimate=pl.CostEstimate(flops=2 * 10**11, bytes_accessed=30 * 2**20, transcendentals=0),
        name="last",
    )(total, sums, rows, slots, mid, dqkv, w_pieces, x, d_mid, gain, gain_two, po, pw)


def widen_kernel(x_ref, *refs):
    c = pl.program_id(1)
    count = (len(refs) - 2) // 2
    in_ref, down_ref = refs[count : count + 2]

    @pl.when(c < 2)
    def _():
        in_ref[...] = x_ref[...].astype(F32)

    @pl.when(c == 2)
    def _():
        down_ref[...] = x_ref[...].astype(F32)

    @pl.when(c == 0)
    def _():
        for src, dst in zip(refs[:count], refs[count + 2 :]):
            if len(dst.shape) == 2:
                dst[...] = src[...]
            else:
                for q in range(dst.shape[1]):
                    dst[:, q, :] = src[q]


def widen(sums, ff, others, turned):
    here, rows, width = sums.shape
    blocks = [pl.BlockSpec((v.shape[0] // here, v.shape[1]), lambda j, c: (j, 0)) for v in others]
    count, length, _ = turned.shape
    part = length // here
    turn_in = pl.BlockSpec((count, part, width), lambda j, c: (0, j, 0))
    turn_out = pl.BlockSpec((part, count, width), lambda j, c: (j, 0, 0))
    return pl.pallas_call(
        widen_kernel,
        grid=(here, 3),
        in_specs=[pl.BlockSpec((1, ff, width), lambda j, c: (j, c, 0))] + blocks + [turn_in],
        out_specs=[
            pl.BlockSpec((1, ff, width), lambda j, c: (j, jnp.minimum(c, 1), 0)),
            pl.BlockSpec((1, ff, width), lambda j, c: (j, 0, 0)),
        ]
        + blocks
        + [turn_out],
        out_shape=[
            jax.ShapeDtypeStruct((here, 2 * ff, width), F32),
            jax.ShapeDtypeStruct((here, ff, width), F32),
        ]
        + [jax.ShapeDtypeStruct(v.shape, v.dtype) for v in others]
        + [jax.ShapeDtypeStruct((length, count, width), turned.dtype)],
        compiler_params=params(2),
        name="widen",
    )(sums, *others, turned)


def body(layer_input, seq_lengths, expert_ids, route_weight, priority, attn_gain, moe_gain,
         query_matrix, key_matrix, value_matrix, output_matrix, expert_in, expert_down, out_grad):
    seg, nseq, width = layer_input.shape
    nh, ne = lax.axis_size("heads"), lax.axis_size("experts")
    z, me = lax.axis_index("heads"), lax.axis_index("experts")
    top = expert_ids.shape[-1]
    tokens = seg * nseq
    groups = key_matrix.shape[1] // HEAD
    here = expert_in.shape[0]
    cap = (5 * tokens * top + 4 * EXPERTS - 1) // (4 * EXPERTS)

    def local(v):
        return jnp.swapaxes(v, 0, 1).reshape((tokens,) + v.shape[2:])

    def unlocal(v):
        return jnp.swapaxes(v.reshape((nseq, seg) + v.shape[1:]), 0, 1)

    ids = local(expert_ids)
    order = local(priority)
    weight = local(route_weight)
    position = z * seg + jnp.arange(seg, dtype=jnp.int32)
    live = (position[None, :] < seq_lengths[:, None]).reshape(tokens)
    match = ids.T[:, None, :] == jnp.arange(EXPERTS, dtype=jnp.int32)[None, :, None]
    weight_e = jnp.sum(jnp.where(match, weight.T[:, None, :], 0.0), axis=0)
    chosen = jnp.any(match, axis=0) & live[None, :]
    earlier = (order[:, None] < order[None, :]).astype(BF)
    before = dot(chosen.astype(BF), earlier)
    slot = jnp.where(chosen & (before < cap), before, -1.0)
    packed = jnp.concatenate([slot.reshape(ne, here, tokens), weight_e.reshape(ne, here, tokens)], axis=1)
    tables = rotary_tables(nh * seg)
    x, grad = local(layer_input), local(out_grad)
    xf = x.astype(F32)
    gain_a, gain_m = attn_gain.reshape(1, width), moe_gain.reshape(1, width)
    fast = nh == 4 and ne == 8
    if fast:
        gathered, qkv, lse, heads_in, o_full, w_pieces, mid, pack, d_rows, x_rows = front(
            seq_lengths, x, grad, query_matrix, key_matrix, value_matrix, output_matrix, packed, gain_a, gain_m, tables, nh, nseq, cap)
        o_parts = o_full.reshape(nh, groups * 128, width)
    else:
        wq = query_matrix.reshape(width, groups, 128)
        wk = key_matrix.reshape(width, groups, HEAD)
        wv = value_matrix.reshape(width, groups, HEAD)
        w_local = jnp.concatenate([wq, wk, wv], axis=2).reshape(width, groups * 256)
        packed = lax.all_to_all(packed, "experts", split_axis=0, concat_axis=0, tiled=True)
        packed = packed[me ^ jnp.arange(ne, dtype=jnp.int32)]
        slots, weights = packed[:, :here].astype(jnp.int32), packed[:, here:]
        inv_one = lax.rsqrt(jnp.mean(xf * xf, axis=-1, keepdims=True) + EPS)
        attn_in = (xf * inv_one * attn_gain).astype(BF)
        gathered = lax.all_gather(attn_in.reshape(nseq, seg, width), "heads", axis=0)
        w_groups = jnp.transpose(w_local.reshape(width, groups, 256), (1, 0, 2))
        rows_in, rows_out = width // ne, output_matrix.shape[0] // ne
        w_piece = lax.dynamic_slice_in_dim(w_local, me * rows_in, rows_in, 0)
        o_piece = lax.dynamic_slice_in_dim(output_matrix, me * rows_out, rows_out, 0)
        o_full = lax.all_gather(o_piece, ("heads", "experts"), axis=0, tiled=True)
        w_full = lax.all_gather(w_piece, ("heads", "experts"), axis=0, tiled=True)
        w_full = w_full.reshape(nh, width, groups * 256)
        qkv, heads_out, lse = attn_forward(gathered, w_groups, seq_lengths, tables)
        heads_in = lax.all_to_all(heads_out, "heads", split_axis=0, concat_axis=0, tiled=True)
        heads_in = heads_in.reshape(nh, tokens, groups * 128)
        o_parts = o_full.reshape(nh, groups * 128, width)
        branch = jnp.einsum("ztm,zmw->tw", heads_in, o_parts, preferred_element_type=F32)
        mid = xf + branch
        inv_two = lax.rsqrt(jnp.mean(mid * mid, axis=-1, keepdims=True) + EPS)
        moe_in = (mid * inv_two * moe_gain).astype(BF)
        d_rows = gather_rows(slots, weights, plane_gather(grad, ne), cap)
        x_rows = gather_rows(slots, None, plane_gather(moe_in, ne), cap)

    if fast:
        chunks = expert_in.shape[0] * (width + expert_down.shape[1]) // CHUNK
        early, half = chunks // 8, (3 * chunks) // 8
        results, drows, sums, total = experts_send(early, pack, x_rows, d_rows, expert_in, expert_down)
        flat = sums.reshape(-1, width)
        total, d_mid, gain_two, dqkv, po, pw = middle(
            early, half, seq_lengths, total, flat, drows, pack, mid, grad, gain_m, o_parts, qkv, lse, tables,
            heads_in, gathered)
        total, out, x_grad, gains, o_grad, q_grad, k_grad, v_grad = last(
            early + half, chunks - early - half, total, flat, results, pack, mid, dqkv, w_pieces, x, d_mid, gain_a, gain_two, po, pw)
        gain_one, gain_two = gains[0], gains[1]
        grad_in, grad_down, o_grad, q_grad, k_grad, v_grad, x_grad = widen(
            total.reshape(sums.shape), expert_down.shape[1], (o_grad, q_grad, k_grad, v_grad),
            x_grad.reshape(nseq, seg, width))
    else:
        results, drows, sums = experts_call(slots, weights, x_rows, d_rows, expert_in, expert_down)
        slots_t = jnp.swapaxes(slots, 1, 2)
        d_parts = combine(slots_t, drows)
        moe_parts = combine(slots_t, results)
        totals = heads_sum(sums, z, nh)
        grad_in, grad_down = totals[:, :width], totals[:, width:]
        d_moe = plane_scatter(d_parts, ne)
        moe_sum = plane_scatter(moe_parts, ne)
        out = (mid + moe_sum).astype(BF)
        zed = moe_gain * d_moe
        d_mid = grad.astype(F32) + inv_two * zed - mid * (inv_two ** 3 * jnp.mean(zed * mid, axis=-1, keepdims=True))
        gain_two = jnp.sum(d_moe * mid * inv_two, axis=0)
        d_branch = d_mid.astype(BF)
        d_heads = jnp.einsum("tw,zmw->ztm", d_branch, o_parts, preferred_element_type=F32).astype(BF)
        d_heads = d_heads.reshape(nh, nseq, seg, groups * 128)
        d_heads = lax.all_to_all(d_heads, "heads", split_axis=0, concat_axis=0, tiled=True)
        dqkv = attn_backward(qkv, d_heads, lse, seq_lengths, tables)
        dqkv = dqkv.reshape(nh, tokens, groups * 256)
        back = lax.all_to_all(dqkv, "heads", split_axis=0, concat_axis=0, tiled=True)
        d_attn = jnp.einsum("ztc,zmc->tm", back, w_full, preferred_element_type=F32)
        o_grad, w_grad = weight_sums(heads_in, d_branch, gathered, dqkv, ne)
        wed = attn_gain * d_attn
        x_grad = d_mid + inv_one * wed - xf * (inv_one ** 3 * jnp.mean(wed * xf, axis=-1, keepdims=True))
        gain_one = jnp.sum(d_attn * xf * inv_one, axis=0)
        gain_one, gain_two = lax.psum((gain_one, gain_two), ("heads", "experts"))
        w_grad = w_grad.reshape(width, groups, 256)
        q_grad = w_grad[:, :, :128].reshape(query_matrix.shape)
        k_grad = w_grad[:, :, 128:192].reshape(key_matrix.shape)
        v_grad = w_grad[:, :, 192:].reshape(value_matrix.shape)
    return (
        unlocal(out),
        x_grad if fast else unlocal(x_grad),
        gain_one,
        gain_two,
        q_grad,
        k_grad,
        v_grad,
        o_grad,
        grad_in,
        grad_down,
    )


def solution(mesh):
    rows = P("heads", "experts", None)
    in_specs = (
        rows,
        P("experts"),
        rows,
        rows,
        P("heads", "experts"),
        P(),
        P(),
        P(None, "heads"),
        P(None, "heads"),
        P(None, "heads"),
        P("heads", None),
        P("experts", None, None),
        P("experts", None, None),
        rows,
    )
    out_specs = (
        rows,
        rows,
        P(),
        P(),
        P(None, "heads"),
        P(None, "heads"),
        P(None, "heads"),
        P("heads", None),
        P("experts", None, None),
        P("experts", None, None),
    )
    return jax.shard_map(body, mesh=mesh, in_specs=in_specs, out_specs=out_specs, check_vma=False)
```
